32 devices in a mesh: ctx: 16 (over z, y, x), tp: 2 (over core).
Axes of the slice: x: 2, y: 2, z: 4, core: 2. Of those that a mesh axis runs over, the one named last changes fastest.
Arguments:
- hyena_q: bfloat16 [4096, 4096], P('ctx', 'tp'), may hold values from -6 to 6
- hyena_k: bfloat16 [4096, 4096], P('ctx', 'tp'), may hold values from -6 to 6
- hyena_v: bfloat16 [4096, 4096], P('ctx', 'tp'), may hold values from -6 to 6
- filters: bfloat16 [256, 128], P('tp'), may hold values from -0.5 to 0.5
- direct: bfloat16 [4096], P('tp'), may hold values from -4 to 4
- queries: bfloat16 [4096, 2048], P('ctx', 'tp'), may hold values from -64 to 64
- keys: bfloat16 [4096, 2048], P('ctx', 'tp'), may hold values from -4 to 4
- values: bfloat16 [4096, 2048], P('ctx', 'tp'), may hold values from -6 to 6
- segment_ids: int32 [4096], P('ctx'), may hold values from 0 to 7, never falling along the last dimension, each value on 1 to 1793 neighbouring positions
- out_weight: bfloat16 [2048, 4096], P(None, 'tp'), may hold values from -0.125 to 0.125
Outputs:
- hyena_out: bfloat16 [4096, 4096], P('ctx', 'tp')
- attn_out: bfloat16 [4096, 4096], P('ctx', 'tp')
The draws below stay inside these ranges and needn't reach their ends.
Inputs may be any that keep to these rules, and one draw needn't show every extreme that they name: `segment_ids`: ids never fall along the sequence; each document holds 1 to 1793 tokens and one holds exactly 1793.
All inputs are finite; a program needn't handle non-finite values.
Results may differ from the reference program's by a relative error of at most 0.006.
Values may be sent and summed in bfloat16 or wider, within the bound.
No kernel may reach another device: no remote copies, remote signals or barrier semaphores. Data moves between devices by JAX's collectives and lax.ppermute only.
A program may use at most 64 MiB of HBM per device.

```python
import math
import jax
import jax.numpy as jnp
import numpy as np
from jax import lax

D = 4096
HD = 128
KERNEL = 128
GROUP = 16
HEADS = 16
TOK_DEV = 256
WINDOW = 8
TOKENS = 4096
FEAT = 2048
GROUPS = 256
MAXDOC = 1793
DOCS = 8
N_CTX = 16


def query_key_pair(key):
    base = jax.random.fold_in(key, 4242)
    shape = (TOKENS, FEAT)
    keys = jnp.clip(jax.random.normal(jax.random.fold_in(base, 1), shape, jnp.float32), -4.0, 4.0)
    queries = jnp.clip(2.0 * jax.random.normal(jax.random.fold_in(base, 2), shape, jnp.float32), -8.0, 8.0)
    return (queries, keys)


def draw_queries(key, part):
    return query_key_pair(key)[0].astype(jnp.bfloat16)


def draw_keys(key, part):
    return query_key_pair(key)[1].astype(jnp.bfloat16)


def levels(stream_key, dims, cuts, low, top_value):
    level, own = 1.0, jax.random.fold_in(stream_key, 6)
    for dim, blocks in cuts:
        heights = jnp.exp(jax.random.uniform(jax.random.fold_in(own, dim), (blocks,), jnp.float32, low / len(cuts), top_value / len(cuts)))
        level = level * jnp.repeat(heights, dims[dim] // blocks).reshape([-1 if axis == dim else 1 for axis in range(len(dims))])
    return level


def length_profile(amount, total, bound, skew):
    weights = [(1 << 20) // math.isqrt(standing ** skew) + 1 for standing in range(2, amount + 1)]
    surplus, given = total - bound - (amount - 1), [1] * (amount - 1)
    while surplus > 0:
        free = [i for i in range(amount - 1) if given[i] < bound]
        pool, budget = sum([weights[i] for i in free]), surplus
        for i in free:
            more = min(bound - given[i], max(1, budget * weights[i] // pool), surplus)
            given[i] = given[i] + more
            surplus = surplus - more
    return np.array([bound] + given)


def uneven(own_key, number_of, total, most, lean):
    if number_of == 2:
        one = jax.random.randint(own_key, (), max(1, total - most), min(most, total - 1) + 1)
        return jnp.stack([one, total - one])
    lengths = jnp.asarray(length_profile(number_of, total, most, lean), jnp.int32)
    pairs = (number_of - 1) // 2
    giver, sink = lengths[1:1 + 2 * pairs:2], lengths[2:2 + 2 * pairs:2]
    room = jnp.minimum(giver - 1, most - sink)
    passed = jax.random.randint(jax.random.fold_in(own_key, 1), (pairs,), 0, 1 << 20) % (room + 1)
    lengths = lengths.at[1:1 + 2 * pairs:2].set(giver - passed).at[2:2 + 2 * pairs:2].set(sink + passed)
    return lengths[jax.random.permutation(jax.random.fold_in(own_key, 2), number_of)]


def normal_values(rng, extent, scale, most, split=(), held_as=jnp.bfloat16):
    result = jax.random.normal(rng, extent, jnp.float32) * scale
    if len(split) > 0:
        result = levels(rng, extent, split, -0.22, 0.18) * result
    return jnp.clip(result, min=-most, max=most).astype(held_as)


def setup_inputs(seed: int = 0) -> dict:
    seeds = jax.random.split(jax.random.key(seed), 11)
    hyena_q = normal_values(seeds[0], (TOKENS, D), 1.0, 6.0, ((0, 16), (1, 2)))
    hyena_k = normal_values(seeds[1], (TOKENS, D), 1.0, 6.0, ((0, 16), (1, 2)))
    hyena_v = normal_values(seeds[2], (TOKENS, D), 1.0, 6.0, ((0, 16), (1, 2)))
    filters = normal_values(seeds[3], (GROUPS, KERNEL), KERNEL ** -0.5, 0.5, ((0, 2),))
    direct = normal_values(seeds[4], (D,), 1.0, 4.0, ((0, 2),))
    queries = draw_queries(jax.random.fold_in(seeds[10], 71), 0)
    keys = draw_keys(jax.random.fold_in(seeds[10], 71), 0)
    values = normal_values(seeds[7], (TOKENS, FEAT), 1.0, 6.0, ((0, 16), (1, 2)))
    segment_ids = jnp.searchsorted(jnp.cumsum(uneven(seeds[8], DOCS, TOKENS, MAXDOC, 2)), jnp.arange(TOKENS), side="right").astype(jnp.int32)
    out_weight = normal_values(seeds[9], (FEAT, D), FEAT ** -0.5, 0.125, ((1, 2),))
    return dict(hyena_q=hyena_q, hyena_k=hyena_k, hyena_v=hyena_v, filters=filters, direct=direct, queries=queries, keys=keys, values=values, segment_ids=segment_ids, out_weight=out_weight)


NEG = -1e+30

def toeplitz(filters, rows):
    kernel = filters.shape[1]
    span = rows + kernel - 1
    flipped = filters[:, ::-1].astype(jnp.float32)
    padded = jnp.concatenate([flipped, jnp.zeros((filters.shape[0], span + 1 - kernel), jnp.float32)], axis=1)
    tiled = jnp.tile(padded, (1, rows))[:, :rows * span]
    return tiled.reshape(filters.shape[0], rows, span)

def reference(hyena_q, hyena_k, hyena_v, filters, direct, queries, keys, values, segment_ids, out_weight):
    mixed = (hyena_k.astype(jnp.float32) * hyena_v.astype(jnp.float32)).astype(jnp.bfloat16)
    mixed = lax.optimization_barrier(mixed)
    table = toeplitz(filters, KERNEL)
    padded = jnp.concatenate([jnp.zeros((KERNEL - 1, D), jnp.bfloat16), mixed], axis=0)

    def conv_block(index):
        window = lax.dynamic_slice_in_dim(padded, (index * KERNEL).astype(jnp.int32), 2 * KERNEL - 1, 0)
        window = window.reshape(2 * KERNEL - 1, GROUPS, GROUP).astype(jnp.float32)
        return jnp.einsum('gts,sgc->tgc', table, window).reshape(KERNEL, D)
    conv = lax.map(conv_block, jnp.arange(TOKENS // KERNEL, dtype=jnp.int32)).reshape(TOKENS, D)
    hyena_out = (hyena_q.astype(jnp.float32) * (conv + direct.astype(jnp.float32) * mixed.astype(jnp.float32))).astype(jnp.bfloat16)
    reach = (WINDOW - 1) * TOK_DEV
    key_pad = jnp.concatenate([jnp.zeros((reach, FEAT), jnp.bfloat16), keys], axis=0)
    value_pad = jnp.concatenate([jnp.zeros((reach, FEAT), jnp.bfloat16), values], axis=0)
    seg_pad = jnp.concatenate([jnp.full((reach,), -1, jnp.int32), segment_ids], axis=0)
    query_pos = jnp.arange(TOK_DEV, dtype=jnp.int32) + reach
    key_pos = jnp.arange(WINDOW * TOK_DEV, dtype=jnp.int32)
    causal = key_pos[None, :] <= query_pos[:, None]

    def attend(index):
        start = (index * TOK_DEV).astype(jnp.int32)
        query_blk = lax.dynamic_slice_in_dim(queries, start, TOK_DEV, 0).reshape(TOK_DEV, HEADS, HD).astype(jnp.float32)
        key_blk = lax.dynamic_slice_in_dim(key_pad, start, WINDOW * TOK_DEV, 0).reshape(WINDOW * TOK_DEV, HEADS, HD).astype(jnp.float32)
        value_blk = lax.dynamic_slice_in_dim(value_pad, start, WINDOW * TOK_DEV, 0).reshape(WINDOW * TOK_DEV, HEADS, HD).astype(jnp.float32)
        query_seg = lax.dynamic_slice_in_dim(segment_ids, start, TOK_DEV, 0)
        key_seg = lax.dynamic_slice_in_dim(seg_pad, start, WINDOW * TOK_DEV, 0)
        allowed = (query_seg[:, None] == key_seg[None, :]) & causal
        score = jnp.einsum('qhd,khd->hqk', query_blk, key_blk) / jnp.sqrt(jnp.float32(HD))
        score = jnp.where(allowed[None], score, NEG)
        highest = lax.optimization_barrier(jnp.max(score, axis=-1, keepdims=True))
        expo = jnp.exp(score - highest)
        total = lax.optimization_barrier(jnp.sum(expo, axis=-1))
        weight = lax.optimization_barrier(expo.astype(jnp.bfloat16))
        summed = jnp.einsum('hqk,khd->qhd', weight.astype(jnp.float32), value_blk)
        return (summed / total.T[:, :, None]).reshape(TOK_DEV, FEAT).astype(jnp.bfloat16)
    attn = lax.map(attend, jnp.arange(N_CTX, dtype=jnp.int32)).reshape(TOKENS, FEAT)
    attn_out = jnp.dot(attn, out_weight, preferred_element_type=jnp.float32).astype(jnp.bfloat16)
    return (hyena_out, attn_out)
```

```python
import functools
import math

import jax
import jax.numpy as jnp
from jax import lax
from jax.experimental import pallas as pl
from jax.experimental.pallas import tpu as pltpu
from jax.sharding import PartitionSpec as P

HD = 128
SQUAD = 4
CHUNKS = 2
NEG = -1e30
LANES = 128
VMEM_LIMIT = 32 * 1024 * 1024


def pair_list(count, mask):
    return [(i, i ^ mask) for i in range(count)]


def lse_rows(heads):
    return -(-3 * heads // 16) * 16


def hyena_kernel(q_ref, k_ref, v_ref, rim_ref, taps_ref, direct_ref, out_ref):
    rows, width = q_ref.shape
    per_tile = taps_ref.shape[0] * LANES // width
    group = LANES // per_tile
    windows = rows // LANES
    lane_group = lax.broadcasted_iota(jnp.int32, (LANES, windows * LANES), 1) % LANES // group
    for tile in range(width // LANES):
        cols = slice(tile * LANES, (tile + 1) * LANES)
        mixed = (k_ref[:, cols].astype(jnp.float32) * v_ref[:, cols].astype(jnp.float32)).astype(
            jnp.bfloat16
        )
        full = jnp.concatenate([rim_ref[:, cols], mixed], axis=0)
        stacked = jnp.concatenate(
            [full[w * LANES : (w + 2) * LANES] for w in range(windows)], axis=1
        )
        conv = jnp.zeros((LANES, windows * LANES), jnp.float32)
        for g in range(per_tile):
            row = taps_ref[pl.ds(tile * per_tile + g, 1), :]
            table = pltpu.roll(
                jnp.broadcast_to(row, (LANES, 2 * LANES)), 0, 1, stride=1, stride_axis=0
            ).astype(jnp.bfloat16)
            part = jnp.dot(table, stacked, preferred_element_type=jnp.float32)
            conv = jnp.where(lane_group == g, part, conv)
        conv = jnp.concatenate(
            [conv[:, w * LANES : (w + 1) * LANES] for w in range(windows)], axis=0
        )
        out_ref[:, cols] = (
            q_ref[:, cols].astype(jnp.float32)
            * (conv + direct_ref[:, cols] * mixed.astype(jnp.float32))
        ).astype(jnp.bfloat16)


def hyena(hyena_q, hyena_k, hyena_v, rim, filters, direct):
    rows, chans = hyena_q.shape
    groups, kernel = filters.shape
    taps = jnp.zeros((groups, 2 * LANES), jnp.float32)
    taps = taps.at[:, LANES + 1 - kernel : LANES + 1].set(filters[:, ::-1].astype(jnp.float32))
    block = 2 * LANES
    steps = chans // block
    wide = pl.BlockSpec((rows, block), lambda i: (0, i))
    return pl.pallas_call(
        hyena_kernel,
        grid=(steps,),
        in_specs=[
            wide,
            wide,
            wide,
            pl.BlockSpec((LANES, block), lambda i: (0, i)),
            pl.BlockSpec((groups // steps, 2 * LANES), lambda i: (i, 0)),
            pl.BlockSpec((1, block), lambda i: (0, i)),
        ],
        out_specs=wide,
        out_shape=jax.ShapeDtypeStruct((rows, chans), jnp.bfloat16),
        compiler_params=pltpu.CompilerParams(vmem_limit_bytes=VMEM_LIMIT),
        cost_estimate=pl.CostEstimate(
            flops=4 * rows * chans * 2 * LANES * 8,
            bytes_accessed=10 * rows * chans,
            transcendentals=0,
        ),
        name="hyena",
    )(hyena_q, hyena_k, hyena_v, rim, taps, direct.astype(jnp.float32)[None])


def attention_kernel(
    place_ref, seg_ref, q0, q1, q2, q3, own_ref, near_ref, far_ref, p0, p1, p2, p3, kv, bias
):
    rows, width = q0.shape
    heads = width // HD
    me = place_ref[0]
    corner = lax.rem(me, SQUAD)
    kv[0] = own_ref[...]
    kv[1] = far_ref[...]

    def seg_row(index):
        row = seg_ref[pl.ds(jnp.maximum(index, 0), 1), :]
        return jnp.where(index >= 0, row, -1.0)

    def seg_col(index):
        return jnp.broadcast_to(seg_row(index), (LANES, rows)).T

    factor = math.log2(math.e) / math.sqrt(HD)
    near_col = seg_col(me - SQUAD)
    older = lax.broadcasted_iota(jnp.int32, (rows, rows), 0) <= lax.broadcasted_iota(
        jnp.int32, (rows, rows), 1
    )
    tiles = rows // LANES
    for k, (q_ref, p_ref) in enumerate(zip((q0, q1, q2, q3), (p0, p1, p2, p3))):
        target = jnp.bitwise_xor(corner, k)
        late = target < corner
        query_seg = jnp.broadcast_to(seg_row(me - corner + target), (rows, rows))
        key_col = seg_col(jnp.where(late, me - 2 * SQUAD, me))
        allowed = jnp.concatenate([key_col] * tiles, axis=1) == query_seg
        if k == 0:
            allowed = allowed & older
        bias[0] = jnp.where(allowed, 0.0, NEG)
        allowed = jnp.concatenate([near_col] * tiles, axis=1) == query_seg
        bias[1] = jnp.where(allowed, 0.0, NEG)
        which = late.astype(jnp.int32)
        stats = []
        for h in range(heads):
            cols = slice(h * HD, (h + 1) * HD)
            query = q_ref[:, cols]

            def score(keys):
                return lax.dot_general(
                    keys, query, (((1,), (1,)), ((), ())), preferred_element_type=jnp.float32
                )

            first = score(kv[which, :rows, cols]) + bias[0]
            second = score(near_ref[:rows, cols]) + bias[1]
            high = jnp.maximum(
                jnp.max(first, axis=0, keepdims=True), jnp.max(second, axis=0, keepdims=True)
            )
            first = jnp.exp2((first - high) * factor)
            second = jnp.exp2((second - high) * factor)
            total = jnp.sum(first, axis=0, keepdims=True) + jnp.sum(second, axis=0, keepdims=True)

            def mix(values, weight):
                return lax.dot_general(
                    values,
                    weight.astype(jnp.bfloat16),
                    (((0,), (0,)), ((), ())),
                    preferred_element_type=jnp.float32,
                )

            summed = mix(kv[which, rows:, cols], first) + mix(near_ref[rows:, cols], second)
            p_ref[cols, :] = (summed / total).astype(p_ref.dtype)
            lse = high * factor + jnp.log2(total)
            if k == 0:
                stats += [lse, jnp.zeros_like(lse), jnp.zeros_like(lse)]
            else:
                top = lse.astype(jnp.bfloat16).astype(jnp.float32)
                mid = (lse - top).astype(jnp.bfloat16).astype(jnp.float32)
                stats += [top, mid, lse - top - mid]
        spare = lse_rows(heads) - len(stats)
        if spare:
            stats.append(jnp.zeros((spare, rows), jnp.float32))
        p_ref[width:, :] = jnp.concatenate(stats, axis=0).astype(p_ref.dtype)


def attention(place, segs, queries, own, near, far, rows, width):
    tall = width + lse_rows(width // HD)
    shapes = [jax.ShapeDtypeStruct((tall, rows), jnp.float32)] + [
        jax.ShapeDtypeStruct((tall, rows), jnp.bfloat16)
    ] * (SQUAD - 1)
    vmem = pl.BlockSpec(memory_space=pltpu.VMEM)
    pairs = 2 * SQUAD * rows * rows * width
    return pl.pallas_call(
        attention_kernel,
        in_specs=[pl.BlockSpec(memory_space=pltpu.SMEM)] + [vmem] * (1 + SQUAD + 3),
        out_specs=[vmem] * SQUAD,
        out_shape=shapes,
        scratch_shapes=[
            pltpu.VMEM((2, 2 * rows, width), jnp.bfloat16),
            pltpu.VMEM((2, rows, rows), jnp.float32),
        ],
        compiler_params=pltpu.CompilerParams(vmem_limit_bytes=VMEM_LIMIT),
        cost_estimate=pl.CostEstimate(
            flops=4 * pairs, bytes_accessed=12 * rows * width * 2, transcendentals=pairs // HD
        ),
        name="attention",
    )(place, segs, *queries, own, near, far)


def merge_kernel(p0, p1, p2, p3, out_ref):
    rows, width = out_ref.shape
    parts = (p0, p1, p2, p3)
    stats = [p[width:, :].astype(jnp.float32) for p in parts]
    for h in range(width // HD):
        lse = [s[3 * h : 3 * h + 1] + s[3 * h + 1 : 3 * h + 2] + s[3 * h + 2 : 3 * h + 3] for s in stats]
        high = functools.reduce(jnp.maximum, lse)
        share = [jnp.exp2(x - high) for x in lse]
        total = functools.reduce(jnp.add, share)
        cols = slice(h * HD, (h + 1) * HD)
        mixed = functools.reduce(
            jnp.add, [p[cols, :].astype(jnp.float32) * (w / total) for p, w in zip(parts, share)]
        )
        out_ref[:, cols] = mixed.T.astype(out_ref.dtype)


def merge(parts, rows, width):
    vmem = pl.BlockSpec(memory_space=pltpu.VMEM)
    return pl.pallas_call(
        merge_kernel,
        in_specs=[vmem] * SQUAD,
        out_specs=vmem,
        out_shape=jax.ShapeDtypeStruct((rows, width), jnp.bfloat16),
        compiler_params=pltpu.CompilerParams(vmem_limit_bytes=VMEM_LIMIT),
        cost_estimate=pl.CostEstimate(
            flops=8 * rows * width, bytes_accessed=12 * rows * width, transcendentals=0
        ),
        name="merge",
    )(*parts)


def project_kernel(ranks, chunks, place_ref, *refs):
    parts, weight_ref, out_ref = refs[:-2], refs[-2], refs[-1]
    mine = place_ref[1]
    total = None
    width = parts[0].shape[1]
    for r in range(ranks):
        source = lax.rem(mine + ranks - r, ranks)
        for c in range(chunks):
            begin = pl.multiple_of((source * chunks + c) * width, width)
            term = jnp.dot(
                parts[r * chunks + c][...],
                weight_ref[pl.ds(begin, width), :],
                preferred_element_type=jnp.float32,
            )
            total = term if total is None else total + term
    out_ref[...] = total.astype(out_ref.dtype)


def project(place, parts, out_weight, ranks, chunks):
    rows, width = parts[0].shape
    feat, cols = out_weight.shape
    block = 512
    return pl.pallas_call(
        functools.partial(project_kernel, ranks, chunks),
        grid=(cols // block,),
        in_specs=[pl.BlockSpec(memory_space=pltpu.SMEM)]
        + [pl.BlockSpec((rows, width), lambda i: (0, 0))] * len(parts)
        + [pl.BlockSpec((feat, block), lambda i: (0, i))],
        out_specs=pl.BlockSpec((rows, block), lambda i: (0, i)),
        out_shape=jax.ShapeDtypeStruct((rows, cols), jnp.bfloat16),
        compiler_params=pltpu.CompilerParams(vmem_limit_bytes=VMEM_LIMIT),
        cost_estimate=pl.CostEstimate(
            flops=2 * rows * feat * cols, bytes_accessed=2 * feat * cols, transcendentals=0
        ),
        name="project",
    )(place, *parts, out_weight)


def local(
    hyena_q, hyena_k, hyena_v, filters, direct, queries, keys, values, segment_ids, out_weight
):
    rows, feat = queries.shape
    count, ranks = lax.axis_size("ctx"), lax.axis_size("tp")
    width = feat // CHUNKS
    spans = [slice(c * width, (c + 1) * width) for c in range(CHUNKS)]
    place = jnp.stack([lax.axis_index("ctx"), lax.axis_index("tp")]).astype(jnp.int32)
    segs = lax.all_gather(segment_ids, "ctx").astype(jnp.float32)

    up = [(i, i + SQUAD) for i in range(count - SQUAD)]
    onward = [(i, i + SQUAD) for i in range(SQUAD, count - SQUAD) if i % SQUAD]
    own = [jnp.concatenate([keys[:, s], values[:, s]], axis=0) for s in spans]
    near = [lax.ppermute(x, "ctx", up) for x in own]
    seen = [queries] + [lax.ppermute(queries, "ctx", pair_list(count, k)) for k in range(1, SQUAD)]
    far = [lax.ppermute(x, "ctx", onward) for x in near]

    tail_k = hyena_k[rows - LANES :].astype(jnp.float32)
    tail_v = hyena_v[rows - LANES :].astype(jnp.float32)
    rim = lax.ppermute(
        (tail_k * tail_v).astype(jnp.bfloat16), "ctx", [(i, i + 1) for i in range(count - 1)]
    )
    hyena_out = hyena(hyena_q, hyena_k, hyena_v, rim, filters, direct)

    gathered = [[] for _ in range(ranks)]
    for c, span in enumerate(spans):
        parts = attention(
            place, segs, [q[:, span] for q in seen], own[c], near[c], far[c], rows, width
        )
        parts = [parts[0]] + [
            lax.ppermute(parts[k], "ctx", pair_list(count, k)) for k in range(1, SQUAD)
        ]
        attn = merge(parts, rows, width)
        gathered[0].append(attn)
        for r in range(1, ranks):
            gathered[r].append(
                lax.ppermute(attn, "tp", [(t, (t + r) % ranks) for t in range(ranks)])
            )
    attn_out = project(place, sum(gathered, []), out_weight, ranks, CHUNKS)
    return (hyena_out, attn_out)


def solution(mesh):
    placed = (
        P("ctx", "tp"),
        P("ctx", "tp"),
        P("ctx", "tp"),
        P("tp", None),
        P("tp"),
        P("ctx", "tp"),
        P("ctx", "tp"),
        P("ctx", "tp"),
        P("ctx"),
        P(None, "tp"),
    )
    return jax.shard_map(
        local,
        mesh=mesh,
        in_specs=placed,
        out_specs=(P("ctx", "tp"), P("ctx", "tp")),
        check_vma=False,
    )
```

```python
import functools
import math

import jax
import jax.numpy as jnp
from jax import lax
from jax.experimental import pallas as pl
from jax.experimental.pallas import tpu as pltpu
from jax.sharding import PartitionSpec as P

HD = 128
SQUAD = 4
CHUNKS = 2
NEG = -1e30
TAG = 16
LANES = 128
VMEM_LIMIT = 32 * 1024 * 1024


def pair_list(count, mask):
    return [(i, i ^ mask) for i in range(count)]


def lse_rows(heads):
    return -(-3 * heads // 16) * 16


def hyena_kernel(q_ref, k_ref, v_ref, rim_ref, taps_ref, direct_ref, out_ref):
    rows, width = q_ref.shape
    per_tile = taps_ref.shape[0] * LANES // width
    group = LANES // per_tile
    windows = rows // LANES
    lane_group = lax.broadcasted_iota(jnp.int32, (LANES, windows * LANES), 1) % LANES // group
    for tile in range(width // LANES):
        cols = slice(tile * LANES, (tile + 1) * LANES)
        mixed = (k_ref[:, cols].astype(jnp.float32) * v_ref[:, cols].astype(jnp.float32)).astype(
            jnp.bfloat16
        )
        full = jnp.concatenate([rim_ref[:, cols], mixed], axis=0)
        stacked = jnp.concatenate(
            [full[w * LANES : (w + 2) * LANES] for w in range(windows)], axis=1
        )
        conv = jnp.zeros((LANES, windows * LANES), jnp.float32)
        for g in range(per_tile):
            row = taps_ref[pl.ds(tile * per_tile + g, 1), :]
            table = pltpu.roll(
                jnp.broadcast_to(row, (LANES, 2 * LANES)), 0, 1, stride=1, stride_axis=0
            ).astype(jnp.bfloat16)
            part = jnp.dot(table, stacked, preferred_element_type=jnp.float32)
            conv = jnp.where(lane_group == g, part, conv)
        conv = jnp.concatenate(
            [conv[:, w * LANES : (w + 1) * LANES] for w in range(windows)], axis=0
        )
        out_ref[:, cols] = (
            q_ref[:, cols].astype(jnp.float32)
            * (conv + direct_ref[:, cols] * mixed.astype(jnp.float32))
        ).astype(jnp.bfloat16)


def hyena(hyena_q, hyena_k, hyena_v, rim, filters, direct):
    rows, chans = hyena_q.shape
    groups, kernel = filters.shape
    taps = jnp.zeros((groups, 2 * LANES), jnp.float32)
    taps = taps.at[:, LANES + 1 - kernel : LANES + 1].set(filters[:, ::-1].astype(jnp.float32))
    block = 2 * LANES
    steps = chans // block
    wide = pl.BlockSpec((rows, block), lambda i: (0, i))
    return pl.pallas_call(
        hyena_kernel,
        grid=(steps,),
        in_specs=[
            wide,
            wide,
            wide,
            pl.BlockSpec((LANES, block), lambda i: (0, i)),
            pl.BlockSpec((groups // steps, 2 * LANES), lambda i: (i, 0)),
            pl.BlockSpec((1, block), lambda i: (0, i)),
        ],
        out_specs=wide,
        out_shape=jax.ShapeDtypeStruct((rows, chans), jnp.bfloat16),
        compiler_params=pltpu.CompilerParams(vmem_limit_bytes=VMEM_LIMIT),
        cost_estimate=pl.CostEstimate(
            flops=4 * rows * chans * 2 * LANES * 8,
            bytes_accessed=10 * rows * chans,
            transcendentals=0,
        ),
        name="hyena",
    )(hyena_q, hyena_k, hyena_v, rim, taps, direct.astype(jnp.float32)[None])


def attention_kernel(
    place_ref,
    q0,
    q1,
    q2,
    q3,
    id0,
    id1,
    id2,
    id3,
    own_ref,
    near_ref,
    far_ref,
    own_id,
    near_id,
    far_id,
    p0,
    p1,
    p2,
    p3,
    kv,
    bias,
):
    rows, width = q0.shape
    heads = width // HD
    corner = lax.rem(place_ref[0], SQUAD)
    kv[0] = own_ref[...]
    kv[1] = far_ref[...]
    tiles = rows // LANES

    def id_row(ref):
        block = ref[:, :LANES].astype(jnp.float32)
        return jnp.concatenate([block[t : t + 1] for t in range(tiles)], axis=1)

    def id_square(row):
        column = jnp.broadcast_to(row, (LANES, rows)).T
        return jnp.concatenate([column] * tiles, axis=1)

    factor = math.log2(math.e) / math.sqrt(HD)
    own_row, far_row = id_row(own_id), id_row(far_id)
    near_square = id_square(id_row(near_id))
    older = lax.broadcasted_iota(jnp.int32, (rows, rows), 0) <= lax.broadcasted_iota(
        jnp.int32, (rows, rows), 1
    )
    lates = []
    for k, id_ref in enumerate((id0, id1, id2, id3)):
        late = jnp.bitwise_xor(corner, k) < corner
        lates.append(late.astype(jnp.int32))
        query_ids = jnp.broadcast_to(id_row(id_ref), (rows, rows))
        allowed = id_square(jnp.where(late, far_row, own_row)) == query_ids
        if k == 0:
            allowed = allowed & older
        bias[k, 0] = jnp.where(allowed, 0.0, NEG)
        bias[k, 1] = jnp.where(near_square == query_ids, 0.0, NEG)
    stats = [[] for _ in range(SQUAD)]
    for h in range(heads):
        cols = slice(h * HD, (h + 1) * HD)
        for k, (q_ref, p_ref) in enumerate(zip((q0, q1, q2, q3), (p0, p1, p2, p3))):
            query = q_ref[:, cols]
            which = lates[k]

            def score(keys):
                return lax.dot_general(
                    keys, query, (((1,), (1,)), ((), ())), preferred_element_type=jnp.float32
                )

            first = score(kv[which, :rows, cols]) + bias[k, 0]
            second = score(near_ref[:rows, cols]) + bias[k, 1]
            high = jnp.maximum(
                jnp.max(first, axis=0, keepdims=True), jnp.max(second, axis=0, keepdims=True)
            )
            first = jnp.exp2((first - high) * factor)
            second = jnp.exp2((second - high) * factor)
            total = jnp.sum(first, axis=0, keepdims=True) + jnp.sum(second, axis=0, keepdims=True)

            def mix(values, weight):
                return lax.dot_general(
                    values,
                    weight.astype(jnp.bfloat16),
                    (((0,), (0,)), ((), ())),
                    preferred_element_type=jnp.float32,
                )

            summed = mix(kv[which, rows:, cols], first) + mix(near_ref[rows:, cols], second)
            p_ref[cols, :] = (summed / total).astype(p_ref.dtype)
            lse = high * factor + jnp.log2(total)
            if k == 0:
                stats[k] += [lse, jnp.zeros_like(lse), jnp.zeros_like(lse)]
            else:
                top = lse.astype(jnp.bfloat16).astype(jnp.float32)
                mid = (lse - top).astype(jnp.bfloat16).astype(jnp.float32)
                stats[k] += [top, mid, lse - top - mid]
    spare = lse_rows(heads) - 3 * heads
    for stat, p_ref in zip(stats, (p0, p1, p2, p3)):
        if spare:
            stat.append(jnp.zeros((spare, rows), jnp.float32))
        p_ref[width:, :] = jnp.concatenate(stat, axis=0).astype(p_ref.dtype)


def attention(place, queries, column, tagged, own, near, far):
    rows, width = queries[0].shape[0] - TAG, own.shape[1]
    tall = width + lse_rows(width // HD)
    shapes = [jax.ShapeDtypeStruct((tall, rows), jnp.float32)] + [
        jax.ShapeDtypeStruct((tall, rows), jnp.bfloat16)
    ] * (SQUAD - 1)
    pairs = 2 * SQUAD * rows * rows * width
    keyed = pl.BlockSpec((2 * rows, width), lambda i: (0, 0))
    return pl.pallas_call(
        attention_kernel,
        grid=(1,),
        in_specs=[pl.BlockSpec(memory_space=pltpu.SMEM)]
        + [pl.BlockSpec((rows, width), lambda i: (0, column))] * SQUAD
        + [pl.BlockSpec((TAG, LANES), lambda i: (rows // TAG, 0))] * SQUAD
        + [keyed] * 3
        + [pl.BlockSpec((TAG, LANES), lambda i: (2 * rows // TAG, 0))] * 3,
        out_specs=[pl.BlockSpec((tall, rows), lambda i: (0, 0))] * SQUAD,
        out_shape=shapes,
        scratch_shapes=[
            pltpu.VMEM((2, 2 * rows, width), jnp.bfloat16),
            pltpu.VMEM((SQUAD, 2, rows, rows), jnp.float32),
        ],
        compiler_params=pltpu.CompilerParams(vmem_limit_bytes=VMEM_LIMIT),
        cost_estimate=pl.CostEstimate(
            flops=4 * pairs, bytes_accessed=12 * rows * width * 2, transcendentals=pairs // HD
        ),
        name="attention",
    )(place, *queries, *queries, own, near, far, *tagged)


def merge_kernel(p0, p1, p2, p3, out_ref):
    rows, width = out_ref.shape
    parts = (p0, p1, p2, p3)
    stats = [p[width:, :].astype(jnp.float32) for p in parts]
    for h in range(width // HD):
        lse = [s[3 * h : 3 * h + 1] + s[3 * h + 1 : 3 * h + 2] + s[3 * h + 2 : 3 * h + 3] for s in stats]
        high = functools.reduce(jnp.maximum, lse)
        share = [jnp.exp2(x - high) for x in lse]
        total = functools.reduce(jnp.add, share)
        cols = slice(h * HD, (h + 1) * HD)
        mixed = functools.reduce(
            jnp.add, [p[cols, :].astype(jnp.float32) * (w / total) for p, w in zip(parts, share)]
        )
        out_ref[:, cols] = mixed.T.astype(out_ref.dtype)


def merge(parts, rows, width):
    vmem = pl.BlockSpec(memory_space=pltpu.VMEM)
    return pl.pallas_call(
        merge_kernel,
        in_specs=[vmem] * SQUAD,
        out_specs=vmem,
        out_shape=jax.ShapeDtypeStruct((rows, width), jnp.bfloat16),
        compiler_params=pltpu.CompilerParams(vmem_limit_bytes=VMEM_LIMIT),
        cost_estimate=pl.CostEstimate(
            flops=8 * rows * width, bytes_accessed=12 * rows * width, transcendentals=0
        ),
        name="merge",
    )(*parts)


def project_kernel(ranks, chunks, place_ref, *refs):
    parts, weight_ref, out_ref = refs[:-2], refs[-2], refs[-1]
    mine = place_ref[1]
    total = None
    width = parts[0].shape[1]
    for r in range(ranks):
        source = lax.rem(mine + ranks - r, ranks)
        for c in range(chunks):
            begin = pl.multiple_of((source * chunks + c) * width, width)
            term = jnp.dot(
                parts[r * chunks + c][...],
                weight_ref[pl.ds(begin, width), :],
                preferred_element_type=jnp.float32,
            )
            total = term if total is None else total + term
    out_ref[...] = total.astype(out_ref.dtype)


def project(place, parts, out_weight, ranks, chunks):
    rows, width = parts[0].shape
    feat, cols = out_weight.shape
    block = 512
    return pl.pallas_call(
        functools.partial(project_kernel, ranks, chunks),
        grid=(cols // block,),
        in_specs=[pl.BlockSpec(memory_space=pltpu.SMEM)]
        + [pl.BlockSpec((rows, width), lambda i: (0, 0))] * len(parts)
        + [pl.BlockSpec((feat, block), lambda i: (0, i))],
        out_specs=pl.BlockSpec((rows, block), lambda i: (0, i)),
        out_shape=jax.ShapeDtypeStruct((rows, cols), jnp.bfloat16),
        compiler_params=pltpu.CompilerParams(vmem_limit_bytes=VMEM_LIMIT),
        cost_estimate=pl.CostEstimate(
            flops=2 * rows * feat * cols, bytes_accessed=2 * feat * cols, transcendentals=0
        ),
        name="project",
    )(place, *parts, out_weight)


def local(
    hyena_q, hyena_k, hyena_v, filters, direct, queries, keys, values, segment_ids, out_weight
):
    rows, feat = queries.shape
    count, ranks = lax.axis_size("ctx"), lax.axis_size("tp")
    width = feat // CHUNKS
    spans = [slice(c * width, (c + 1) * width) for c in range(CHUNKS)]
    place = jnp.stack([lax.axis_index("ctx"), lax.axis_index("tp")]).astype(jnp.int32)
    ids = (segment_ids + 1).astype(jnp.bfloat16).reshape(rows // LANES, LANES)

    def tagged(parts, wide):
        tag = jnp.pad(ids, ((0, TAG - ids.shape[0]), (0, wide - LANES)))
        return jnp.concatenate(parts + [tag], axis=0)

    up = [(i, i + SQUAD) for i in range(count - SQUAD)]
    onward = [(i, i + SQUAD) for i in range(SQUAD, count - SQUAD) if i % SQUAD]
    tail_k = hyena_k[rows - LANES :].astype(jnp.float32)
    tail_v = hyena_v[rows - LANES :].astype(jnp.float32)
    rim = lax.ppermute(
        (tail_k * tail_v).astype(jnp.bfloat16), "ctx", [(i, i + 1) for i in range(count - 1)]
    )
    own = [
        tagged([keys[:, s], values[:, s]], width)
        if c == 0
        else jnp.concatenate([keys[:, s], values[:, s]], axis=0)
        for c, s in enumerate(spans)
    ]
    asked = tagged([queries], feat)
    near = [lax.ppermute(x, "ctx", up) for x in own]
    seen = [asked] + [lax.ppermute(asked, "ctx", pair_list(count, k)) for k in range(1, SQUAD)]
    far = [lax.ppermute(x, "ctx", onward) for x in near]
    rim, *near = lax.optimization_barrier((rim, *near))
    hyena_out = hyena(hyena_q, hyena_k, hyena_v, rim, filters, direct)
    hyena_out, far[0] = lax.optimization_barrier((hyena_out, far[0]))

    gathered = [[] for _ in range(ranks)]
    for c in range(CHUNKS):
        parts = attention(place, seen, c, (own[0], near[0], far[0]), own[c], near[c], far[c])
        parts = [parts[0]] + [
            lax.ppermute(parts[k], "ctx", pair_list(count, k)) for k in range(1, SQUAD)
        ]
        attn = merge(parts, rows, width)
        gathered[0].append(attn)
        for r in range(1, ranks):
            gathered[r].append(
                lax.ppermute(attn, "tp", [(t, (t + r) % ranks) for t in range(ranks)])
            )
    attn_out = project(place, sum(gathered, []), out_weight, ranks, CHUNKS)
    return (hyena_out, attn_out)


def solution(mesh):
    placed = (
        P("ctx", "tp"),
        P("ctx", "tp"),
        P("ctx", "tp"),
        P("tp", None),
        P("tp"),
        P("ctx", "tp"),
        P("ctx", "tp"),
        P("ctx", "tp"),
        P("ctx"),
        P(None, "tp"),
    )
    return jax.shard_map(
        local,
        mesh=mesh,
        in_specs=placed,
        out_specs=(P("ctx", "tp"), P("ctx", "tp")),
        check_vma=False,
    )
```

```python
import functools
import math

import jax
import jax.numpy as jnp
from jax import lax
from jax.experimental import pallas as pl
from jax.experimental.pallas import tpu as pltpu
from jax.sharding import PartitionSpec as P

HD = 128
SQUAD = 4
NEG = -1e30
TAG = 16
LANES = 128
VMEM_LIMIT = 32 * 1024 * 1024
VMEM = pl.BlockSpec(memory_space=pltpu.VMEM)
SMEM = pl.BlockSpec(memory_space=pltpu.SMEM)


def corner_of(place_ref):
    return lax.rem(place_ref[0], SQUAD)


def kernel_call(kernel, args, shapes, name, scratch=(), flops=0, exps=0):
    total = sum(math.prod(x.shape) * x.dtype.itemsize for x in (*args, *shapes))
    return list(pl.pallas_call(
        kernel,
        in_specs=[SMEM] + [VMEM] * (len(args) - 1),
        out_specs=[VMEM] * len(shapes),
        out_shape=shapes,
        scratch_shapes=scratch,
        compiler_params=pltpu.CompilerParams(vmem_limit_bytes=VMEM_LIMIT),
        cost_estimate=pl.CostEstimate(flops=flops, bytes_accessed=total, transcendentals=exps),
        name=name,
    )(*args))


def hyena_kernel(q_ref, k_ref, v_ref, rim_ref, taps_ref, direct_ref, out_ref):
    rows, width = q_ref.shape
    per_tile = taps_ref.shape[0] * LANES // width
    group = LANES // per_tile
    windows = rows // LANES
    lane_group = lax.broadcasted_iota(jnp.int32, (LANES, windows * LANES), 1) % LANES // group
    for tile in range(width // LANES):
        cols = slice(tile * LANES, (tile + 1) * LANES)
        mixed = (k_ref[:, cols].astype(jnp.float32) * v_ref[:, cols].astype(jnp.float32)).astype(
            jnp.bfloat16
        )
        full = jnp.concatenate([rim_ref[:, cols], mixed], axis=0)
        stacked = jnp.concatenate(
            [full[w * LANES : (w + 2) * LANES] for w in range(windows)], axis=1
        )
        conv = jnp.zeros((LANES, windows * LANES), jnp.float32)
        for g in range(per_tile):
            row = taps_ref[pl.ds(tile * per_tile + g, 1), :]
            table = pltpu.roll(
                jnp.broadcast_to(row, (LANES, 2 * LANES)), 0, 1, stride=1, stride_axis=0
            ).astype(jnp.bfloat16)
            part = jnp.dot(table, stacked, preferred_element_type=jnp.float32)
            conv = jnp.where(lane_group == g, part, conv)
        conv = jnp.concatenate(
            [conv[:, w * LANES : (w + 1) * LANES] for w in range(windows)], axis=0
        )
        out_ref[:, cols] = (
            q_ref[:, cols].astype(jnp.float32)
            * (conv + direct_ref[:, cols] * mixed.astype(jnp.float32))
        ).astype(jnp.bfloat16)


def hyena(hyena_q, hyena_k, hyena_v, rim, filters, direct):
    rows, chans = hyena_q.shape
    groups, kernel = filters.shape
    taps = jnp.zeros((groups, 2 * LANES), jnp.float32)
    taps = taps.at[:, LANES + 1 - kernel : LANES + 1].set(filters[:, ::-1].astype(jnp.float32))
    block = 2 * LANES
    steps = chans // block
    wide = pl.BlockSpec((rows, block), lambda i: (0, i))
    return pl.pallas_call(
        hyena_kernel,
        grid=(steps,),
        in_specs=[
            wide,
            wide,
            wide,
            pl.BlockSpec((LANES, block), lambda i: (0, i)),
            pl.BlockSpec((groups // steps, 2 * LANES), lambda i: (i, 0)),
            pl.BlockSpec((1, block), lambda i: (0, i)),
        ],
        out_specs=wide,
        out_shape=jax.ShapeDtypeStruct((rows, chans), jnp.bfloat16),
        compiler_params=pltpu.CompilerParams(vmem_limit_bytes=VMEM_LIMIT),
        cost_estimate=pl.CostEstimate(
            flops=4 * rows * chans * 2 * LANES * 8,
            bytes_accessed=10 * rows * chans,
            transcendentals=0,
        ),
        name="hyena",
    )(hyena_q, hyena_k, hyena_v, rim, taps, direct.astype(jnp.float32)[None])


def deal_kernel(place_ref, q_ref, k_ref, v_ref, id_ref, *outs):
    rows, feat = q_ref.shape
    width = feat // SQUAD
    corner = corner_of(place_ref)
    ids = (id_ref[...] + 1).astype(jnp.float32)
    spare = jnp.zeros((TAG - ids.shape[0], LANES), jnp.float32)
    tag = jnp.concatenate([ids, spare], axis=0)
    tag = jnp.concatenate([tag] * (width // LANES), axis=1).astype(jnp.bfloat16)
    for k, out in enumerate(outs):
        cols = pl.ds(pl.multiple_of(jnp.bitwise_xor(corner, k) * width, width), width)
        out[:rows, :] = q_ref[:, cols]
        out[rows : rows + TAG, :] = tag
        out[rows + TAG : 2 * rows + TAG, :] = k_ref[:, cols]
        out[2 * rows + TAG :, :] = v_ref[:, cols]


def id_columns(tag_ref, rows):
    tag = tag_ref[:, :LANES].astype(jnp.float32)
    tiles = [jnp.broadcast_to(tag[t : t + 1], (LANES, LANES)).T for t in range(rows // LANES)]
    return jnp.concatenate(tiles, axis=0)


def place_keys(parts, corner, base, rows, keys, values):
    heads = keys.shape[0]
    marks = lax.broadcasted_iota(jnp.int32, (rows, LANES), 1).astype(jnp.float32) + 1.0
    for k, part in enumerate(parts):
        begin = pl.multiple_of((jnp.bitwise_xor(corner, k) + base) * rows, rows)
        span = pl.ds(begin, rows)
        ids = id_columns(part.at[:TAG], rows)
        mask = jnp.where(ids == marks, 0.0, -NEG).astype(jnp.bfloat16)
        for h in range(heads):
            cols = slice(h * HD, (h + 1) * HD)
            keys[h, span, :HD] = part[TAG : TAG + rows, cols]
            keys[h, span, HD:] = mask
            values[h, span, :] = part[TAG + rows : TAG + 2 * rows, cols]


def place_queries(parts, corner, rows, queries):
    heads = queries.shape[0]
    marks = lax.broadcasted_iota(jnp.int32, (rows, LANES), 1).astype(jnp.float32) + 1.0
    for k, part in enumerate(parts):
        begin = pl.multiple_of(jnp.bitwise_xor(corner, k) * rows, rows)
        span = pl.ds(begin, rows)
        ids = id_columns(part.at[rows : rows + TAG], rows)
        mask = jnp.where(ids == marks, -1.0, 0.0).astype(jnp.bfloat16)
        for h in range(heads):
            queries[h, span, :HD] = part[:rows, h * HD : (h + 1) * HD]
            queries[h, span, HD:] = mask


def attend(query, keys, values, diagonal):
    factor = math.log2(math.e) / math.sqrt(HD)
    rows = query.shape[0]
    score = lax.dot_general(
        keys, query, (((1,), (1,)), ((), ())), preferred_element_type=jnp.float32
    )
    if diagonal:
        older = lax.broadcasted_iota(jnp.int32, (rows, rows), 0) <= lax.broadcasted_iota(
            jnp.int32, (rows, rows), 1
        )
        score = jnp.concatenate(
            [score[:-rows], jnp.where(older, score[-rows:], NEG)], axis=0
        )
    high = jnp.max(score, axis=0, keepdims=True)
    expo = jnp.exp2((score - high) * factor)
    total = jnp.sum(expo, axis=0, keepdims=True)
    summed = lax.dot_general(
        values,
        expo.astype(jnp.bfloat16),
        (((0,), (0,)), ((), ())),
        preferred_element_type=jnp.float32,
    )
    return summed / total, high * factor + jnp.log2(total)


def main_kernel(place_ref, *refs):
    own, near, out, (queries, keys, values) = refs[:4], refs[4:8], refs[8], refs[9:]
    heads, span, _ = queries.shape
    rows = span // SQUAD
    width = heads * HD
    corner = corner_of(place_ref)
    place_queries([p.at[: rows + TAG] for p in own], corner, rows, queries)
    place_keys([p.at[rows:] for p in own], corner, SQUAD, rows, keys, values)
    place_keys(near, corner, 0, rows, keys, values)
    for j in range(SQUAD):
        cols = slice(j * rows, (j + 1) * rows)
        reach = (SQUAD + 1 + j) * rows
        for h in range(heads):
            mixed, lse = attend(queries[h, cols], keys[h, :reach], values[h, :reach], True)
            out[h * HD : (h + 1) * HD, cols] = mixed
            out[width + h : width + h + 1, cols] = lse
        out[width + heads :, cols] = jnp.zeros((TAG - heads, rows), jnp.float32)


def far_kernel(place_ref, *refs):
    asked, near, out, (queries, keys, values) = refs[0], refs[1:5], refs[5], refs[6:]
    heads, span, _ = queries.shape
    rows = span // SQUAD
    width = heads * HD
    corner = corner_of(place_ref)
    tall = rows + TAG
    place_queries(
        [asked.at[k * tall : (k + 1) * tall] for k in range(SQUAD)], corner, rows, queries
    )
    place_keys(near, corner, 0, rows, keys, values)
    for j in range(SQUAD - 1):
        cols = slice(j * rows, (j + 1) * rows)
        stats = []
        for h in range(heads):
            mixed, lse = attend(
                queries[h, cols], keys[h, cols.stop :], values[h, cols.stop :], False
            )
            out[h * HD : (h + 1) * HD, cols] = mixed.astype(out.dtype)
            top = lse.astype(jnp.bfloat16).astype(jnp.float32)
            mid = (lse - top).astype(jnp.bfloat16).astype(jnp.float32)
            stats += [top, mid, lse - top - mid]
        stats.append(jnp.zeros((TAG - len(stats), rows), jnp.float32))
        out[width:, cols] = jnp.concatenate(stats, axis=0).astype(out.dtype)


def merge_kernel(place_ref, main_ref, far_ref, *refs):
    outs, ready = refs[:-1], refs[-1]
    _, rows, width = ready.shape
    corner = corner_of(place_ref)
    served = place_ref[0] >= 2 * SQUAD
    for j in range(SQUAD):
        cols = slice(j * rows, (j + 1) * rows)
        for h in range(width // HD):
            feats = slice(h * HD, (h + 1) * HD)
            mixed = main_ref[feats, cols]
            if j < SQUAD - 1:
                here = main_ref[width + h : width + h + 1, cols]
                stats = far_ref[width:, cols].astype(jnp.float32)
                there = stats[3 * h : 3 * h + 1] + stats[3 * h + 1 : 3 * h + 2]
                there = jnp.where(served, there + stats[3 * h + 2 : 3 * h + 3], NEG)
                high = jnp.maximum(here, there)
                here, there = jnp.exp2(here - high), jnp.exp2(there - high)
                total = here + there
                mixed = mixed * (here / total) + far_ref[feats, cols].astype(jnp.float32) * (
                    there / total
                )
            ready[j, :, feats] = mixed.T.astype(ready.dtype)
    for k, out in enumerate(outs):
        out[...] = ready[jnp.bitwise_xor(corner, k)]


def project_kernel(ranks, place_ref, *refs):
    parts, weight_ref, out_ref = refs[:-2], refs[-2], refs[-1]
    mine, corner = place_ref[1], corner_of(place_ref)
    total = None
    width = parts[0].shape[1] // SQUAD
    for r, part in enumerate(parts):
        source = lax.rem(mine + ranks - r, ranks)
        for k in range(SQUAD):
            begin = (source * SQUAD + jnp.bitwise_xor(corner, k)) * width
            term = jnp.dot(
                part[:, k * width : (k + 1) * width],
                weight_ref[pl.ds(pl.multiple_of(begin, width), width), :],
                preferred_element_type=jnp.float32,
            )
            total = term if total is None else total + term
    out_ref[...] = total.astype(out_ref.dtype)


def project(place, parts, out_weight):
    rows, width = parts[0].shape
    feat, cols = out_weight.shape
    block = 512
    return pl.pallas_call(
        functools.partial(project_kernel, len(parts)),
        grid=(cols // block,),
        in_specs=[SMEM]
        + [pl.BlockSpec((rows, width), lambda i: (0, 0))] * len(parts)
        + [pl.BlockSpec((feat, block), lambda i: (0, i))],
        out_specs=pl.BlockSpec((rows, block), lambda i: (0, i)),
        out_shape=jax.ShapeDtypeStruct((rows, cols), jnp.bfloat16),
        compiler_params=pltpu.CompilerParams(vmem_limit_bytes=VMEM_LIMIT),
        cost_estimate=pl.CostEstimate(
            flops=2 * rows * feat * cols, bytes_accessed=2 * feat * cols, transcendentals=0
        ),
        name="project",
    )(place, *parts, out_weight)


def local(
    hyena_q, hyena_k, hyena_v, filters, direct, queries, keys, values, segment_ids, out_weight
):
    rows, feat = queries.shape
    count, ranks = lax.axis_size("ctx"), lax.axis_size("tp")
    width = feat // SQUAD
    heads = width // HD
    bf16, f32 = jnp.bfloat16, jnp.float32
    place = jnp.stack([lax.axis_index("ctx"), lax.axis_index("tp")]).astype(jnp.int32)

    def swap(value, mask):
        return lax.ppermute(value, "ctx", [(i, i ^ mask) for i in range(count)])

    def climb(value, first=0):
        return lax.ppermute(value, "ctx", [(i, i + SQUAD) for i in range(first, count - SQUAD)])

    dealt = kernel_call(
        deal_kernel,
        (place, queries, keys, values, segment_ids.reshape(rows // LANES, LANES)),
        [jax.ShapeDtypeStruct((3 * rows + TAG, width), bf16)] * SQUAD,
        "deal",
    )
    own = [dealt[0]] + [swap(dealt[k], k) for k in range(1, SQUAD)]
    near = [climb(x[rows:]) for x in own]
    asked = lax.ppermute(
        jnp.concatenate([x[: rows + TAG] for x in own], axis=0),
        "ctx",
        [(i, i - SQUAD) for i in range(2 * SQUAD, count)],
    )
    tail_k = hyena_k[rows - LANES :].astype(f32)
    tail_v = hyena_v[rows - LANES :].astype(f32)
    rim = lax.ppermute(
        (tail_k * tail_v).astype(bf16), "ctx", [(i, i + 1) for i in range(count - 1)]
    )

    def store(blocks):
        return [
            pltpu.VMEM((heads, SQUAD * rows, 2 * HD), bf16),
            pltpu.VMEM((heads, blocks * rows, 2 * HD), bf16),
            pltpu.VMEM((heads, blocks * rows, HD), bf16),
        ]

    (far,) = kernel_call(
        far_kernel,
        (place, asked, *near),
        [jax.ShapeDtypeStruct((width + TAG, (SQUAD - 1) * rows), bf16)],
        "far",
        store(SQUAD),
        flops=6 * 4 * rows * rows * width,
        exps=6 * rows * rows * heads,
    )
    far = climb(far, SQUAD)
    (main,) = kernel_call(
        main_kernel,
        (place, *own, *near),
        [jax.ShapeDtypeStruct((width + TAG, SQUAD * rows), f32)],
        "main",
        store(2 * SQUAD),
        flops=26 * 4 * rows * rows * width,
        exps=26 * rows * rows * heads,
    )
    done = kernel_call(
        merge_kernel,
        (place, main, far),
        [jax.ShapeDtypeStruct((rows, width), bf16)] * SQUAD,
        "merge",
        [pltpu.VMEM((SQUAD, rows, width), bf16)],
    )
    rim, done[0] = lax.optimization_barrier((rim, done[0]))
    hyena_out = hyena(hyena_q, hyena_k, hyena_v, rim, filters, direct)
    mixed = jnp.concatenate([done[0]] + [swap(done[k], k) for k in range(1, SQUAD)], axis=1)
    gathered = [mixed] + [
        lax.ppermute(mixed, "tp", [(t, (t + r) % ranks) for t in range(ranks)])
        for r in range(1, ranks)
    ]
    return (hyena_out, project(place, gathered, out_weight))


def solution(mesh):
    placed = (
        P("ctx", "tp"),
        P("ctx", "tp"),
        P("ctx", "tp"),
        P("tp", None),
        P("tp"),
        P("ctx", "tp"),
        P("ctx", "tp"),
        P("ctx", "tp"),
        P("ctx"),
        P(None, "tp"),
    )
    return jax.shard_map(
        local,
        mesh=mesh,
        in_specs=placed,
        out_specs=(P("ctx", "tp"), P("ctx", "tp")),
        check_vma=False,
    )
```

```python
import functools
import math

import jax
import jax.numpy as jnp
from jax import lax
from jax.experimental import pallas as pl
from jax.experimental.pallas import tpu as pltpu
from jax.sharding import PartitionSpec as P

HD = 128
SQUAD = 4
NEG = -1e30
TAG = 16
LANES = 128
VMEM_LIMIT = 32 * 1024 * 1024
ALL_VMEM = 62 * 1024 * 1024
VMEM = pl.BlockSpec(memory_space=pltpu.VMEM)
SMEM = pl.BlockSpec(memory_space=pltpu.SMEM)


def corner_of(place_ref):
    return lax.rem(place_ref[0], SQUAD)


def kernel_call(kernel, args, shapes, name, scratch=(), flops=0, exps=0):
    total = sum(math.prod(x.shape) * x.dtype.itemsize for x in (*args, *shapes))
    return list(pl.pallas_call(
        kernel,
        in_specs=[SMEM] + [VMEM] * (len(args) - 1),
        out_specs=[VMEM] * len(shapes),
        out_shape=shapes,
        scratch_shapes=scratch,
        compiler_params=pltpu.CompilerParams(vmem_limit_bytes=VMEM_LIMIT),
        cost_estimate=pl.CostEstimate(flops=flops, bytes_accessed=total, transcendentals=exps),
        name=name,
    )(*args))


def hyena_kernel(q_ref, k_ref, v_ref, rim_ref, taps_ref, direct_ref, out_ref):
    rows, width = q_ref.shape
    per_tile = taps_ref.shape[0] * LANES // width
    group = LANES // per_tile
    windows = rows // LANES
    shape = (LANES, 2 * LANES)
    turn = lax.broadcasted_iota(jnp.int32, shape, 0) + lax.broadcasted_iota(jnp.int32, shape, 1)
    turn = jnp.where(turn == LANES, 1.0, 0.0).astype(jnp.bfloat16)
    taps = jnp.dot(taps_ref[...], turn, preferred_element_type=jnp.float32)
    lane_group = lax.broadcasted_iota(jnp.int32, (LANES, windows * LANES), 1) % LANES // group
    for tile in range(width // LANES):
        cols = slice(tile * LANES, (tile + 1) * LANES)
        mixed = (k_ref[:, cols].astype(jnp.float32) * v_ref[:, cols].astype(jnp.float32)).astype(
            jnp.bfloat16
        )
        full = jnp.concatenate([rim_ref[:, cols], mixed], axis=0)
        stacked = jnp.concatenate(
            [full[w * LANES : (w + 2) * LANES] for w in range(windows)], axis=1
        )
        conv = jnp.zeros((LANES, windows * LANES), jnp.float32)
        for g in range(per_tile):
            at = tile * per_tile + g
            row = taps[at : at + 1]
            table = pltpu.roll(
                jnp.broadcast_to(row, (LANES, 2 * LANES)), 0, 1, stride=1, stride_axis=0
            ).astype(jnp.bfloat16)
            part = jnp.dot(table, stacked, preferred_element_type=jnp.float32)
            conv = jnp.where(lane_group == g, part, conv)
        conv = jnp.concatenate(
            [conv[:, w * LANES : (w + 1) * LANES] for w in range(windows)], axis=0
        )
        out_ref[:, cols] = (
            q_ref[:, cols].astype(jnp.float32)
            * (conv + direct_ref[:, cols].astype(jnp.float32) * mixed.astype(jnp.float32))
        ).astype(jnp.bfloat16)


def hyena(hyena_q, hyena_k, hyena_v, rim, filters, direct):
    rows, chans = hyena_q.shape
    groups, kernel = filters.shape
    taps = jnp.pad(filters, ((0, 0), (0, LANES - kernel)))
    block = 2 * LANES
    steps = chans // block
    wide = pl.BlockSpec((rows, block), lambda i: (0, i))
    return pl.pallas_call(
        hyena_kernel,
        grid=(steps,),
        in_specs=[
            wide,
            wide,
            wide,
            pl.BlockSpec((LANES, block), lambda i: (0, i)),
            pl.BlockSpec((groups // steps, LANES), lambda i: (i, 0)),
            pl.BlockSpec((1, block), lambda i: (0, i)),
        ],
        out_specs=wide,
        out_shape=jax.ShapeDtypeStruct((rows, chans), jnp.bfloat16),
        compiler_params=pltpu.CompilerParams(vmem_limit_bytes=VMEM_LIMIT),
        cost_estimate=pl.CostEstimate(
            flops=4 * rows * chans * 2 * LANES * 8,
            bytes_accessed=10 * rows * chans,
            transcendentals=0,
        ),
        name="hyena",
    )(hyena_q, hyena_k, hyena_v, rim, taps, direct[None])


def deal_kernel(place_ref, q_ref, k_ref, v_ref, id_ref, *refs):
    outs, (tag, sems) = refs[:SQUAD], refs[SQUAD:]
    rows, feat = q_ref.shape
    width = feat // SQUAD
    corner = corner_of(place_ref)
    ends = (0, rows, rows + TAG, 2 * rows + TAG, 3 * rows + TAG)
    copies = []
    for k, out in enumerate(outs):
        cols = pl.ds(pl.multiple_of(jnp.bitwise_xor(corner, k) * width, width), width)
        sources = (q_ref.at[:, cols], tag, k_ref.at[:, cols], v_ref.at[:, cols])
        copies += [
            pltpu.make_async_copy(source, out.at[pl.ds(begin, end - begin)], sems.at[k, i])
            for i, (source, begin, end) in enumerate(zip(sources, ends, ends[1:]))
        ]
    for i, copy in enumerate(copies):
        if i % 4 != 1:
            copy.start()
    ids = (id_ref[...] + 1).astype(jnp.float32)
    spare = jnp.zeros((TAG - ids.shape[0], LANES), jnp.float32)
    ids = jnp.concatenate([ids, spare], axis=0)
    tag[...] = jnp.concatenate([ids] * (width // LANES), axis=1).astype(jnp.bfloat16)
    for copy in copies[1::4]:
        copy.start()
    for copy in copies:
        copy.wait()


def deal(place, queries, keys, values, ids):
    rows, feat = queries.shape
    width = feat // SQUAD
    shape = jax.ShapeDtypeStruct((3 * rows + TAG, width), jnp.bfloat16)
    anywhere = pl.BlockSpec(memory_space=pl.ANY)
    return list(
        pl.pallas_call(
            deal_kernel,
            in_specs=[SMEM] + [anywhere] * 3 + [VMEM],
            out_specs=[anywhere] * SQUAD,
            out_shape=[shape] * SQUAD,
            scratch_shapes=[
                pltpu.VMEM((TAG, width), jnp.bfloat16),
                pltpu.SemaphoreType.DMA((SQUAD, 4)),
            ],
            compiler_params=pltpu.CompilerParams(vmem_limit_bytes=ALL_VMEM),
            cost_estimate=pl.CostEstimate(
                flops=0, bytes_accessed=12 * rows * feat, transcendentals=0
            ),
            name="deal",
        )(place, queries, keys, values, ids)
    )


def id_columns(tag_ref, rows):
    tag = tag_ref[:, :LANES].astype(jnp.float32)
    tiles = [jnp.broadcast_to(tag[t : t + 1], (LANES, LANES)).T for t in range(rows // LANES)]
    return jnp.concatenate(tiles, axis=0)


def place_keys(parts, corner, base, rows, keys, values):
    heads = keys.shape[0]
    marks = lax.broadcasted_iota(jnp.int32, (rows, LANES), 1).astype(jnp.float32) + 1.0
    for k, part in enumerate(parts):
        begin = pl.multiple_of((jnp.bitwise_xor(corner, k) + base) * rows, rows)
        span = pl.ds(begin, rows)
        ids = id_columns(part.at[:TAG], rows)
        mask = jnp.where(ids == marks, 0.0, -NEG).astype(jnp.bfloat16)
        for h in range(heads):
            cols = slice(h * HD, (h + 1) * HD)
            keys[h, span, :HD] = part[TAG : TAG + rows, cols]
            keys[h, span, HD:] = mask
            values[h, span, :] = part[TAG + rows : TAG + 2 * rows, cols]


def place_queries(parts, corner, rows, queries):
    heads = queries.shape[0]
    marks = lax.broadcasted_iota(jnp.int32, (rows, LANES), 1).astype(jnp.float32) + 1.0
    for k, part in enumerate(parts):
        begin = pl.multiple_of(jnp.bitwise_xor(corner, k) * rows, rows)
        span = pl.ds(begin, rows)
        ids = id_columns(part.at[rows : rows + TAG], rows)
        mask = jnp.where(ids == marks, -1.0, 0.0).astype(jnp.bfloat16)
        for h in range(heads):
            queries[h, span, :HD] = part[:rows, h * HD : (h + 1) * HD]
            queries[h, span, HD:] = mask


def attend(query, keys, values, diagonal):
    factor = math.log2(math.e) / math.sqrt(HD)
    rows = query.shape[0]
    score = lax.dot_general(
        keys, query, (((1,), (1,)), ((), ())), preferred_element_type=jnp.float32
    )
    if diagonal:
        older = lax.broadcasted_iota(jnp.int32, (rows, rows), 0) <= lax.broadcasted_iota(
            jnp.int32, (rows, rows), 1
        )
        score = jnp.concatenate(
            [score[:-rows], jnp.where(older, score[-rows:], NEG)], axis=0
        )
    high = jnp.max(score, axis=0, keepdims=True)
    expo = jnp.exp2((score - high) * factor)
    total = jnp.sum(expo, axis=0, keepdims=True)
    summed = lax.dot_general(
        values,
        expo.astype(jnp.bfloat16),
        (((0,), (0,)), ((), ())),
        preferred_element_type=jnp.float32,
    )
    return summed / total, high * factor + jnp.log2(total)


def main_kernel(place_ref, *refs):
    own, near, out, (queries, keys, values) = refs[:4], refs[4:8], refs[8], refs[9:]
    heads, span, _ = queries.shape
    rows = span // SQUAD
    width = heads * HD
    corner = corner_of(place_ref)
    place_queries([p.at[: rows + TAG] for p in own], corner, rows, queries)
    place_keys([p.at[rows:] for p in own], corner, SQUAD, rows, keys, values)
    place_keys(near, corner, 0, rows, keys, values)
    for j in range(SQUAD):
        cols = slice(j * rows, (j + 1) * rows)
        reach = (SQUAD + 1 + j) * rows
        for h in range(heads):
            mixed, lse = attend(queries[h, cols], keys[h, :reach], values[h, :reach], True)
            out[h * HD : (h + 1) * HD, cols] = mixed
            out[width + h : width + h + 1, cols] = lse
        out[width + heads :, cols] = jnp.zeros((TAG - heads, rows), jnp.float32)


def far_kernel(place_ref, *refs):
    asked, near, out, (queries, keys, values) = refs[:4], refs[4:8], refs[8], refs[9:]
    heads, span, _ = queries.shape
    rows = span // SQUAD
    width = heads * HD
    corner = corner_of(place_ref)
    place_queries(asked, corner, rows, queries)
    place_keys(near, corner, 0, rows, keys, values)
    for j in range(SQUAD - 1):
        cols = slice(j * rows, (j + 1) * rows)
        stats = []
        for h in range(heads):
            mixed, lse = attend(
                queries[h, cols], keys[h, cols.stop :], values[h, cols.stop :], False
            )
            out[h * HD : (h + 1) * HD, cols] = mixed.astype(out.dtype)
            top = lse.astype(jnp.bfloat16).astype(jnp.float32)
            mid = (lse - top).astype(jnp.bfloat16).astype(jnp.float32)
            stats += [top, mid, lse - top - mid]
        stats.append(jnp.zeros((TAG - len(stats), rows), jnp.float32))
        out[width:, cols] = jnp.concatenate(stats, axis=0).astype(out.dtype)


def merge_kernel(place_ref, main_ref, far_ref, *refs):
    outs, ready = refs[:-1], refs[-1]
    _, rows, width = ready.shape
    corner = corner_of(place_ref)
    served = place_ref[0] >= 2 * SQUAD
    for j in range(SQUAD):
        cols = slice(j * rows, (j + 1) * rows)
        for h in range(width // HD):
            feats = slice(h * HD, (h + 1) * HD)
            mixed = main_ref[feats, cols]
            if j < SQUAD - 1:
                here = main_ref[width + h : width + h + 1, cols]
                stats = far_ref[width:, cols].astype(jnp.float32)
                there = stats[3 * h : 3 * h + 1] + stats[3 * h + 1 : 3 * h + 2]
                there = jnp.where(served, there + stats[3 * h + 2 : 3 * h + 3], NEG)
                high = jnp.maximum(here, there)
                here, there = jnp.exp2(here - high), jnp.exp2(there - high)
                total = here + there
                mixed = mixed * (here / total) + far_ref[feats, cols].astype(jnp.float32) * (
                    there / total
                )
            ready[j, :, feats] = mixed.T.astype(ready.dtype)
    for k, out in enumerate(outs):
        out[...] = ready[jnp.bitwise_xor(corner, k)]


def project_kernel(ranks, place_ref, *refs):
    parts, weight_ref, out_ref, whole = refs[:-3], refs[-3], refs[-2], refs[-1]
    mine, corner = place_ref[1], corner_of(place_ref)
    width = parts[0].shape[1]
    for r in range(ranks):
        source = lax.rem(mine + ranks - r, ranks)
        for k in range(SQUAD):
            begin = (source * SQUAD + jnp.bitwise_xor(corner, k)) * width
            whole[:, pl.ds(pl.multiple_of(begin, width), width)] = parts[r * SQUAD + k][...]
    block = 2 * LANES
    for c in range(out_ref.shape[1] // block):
        cols = slice(c * block, (c + 1) * block)
        out_ref[:, cols] = jnp.dot(
            whole[...], weight_ref[:, cols], preferred_element_type=jnp.float32
        ).astype(out_ref.dtype)


def local(
    hyena_q, hyena_k, hyena_v, filters, direct, queries, keys, values, segment_ids, out_weight
):
    rows, feat = queries.shape
    count, ranks = lax.axis_size("ctx"), lax.axis_size("tp")
    width = feat // SQUAD
    heads = width // HD
    bf16, f32 = jnp.bfloat16, jnp.float32
    place = jnp.stack([lax.axis_index("ctx"), lax.axis_index("tp")]).astype(jnp.int32)

    def swap(value, mask):
        return lax.ppermute(value, "ctx", [(i, i ^ mask) for i in range(count)])

    def climb(value, first=0):
        return lax.ppermute(value, "ctx", [(i, i + SQUAD) for i in range(first, count - SQUAD)])

    def descend(value):
        return lax.ppermute(
            value, "ctx", [(i, i - SQUAD) for i in range(2 * SQUAD, count)]
        )

    own = deal(place, queries, keys, values, segment_ids.reshape(rows // LANES, LANES))
    near = [climb(own[0][rows:])]
    asked = [descend(own[0][: rows + TAG])]
    for k in range(1, SQUAD):
        own[k] = swap(own[k], k)
        earlier = max(k - 2, 0)
        own[k], near[earlier] = lax.optimization_barrier((own[k], near[earlier]))
        near.append(climb(own[k][rows:]))
        asked.append(descend(own[k][: rows + TAG]))
    tail_k = hyena_k[rows - LANES :].astype(f32)
    tail_v = hyena_v[rows - LANES :].astype(f32)
    rim = lax.ppermute(
        (tail_k * tail_v).astype(bf16), "ctx", [(i, i + 1) for i in range(count - 1)]
    )

    def store(blocks):
        return [
            pltpu.VMEM((heads, SQUAD * rows, 2 * HD), bf16),
            pltpu.VMEM((heads, blocks * rows, 2 * HD), bf16),
            pltpu.VMEM((heads, blocks * rows, HD), bf16),
        ]

    (far,) = kernel_call(
        far_kernel,
        (place, *asked, *near),
        [jax.ShapeDtypeStruct((width + TAG, (SQUAD - 1) * rows), bf16)],
        "far",
        store(SQUAD),
        flops=6 * 4 * rows * rows * width,
        exps=6 * rows * rows * heads,
    )
    far = climb(far, SQUAD)
    (main,) = kernel_call(
        main_kernel,
        (place, *own, *near),
        [jax.ShapeDtypeStruct((width + TAG, SQUAD * rows), f32)],
        "main",
        store(2 * SQUAD),
        flops=26 * 4 * rows * rows * width,
        exps=26 * rows * rows * heads,
    )
    done = kernel_call(
        merge_kernel,
        (place, main, far),
        [jax.ShapeDtypeStruct((rows, width), bf16)] * SQUAD,
        "merge",
        [pltpu.VMEM((SQUAD, rows, width), bf16)],
    )
    rim, done[0] = lax.optimization_barrier((rim, done[0]))
    hyena_out = hyena(hyena_q, hyena_k, hyena_v, rim, filters, direct)

    def turn(value, r):
        return lax.ppermute(value, "tp", [(t, (t + r) % ranks) for t in range(ranks)])

    pieces = [swap(done[k], k) for k in range(1, SQUAD)]
    hyena_out, *pieces = lax.optimization_barrier((hyena_out, *pieces))
    pieces = [done[0]] + pieces
    pieces += [turn(piece, r) for r in range(1, ranks) for piece in pieces]
    (attn_out,) = kernel_call(
        functools.partial(project_kernel, ranks),
        (place, *pieces, out_weight),
        [jax.ShapeDtypeStruct((rows, out_weight.shape[1]), bf16)],
        "project",
        [pltpu.VMEM((rows, ranks * feat), bf16)],
        flops=2 * rows * math.prod(out_weight.shape),
    )
    return (hyena_out, attn_out)


def solution(mesh):
    placed = (
        P("ctx", "tp"),
        P("ctx", "tp"),
        P("ctx", "tp"),
        P("tp", None),
        P("tp"),
        P("ctx", "tp"),
        P("ctx", "tp"),
        P("ctx", "tp"),
        P("ctx"),
        P(None, "tp"),
    )
    return jax.shard_map(
        local,
        mesh=mesh,
        in_specs=placed,
        out_specs=(P("ctx", "tp"), P("ctx", "tp")),
        check_vma=False,
    )
```

```python
import functools
import math

import jax
import jax.numpy as jnp
from jax import lax
from jax.experimental import pallas as pl
from jax.experimental.pallas import tpu as pltpu
from jax.sharding import PartitionSpec as P

HD = 128
SQUAD = 4
NEG = -1e30
TAG = 16
LANES = 128
VMEM_LIMIT = 32 * 1024 * 1024
ALL_VMEM = 62 * 1024 * 1024
VMEM = pl.BlockSpec(memory_space=pltpu.VMEM)
SMEM = pl.BlockSpec(memory_space=pltpu.SMEM)


def corner_of(place_ref):
    return lax.rem(place_ref[0], SQUAD)


def kernel_call(kernel, args, shapes, name, scratch=(), flops=0, exps=0):
    total = sum(math.prod(x.shape) * x.dtype.itemsize for x in (*args, *shapes))
    return list(pl.pallas_call(
        kernel,
        in_specs=[SMEM] + [VMEM] * (len(args) - 1),
        out_specs=[VMEM] * len(shapes),
        out_shape=shapes,
        scratch_shapes=scratch,
        compiler_params=pltpu.CompilerParams(vmem_limit_bytes=VMEM_LIMIT),
        cost_estimate=pl.CostEstimate(flops=flops, bytes_accessed=total, transcendentals=exps),
        name=name,
    )(*args))


def hyena_kernel(q_ref, k_ref, v_ref, rim_ref, taps_ref, direct_ref, out_ref):
    rows, width = q_ref.shape
    per_tile = taps_ref.shape[0] * LANES // width
    group = LANES // per_tile
    windows = rows // LANES
    shape = (LANES, 2 * LANES)
    turn = lax.broadcasted_iota(jnp.int32, shape, 0) + lax.broadcasted_iota(jnp.int32, shape, 1)
    turn = jnp.where(turn == LANES, 1.0, 0.0).astype(jnp.bfloat16)
    taps = jnp.dot(taps_ref[...], turn, preferred_element_type=jnp.float32)
    lane_group = lax.broadcasted_iota(jnp.int32, (LANES, windows * LANES), 1) % LANES // group
    for tile in range(width // LANES):
        cols = slice(tile * LANES, (tile + 1) * LANES)
        mixed = (k_ref[:, cols].astype(jnp.float32) * v_ref[:, cols].astype(jnp.float32)).astype(
            jnp.bfloat16
        )
        full = jnp.concatenate([rim_ref[:, cols], mixed], axis=0)
        stacked = jnp.concatenate(
            [full[w * LANES : (w + 2) * LANES] for w in range(windows)], axis=1
        )
        conv = jnp.zeros((LANES, windows * LANES), jnp.float32)
        for g in range(per_tile):
            at = tile * per_tile + g
            row = taps[at : at + 1]
            table = pltpu.roll(
                jnp.broadcast_to(row, (LANES, 2 * LANES)), 0, 1, stride=1, stride_axis=0
            ).astype(jnp.bfloat16)
            part = jnp.dot(table, stacked, preferred_element_type=jnp.float32)
            conv = jnp.where(lane_group == g, part, conv)
        conv = jnp.concatenate(
            [conv[:, w * LANES : (w + 1) * LANES] for w in range(windows)], axis=0
        )
        out_ref[:, cols] = (
            q_ref[:, cols].astype(jnp.float32)
            * (conv + direct_ref[:, cols].astype(jnp.float32) * mixed.astype(jnp.float32))
        ).astype(jnp.bfloat16)


def hyena(hyena_q, hyena_k, hyena_v, rim, filters, direct):
    rows, chans = hyena_q.shape
    groups, kernel = filters.shape
    taps = jnp.pad(filters, ((0, 0), (0, LANES - kernel)))
    block = 2 * LANES
    steps = chans // block
    wide = pl.BlockSpec((rows, block), lambda i: (0, i))
    return pl.pallas_call(
        hyena_kernel,
        grid=(steps,),
        in_specs=[
            wide,
            wide,
            wide,
            pl.BlockSpec((LANES, block), lambda i: (0, i)),
            pl.BlockSpec((groups // steps, LANES), lambda i: (i, 0)),
            pl.BlockSpec((1, block), lambda i: (0, i)),
        ],
        out_specs=wide,
        out_shape=jax.ShapeDtypeStruct((rows, chans), jnp.bfloat16),
        compiler_params=pltpu.CompilerParams(vmem_limit_bytes=VMEM_LIMIT),
        cost_estimate=pl.CostEstimate(
            flops=4 * rows * chans * 2 * LANES * 8,
            bytes_accessed=10 * rows * chans,
            transcendentals=0,
        ),
        name="hyena",
    )(hyena_q, hyena_k, hyena_v, rim, taps, direct[None])


def deal_kernel(place_ref, q_ref, k_ref, v_ref, id_ref, *refs):
    asked, outs, sems = refs[0], refs[1:-1], refs[-1]
    rows, feat = q_ref.shape
    width = feat // SQUAD
    corner = corner_of(place_ref)
    copies, tags = [], []
    for k, out in enumerate(outs):
        cols = pl.ds(pl.multiple_of(jnp.bitwise_xor(corner, k) * width, width), width)
        query = asked if k == 0 else out
        base = 0 if k == 0 else rows
        places = (
            (q_ref, query, 0),
            (k_ref, out, base + TAG),
            (v_ref, out, base + TAG + rows),
        )
        copies += [
            pltpu.make_async_copy(
                source.at[:, cols], target.at[pl.ds(begin, rows)], sems.at[k, i]
            )
            for i, (source, target, begin) in enumerate(places)
        ]
        tags.append((out, base))
    for copy in copies:
        copy.start()
    ids = (id_ref[...] + 1).astype(jnp.float32)
    spare = jnp.zeros((TAG - ids.shape[0], LANES), jnp.float32)
    ids = jnp.concatenate([ids, spare], axis=0)
    tag = jnp.concatenate([ids] * (width // LANES), axis=1).astype(jnp.bfloat16)
    for target, begin in tags + [(asked, rows)]:
        target[begin : begin + TAG, :] = tag
    for copy in copies:
        copy.wait()


def deal(place, queries, keys, values, ids):
    rows, feat = queries.shape
    tall = [rows + TAG, 2 * rows + TAG] + [3 * rows + TAG] * (SQUAD - 1)
    return list(
        pl.pallas_call(
            deal_kernel,
            in_specs=[SMEM] + [pl.BlockSpec(memory_space=pl.ANY)] * 3 + [VMEM],
            out_specs=[VMEM] * len(tall),
            out_shape=[jax.ShapeDtypeStruct((x, feat // SQUAD), jnp.bfloat16) for x in tall],
            scratch_shapes=[pltpu.SemaphoreType.DMA((SQUAD, 3))],
            compiler_params=pltpu.CompilerParams(vmem_limit_bytes=ALL_VMEM),
            cost_estimate=pl.CostEstimate(
                flops=0, bytes_accessed=12 * rows * feat, transcendentals=0
            ),
            name="deal",
        )(place, queries, keys, values, ids)
    )


def id_columns(tag_ref, rows):
    tag = tag_ref[:, :LANES].astype(jnp.float32)
    tiles = [jnp.broadcast_to(tag[t : t + 1], (LANES, LANES)).T for t in range(rows // LANES)]
    return jnp.concatenate(tiles, axis=0)


def place_keys(parts, corner, base, rows, keys, values):
    heads = keys.shape[0]
    marks = lax.broadcasted_iota(jnp.int32, (rows, LANES), 1).astype(jnp.float32) + 1.0
    for k, part in enumerate(parts):
        begin = pl.multiple_of((jnp.bitwise_xor(corner, k) + base) * rows, rows)
        span = pl.ds(begin, rows)
        ids = id_columns(part.at[:TAG], rows)
        mask = jnp.where(ids == marks, 0.0, -NEG).astype(jnp.bfloat16)
        for h in range(heads):
            cols = slice(h * HD, (h + 1) * HD)
            keys[h, span, :HD] = part[TAG : TAG + rows, cols]
            keys[h, span, HD:] = mask
            values[h, span, :] = part[TAG + rows : TAG + 2 * rows, cols]


def near_parts(near, rows):
    tall = 2 * rows + TAG
    return [near[0], near[1].at[:tall], near[1].at[tall:], near[2]]


def place_queries(parts, corner, rows, queries):
    heads = queries.shape[0]
    marks = lax.broadcasted_iota(jnp.int32, (rows, LANES), 1).astype(jnp.float32) + 1.0
    for k, part in enumerate(parts):
        begin = pl.multiple_of(jnp.bitwise_xor(corner, k) * rows, rows)
        span = pl.ds(begin, rows)
        ids = id_columns(part.at[rows : rows + TAG], rows)
        mask = jnp.where(ids == marks, -1.0, 0.0).astype(jnp.bfloat16)
        for h in range(heads):
            queries[h, span, :HD] = part[:rows, h * HD : (h + 1) * HD]
            queries[h, span, HD:] = mask


def attend(query, keys, values, diagonal):
    factor = math.log2(math.e) / math.sqrt(HD)
    rows = query.shape[0]
    score = lax.dot_general(
        keys, query, (((1,), (1,)), ((), ())), preferred_element_type=jnp.float32
    )
    if diagonal:
        older = lax.broadcasted_iota(jnp.int32, (rows, rows), 0) <= lax.broadcasted_iota(
            jnp.int32, (rows, rows), 1
        )
        score = jnp.concatenate(
            [score[:-rows], jnp.where(older, score[-rows:], NEG)], axis=0
        )
    high = jnp.max(score, axis=0, keepdims=True)
    expo = jnp.exp2((score - high) * factor)
    total = jnp.sum(expo, axis=0, keepdims=True)
    summed = lax.dot_general(
        values,
        expo.astype(jnp.bfloat16),
        (((0,), (0,)), ((), ())),
        preferred_element_type=jnp.float32,
    )
    return summed / total, high * factor + jnp.log2(total)


def main_kernel(place_ref, *refs):
    own, near, out, (queries, keys, values) = refs[:5], refs[5:8], refs[8], refs[9:]
    heads, span, _ = queries.shape
    rows = span // SQUAD
    width = heads * HD
    corner = corner_of(place_ref)
    asked = [own[0]] + [p.at[: rows + TAG] for p in own[2:]]
    held = [own[1]] + [p.at[rows:] for p in own[2:]]
    place_queries(asked, corner, rows, queries)
    place_keys(held, corner, SQUAD, rows, keys, values)
    place_keys(near_parts(near, rows), corner, 0, rows, keys, values)
    for j in range(SQUAD):
        cols = slice(j * rows, (j + 1) * rows)
        reach = (SQUAD + 1 + j) * rows
        for h in range(heads):
            mixed, lse = attend(queries[h, cols], keys[h, :reach], values[h, :reach], True)
            out[h * HD : (h + 1) * HD, cols] = mixed
            out[width + h : width + h + 1, cols] = lse
        out[width + heads :, cols] = jnp.zeros((TAG - heads, rows), jnp.float32)


def far_kernel(place_ref, *refs):
    asked, near, out, (queries, keys, values) = refs[:2], refs[2:5], refs[5], refs[6:]
    heads, span, _ = queries.shape
    rows = span // SQUAD
    width = heads * HD
    corner = corner_of(place_ref)
    tall = rows + TAG
    asked = [asked[0].at[k * tall : (k + 1) * tall] for k in range(SQUAD - 1)] + [asked[1]]
    place_queries(asked, corner, rows, queries)
    place_keys(near_parts(near, rows), corner, 0, rows, keys, values)
    for j in range(SQUAD - 1):
        cols = slice(j * rows, (j + 1) * rows)
        stats = []
        for h in range(heads):
            mixed, lse = attend(
                queries[h, cols], keys[h, cols.stop :], values[h, cols.stop :], False
            )
            out[h * HD : (h + 1) * HD, cols] = mixed.astype(out.dtype)
            top = lse.astype(jnp.bfloat16).astype(jnp.float32)
            mid = (lse - top).astype(jnp.bfloat16).astype(jnp.float32)
            stats += [top, mid, lse - top - mid]
        stats.append(jnp.zeros((TAG - len(stats), rows), jnp.float32))
        out[width:, cols] = jnp.concatenate(stats, axis=0).astype(out.dtype)


def merge_kernel(place_ref, main_ref, far_ref, *refs):
    outs, ready = refs[:-1], refs[-1]
    _, rows, width = ready.shape
    corner = corner_of(place_ref)
    served = place_ref[0] >= 2 * SQUAD
    for j in range(SQUAD):
        cols = slice(j * rows, (j + 1) * rows)
        for h in range(width // HD):
            feats = slice(h * HD, (h + 1) * HD)
            mixed = main_ref[feats, cols]
            if j < SQUAD - 1:
                here = main_ref[width + h : width + h + 1, cols]
                stats = far_ref[width:, cols].astype(jnp.float32)
                there = stats[3 * h : 3 * h + 1] + stats[3 * h + 1 : 3 * h + 2]
                there = jnp.where(served, there + stats[3 * h + 2 : 3 * h + 3], NEG)
                high = jnp.maximum(here, there)
                here, there = jnp.exp2(here - high), jnp.exp2(there - high)
                total = here + there
                mixed = mixed * (here / total) + far_ref[feats, cols].astype(jnp.float32) * (
                    there / total
                )
            ready[j, :, feats] = mixed.T.astype(ready.dtype)
    for k, out in enumerate(outs):
        out[...] = ready[jnp.bitwise_xor(corner, k)]


def project_kernel(ranks, place_ref, *refs):
    parts, weight_ref, out_ref, whole = refs[:-3], refs[-3], refs[-2], refs[-1]
    mine, corner = place_ref[1], corner_of(place_ref)
    width = parts[0].shape[1]
    for r in range(ranks):
        source = lax.rem(mine + ranks - r, ranks)
        for k in range(SQUAD):
            begin = (source * SQUAD + jnp.bitwise_xor(corner, k)) * width
            whole[:, pl.ds(pl.multiple_of(begin, width), width)] = parts[r * SQUAD + k][...]
    block = 2 * LANES
    for c in range(out_ref.shape[1] // block):
        cols = slice(c * block, (c + 1) * block)
        out_ref[:, cols] = jnp.dot(
            whole[...], weight_ref[:, cols], preferred_element_type=jnp.float32
        ).astype(out_ref.dtype)


def local(
    hyena_q, hyena_k, hyena_v, filters, direct, queries, keys, values, segment_ids, out_weight
):
    rows, feat = queries.shape
    count, ranks = lax.axis_size("ctx"), lax.axis_size("tp")
    width = feat // SQUAD
    heads = width // HD
    bf16, f32 = jnp.bfloat16, jnp.float32
    place = jnp.stack([lax.axis_index("ctx"), lax.axis_index("tp")]).astype(jnp.int32)

    def swap(value, mask):
        return lax.ppermute(value, "ctx", [(i, i ^ mask) for i in range(count)])

    def climb(value, first=0):
        return lax.ppermute(value, "ctx", [(i, i + SQUAD) for i in range(first, count - SQUAD)])

    def descend(value):
        return lax.ppermute(
            value, "ctx", [(i, i - SQUAD) for i in range(2 * SQUAD, count)]
        )

    asked, kept, *sent = deal(
        place, queries, keys, values, segment_ids.reshape(rows // LANES, LANES)
    )
    tall = rows + TAG
    near = [climb(kept)]
    beside = [swap(sent[0], 1), swap(sent[1], 2)]
    sent[2], near[0] = lax.optimization_barrier((sent[2], near[0]))
    across = swap(sent[2], 3)
    near.append(climb(jnp.concatenate([x[rows:] for x in beside], axis=0)))
    back = [descend(jnp.concatenate([asked] + [x[:tall] for x in beside], axis=0))]
    near.append(climb(across[rows:]))
    back.append(descend(across[:tall]))
    own = [asked, kept, *beside, across]
    tail_k = hyena_k[rows - LANES :].astype(f32)
    tail_v = hyena_v[rows - LANES :].astype(f32)
    rim = lax.ppermute(
        (tail_k * tail_v).astype(bf16), "ctx", [(i, i + 1) for i in range(count - 1)]
    )

    def store(blocks):
        return [
            pltpu.VMEM((heads, SQUAD * rows, 2 * HD), bf16),
            pltpu.VMEM((heads, blocks * rows, 2 * HD), bf16),
            pltpu.VMEM((heads, blocks * rows, HD), bf16),
        ]

    (far,) = kernel_call(
        far_kernel,
        (place, *back, *near),
        [jax.ShapeDtypeStruct((width + TAG, (SQUAD - 1) * rows), bf16)],
        "far",
        store(SQUAD),
        flops=6 * 4 * rows * rows * width,
        exps=6 * rows * rows * heads,
    )
    far = climb(far, SQUAD)
    (main,) = kernel_call(
        main_kernel,
        (place, *own, *near),
        [jax.ShapeDtypeStruct((width + TAG, SQUAD * rows), f32)],
        "main",
        store(2 * SQUAD),
        flops=26 * 4 * rows * rows * width,
        exps=26 * rows * rows * heads,
    )
    done = kernel_call(
        merge_kernel,
        (place, main, far),
        [jax.ShapeDtypeStruct((rows, width), bf16)] * SQUAD,
        "merge",
        [pltpu.VMEM((SQUAD, rows, width), bf16)],
    )
    rim, done[0] = lax.optimization_barrier((rim, done[0]))
    hyena_out = hyena(hyena_q, hyena_k, hyena_v, rim, filters, direct)

    def turn(value, r):
        return lax.ppermute(value, "tp", [(t, (t + r) % ranks) for t in range(ranks)])

    pieces = [swap(done[k], k) for k in range(1, SQUAD)]
    hyena_out, *pieces = lax.optimization_barrier((hyena_out, *pieces))
    pieces = [done[0]] + pieces
    pieces += [turn(piece, r) for r in range(1, ranks) for piece in pieces]
    (attn_out,) = kernel_call(
        functools.partial(project_kernel, ranks),
        (place, *pieces, out_weight),
        [jax.ShapeDtypeStruct((rows, out_weight.shape[1]), bf16)],
        "project",
        [pltpu.VMEM((rows, ranks * feat), bf16)],
        flops=2 * rows * math.prod(out_weight.shape),
    )
    return (hyena_out, attn_out)


def solution(mesh):
    placed = (
        P("ctx", "tp"),
        P("ctx", "tp"),
        P("ctx", "tp"),
        P("tp", None),
        P("tp"),
        P("ctx", "tp"),
        P("ctx", "tp"),
        P("ctx", "tp"),
        P("ctx"),
        P(None, "tp"),
    )
    return jax.shard_map(
        local,
        mesh=mesh,
        in_specs=placed,
        out_specs=(P("ctx", "tp"), P("ctx", "tp")),
        check_vma=False,
    )
```

```python
import functools
import math

import jax
import jax.numpy as jnp
from jax import lax
from jax.experimental import pallas as pl
from jax.experimental.pallas import tpu as pltpu
from jax.sharding import PartitionSpec as P

HD = 128
SQUAD = 4
NEG = -1e30
TAG = 16
LANES = 128
VMEM_LIMIT = 32 * 1024 * 1024
ALL_VMEM = 62 * 1024 * 1024
VMEM = pl.BlockSpec(memory_space=pltpu.VMEM)
SMEM = pl.BlockSpec(memory_space=pltpu.SMEM)


def corner_of(place_ref):
    return lax.rem(place_ref[0], SQUAD)


def kernel_call(kernel, args, shapes, name, scratch=(), flops=0, exps=0):
    total = sum(math.prod(x.shape) * x.dtype.itemsize for x in (*args, *shapes))
    return list(pl.pallas_call(
        kernel,
        in_specs=[SMEM] + [VMEM] * (len(args) - 1),
        out_specs=[VMEM] * len(shapes),
        out_shape=shapes,
        scratch_shapes=scratch,
        compiler_params=pltpu.CompilerParams(vmem_limit_bytes=VMEM_LIMIT),
        cost_estimate=pl.CostEstimate(flops=flops, bytes_accessed=total, transcendentals=exps),
        name=name,
    )(*args))


def hyena_kernel(q_ref, k_ref, v_ref, rim_ref, taps_ref, direct_ref, out_ref):
    rows, width = q_ref.shape
    per_tile = taps_ref.shape[0] * LANES // width
    group = LANES // per_tile
    windows = rows // LANES
    shape = (LANES, 2 * LANES)
    turn = lax.broadcasted_iota(jnp.int32, shape, 0) + lax.broadcasted_iota(jnp.int32, shape, 1)
    turn = jnp.where(turn == LANES, 1.0, 0.0).astype(jnp.bfloat16)
    taps = jnp.dot(taps_ref[...], turn, preferred_element_type=jnp.float32)
    lane_group = lax.broadcasted_iota(jnp.int32, (LANES, windows * LANES), 1) % LANES // group
    for tile in range(width // LANES):
        cols = slice(tile * LANES, (tile + 1) * LANES)
        mixed = (k_ref[:, cols].astype(jnp.float32) * v_ref[:, cols].astype(jnp.float32)).astype(
            jnp.bfloat16
        )
        full = jnp.concatenate([rim_ref[:, cols], mixed], axis=0)
        stacked = jnp.concatenate(
            [full[w * LANES : (w + 2) * LANES] for w in range(windows)], axis=1
        )
        conv = jnp.zeros((LANES, windows * LANES), jnp.float32)
        for g in range(per_tile):
            at = tile * per_tile + g
            row = taps[at : at + 1]
            first = pltpu.roll(
                jnp.broadcast_to(row, (TAG, 2 * LANES)), 0, 1, stride=1, stride_axis=0
            ).astype(jnp.bfloat16)
            table = jnp.concatenate(
                [first] + [pltpu.roll(first, t, 1) for t in range(TAG, LANES, TAG)], axis=0
            )
            part = jnp.dot(table, stacked, preferred_element_type=jnp.float32)
            conv = jnp.where(lane_group == g, part, conv)
        conv = jnp.concatenate(
            [conv[:, w * LANES : (w + 1) * LANES] for w in range(windows)], axis=0
        )
        out_ref[:, cols] = (
            q_ref[:, cols].astype(jnp.float32)
            * (conv + direct_ref[:, cols].astype(jnp.float32) * mixed.astype(jnp.float32))
        ).astype(jnp.bfloat16)


def hyena(hyena_q, hyena_k, hyena_v, rim, filters, direct):
    rows, chans = hyena_q.shape
    groups, kernel = filters.shape
    taps = jnp.pad(filters, ((0, 0), (0, LANES - kernel)))
    block = 2 * LANES
    steps = chans // block
    wide = pl.BlockSpec((rows, block), lambda i: (0, i))
    return pl.pallas_call(
        hyena_kernel,
        grid=(steps,),
        in_specs=[
            wide,
            wide,
            wide,
            pl.BlockSpec((LANES, block), lambda i: (0, i)),
            pl.BlockSpec((groups // steps, LANES), lambda i: (i, 0)),
            pl.BlockSpec((1, block), lambda i: (0, i)),
        ],
        out_specs=wide,
        out_shape=jax.ShapeDtypeStruct((rows, chans), jnp.bfloat16),
        compiler_params=pltpu.CompilerParams(vmem_limit_bytes=VMEM_LIMIT),
        cost_estimate=pl.CostEstimate(
            flops=4 * rows * chans * 2 * LANES * 8,
            bytes_accessed=10 * rows * chans,
            transcendentals=0,
        ),
        name="hyena",
    )(hyena_q, hyena_k, hyena_v, rim, taps, direct[None])


def deal_kernel(place_ref, q_ref, k_ref, v_ref, id_ref, *refs):
    outs, held, (arrive, leave) = refs[: SQUAD + 1], refs[SQUAD + 1 : -2], refs[-2:]
    rows, feat = q_ref.shape
    width = feat // SQUAD
    corner = corner_of(place_ref)
    order = list(range(1, SQUAD)) + [0]
    copies = {}
    for k in order:
        cols = pl.ds(pl.multiple_of(jnp.bitwise_xor(corner, k) * width, width), width)
        base = rows if k else 0
        places = (
            (q_ref, held[k + 1] if k else held[0], 0),
            (k_ref, held[k + 1], base + TAG),
            (v_ref, held[k + 1], base + TAG + rows),
        )
        copies[k] = [
            pltpu.make_async_copy(
                source.at[:, cols], target.at[pl.ds(begin, rows)], arrive.at[k, i]
            )
            for i, (source, target, begin) in enumerate(places)
        ]
        for copy in copies[k]:
            copy.start()
    ids = (id_ref[...] + 1).astype(jnp.float32)
    spare = jnp.zeros((TAG - ids.shape[0], LANES), jnp.float32)
    ids = jnp.concatenate([ids, spare], axis=0)
    tag = jnp.concatenate([ids] * (width // LANES), axis=1).astype(jnp.bfloat16)
    for i, target in enumerate(held):
        begin = 0 if i == 1 else rows
        target[begin : begin + TAG, :] = tag
    leaving = [
        pltpu.make_async_copy(source, out, leave.at[i])
        for i, (source, out) in enumerate(zip(held, outs))
    ]
    for k in order:
        for copy in copies[k]:
            copy.wait()
        leaving[k + 1].start()
    leaving[0].start()
    for copy in leaving:
        copy.wait()


def deal(place, queries, keys, values, ids):
    rows, feat = queries.shape
    tall = [rows + TAG, 2 * rows + TAG] + [3 * rows + TAG] * (SQUAD - 1)
    shapes = [(x, feat // SQUAD) for x in tall]
    anywhere = pl.BlockSpec(memory_space=pl.ANY)
    return list(
        pl.pallas_call(
            deal_kernel,
            in_specs=[SMEM] + [anywhere] * 3 + [VMEM],
            out_specs=[anywhere] * len(tall),
            out_shape=[jax.ShapeDtypeStruct(x, jnp.bfloat16) for x in shapes],
            scratch_shapes=[pltpu.VMEM(x, jnp.bfloat16) for x in shapes]
            + [pltpu.SemaphoreType.DMA((SQUAD, 3)), pltpu.SemaphoreType.DMA((SQUAD + 1,))],
            compiler_params=pltpu.CompilerParams(vmem_limit_bytes=ALL_VMEM),
            cost_estimate=pl.CostEstimate(
                flops=0, bytes_accessed=12 * rows * feat, transcendentals=0
            ),
            name="deal",
        )(place, queries, keys, values, ids)
    )


def id_columns(tag_ref, rows):
    tag = tag_ref[:, :LANES].astype(jnp.float32)
    tiles = [jnp.broadcast_to(tag[t : t + 1], (LANES, LANES)).T for t in range(rows // LANES)]
    return jnp.concatenate(tiles, axis=0)


def place_keys(parts, corner, base, rows, keys, values):
    heads = keys.shape[0]
    marks = lax.broadcasted_iota(jnp.int32, (rows, LANES), 1).astype(jnp.float32) + 1.0
    for k, part in enumerate(parts):
        begin = pl.multiple_of((jnp.bitwise_xor(corner, k) + base) * rows, rows)
        span = pl.ds(begin, rows)
        ids = id_columns(part.at[:TAG], rows)
        mask = jnp.where(ids == marks, 0.0, -NEG).astype(jnp.bfloat16)
        for h in range(heads):
            cols = slice(h * HD, (h + 1) * HD)
            keys[h, span, :HD] = part[TAG : TAG + rows, cols]
            keys[h, span, HD:] = mask
            values[h, span, :] = part[TAG + rows : TAG + 2 * rows, cols]


def near_parts(near, rows):
    tall = 2 * rows + TAG
    return [near[0], near[1].at[:tall], near[1].at[tall:], near[2]]


def place_queries(parts, corner, rows, queries):
    heads = queries.shape[0]
    marks = lax.broadcasted_iota(jnp.int32, (rows, LANES), 1).astype(jnp.float32) + 1.0
    for k, part in enumerate(parts):
        begin = pl.multiple_of(jnp.bitwise_xor(corner, k) * rows, rows)
        span = pl.ds(begin, rows)
        ids = id_columns(part.at[rows : rows + TAG], rows)
        mask = jnp.where(ids == marks, -1.0, 0.0).astype(jnp.bfloat16)
        for h in range(heads):
            queries[h, span, :HD] = part[:rows, h * HD : (h + 1) * HD]
            queries[h, span, HD:] = mask


def attend(query, keys, values, diagonal):
    factor = math.log2(math.e) / math.sqrt(HD)
    rows = query.shape[0]
    score = lax.dot_general(
        keys, query, (((1,), (1,)), ((), ())), preferred_element_type=jnp.float32
    )
    if diagonal:
        older = lax.broadcasted_iota(jnp.int32, (rows, rows), 0) <= lax.broadcasted_iota(
            jnp.int32, (rows, rows), 1
        )
        score = jnp.concatenate(
            [score[:-rows], jnp.where(older, score[-rows:], NEG)], axis=0
        )
    high = jnp.max(score, axis=0, keepdims=True)
    expo = jnp.exp2((score - high) * factor)
    total = jnp.sum(expo, axis=0, keepdims=True)
    summed = lax.dot_general(
        values,
        expo.astype(jnp.bfloat16),
        (((0,), (0,)), ((), ())),
        preferred_element_type=jnp.float32,
    )
    return summed / total, high * factor + jnp.log2(total)


def main_kernel(place_ref, *refs):
    own, near, out, (queries, keys, values) = refs[:5], refs[5:8], refs[8], refs[9:]
    heads, span, _ = queries.shape
    rows = span // SQUAD
    width = heads * HD
    corner = corner_of(place_ref)
    asked = [own[0]] + [p.at[: rows + TAG] for p in own[2:]]
    held = [own[1]] + [p.at[rows:] for p in own[2:]]
    place_queries(asked, corner, rows, queries)
    place_keys(held, corner, SQUAD, rows, keys, values)
    place_keys(near_parts(near, rows), corner, 0, rows, keys, values)
    for j in range(SQUAD):
        cols = slice(j * rows, (j + 1) * rows)
        reach = (SQUAD + 1 + j) * rows
        for h in range(heads):
            mixed, lse = attend(queries[h, cols], keys[h, :reach], values[h, :reach], True)
            out[h * HD : (h + 1) * HD, cols] = mixed
            out[width + h : width + h + 1, cols] = lse
        out[width + heads :, cols] = jnp.zeros((TAG - heads, rows), jnp.float32)


def far_kernel(place_ref, *refs):
    asked, near, out, (queries, keys, values) = refs[:2], refs[2:5], refs[5], refs[6:]
    heads, span, _ = queries.shape
    rows = span // SQUAD
    width = heads * HD
    corner = corner_of(place_ref)
    tall = rows + TAG
    asked = [asked[0].at[k * tall : (k + 1) * tall] for k in range(SQUAD - 1)] + [asked[1]]
    place_queries(asked, corner, rows, queries)
    place_keys(near_parts(near, rows), corner, 0, rows, keys, values)
    for j in range(SQUAD - 1):
        cols = slice(j * rows, (j + 1) * rows)
        stats = []
        for h in range(heads):
            mixed, lse = attend(
                queries[h, cols], keys[h, cols.stop :], values[h, cols.stop :], False
            )
            out[h * HD : (h + 1) * HD, cols] = mixed.astype(out.dtype)
            top = lse.astype(jnp.bfloat16).astype(jnp.float32)
            mid = (lse - top).astype(jnp.bfloat16).astype(jnp.float32)
            stats += [top, mid, lse - top - mid]
        stats.append(jnp.zeros((TAG - len(stats), rows), jnp.float32))
        out[width:, cols] = jnp.concatenate(stats, axis=0).astype(out.dtype)


def merge_kernel(place_ref, main_ref, far_ref, *refs):
    outs, ready = refs[:-1], refs[-1]
    _, rows, width = ready.shape
    corner = corner_of(place_ref)
    served = place_ref[0] >= 2 * SQUAD
    for j in range(SQUAD):
        cols = slice(j * rows, (j + 1) * rows)
        for h in range(width // HD):
            feats = slice(h * HD, (h + 1) * HD)
            mixed = main_ref[feats, cols]
            if j < SQUAD - 1:
                here = main_ref[width + h : width + h + 1, cols]
                stats = far_ref[width:, cols].astype(jnp.float32)
                there = stats[3 * h : 3 * h + 1] + stats[3 * h + 1 : 3 * h + 2]
                there = jnp.where(served, there + stats[3 * h + 2 : 3 * h + 3], NEG)
                high = jnp.maximum(here, there)
                here, there = jnp.exp2(here - high), jnp.exp2(there - high)
                total = here + there
                mixed = mixed * (here / total) + far_ref[feats, cols].astype(jnp.float32) * (
                    there / total
                )
            ready[j, :, feats] = mixed.T.astype(ready.dtype)
    for k, out in enumerate(outs):
        out[...] = ready[jnp.bitwise_xor(corner, k)]


def project_kernel(ranks, place_ref, *refs):
    parts, weight_ref, out_ref, whole = refs[:-3], refs[-3], refs[-2], refs[-1]
    mine, corner = place_ref[1], corner_of(place_ref)
    width = parts[0].shape[1]
    for r in range(ranks):
        source = lax.rem(mine + ranks - r, ranks)
        for k in range(SQUAD):
            begin = (source * SQUAD + jnp.bitwise_xor(corner, k)) * width
            whole[:, pl.ds(pl.multiple_of(begin, width), width)] = parts[r * SQUAD + k][...]
    block = 2 * LANES
    for c in range(out_ref.shape[1] // block):
        cols = slice(c * block, (c + 1) * block)
        out_ref[:, cols] = jnp.dot(
            whole[...], weight_ref[:, cols], preferred_element_type=jnp.float32
        ).astype(out_ref.dtype)


def local(
    hyena_q, hyena_k, hyena_v, filters, direct, queries, keys, values, segment_ids, out_weight
):
    rows, feat = queries.shape
    count, ranks = lax.axis_size("ctx"), lax.axis_size("tp")
    width = feat // SQUAD
    heads = width // HD
    bf16, f32 = jnp.bfloat16, jnp.float32
    place = jnp.stack([lax.axis_index("ctx"), lax.axis_index("tp")]).astype(jnp.int32)

    def swap(value, mask):
        return lax.ppermute(value, "ctx", [(i, i ^ mask) for i in range(count)])

    def climb(value, first=0):
        return lax.ppermute(value, "ctx", [(i, i + SQUAD) for i in range(first, count - SQUAD)])

    def descend(value):
        return lax.ppermute(
            value, "ctx", [(i, i - SQUAD) for i in range(2 * SQUAD, count)]
        )

    asked, kept, *sent = deal(
        place, queries, keys, values, segment_ids.reshape(rows // LANES, LANES)
    )
    tall = rows + TAG
    near = [climb(kept)]
    beside = [swap(sent[0], 1), swap(sent[1], 2)]
    sent[2], beside[0] = lax.optimization_barrier((sent[2], beside[0]))
    across = swap(sent[2], 3)
    near.append(climb(jnp.concatenate([x[rows:] for x in beside], axis=0)))
    back = [descend(jnp.concatenate([asked] + [x[:tall] for x in beside], axis=0))]
    near.append(climb(across[rows:]))
    back.append(descend(across[:tall]))
    own = [asked, kept, *beside, across]
    tail_k = hyena_k[rows - LANES :].astype(f32)
    tail_v = hyena_v[rows - LANES :].astype(f32)
    rim = lax.ppermute(
        (tail_k * tail_v).astype(bf16), "ctx", [(i, i + 1) for i in range(count - 1)]
    )

    def store(blocks):
        return [
            pltpu.VMEM((heads, SQUAD * rows, 2 * HD), bf16),
            pltpu.VMEM((heads, blocks * rows, 2 * HD), bf16),
            pltpu.VMEM((heads, blocks * rows, HD), bf16),
        ]

    (far,) = kernel_call(
        far_kernel,
        (place, *back, *near),
        [jax.ShapeDtypeStruct((width + TAG, (SQUAD - 1) * rows), bf16)],
        "far",
        store(SQUAD),
        flops=6 * 4 * rows * rows * width,
        exps=6 * rows * rows * heads,
    )
    far = climb(far, SQUAD)
    (main,) = kernel_call(
        main_kernel,
        (place, *own, *near),
        [jax.ShapeDtypeStruct((width + TAG, SQUAD * rows), f32)],
        "main",
        store(2 * SQUAD),
        flops=26 * 4 * rows * rows * width,
        exps=26 * rows * rows * heads,
    )
    done = kernel_call(
        merge_kernel,
        (place, main, far),
        [jax.ShapeDtypeStruct((rows, width), bf16)] * SQUAD,
        "merge",
        [pltpu.VMEM((SQUAD, rows, width), bf16)],
    )
    rim, done[0] = lax.optimization_barrier((rim, done[0]))
    hyena_out = hyena(hyena_q, hyena_k, hyena_v, rim, filters, direct)

    def turn(value, r):
        return lax.ppermute(value, "tp", [(t, (t + r) % ranks) for t in range(ranks)])

    pieces = [swap(done[k], k) for k in range(1, SQUAD)]
    hyena_out, *pieces = lax.optimization_barrier((hyena_out, done[0], *pieces))
    pieces += [turn(piece, r) for r in range(1, ranks) for piece in pieces]
    (attn_out,) = kernel_call(
        functools.partial(project_kernel, ranks),
        (place, *pieces, out_weight),
        [jax.ShapeDtypeStruct((rows, out_weight.shape[1]), bf16)],
        "project",
        [pltpu.VMEM((rows, ranks * feat), bf16)],
        flops=2 * rows * math.prod(out_weight.shape),
    )
    return (hyena_out, attn_out)


def solution(mesh):
    placed = (
        P("ctx", "tp"),
        P("ctx", "tp"),
        P("ctx", "tp"),
        P("tp", None),
        P("tp"),
        P("ctx", "tp"),
        P("ctx", "tp"),
        P("ctx", "tp"),
        P("ctx"),
        P(None, "tp"),
    )
    return jax.shard_map(
        local,
        mesh=mesh,
        in_specs=placed,
        out_specs=(P("ctx", "tp"), P("ctx", "tp")),
        check_vma=False,
    )
```

```python
import functools
import math

import jax
import jax.numpy as jnp
from jax import lax
from jax.experimental import pallas as pl
from jax.experimental.pallas import tpu as pltpu
from jax.sharding import PartitionSpec as P

HD = 128
SQUAD = 4
NEG = -1e30
TAG = 16
LANES = 128
VMEM_LIMIT = 32 * 1024 * 1024
ALL_VMEM = 62 * 1024 * 1024
VMEM = pl.BlockSpec(memory_space=pltpu.VMEM)
SMEM = pl.BlockSpec(memory_space=pltpu.SMEM)


def corner_of(place_ref):
    return lax.rem(place_ref[0], SQUAD)


def kernel_call(kernel, args, shapes, name, scratch=(), flops=0, exps=0):
    total = sum(math.prod(x.shape) * x.dtype.itemsize for x in (*args, *shapes))
    return list(pl.pallas_call(
        kernel,
        in_specs=[SMEM] + [VMEM] * (len(args) - 1),
        out_specs=[VMEM] * len(shapes),
        out_shape=shapes,
        scratch_shapes=scratch,
        compiler_params=pltpu.CompilerParams(vmem_limit_bytes=VMEM_LIMIT),
        cost_estimate=pl.CostEstimate(flops=flops, bytes_accessed=total, transcendentals=exps),
        name=name,
    )(*args))


def hyena_kernel(q_ref, k_ref, v_ref, rim_ref, taps_ref, direct_ref, out_ref):
    rows, width = q_ref.shape
    per_tile = taps_ref.shape[0] * LANES // width
    group = LANES // per_tile
    windows = rows // LANES
    shape = (LANES, LANES)
    down, along = (lax.broadcasted_iota(jnp.int32, shape, i) for i in range(2))
    turn = jnp.where((down + along) % LANES == 0, 1.0, 0.0).astype(jnp.bfloat16)
    before = jnp.where(along > down, 1.0, 0.0).astype(jnp.bfloat16)
    within = jnp.where(along > down, 0.0, 1.0).astype(jnp.bfloat16)
    taps = jnp.dot(taps_ref[...], turn, preferred_element_type=jnp.float32)
    lane_group = lax.broadcasted_iota(jnp.int32, (LANES, windows * LANES), 1) % LANES // group
    for tile in range(width // LANES):
        cols = slice(tile * LANES, (tile + 1) * LANES)
        mixed = (k_ref[:, cols].astype(jnp.float32) * v_ref[:, cols].astype(jnp.float32)).astype(
            jnp.bfloat16
        )
        full = jnp.concatenate([rim_ref[:, cols], mixed], axis=0)
        stacked = jnp.concatenate(
            [full[w * LANES : (w + 2) * LANES] for w in range(windows)], axis=1
        )
        conv = jnp.zeros((LANES, windows * LANES), jnp.float32)
        for g in range(per_tile):
            at = tile * per_tile + g
            row = taps[at : at + 1]
            ring = pltpu.roll(
                jnp.broadcast_to(row, shape), 0, 1, stride=1, stride_axis=0
            ).astype(jnp.bfloat16)
            table = jnp.concatenate([ring * before, ring * within], axis=1)
            part = jnp.dot(table, stacked, preferred_element_type=jnp.float32)
            conv = jnp.where(lane_group == g, part, conv)
        conv = jnp.concatenate(
            [conv[:, w * LANES : (w + 1) * LANES] for w in range(windows)], axis=0
        )
        out_ref[:, cols] = (
            q_ref[:, cols].astype(jnp.float32)
            * (conv + direct_ref[:, cols].astype(jnp.float32) * mixed.astype(jnp.float32))
        ).astype(jnp.bfloat16)


def hyena(hyena_q, hyena_k, hyena_v, rim, filters, direct):
    rows, chans = hyena_q.shape
    groups, kernel = filters.shape
    taps = jnp.pad(filters, ((0, 0), (0, LANES - kernel)))
    block = 2 * LANES
    steps = chans // block
    wide = pl.BlockSpec((rows, block), lambda i: (0, i))
    return pl.pallas_call(
        hyena_kernel,
        grid=(steps,),
        in_specs=[
            wide,
            wide,
            wide,
            pl.BlockSpec((LANES, block), lambda i: (0, i)),
            pl.BlockSpec((groups // steps, LANES), lambda i: (i, 0)),
            pl.BlockSpec((1, block), lambda i: (0, i)),
        ],
        out_specs=wide,
        out_shape=jax.ShapeDtypeStruct((rows, chans), jnp.bfloat16),
        compiler_params=pltpu.CompilerParams(vmem_limit_bytes=VMEM_LIMIT),
        cost_estimate=pl.CostEstimate(
            flops=4 * rows * chans * 2 * LANES * 8,
            bytes_accessed=10 * rows * chans,
            transcendentals=0,
        ),
        name="hyena",
    )(hyena_q, hyena_k, hyena_v, rim, taps, direct[None])


def deal_kernel(place_ref, q_ref, k_ref, v_ref, id_ref, *refs):
    outs, held, (arrive, leave) = refs[: SQUAD + 1], refs[SQUAD + 1 : -2], refs[-2:]
    rows, feat = q_ref.shape
    width = feat // SQUAD
    corner = corner_of(place_ref)
    order = list(range(1, SQUAD)) + [0]
    copies = {}
    for k in order:
        cols = pl.ds(pl.multiple_of(jnp.bitwise_xor(corner, k) * width, width), width)
        base = rows if k else 0
        places = (
            (q_ref, held[k + 1] if k else held[0], 0),
            (k_ref, held[k + 1], base + TAG),
            (v_ref, held[k + 1], base + TAG + rows),
        )
        copies[k] = [
            pltpu.make_async_copy(
                source.at[:, cols], target.at[pl.ds(begin, rows)], arrive.at[k, i]
            )
            for i, (source, target, begin) in enumerate(places)
        ]
        for copy in copies[k]:
            copy.start()
    ids = (id_ref[...] + 1).astype(jnp.float32)
    spare = jnp.zeros((TAG - ids.shape[0], LANES), jnp.float32)
    ids = jnp.concatenate([ids, spare], axis=0)
    tag = jnp.concatenate([ids] * (width // LANES), axis=1).astype(jnp.bfloat16)
    for i, target in enumerate(held):
        begin = 0 if i == 1 else rows
        target[begin : begin + TAG, :] = tag
    leaving = [
        pltpu.make_async_copy(source, out, leave.at[i])
        for i, (source, out) in enumerate(zip(held, outs))
    ]
    for k in order:
        for copy in copies[k]:
            copy.wait()
        leaving[k + 1].start()
    leaving[0].start()
    for copy in leaving:
        copy.wait()


def deal(place, queries, keys, values, ids):
    rows, feat = queries.shape
    tall = [rows + TAG, 2 * rows + TAG] + [3 * rows + TAG] * (SQUAD - 1)
    shapes = [(x, feat // SQUAD) for x in tall]
    anywhere = pl.BlockSpec(memory_space=pl.ANY)
    return list(
        pl.pallas_call(
            deal_kernel,
            in_specs=[SMEM] + [anywhere] * 3 + [VMEM],
            out_specs=[anywhere] * len(tall),
            out_shape=[jax.ShapeDtypeStruct(x, jnp.bfloat16) for x in shapes],
            scratch_shapes=[pltpu.VMEM(x, jnp.bfloat16) for x in shapes]
            + [pltpu.SemaphoreType.DMA((SQUAD, 3)), pltpu.SemaphoreType.DMA((SQUAD + 1,))],
            compiler_params=pltpu.CompilerParams(vmem_limit_bytes=ALL_VMEM),
            cost_estimate=pl.CostEstimate(
                flops=0, bytes_accessed=12 * rows * feat, transcendentals=0
            ),
            name="deal",
        )(place, queries, keys, values, ids)
    )


def id_columns(tag_ref, rows):
    tag = tag_ref[:, :LANES].astype(jnp.float32)
    tiles = [jnp.broadcast_to(tag[t : t + 1], (LANES, LANES)).T for t in range(rows // LANES)]
    return jnp.concatenate(tiles, axis=0)


def place_keys(parts, corner, base, rows, keys, values):
    heads = keys.shape[0]
    marks = lax.broadcasted_iota(jnp.int32, (rows, LANES), 1).astype(jnp.float32) + 1.0
    for k, part in enumerate(parts):
        begin = pl.multiple_of((jnp.bitwise_xor(corner, k) + base) * rows, rows)
        span = pl.ds(begin, rows)
        ids = id_columns(part.at[:TAG], rows)
        mask = jnp.where(ids == marks, 0.0, -NEG).astype(jnp.bfloat16)
        for h in range(heads):
            cols = slice(h * HD, (h + 1) * HD)
            keys[h, span, :HD] = part[TAG : TAG + rows, cols]
            keys[h, span, HD:] = mask
            values[h, span, :] = part[TAG + rows : TAG + 2 * rows, cols]


def near_parts(near, rows):
    tall = 2 * rows + TAG
    return [near[0], near[1].at[:tall], near[1].at[tall:], near[2]]


def place_queries(parts, corner, rows, queries):
    heads = queries.shape[0]
    marks = lax.broadcasted_iota(jnp.int32, (rows, LANES), 1).astype(jnp.float32) + 1.0
    for k, part in enumerate(parts):
        begin = pl.multiple_of(jnp.bitwise_xor(corner, k) * rows, rows)
        span = pl.ds(begin, rows)
        ids = id_columns(part.at[rows : rows + TAG], rows)
        mask = jnp.where(ids == marks, -1.0, 0.0).astype(jnp.bfloat16)
        for h in range(heads):
            queries[h, span, :HD] = part[:rows, h * HD : (h + 1) * HD]
            queries[h, span, HD:] = mask


def attend(query, keys, values, diagonal):
    factor = 1.0 / math.sqrt(HD)
    rows = query.shape[0]
    score = lax.dot_general(
        keys, query, (((1,), (1,)), ((), ())), preferred_element_type=jnp.float32
    )
    if diagonal:
        older = lax.broadcasted_iota(jnp.int32, (rows, rows), 0) <= lax.broadcasted_iota(
            jnp.int32, (rows, rows), 1
        )
        score = jnp.concatenate(
            [score[:-rows], jnp.where(older, score[-rows:], NEG)], axis=0
        )
    high = jnp.max(score, axis=0, keepdims=True)
    expo = jnp.exp((score - high) * factor)
    total = jnp.sum(expo, axis=0, keepdims=True)
    summed = lax.dot_general(
        values,
        expo.astype(jnp.bfloat16),
        (((0,), (0,)), ((), ())),
        preferred_element_type=jnp.float32,
    )
    return summed / total, high * factor + jnp.log(total)


def main_kernel(place_ref, *refs):
    own, near, out, (queries, keys, values) = refs[:5], refs[5:8], refs[8], refs[9:]
    heads, span, _ = queries.shape
    rows = span // SQUAD
    width = heads * HD
    corner = corner_of(place_ref)
    asked = [own[0]] + [p.at[: rows + TAG] for p in own[2:]]
    held = [own[1]] + [p.at[rows:] for p in own[2:]]
    place_queries(asked, corner, rows, queries)
    place_keys(held, corner, SQUAD, rows, keys, values)
    place_keys(near_parts(near, rows), corner, 0, rows, keys, values)
    for j in range(SQUAD):
        cols = slice(j * rows, (j + 1) * rows)
        reach = (SQUAD + 1 + j) * rows
        for h in range(heads):
            mixed, lse = attend(queries[h, cols], keys[h, :reach], values[h, :reach], True)
            out[h * HD : (h + 1) * HD, cols] = mixed
            out[width + h : width + h + 1, cols] = lse
        out[width + heads :, cols] = jnp.zeros((TAG - heads, rows), jnp.float32)


def far_kernel(place_ref, *refs):
    asked, near, out, (queries, keys, values) = refs[:2], refs[2:5], refs[5], refs[6:]
    heads, span, _ = queries.shape
    rows = span // SQUAD
    width = heads * HD
    corner = corner_of(place_ref)
    tall = rows + TAG
    asked = [asked[0].at[k * tall : (k + 1) * tall] for k in range(SQUAD - 1)] + [asked[1]]
    place_queries(asked, corner, rows, queries)
    place_keys(near_parts(near, rows), corner, 0, rows, keys, values)
    for j in range(SQUAD - 1):
        cols = slice(j * rows, (j + 1) * rows)
        stats = []
        for h in range(heads):
            mixed, lse = attend(
                queries[h, cols], keys[h, cols.stop :], values[h, cols.stop :], False
            )
            out[h * HD : (h + 1) * HD, cols] = mixed.astype(out.dtype)
            top = lse.astype(jnp.bfloat16).astype(jnp.float32)
            mid = (lse - top).astype(jnp.bfloat16).astype(jnp.float32)
            stats += [top, mid, lse - top - mid]
        stats.append(jnp.zeros((TAG - len(stats), rows), jnp.float32))
        out[width:, cols] = jnp.concatenate(stats, axis=0).astype(out.dtype)


def merge_kernel(place_ref, main_ref, far_ref, *refs):
    outs, ready = refs[:-1], refs[-1]
    _, rows, width = ready.shape
    corner = corner_of(place_ref)
    served = place_ref[0] >= 2 * SQUAD
    for j in range(SQUAD):
        cols = slice(j * rows, (j + 1) * rows)
        for h in range(width // HD):
            feats = slice(h * HD, (h + 1) * HD)
            mixed = main_ref[feats, cols]
            if j < SQUAD - 1:
                here = main_ref[width + h : width + h + 1, cols]
                stats = far_ref[width:, cols].astype(jnp.float32)
                there = stats[3 * h : 3 * h + 1] + stats[3 * h + 1 : 3 * h + 2]
                there = jnp.where(served, there + stats[3 * h + 2 : 3 * h + 3], NEG)
                high = jnp.maximum(here, there)
                here, there = jnp.exp(here - high), jnp.exp(there - high)
                total = here + there
                mixed = mixed * (here / total) + far_ref[feats, cols].astype(jnp.float32) * (
                    there / total
                )
            ready[j, :, feats] = mixed.T.astype(ready.dtype)
    for k, out in enumerate(outs):
        out[...] = ready[jnp.bitwise_xor(corner, k)]


def project_kernel(ranks, place_ref, *refs):
    parts, weight_ref, out_ref, whole = refs[:-3], refs[-3], refs[-2], refs[-1]
    mine, corner = place_ref[1], corner_of(place_ref)
    width = parts[0].shape[1]
    for r in range(ranks):
        source = lax.rem(mine + ranks - r, ranks)
        for k in range(SQUAD):
            begin = (source * SQUAD + jnp.bitwise_xor(corner, k)) * width
            whole[:, pl.ds(pl.multiple_of(begin, width), width)] = parts[r * SQUAD + k][...]
    block = 2 * LANES
    for c in range(out_ref.shape[1] // block):
        cols = slice(c * block, (c + 1) * block)
        out_ref[:, cols] = jnp.dot(
            whole[...], weight_ref[:, cols], preferred_element_type=jnp.float32
        ).astype(out_ref.dtype)


def local(
    hyena_q, hyena_k, hyena_v, filters, direct, queries, keys, values, segment_ids, out_weight
):
    rows, feat = queries.shape
    count, ranks = lax.axis_size("ctx"), lax.axis_size("tp")
    width = feat // SQUAD
    heads = width // HD
    bf16, f32 = jnp.bfloat16, jnp.float32
    place = jnp.stack([lax.axis_index("ctx"), lax.axis_index("tp")]).astype(jnp.int32)

    def swap(value, mask):
        return lax.ppermute(value, "ctx", [(i, i ^ mask) for i in range(count)])

    def climb(value, first=0):
        return lax.ppermute(value, "ctx", [(i, i + SQUAD) for i in range(first, count - SQUAD)])

    def descend(value):
        return lax.ppermute(
            value, "ctx", [(i, i - SQUAD) for i in range(2 * SQUAD, count)]
        )

    asked, kept, *sent = deal(
        place, queries, keys, values, segment_ids.reshape(rows // LANES, LANES)
    )
    tall = rows + TAG
    near = [climb(kept)]
    tail_k, tail_v, kept = lax.optimization_barrier(
        (hyena_k[rows - LANES :], hyena_v[rows - LANES :], kept)
    )
    rim = lax.ppermute(
        (tail_k.astype(f32) * tail_v.astype(f32)).astype(bf16),
        "ctx",
        [(i, i + 1) for i in range(count - 1)],
    )
    beside = [swap(sent[0], 1), swap(sent[1], 2)]
    sent[2], beside[0] = lax.optimization_barrier((sent[2], beside[0]))
    across = swap(sent[2], 3)
    beside[1], near[0] = lax.optimization_barrier((beside[1], near[0]))
    near.append(climb(jnp.concatenate([x[rows:] for x in beside], axis=0)))
    back = [descend(jnp.concatenate([asked] + [x[:tall] for x in beside], axis=0))]
    across, rim = lax.optimization_barrier((across, rim))
    near.append(climb(across[rows:]))
    back.append(descend(across[:tall]))
    own = [asked, kept, *beside, across]
    def store(blocks):
        return [
            pltpu.VMEM((heads, SQUAD * rows, 2 * HD), bf16),
            pltpu.VMEM((heads, blocks * rows, 2 * HD), bf16),
            pltpu.VMEM((heads, blocks * rows, HD), bf16),
        ]

    (far,) = kernel_call(
        far_kernel,
        (place, *back, *near),
        [jax.ShapeDtypeStruct((width + TAG, (SQUAD - 1) * rows), bf16)],
        "far",
        store(SQUAD),
        flops=6 * 4 * rows * rows * width,
        exps=6 * rows * rows * heads,
    )
    far = climb(far, SQUAD)
    (main,) = kernel_call(
        main_kernel,
        (place, *own, *near),
        [jax.ShapeDtypeStruct((width + TAG, SQUAD * rows), f32)],
        "main",
        store(2 * SQUAD),
        flops=26 * 4 * rows * rows * width,
        exps=26 * rows * rows * heads,
    )
    done = kernel_call(
        merge_kernel,
        (place, main, far),
        [jax.ShapeDtypeStruct((rows, width), bf16)] * SQUAD,
        "merge",
        [pltpu.VMEM((SQUAD, rows, width), bf16)],
    )
    rim, done[0] = lax.optimization_barrier((rim, done[0]))
    hyena_out = hyena(hyena_q, hyena_k, hyena_v, rim, filters, direct)

    def turn(value, r):
        return lax.ppermute(value, "tp", [(t, (t + r) % ranks) for t in range(ranks)])

    pieces = [swap(done[k], k) for k in range(1, SQUAD)]
    hyena_out, *pieces = lax.optimization_barrier((hyena_out, done[0], *pieces))
    pieces += [turn(piece, r) for r in range(1, ranks) for piece in pieces]
    (attn_out,) = kernel_call(
        functools.partial(project_kernel, ranks),
        (place, *pieces, out_weight),
        [jax.ShapeDtypeStruct((rows, out_weight.shape[1]), bf16)],
        "project",
        [pltpu.VMEM((rows, ranks * feat), bf16)],
        flops=2 * rows * math.prod(out_weight.shape),
    )
    return (hyena_out, attn_out)


def solution(mesh):
    placed = (
        P("ctx", "tp"),
        P("ctx", "tp"),
        P("ctx", "tp"),
        P("tp", None),
        P("tp"),
        P("ctx", "tp"),
        P("ctx", "tp"),
        P("ctx", "tp"),
        P("ctx"),
        P(None, "tp"),
    )
    return jax.shard_map(
        local,
        mesh=mesh,
        in_specs=placed,
        out_specs=(P("ctx", "tp"), P("ctx", "tp")),
        check_vma=False,
    )
```

```python
import functools
import math

import jax
import jax.numpy as jnp
from jax import lax
from jax.experimental import pallas as pl
from jax.experimental.pallas import tpu as pltpu
from jax.sharding import PartitionSpec as P

HD = 128
SQUAD = 4
NEG = -1e30
TAG = 16
LANES = 128
VMEM_LIMIT = 32 * 1024 * 1024
ALL_VMEM = 62 * 1024 * 1024
VMEM = pl.BlockSpec(memory_space=pltpu.VMEM)


def corner_of():
    return lax.rem(lax.axis_index("ctx"), SQUAD)


def kernel_call(kernel, args, shapes, name, scratch=(), flops=0, exps=0):
    total = sum(math.prod(x.shape) * x.dtype.itemsize for x in (*args, *shapes))
    return list(pl.pallas_call(
        kernel,
        in_specs=[VMEM] * len(args),
        out_specs=[VMEM] * len(shapes),
        out_shape=shapes,
        scratch_shapes=scratch,
        compiler_params=pltpu.CompilerParams(vmem_limit_bytes=VMEM_LIMIT),
        cost_estimate=pl.CostEstimate(flops=flops, bytes_accessed=total, transcendentals=exps),
        name=name,
    )(*args))


def hyena_kernel(q_ref, k_ref, v_ref, rim_ref, taps_ref, direct_ref, out_ref):
    rows, width = q_ref.shape
    per_tile = taps_ref.shape[0] * LANES // width
    group = LANES // per_tile
    windows = rows // LANES
    shape = (LANES, LANES)
    down, along = (lax.broadcasted_iota(jnp.int32, shape, i) for i in range(2))
    turn = jnp.where((down + along) % LANES == 0, 1.0, 0.0).astype(jnp.bfloat16)
    before = jnp.where(along > down, 1.0, 0.0).astype(jnp.bfloat16)
    within = jnp.where(along > down, 0.0, 1.0).astype(jnp.bfloat16)
    taps = jnp.dot(taps_ref[...], turn, preferred_element_type=jnp.float32)
    lane_group = lax.broadcasted_iota(jnp.int32, (LANES, windows * LANES), 1) % LANES // group
    for tile in range(width // LANES):
        cols = slice(tile * LANES, (tile + 1) * LANES)
        mixed = (k_ref[:, cols].astype(jnp.float32) * v_ref[:, cols].astype(jnp.float32)).astype(
            jnp.bfloat16
        )
        full = jnp.concatenate([rim_ref[:, cols], mixed], axis=0)
        stacked = jnp.concatenate(
            [full[w * LANES : (w + 2) * LANES] for w in range(windows)], axis=1
        )
        conv = jnp.zeros((LANES, windows * LANES), jnp.float32)
        for g in range(per_tile):
            at = tile * per_tile + g
            row = taps[at : at + 1]
            ring = pltpu.roll(
                jnp.broadcast_to(row, shape), 0, 1, stride=1, stride_axis=0
            ).astype(jnp.bfloat16)
            table = jnp.concatenate([ring * before, ring * within], axis=1)
            part = jnp.dot(table, stacked, preferred_element_type=jnp.float32)
            conv = jnp.where(lane_group == g, part, conv)
        conv = jnp.concatenate(
            [conv[:, w * LANES : (w + 1) * LANES] for w in range(windows)], axis=0
        )
        out_ref[:, cols] = (
            q_ref[:, cols].astype(jnp.float32)
            * (conv + direct_ref[:, cols].astype(jnp.float32) * mixed.astype(jnp.float32))
        ).astype(jnp.bfloat16)


def hyena(hyena_q, hyena_k, hyena_v, rim, filters, direct):
    rows, chans = hyena_q.shape
    groups, kernel = filters.shape
    taps = jnp.pad(filters, ((0, 0), (0, LANES - kernel)))
    block = 2 * LANES
    steps = chans // block
    wide = pl.BlockSpec((rows, block), lambda i: (0, i))
    return pl.pallas_call(
        hyena_kernel,
        grid=(steps,),
        in_specs=[
            wide,
            wide,
            wide,
            pl.BlockSpec((LANES, block), lambda i: (0, i)),
            pl.BlockSpec((groups // steps, LANES), lambda i: (i, 0)),
            pl.BlockSpec((1, block), lambda i: (0, i)),
        ],
        out_specs=wide,
        out_shape=jax.ShapeDtypeStruct((rows, chans), jnp.bfloat16),
        compiler_params=pltpu.CompilerParams(vmem_limit_bytes=VMEM_LIMIT),
        cost_estimate=pl.CostEstimate(
            flops=4 * rows * chans * 2 * LANES * 8,
            bytes_accessed=10 * rows * chans,
            transcendentals=0,
        ),
        name="hyena",
    )(hyena_q, hyena_k, hyena_v, rim, taps, direct[None])


def deal_kernel(q_ref, k_ref, v_ref, id_ref, *refs):
    outs, held, (arrive, leave) = refs[: SQUAD + 1], refs[SQUAD + 1 : -2], refs[-2:]
    rows, feat = q_ref.shape
    width = feat // SQUAD
    corner = corner_of()
    order = list(range(1, SQUAD)) + [0]
    copies = {}
    for k in order:
        cols = pl.ds(pl.multiple_of(jnp.bitwise_xor(corner, k) * width, width), width)
        base = rows if k else 0
        places = (
            (q_ref, held[k + 1] if k else held[0], 0),
            (k_ref, held[k + 1], base + TAG),
            (v_ref, held[k + 1], base + TAG + rows),
        )
        copies[k] = [
            pltpu.make_async_copy(
                source.at[:, cols], target.at[pl.ds(begin, rows)], arrive.at[k, i]
            )
            for i, (source, target, begin) in enumerate(places)
        ]
        for copy in copies[k]:
            copy.start()
    ids = (id_ref[...] + 1).astype(jnp.float32)
    spare = jnp.zeros((TAG - ids.shape[0], LANES), jnp.float32)
    ids = jnp.concatenate([ids, spare], axis=0)
    tag = jnp.concatenate([ids] * (width // LANES), axis=1).astype(jnp.bfloat16)
    for i, target in enumerate(held):
        begin = 0 if i == 1 else rows
        target[begin : begin + TAG, :] = tag
    leaving = [
        pltpu.make_async_copy(source, out, leave.at[i])
        for i, (source, out) in enumerate(zip(held, outs))
    ]
    for k in order:
        for copy in copies[k]:
            copy.wait()
        leaving[k + 1].start()
    leaving[0].start()
    for copy in leaving:
        copy.wait()


def deal(queries, keys, values, ids):
    rows, feat = queries.shape
    tall = [rows + TAG, 2 * rows + TAG] + [3 * rows + TAG] * (SQUAD - 1)
    shapes = [(x, feat // SQUAD) for x in tall]
    anywhere = pl.BlockSpec(memory_space=pl.ANY)
    return list(
        pl.pallas_call(
            deal_kernel,
            in_specs=[anywhere] * 3 + [VMEM],
            out_specs=[anywhere] * len(tall),
            out_shape=[jax.ShapeDtypeStruct(x, jnp.bfloat16) for x in shapes],
            scratch_shapes=[pltpu.VMEM(x, jnp.bfloat16) for x in shapes]
            + [pltpu.SemaphoreType.DMA((SQUAD, 3)), pltpu.SemaphoreType.DMA((SQUAD + 1,))],
            compiler_params=pltpu.CompilerParams(vmem_limit_bytes=ALL_VMEM),
            cost_estimate=pl.CostEstimate(
                flops=0, bytes_accessed=12 * rows * feat, transcendentals=0
            ),
            name="deal",
        )(queries, keys, values, ids)
    )


def id_columns(tag_ref, rows):
    tag = tag_ref[:, :LANES].astype(jnp.float32)
    tiles = [jnp.broadcast_to(tag[t : t + 1], (LANES, LANES)).T for t in range(rows // LANES)]
    return jnp.concatenate(tiles, axis=0)


def place_keys(parts, corner, base, rows, keys, values):
    heads = keys.shape[0]
    marks = lax.broadcasted_iota(jnp.int32, (rows, LANES), 1).astype(jnp.float32) + 1.0
    for k, part in enumerate(parts):
        begin = pl.multiple_of((jnp.bitwise_xor(corner, k) + base) * rows, rows)
        span = pl.ds(begin, rows)
        ids = id_columns(part.at[:TAG], rows)
        mask = jnp.where(ids == marks, 0.0, -NEG).astype(jnp.bfloat16)
        for h in range(heads):
            cols = slice(h * HD, (h + 1) * HD)
            keys[h, span, :HD] = part[TAG : TAG + rows, cols]
            keys[h, span, HD:] = mask
            values[h, span, :] = part[TAG + rows : TAG + 2 * rows, cols]


def near_parts(near, rows):
    tall = 2 * rows + TAG
    return [near[0], near[1].at[:tall], near[1].at[tall:], near[2]]


def place_queries(parts, corner, rows, queries):
    heads = queries.shape[0]
    marks = lax.broadcasted_iota(jnp.int32, (rows, LANES), 1).astype(jnp.float32) + 1.0
    for k, part in enumerate(parts):
        begin = pl.multiple_of(jnp.bitwise_xor(corner, k) * rows, rows)
        span = pl.ds(begin, rows)
        ids = id_columns(part.at[rows : rows + TAG], rows)
        mask = jnp.where(ids == marks, -1.0, 0.0).astype(jnp.bfloat16)
        for h in range(heads):
            queries[h, span, :HD] = part[:rows, h * HD : (h + 1) * HD]
            queries[h, span, HD:] = mask


def attend(query, keys, values, diagonal):
    factor = math.log2(math.e) / math.sqrt(HD)
    rows = query.shape[0]
    score = lax.dot_general(
        keys, query, (((1,), (1,)), ((), ())), preferred_element_type=jnp.float32
    )
    if diagonal:
        older = lax.broadcasted_iota(jnp.int32, (rows, rows), 0) <= lax.broadcasted_iota(
            jnp.int32, (rows, rows), 1
        )
        score = jnp.concatenate(
            [score[:-rows], jnp.where(older, score[-rows:], NEG)], axis=0
        )
    high = jnp.max(score, axis=0, keepdims=True)
    expo = jnp.exp2((score - high) * factor)
    total = jnp.sum(expo, axis=0, keepdims=True)
    summed = lax.dot_general(
        values,
        expo.astype(jnp.bfloat16),
        (((0,), (0,)), ((), ())),
        preferred_element_type=jnp.float32,
    )
    return summed / total, high * factor + jnp.log2(total)


def main_kernel(*refs):
    own, near, out, (queries, keys, values) = refs[:5], refs[5:8], refs[8], refs[9:]
    heads, span, _ = queries.shape
    rows = span // SQUAD
    width = heads * HD
    corner = corner_of()
    asked = [own[0]] + [p.at[: rows + TAG] for p in own[2:]]
    held = [own[1]] + [p.at[rows:] for p in own[2:]]
    place_queries(asked, corner, rows, queries)
    place_keys(held, corner, SQUAD, rows, keys, values)
    place_keys(near_parts(near, rows), corner, 0, rows, keys, values)
    for j in range(SQUAD):
        cols = slice(j * rows, (j + 1) * rows)
        reach = (SQUAD + 1 + j) * rows
        for h in range(heads):
            mixed, lse = attend(queries[h, cols], keys[h, :reach], values[h, :reach], True)
            out[h * HD : (h + 1) * HD, cols] = mixed
            out[width + h : width + h + 1, cols] = lse
        out[width + heads :, cols] = jnp.zeros((TAG - heads, rows), jnp.float32)


def far_kernel(*refs):
    asked, near, out, (queries, keys, values) = refs[:2], refs[2:5], refs[5], refs[6:]
    heads, span, _ = queries.shape
    rows = span // SQUAD
    width = heads * HD
    corner = corner_of()
    tall = rows + TAG
    asked = [asked[0].at[k * tall : (k + 1) * tall] for k in range(SQUAD - 1)] + [asked[1]]
    place_queries(asked, corner, rows, queries)
    place_keys(near_parts(near, rows), corner, 0, rows, keys, values)
    for j in range(SQUAD - 1):
        cols = slice(j * rows, (j + 1) * rows)
        stats = []
        for h in range(heads):
            mixed, lse = attend(
                queries[h, cols], keys[h, cols.stop :], values[h, cols.stop :], False
            )
            out[h * HD : (h + 1) * HD, cols] = mixed.astype(out.dtype)
            top = lse.astype(jnp.bfloat16).astype(jnp.float32)
            mid = (lse - top).astype(jnp.bfloat16).astype(jnp.float32)
            stats += [top, mid, lse - top - mid]
        stats.append(jnp.zeros((TAG - len(stats), rows), jnp.float32))
        out[width:, cols] = jnp.concatenate(stats, axis=0).astype(out.dtype)


def merge_kernel(main_ref, far_ref, *refs):
    outs, ready = refs[:-1], refs[-1]
    _, rows, width = ready.shape
    corner = corner_of()
    served = lax.axis_index("ctx") >= 2 * SQUAD
    for j in range(SQUAD):
        cols = slice(j * rows, (j + 1) * rows)
        for h in range(width // HD):
            feats = slice(h * HD, (h + 1) * HD)
            mixed = main_ref[feats, cols]
            if j < SQUAD - 1:
                here = main_ref[width + h : width + h + 1, cols]
                stats = far_ref[width:, cols].astype(jnp.float32)
                there = stats[3 * h : 3 * h + 1] + stats[3 * h + 1 : 3 * h + 2]
                there = jnp.where(served, there + stats[3 * h + 2 : 3 * h + 3], NEG)
                high = jnp.maximum(here, there)
                here, there = jnp.exp2(here - high), jnp.exp2(there - high)
                total = here + there
                mixed = mixed * (here / total) + far_ref[feats, cols].astype(jnp.float32) * (
                    there / total
                )
            ready[j, :, feats] = mixed.T.astype(ready.dtype)
    for k, out in enumerate(outs):
        out[...] = ready[jnp.bitwise_xor(corner, k)]


def project_kernel(ranks, *refs):
    parts, weight_ref, out_ref, whole = refs[:-3], refs[-3], refs[-2], refs[-1]
    mine, corner = lax.axis_index("tp"), corner_of()
    width = parts[0].shape[1]
    for r in range(ranks):
        source = lax.rem(mine + ranks - r, ranks)
        for k in range(SQUAD):
            begin = (source * SQUAD + jnp.bitwise_xor(corner, k)) * width
            whole[:, pl.ds(pl.multiple_of(begin, width), width)] = parts[r * SQUAD + k][...]
    block = 2 * LANES
    for c in range(out_ref.shape[1] // block):
        cols = slice(c * block, (c + 1) * block)
        out_ref[:, cols] = jnp.dot(
            whole[...], weight_ref[:, cols], preferred_element_type=jnp.float32
        ).astype(out_ref.dtype)


def local(
    hyena_q, hyena_k, hyena_v, filters, direct, queries, keys, values, segment_ids, out_weight
):
    rows, feat = queries.shape
    count, ranks = lax.axis_size("ctx"), lax.axis_size("tp")
    width = feat // SQUAD
    heads = width // HD
    bf16, f32 = jnp.bfloat16, jnp.float32

    def swap(value, mask):
        return lax.ppermute(value, "ctx", [(i, i ^ mask) for i in range(count)])

    def climb(value, first=0):
        return lax.ppermute(value, "ctx", [(i, i + SQUAD) for i in range(first, count - SQUAD)])

    def descend(value):
        return lax.ppermute(
            value, "ctx", [(i, i - SQUAD) for i in range(2 * SQUAD, count)]
        )

    asked, kept, *sent = deal(
        queries, keys, values, segment_ids.reshape(rows // LANES, LANES)
    )
    tall = rows + TAG
    near = [climb(kept)]
    beside = [swap(sent[0], 1), swap(sent[1], 2)]
    sent[2], beside[0] = lax.optimization_barrier((sent[2], beside[0]))
    across = swap(sent[2], 3)
    beside[1], near[0] = lax.optimization_barrier((beside[1], near[0]))
    near.append(climb(jnp.concatenate([x[rows:] for x in beside], axis=0)))
    back = [descend(jnp.concatenate([asked] + [x[:tall] for x in beside], axis=0))]
    near.append(climb(across[rows:]))
    back.append(descend(across[:tall]))
    tail_k = hyena_k[rows - LANES :].astype(f32)
    tail_v = hyena_v[rows - LANES :].astype(f32)
    rim = lax.ppermute(
        (tail_k * tail_v).astype(bf16),
        "ctx",
        [(i, i + 1) for i in range(count - 1)],
    )
    own = [asked, kept, *beside, across]
    def store(blocks):
        return [
            pltpu.VMEM((heads, SQUAD * rows, 2 * HD), bf16),
            pltpu.VMEM((heads, blocks * rows, 2 * HD), bf16),
            pltpu.VMEM((heads, blocks * rows, HD), bf16),
        ]

    (far,) = kernel_call(
        far_kernel,
        (*back, *near),
        [jax.ShapeDtypeStruct((width + TAG, (SQUAD - 1) * rows), bf16)],
        "far",
        store(SQUAD),
        flops=6 * 4 * rows * rows * width,
        exps=6 * rows * rows * heads,
    )
    far = climb(far, SQUAD)
    (main,) = kernel_call(
        main_kernel,
        (*own, *near),
        [jax.ShapeDtypeStruct((width + TAG, SQUAD * rows), f32)],
        "main",
        store(2 * SQUAD),
        flops=26 * 4 * rows * rows * width,
        exps=26 * rows * rows * heads,
    )
    done = kernel_call(
        merge_kernel,
        (main, far),
        [jax.ShapeDtypeStruct((rows, width), bf16)] * SQUAD,
        "merge",
        [pltpu.VMEM((SQUAD, rows, width), bf16)],
    )
    rim, done[0] = lax.optimization_barrier((rim, done[0]))
    hyena_out = hyena(hyena_q, hyena_k, hyena_v, rim, filters, direct)

    def turn(value, r):
        return lax.ppermute(value, "tp", [(t, (t + r) % ranks) for t in range(ranks)])

    pieces = [swap(done[k], k) for k in range(1, SQUAD)]
    hyena_out, *pieces = lax.optimization_barrier((hyena_out, done[0], *pieces))
    pieces += [turn(piece, r) for r in range(1, ranks) for piece in pieces]
    (attn_out,) = kernel_call(
        functools.partial(project_kernel, ranks),
        (*pieces, out_weight),
        [jax.ShapeDtypeStruct((rows, out_weight.shape[1]), bf16)],
        "project",
        [pltpu.VMEM((rows, ranks * feat), bf16)],
        flops=2 * rows * math.prod(out_weight.shape),
    )
    return (hyena_out, attn_out)


def solution(mesh):
    placed = (
        P("ctx", "tp"),
        P("ctx", "tp"),
        P("ctx", "tp"),
        P("tp", None),
        P("tp"),
        P("ctx", "tp"),
        P("ctx", "tp"),
        P("ctx", "tp"),
        P("ctx"),
        P(None, "tp"),
    )
    return jax.shard_map(
        local,
        mesh=mesh,
        in_specs=placed,
        out_specs=(P("ctx", "tp"), P("ctx", "tp")),
        check_vma=False,
    )
```

```python
import functools
import math

import jax
import jax.numpy as jnp
from jax import lax
from jax.experimental import pallas as pl
from jax.experimental.pallas import tpu as pltpu
from jax.sharding import PartitionSpec as P

HD = 128
SQUAD = 4
NEG = -1e30
TAG = 16
LANES = 128
VMEM_LIMIT = 32 * 1024 * 1024
ALL_VMEM = 62 * 1024 * 1024
VMEM = pl.BlockSpec(memory_space=pltpu.VMEM)


def corner_of():
    return lax.rem(lax.axis_index("ctx"), SQUAD)


def kernel_call(kernel, args, shapes, name, scratch=(), flops=0, exps=0):
    total = sum(math.prod(x.shape) * x.dtype.itemsize for x in (*args, *shapes))
    return list(pl.pallas_call(
        kernel,
        in_specs=[VMEM] * len(args),
        out_specs=[VMEM] * len(shapes),
        out_shape=shapes,
        scratch_shapes=scratch,
        compiler_params=pltpu.CompilerParams(vmem_limit_bytes=VMEM_LIMIT),
        cost_estimate=pl.CostEstimate(flops=flops, bytes_accessed=total, transcendentals=exps),
        name=name,
    )(*args))


def hyena_kernel(q_ref, k_ref, v_ref, rim_ref, taps_ref, direct_ref, out_ref):
    rows, width = q_ref.shape
    per_tile = taps_ref.shape[0] * LANES // width
    group = LANES // per_tile
    windows = rows // LANES
    shape = (LANES, LANES)
    down, along = (lax.broadcasted_iota(jnp.int32, shape, i) for i in range(2))
    turn = jnp.where((down + along) % LANES == 0, 1.0, 0.0).astype(jnp.bfloat16)
    before = jnp.where(along > down, 1.0, 0.0).astype(jnp.bfloat16)
    within = jnp.where(along > down, 0.0, 1.0).astype(jnp.bfloat16)
    taps = jnp.dot(taps_ref[...], turn, preferred_element_type=jnp.float32)
    lane_group = lax.broadcasted_iota(jnp.int32, (LANES, windows * LANES), 1) % LANES // group
    for tile in range(width // LANES):
        cols = slice(tile * LANES, (tile + 1) * LANES)
        mixed = (k_ref[:, cols].astype(jnp.float32) * v_ref[:, cols].astype(jnp.float32)).astype(
            jnp.bfloat16
        )
        full = jnp.concatenate([rim_ref[:, cols], mixed], axis=0)
        stacked = jnp.concatenate(
            [full[w * LANES : (w + 2) * LANES] for w in range(windows)], axis=1
        )
        tables = []
        for g in range(per_tile):
            at = tile * per_tile + g
            row = taps[at : at + 1]
            ring = pltpu.roll(
                jnp.broadcast_to(row, shape), 0, 1, stride=1, stride_axis=0
            ).astype(jnp.bfloat16)
            tables.append(jnp.concatenate([ring * before, ring * within], axis=1))
        parts = jnp.dot(
            jnp.concatenate(tables, axis=0), stacked, preferred_element_type=jnp.float32
        )
        conv = parts[:LANES]
        for g in range(1, per_tile):
            conv = jnp.where(lane_group == g, parts[g * LANES : (g + 1) * LANES], conv)
        conv = jnp.concatenate(
            [conv[:, w * LANES : (w + 1) * LANES] for w in range(windows)], axis=0
        )
        out_ref[:, cols] = (
            q_ref[:, cols].astype(jnp.float32)
            * (conv + direct_ref[:, cols].astype(jnp.float32) * mixed.astype(jnp.float32))
        ).astype(jnp.bfloat16)


def hyena(hyena_q, hyena_k, hyena_v, rim, filters, direct):
    rows, chans = hyena_q.shape
    groups, kernel = filters.shape
    taps = jnp.pad(filters, ((0, 0), (0, LANES - kernel)))
    block = 2 * LANES
    steps = chans // block
    wide = pl.BlockSpec((rows, block), lambda i: (0, i))
    return pl.pallas_call(
        hyena_kernel,
        grid=(steps,),
        in_specs=[
            wide,
            wide,
            wide,
            pl.BlockSpec((LANES, block), lambda i: (0, i)),
            pl.BlockSpec((groups // steps, LANES), lambda i: (i, 0)),
            pl.BlockSpec((1, block), lambda i: (0, i)),
        ],
        out_specs=wide,
        out_shape=jax.ShapeDtypeStruct((rows, chans), jnp.bfloat16),
        compiler_params=pltpu.CompilerParams(vmem_limit_bytes=VMEM_LIMIT),
        cost_estimate=pl.CostEstimate(
            flops=4 * rows * chans * 2 * LANES * 8,
            bytes_accessed=10 * rows * chans,
            transcendentals=0,
        ),
        name="hyena",
    )(hyena_q, hyena_k, hyena_v, rim, taps, direct[None])


def deal_kernel(q_ref, k_ref, v_ref, id_ref, *refs):
    outs, held, (arrive, leave) = refs[: SQUAD + 1], refs[SQUAD + 1 : -2], refs[-2:]
    rows, feat = q_ref.shape
    width = feat // SQUAD
    corner = corner_of()
    order = list(range(1, SQUAD)) + [0]
    copies = {}
    for k in order:
        cols = pl.ds(pl.multiple_of(jnp.bitwise_xor(corner, k) * width, width), width)
        base = rows if k else 0
        places = (
            (q_ref, held[k + 1] if k else held[0], 0),
            (k_ref, held[k + 1], base + TAG),
            (v_ref, held[k + 1], base + TAG + rows),
        )
        copies[k] = [
            pltpu.make_async_copy(
                source.at[:, cols], target.at[pl.ds(begin, rows)], arrive.at[k, i]
            )
            for i, (source, target, begin) in enumerate(places)
        ]
        for copy in copies[k]:
            copy.start()
    ids = (id_ref[...] + 1).astype(jnp.float32)
    spare = jnp.zeros((TAG - ids.shape[0], LANES), jnp.float32)
    ids = jnp.concatenate([ids, spare], axis=0)
    tag = jnp.concatenate([ids] * (width // LANES), axis=1).astype(jnp.bfloat16)
    for i, target in enumerate(held):
        begin = 0 if i == 1 else rows
        target[begin : begin + TAG, :] = tag
    leaving = [
        pltpu.make_async_copy(source, out, leave.at[i])
        for i, (source, out) in enumerate(zip(held, outs))
    ]
    for k in order:
        for copy in copies[k]:
            copy.wait()
        leaving[k + 1].start()
    leaving[0].start()
    for copy in leaving:
        copy.wait()


def deal(queries, keys, values, ids):
    rows, feat = queries.shape
    tall = [rows + TAG, 2 * rows + TAG] + [3 * rows + TAG] * (SQUAD - 1)
    shapes = [(x, feat // SQUAD) for x in tall]
    anywhere = pl.BlockSpec(memory_space=pl.ANY)
    return list(
        pl.pallas_call(
            deal_kernel,
            in_specs=[anywhere] * 3 + [VMEM],
            out_specs=[anywhere] * len(tall),
            out_shape=[jax.ShapeDtypeStruct(x, jnp.bfloat16) for x in shapes],
            scratch_shapes=[pltpu.VMEM(x, jnp.bfloat16) for x in shapes]
            + [pltpu.SemaphoreType.DMA((SQUAD, 3)), pltpu.SemaphoreType.DMA((SQUAD + 1,))],
            compiler_params=pltpu.CompilerParams(vmem_limit_bytes=ALL_VMEM),
            cost_estimate=pl.CostEstimate(
                flops=0, bytes_accessed=12 * rows * feat, transcendentals=0
            ),
            name="deal",
        )(queries, keys, values, ids)
    )


def id_columns(tag_ref, rows):
    tag = tag_ref[:, :LANES].astype(jnp.float32)
    tiles = [jnp.broadcast_to(tag[t : t + 1], (LANES, LANES)).T for t in range(rows // LANES)]
    return jnp.concatenate(tiles, axis=0)


def place_keys(parts, corner, base, rows, keys, values):
    heads = keys.shape[0]
    marks = lax.broadcasted_iota(jnp.int32, (rows, LANES), 1).astype(jnp.float32) + 1.0
    for k, part in enumerate(parts):
        begin = pl.multiple_of((jnp.bitwise_xor(corner, k) + base) * rows, rows)
        span = pl.ds(begin, rows)
        ids = id_columns(part.at[:TAG], rows)
        mask = jnp.where(ids == marks, 0.0, -NEG).astype(jnp.bfloat16)
        for h in range(heads):
            cols = slice(h * HD, (h + 1) * HD)
            keys[h, span, :HD] = part[TAG : TAG + rows, cols]
            keys[h, span, HD:] = mask
            values[h, span, :] = part[TAG + rows : TAG + 2 * rows, cols]


def near_parts(near, rows):
    tall = 2 * rows + TAG
    return [near[0], near[1].at[:tall], near[1].at[tall:], near[2]]


def place_queries(parts, corner, rows, queries):
    heads = queries.shape[0]
    marks = lax.broadcasted_iota(jnp.int32, (rows, LANES), 1).astype(jnp.float32) + 1.0
    for k, part in enumerate(parts):
        begin = pl.multiple_of(jnp.bitwise_xor(corner, k) * rows, rows)
        span = pl.ds(begin, rows)
        ids = id_columns(part.at[rows : rows + TAG], rows)
        mask = jnp.where(ids == marks, -1.0, 0.0).astype(jnp.bfloat16)
        for h in range(heads):
            queries[h, span, :HD] = part[:rows, h * HD : (h + 1) * HD]
            queries[h, span, HD:] = mask


def attend(query, keys, values, diagonal):
    factor = math.log2(math.e) / math.sqrt(HD)
    rows = query.shape[0]
    score = lax.dot_general(
        keys, query, (((1,), (1,)), ((), ())), preferred_element_type=jnp.float32
    )
    if diagonal:
        older = lax.broadcasted_iota(jnp.int32, (rows, rows), 0) <= lax.broadcasted_iota(
            jnp.int32, (rows, rows), 1
        )
        score = jnp.concatenate(
            [score[:-rows], jnp.where(older, score[-rows:], NEG)], axis=0
        )
    high = jnp.max(score, axis=0, keepdims=True)
    expo = jnp.exp2((score - high) * factor)
    total = jnp.sum(expo, axis=0, keepdims=True)
    summed = lax.dot_general(
        values,
        expo.astype(jnp.bfloat16),
        (((0,), (0,)), ((), ())),
        preferred_element_type=jnp.float32,
    )
    return summed / total, high * factor + jnp.log2(total)


def main_kernel(*refs):
    own, near, out, (queries, keys, values) = refs[:5], refs[5:8], refs[8], refs[9:]
    heads, span, _ = queries.shape
    rows = span // SQUAD
    width = heads * HD
    corner = corner_of()
    asked = [own[0]] + [p.at[: rows + TAG] for p in own[2:]]
    held = [own[1]] + [p.at[rows:] for p in own[2:]]
    place_queries(asked, corner, rows, queries)
    place_keys(held, corner, SQUAD, rows, keys, values)
    place_keys(near_parts(near, rows), corner, 0, rows, keys, values)
    for j in range(SQUAD):
        cols = slice(j * rows, (j + 1) * rows)
        reach = (SQUAD + 1 + j) * rows
        for h in range(heads):
            mixed, lse = attend(queries[h, cols], keys[h, :reach], values[h, :reach], True)
            out[h * HD : (h + 1) * HD, cols] = mixed
            out[width + h : width + h + 1, cols] = lse
        out[width + heads :, cols] = jnp.zeros((TAG - heads, rows), jnp.float32)


def far_kernel(*refs):
    asked, near, out, (queries, keys, values) = refs[:2], refs[2:5], refs[5], refs[6:]
    heads, span, _ = queries.shape
    rows = span // SQUAD
    width = heads * HD
    corner = corner_of()
    tall = rows + TAG
    asked = [asked[0].at[k * tall : (k + 1) * tall] for k in range(SQUAD - 1)] + [asked[1]]
    place_queries(asked, corner, rows, queries)
    place_keys(near_parts(near, rows), corner, 0, rows, keys, values)
    for j in range(SQUAD - 1):
        cols = slice(j * rows, (j + 1) * rows)
        stats = []
        for h in range(heads):
            mixed, lse = attend(
                queries[h, cols], keys[h, cols.stop :], values[h, cols.stop :], False
            )
            out[h * HD : (h + 1) * HD, cols] = mixed.astype(out.dtype)
            top = lse.astype(jnp.bfloat16).astype(jnp.float32)
            mid = (lse - top).astype(jnp.bfloat16).astype(jnp.float32)
            stats += [top, mid, lse - top - mid]
        stats.append(jnp.zeros((TAG - len(stats), rows), jnp.float32))
        out[width:, cols] = jnp.concatenate(stats, axis=0).astype(out.dtype)


def merge_kernel(main_ref, far_ref, *refs):
    outs, ready = refs[:-1], refs[-1]
    _, rows, width = ready.shape
    corner = corner_of()
    served = lax.axis_index("ctx") >= 2 * SQUAD
    for j in range(SQUAD):
        cols = slice(j * rows, (j + 1) * rows)
        for h in range(width // HD):
            feats = slice(h * HD, (h + 1) * HD)
            mixed = main_ref[feats, cols]
            if j < SQUAD - 1:
                here = main_ref[width + h : width + h + 1, cols]
                stats = far_ref[width:, cols].astype(jnp.float32)
                there = stats[3 * h : 3 * h + 1] + stats[3 * h + 1 : 3 * h + 2]
                there = jnp.where(served, there + stats[3 * h + 2 : 3 * h + 3], NEG)
                high = jnp.maximum(here, there)
                here, there = jnp.exp2(here - high), jnp.exp2(there - high)
                total = here + there
                mixed = mixed * (here / total) + far_ref[feats, cols].astype(jnp.float32) * (
                    there / total
                )
            ready[j, :, feats] = mixed.T.astype(ready.dtype)
    for k, out in enumerate(outs):
        out[...] = ready[jnp.bitwise_xor(corner, k)]


def project_kernel(ranks, *refs):
    parts, weight_ref, out_ref, whole = refs[:-3], refs[-3], refs[-2], refs[-1]
    mine, corner = lax.axis_index("tp"), corner_of()
    width = parts[0].shape[1]
    for r in range(ranks):
        source = lax.rem(mine + ranks - r, ranks)
        for k in range(SQUAD):
            begin = (source * SQUAD + jnp.bitwise_xor(corner, k)) * width
            whole[:, pl.ds(pl.multiple_of(begin, width), width)] = parts[r * SQUAD + k][...]
    block = 2 * LANES
    for c in range(out_ref.shape[1] // block):
        cols = slice(c * block, (c + 1) * block)
        out_ref[:, cols] = jnp.dot(
            whole[...], weight_ref[:, cols], preferred_element_type=jnp.float32
        ).astype(out_ref.dtype)


def local(
    hyena_q, hyena_k, hyena_v, filters, direct, queries, keys, values, segment_ids, out_weight
):
    rows, feat = queries.shape
    count, ranks = lax.axis_size("ctx"), lax.axis_size("tp")
    width = feat // SQUAD
    heads = width // HD
    bf16, f32 = jnp.bfloat16, jnp.float32

    def swap(value, mask):
        return lax.ppermute(value, "ctx", [(i, i ^ mask) for i in range(count)])

    def climb(value, first=0):
        return lax.ppermute(value, "ctx", [(i, i + SQUAD) for i in range(first, count - SQUAD)])

    def descend(value):
        return lax.ppermute(
            value, "ctx", [(i, i - SQUAD) for i in range(2 * SQUAD, count)]
        )

    asked, kept, *sent = deal(
        queries, keys, values, segment_ids.reshape(rows // LANES, LANES)
    )
    tall = rows + TAG
    near = [climb(kept)]
    beside = [swap(sent[0], 1), swap(sent[1], 2)]
    sent[2], beside[0] = lax.optimization_barrier((sent[2], beside[0]))
    across = swap(sent[2], 3)
    beside[1], near[0] = lax.optimization_barrier((beside[1], near[0]))
    near.append(climb(jnp.concatenate([x[rows:] for x in beside], axis=0)))
    back = [descend(jnp.concatenate([asked] + [x[:tall] for x in beside], axis=0))]
    near.append(climb(across[rows:]))
    back.append(descend(across[:tall]))
    tail_k = hyena_k[rows - LANES :].astype(f32)
    tail_v = hyena_v[rows - LANES :].astype(f32)
    rim = lax.ppermute(
        (tail_k * tail_v).astype(bf16),
        "ctx",
        [(i, i + 1) for i in range(count - 1)],
    )
    own = [asked, kept, *beside, across]
    def store(blocks):
        return [
            pltpu.VMEM((heads, SQUAD * rows, 2 * HD), bf16),
            pltpu.VMEM((heads, blocks * rows, 2 * HD), bf16),
            pltpu.VMEM((heads, blocks * rows, HD), bf16),
        ]

    (far,) = kernel_call(
        far_kernel,
        (*back, *near),
        [jax.ShapeDtypeStruct((width + TAG, (SQUAD - 1) * rows), bf16)],
        "far",
        store(SQUAD),
        flops=6 * 4 * rows * rows * width,
        exps=6 * rows * rows * heads,
    )
    far = climb(far, SQUAD)
    own[1], rim = lax.optimization_barrier((own[1], rim))
    (main,) = kernel_call(
        main_kernel,
        (*own, *near),
        [jax.ShapeDtypeStruct((width + TAG, SQUAD * rows), f32)],
        "main",
        store(2 * SQUAD),
        flops=26 * 4 * rows * rows * width,
        exps=26 * rows * rows * heads,
    )
    done = kernel_call(
        merge_kernel,
        (main, far),
        [jax.ShapeDtypeStruct((rows, width), bf16)] * SQUAD,
        "merge",
        [pltpu.VMEM((SQUAD, rows, width), bf16)],
    )
    rim, done[0] = lax.optimization_barrier((rim, done[0]))
    hyena_out = hyena(hyena_q, hyena_k, hyena_v, rim, filters, direct)

    def turn(value, r):
        return lax.ppermute(value, "tp", [(t, (t + r) % ranks) for t in range(ranks)])

    pieces = [swap(done[k], k) for k in range(1, SQUAD)]
    hyena_out, *pieces = lax.optimization_barrier((hyena_out, done[0], *pieces))
    pieces += [turn(piece, r) for r in range(1, ranks) for piece in pieces]
    (attn_out,) = kernel_call(
        functools.partial(project_kernel, ranks),
        (*pieces, out_weight),
        [jax.ShapeDtypeStruct((rows, out_weight.shape[1]), bf16)],
        "project",
        [pltpu.VMEM((rows, ranks * feat), bf16)],
        flops=2 * rows * math.prod(out_weight.shape),
    )
    return (hyena_out, attn_out)


def solution(mesh):
    placed = (
        P("ctx", "tp"),
        P("ctx", "tp"),
        P("ctx", "tp"),
        P("tp", None),
        P("tp"),
        P("ctx", "tp"),
        P("ctx", "tp"),
        P("ctx", "tp"),
        P("ctx"),
        P(None, "tp"),
    )
    return jax.shard_map(
        local,
        mesh=mesh,
        in_specs=placed,
        out_specs=(P("ctx", "tp"), P("ctx", "tp")),
        check_vma=False,
    )
```

```python
import functools
import math

import jax
import jax.numpy as jnp
from jax import lax
from jax.experimental import pallas as pl
from jax.experimental.pallas import tpu as pltpu
from jax.sharding import PartitionSpec as P

HD = 128
SQUAD = 4
NEG = -1e30
TAG = 16
LANES = 128
VMEM_LIMIT = 32 * 1024 * 1024
VMEM = pl.BlockSpec(memory_space=pltpu.VMEM)


def corner_of():
    return lax.rem(lax.axis_index("ctx"), SQUAD)


def kernel_call(kernel, args, shapes, name, scratch=(), flops=0, exps=0):
    total = sum(math.prod(x.shape) * x.dtype.itemsize for x in (*args, *shapes))
    return list(pl.pallas_call(
        kernel,
        in_specs=[VMEM] * len(args),
        out_specs=[VMEM] * len(shapes),
        out_shape=shapes,
        scratch_shapes=scratch,
        compiler_params=pltpu.CompilerParams(vmem_limit_bytes=VMEM_LIMIT),
        cost_estimate=pl.CostEstimate(flops=flops, bytes_accessed=total, transcendentals=exps),
        name=name,
    )(*args))


def hyena_kernel(q_ref, k_ref, v_ref, rim_ref, taps_ref, direct_ref, out_ref, taps):
    rows, chans = q_ref.shape
    groups = taps_ref.shape[0]
    group = chans // groups
    per_tile = LANES // group
    windows = rows // LANES
    shape = (LANES, LANES)
    down, along = (lax.broadcasted_iota(jnp.int32, shape, i) for i in range(2))
    turn = jnp.where((down + along) % LANES == 0, 1.0, 0.0).astype(jnp.bfloat16)
    before = jnp.where(along > down, 1.0, 0.0).astype(jnp.bfloat16)
    within = jnp.where(along > down, 0.0, 1.0).astype(jnp.bfloat16)
    taps[...] = jnp.dot(taps_ref[...], turn, preferred_element_type=jnp.float32)
    lane_group = lax.broadcasted_iota(jnp.int32, (LANES, windows * LANES), 1) % LANES // group

    @pl.loop(0, chans // LANES, unroll=2)
    def _(tile):
        cols = pl.ds(pl.multiple_of(tile * LANES, LANES), LANES)
        rings = taps[pl.ds(pl.multiple_of(tile * per_tile, per_tile), per_tile), :]
        mixed = (k_ref[:, cols].astype(jnp.float32) * v_ref[:, cols].astype(jnp.float32)).astype(
            jnp.bfloat16
        )
        full = jnp.concatenate([rim_ref[:, cols], mixed], axis=0)
        stacked = jnp.concatenate(
            [full[w * LANES : (w + 2) * LANES] for w in range(windows)], axis=1
        )
        conv = jnp.zeros((LANES, windows * LANES), jnp.float32)
        for g in range(per_tile):
            ring = pltpu.roll(
                jnp.broadcast_to(rings[g : g + 1], shape), 0, 1, stride=1, stride_axis=0
            ).astype(jnp.bfloat16)
            table = jnp.concatenate([ring * before, ring * within], axis=1)
            part = jnp.dot(table, stacked, preferred_element_type=jnp.float32)
            conv = jnp.where(lane_group == g, part, conv)
        conv = jnp.concatenate(
            [conv[:, w * LANES : (w + 1) * LANES] for w in range(windows)], axis=0
        )
        out_ref[:, cols] = (
            q_ref[:, cols].astype(jnp.float32)
            * (conv + direct_ref[:, cols].astype(jnp.float32) * mixed.astype(jnp.float32))
        ).astype(jnp.bfloat16)


def hyena(hyena_q, hyena_k, hyena_v, rim, filters, direct):
    rows, chans = hyena_q.shape
    groups, kernel = filters.shape
    taps = jnp.pad(filters, ((0, 0), (0, LANES - kernel)))
    (out,) = kernel_call(
        hyena_kernel,
        (hyena_q, hyena_k, hyena_v, rim, taps, direct[None]),
        [jax.ShapeDtypeStruct((rows, chans), jnp.bfloat16)],
        "hyena",
        [pltpu.VMEM((groups, LANES), jnp.float32)],
        flops=4 * rows * chans * 2 * LANES * 8,
    )
    return out


def deal_kernel(q_ref, k_ref, v_ref, id_ref, *refs):
    outs, arrive = refs[:-1], refs[-1]
    rows, feat = q_ref.shape
    width = feat // SQUAD
    corner = corner_of()
    copies = []
    for k in (*range(1, SQUAD), 0):
        cols = pl.ds(pl.multiple_of(jnp.bitwise_xor(corner, k) * width, width), width)
        base = rows if k else 0
        places = (
            (q_ref, outs[k + 1] if k else outs[0], 0),
            (k_ref, outs[k + 1], base + TAG),
            (v_ref, outs[k + 1], base + TAG + rows),
        )
        copies += [
            pltpu.make_async_copy(
                source.at[:, cols], target.at[pl.ds(begin, rows)], arrive.at[k, i]
            )
            for i, (source, target, begin) in enumerate(places)
        ]
    for copy in copies:
        copy.start()
    ids = (id_ref[...] + 1).astype(jnp.float32)
    spare = jnp.zeros((TAG - ids.shape[0], LANES), jnp.float32)
    ids = jnp.concatenate([ids, spare], axis=0)
    tag = jnp.concatenate([ids] * (width // LANES), axis=1).astype(jnp.bfloat16)
    for i, target in enumerate(outs):
        begin = 0 if i == 1 else rows
        target[begin : begin + TAG, :] = tag
    for copy in copies:
        copy.wait()


def deal(queries, keys, values, ids):
    rows, feat = queries.shape
    tall = [rows + TAG, 2 * rows + TAG] + [3 * rows + TAG] * (SQUAD - 1)
    shapes = [(x, feat // SQUAD) for x in tall]
    held = [pltpu.with_memory_space_constraint(x, pltpu.HBM) for x in (queries, keys, values)]
    return list(
        pl.pallas_call(
            deal_kernel,
            in_specs=[pl.BlockSpec(memory_space=pl.ANY)] * 3 + [VMEM],
            out_specs=[VMEM] * len(tall),
            out_shape=[jax.ShapeDtypeStruct(x, jnp.bfloat16) for x in shapes],
            scratch_shapes=[pltpu.SemaphoreType.DMA((SQUAD, 3))],
            compiler_params=pltpu.CompilerParams(vmem_limit_bytes=VMEM_LIMIT),
            cost_estimate=pl.CostEstimate(
                flops=0, bytes_accessed=12 * rows * feat, transcendentals=0
            ),
            name="deal",
        )(*held, ids)
    )


def id_columns(tag_ref, rows):
    tag = tag_ref[:, :LANES].astype(jnp.float32)
    tiles = [jnp.broadcast_to(tag[t : t + 1], (LANES, LANES)).T for t in range(rows // LANES)]
    return jnp.concatenate(tiles, axis=0)


def place_keys(parts, corner, base, rows, keys, values):
    heads = keys.shape[0]
    marks = lax.broadcasted_iota(jnp.int32, (rows, LANES), 1).astype(jnp.float32) + 1.0
    for k, part in enumerate(parts):
        begin = pl.multiple_of((jnp.bitwise_xor(corner, k) + base) * rows, rows)
        span = pl.ds(begin, rows)
        ids = id_columns(part.at[:TAG], rows)
        mask = jnp.where(ids == marks, 0.0, -NEG).astype(jnp.bfloat16)
        for h in range(heads):
            cols = slice(h * HD, (h + 1) * HD)
            keys[h, span, :HD] = part[TAG : TAG + rows, cols]
            keys[h, span, HD:] = mask
            values[h, span, :] = part[TAG + rows : TAG + 2 * rows, cols]


def near_parts(near, rows):
    tall = 2 * rows + TAG
    return [near[0], near[1].at[:tall], near[1].at[tall:], near[2]]


def place_queries(parts, corner, rows, queries):
    heads = queries.shape[0]
    marks = lax.broadcasted_iota(jnp.int32, (rows, LANES), 1).astype(jnp.float32) + 1.0
    for k, part in enumerate(parts):
        begin = pl.multiple_of(jnp.bitwise_xor(corner, k) * rows, rows)
        span = pl.ds(begin, rows)
        ids = id_columns(part.at[rows : rows + TAG], rows)
        mask = jnp.where(ids == marks, -1.0, 0.0).astype(jnp.bfloat16)
        for h in range(heads):
            queries[h, span, :HD] = part[:rows, h * HD : (h + 1) * HD]
            queries[h, span, HD:] = mask


def attend(query, keys, values, diagonal):
    factor = math.log2(math.e) / math.sqrt(HD)
    rows = query.shape[0]
    score = lax.dot_general(
        keys, query, (((1,), (1,)), ((), ())), preferred_element_type=jnp.float32
    )
    if diagonal:
        older = lax.broadcasted_iota(jnp.int32, (rows, rows), 0) <= lax.broadcasted_iota(
            jnp.int32, (rows, rows), 1
        )
        score = jnp.concatenate(
            [score[:-rows], jnp.where(older, score[-rows:], NEG)], axis=0
        )
    high = jnp.max(score, axis=0, keepdims=True)
    expo = jnp.exp2((score - high) * factor)
    total = jnp.sum(expo, axis=0, keepdims=True)
    summed = lax.dot_general(
        values,
        expo.astype(jnp.bfloat16),
        (((0,), (0,)), ((), ())),
        preferred_element_type=jnp.float32,
    )
    return summed / total, high * factor + jnp.log2(total)


def main_kernel(*refs):
    own, near, out, (queries, keys, values) = refs[:5], refs[5:8], refs[8], refs[9:]
    heads, span, _ = queries.shape
    rows = span // SQUAD
    width = heads * HD
    corner = corner_of()
    asked = [own[0]] + [p.at[: rows + TAG] for p in own[2:]]
    held = [own[1]] + [p.at[rows:] for p in own[2:]]
    place_queries(asked, corner, rows, queries)
    place_keys(held, corner, SQUAD, rows, keys, values)
    place_keys(near_parts(near, rows), corner, 0, rows, keys, values)
    for j in range(SQUAD):
        cols = slice(j * rows, (j + 1) * rows)
        reach = (SQUAD + 1 + j) * rows
        for h in range(heads):
            mixed, lse = attend(queries[h, cols], keys[h, :reach], values[h, :reach], True)
            out[h * HD : (h + 1) * HD, cols] = mixed
            out[width + h : width + h + 1, cols] = lse
        out[width + heads :, cols] = jnp.zeros((TAG - heads, rows), jnp.float32)


def far_kernel(*refs):
    asked, near, out, (queries, keys, values) = refs[:2], refs[2:5], refs[5], refs[6:]
    heads, span, _ = queries.shape
    rows = span // SQUAD
    width = heads * HD
    corner = corner_of()
    tall = rows + TAG
    asked = [asked[0].at[k * tall : (k + 1) * tall] for k in range(SQUAD - 1)] + [asked[1]]
    place_queries(asked, corner, rows, queries)
    place_keys(near_parts(near, rows), corner, 0, rows, keys, values)
    for j in range(SQUAD - 1):
        cols = slice(j * rows, (j + 1) * rows)
        stats = []
        for h in range(heads):
            mixed, lse = attend(
                queries[h, cols], keys[h, cols.stop :], values[h, cols.stop :], False
            )
            out[h * HD : (h + 1) * HD, cols] = mixed.astype(out.dtype)
            top = lse.astype(jnp.bfloat16).astype(jnp.float32)
            mid = (lse - top).astype(jnp.bfloat16).astype(jnp.float32)
            stats += [top, mid, lse - top - mid]
        stats.append(jnp.zeros((TAG - len(stats), rows), jnp.float32))
        out[width:, cols] = jnp.concatenate(stats, axis=0).astype(out.dtype)


def merge_kernel(main_ref, far_ref, *refs):
    outs, ready = refs[:-1], refs[-1]
    _, rows, width = ready.shape
    corner = corner_of()
    served = lax.axis_index("ctx") >= 2 * SQUAD
    for j in range(SQUAD):
        cols = slice(j * rows, (j + 1) * rows)
        for h in range(width // HD):
            feats = slice(h * HD, (h + 1) * HD)
            mixed = main_ref[feats, cols]
            if j < SQUAD - 1:
                here = main_ref[width + h : width + h + 1, cols]
                stats = far_ref[width:, cols].astype(jnp.float32)
                there = stats[3 * h : 3 * h + 1] + stats[3 * h + 1 : 3 * h + 2]
                there = jnp.where(served, there + stats[3 * h + 2 : 3 * h + 3], NEG)
                high = jnp.maximum(here, there)
                here, there = jnp.exp2(here - high), jnp.exp2(there - high)
                total = here + there
                mixed = mixed * (here / total) + far_ref[feats, cols].astype(jnp.float32) * (
                    there / total
                )
            ready[j, :, feats] = mixed.T.astype(ready.dtype)
    for k, out in enumerate(outs):
        out[...] = ready[jnp.bitwise_xor(corner, k)]


def project_kernel(ranks, *refs):
    parts, weight_ref, out_ref, whole = refs[:-3], refs[-3], refs[-2], refs[-1]
    mine, corner = lax.axis_index("tp"), corner_of()
    width = parts[0].shape[1]
    for r in range(ranks):
        source = lax.rem(mine + ranks - r, ranks)
        for k in range(SQUAD):
            begin = (source * SQUAD + jnp.bitwise_xor(corner, k)) * width
            whole[:, pl.ds(pl.multiple_of(begin, width), width)] = parts[r * SQUAD + k][...]
    block = 2 * LANES
    for c in range(out_ref.shape[1] // block):
        cols = slice(c * block, (c + 1) * block)
        out_ref[:, cols] = jnp.dot(
            whole[...], weight_ref[:, cols], preferred_element_type=jnp.float32
        ).astype(out_ref.dtype)


def local(
    hyena_q, hyena_k, hyena_v, filters, direct, queries, keys, values, segment_ids, out_weight
):
    rows, feat = queries.shape
    count, ranks = lax.axis_size("ctx"), lax.axis_size("tp")
    width = feat // SQUAD
    heads = width // HD
    bf16, f32 = jnp.bfloat16, jnp.float32

    def swap(value, mask):
        return lax.ppermute(value, "ctx", [(i, i ^ mask) for i in range(count)])

    def climb(value, first=0):
        return lax.ppermute(value, "ctx", [(i, i + SQUAD) for i in range(first, count - SQUAD)])

    def descend(value):
        return lax.ppermute(
            value, "ctx", [(i, i - SQUAD) for i in range(2 * SQUAD, count)]
        )

    asked, kept, *sent = deal(
        queries, keys, values, segment_ids.reshape(rows // LANES, LANES)
    )
    tall = rows + TAG
    near = [climb(kept)]
    beside = [swap(sent[0], 1), swap(sent[1], 2)]
    sent[2], beside[0] = lax.optimization_barrier((sent[2], beside[0]))
    across = swap(sent[2], 3)
    beside[1], near[0] = lax.optimization_barrier((beside[1], near[0]))
    near.append(climb(jnp.concatenate([x[rows:] for x in beside], axis=0)))
    back = [descend(jnp.concatenate([asked] + [x[:tall] for x in beside], axis=0))]
    near.append(climb(across[rows:]))
    back.append(descend(across[:tall]))
    tail_k = hyena_k[rows - LANES :].astype(f32)
    tail_v = hyena_v[rows - LANES :].astype(f32)
    rim = lax.ppermute(
        (tail_k * tail_v).astype(bf16),
        "ctx",
        [(i, i + 1) for i in range(count - 1)],
    )
    own = [asked, kept, *beside, across]
    def store(blocks):
        return [
            pltpu.VMEM((heads, SQUAD * rows, 2 * HD), bf16),
            pltpu.VMEM((heads, blocks * rows, 2 * HD), bf16),
            pltpu.VMEM((heads, blocks * rows, HD), bf16),
        ]

    (far,) = kernel_call(
        far_kernel,
        (*back, *near),
        [jax.ShapeDtypeStruct((width + TAG, (SQUAD - 1) * rows), bf16)],
        "far",
        store(SQUAD),
        flops=6 * 4 * rows * rows * width,
        exps=6 * rows * rows * heads,
    )
    far = climb(far, SQUAD)
    (main,) = kernel_call(
        main_kernel,
        (*own, *near),
        [jax.ShapeDtypeStruct((width + TAG, SQUAD * rows), f32)],
        "main",
        store(2 * SQUAD),
        flops=26 * 4 * rows * rows * width,
        exps=26 * rows * rows * heads,
    )
    done = kernel_call(
        merge_kernel,
        (main, far),
        [jax.ShapeDtypeStruct((rows, width), bf16)] * SQUAD,
        "merge",
        [pltpu.VMEM((SQUAD, rows, width), bf16)],
    )
    rim, done[0] = lax.optimization_barrier((rim, done[0]))
    hyena_out = hyena(hyena_q, hyena_k, hyena_v, rim, filters, direct)

    def turn(value, r):
        return lax.ppermute(value, "tp", [(t, (t + r) % ranks) for t in range(ranks)])

    pieces = [swap(done[k], k) for k in range(1, SQUAD)]
    hyena_out, *pieces = lax.optimization_barrier((hyena_out, done[0], *pieces))
    pieces += [turn(piece, r) for r in range(1, ranks) for piece in pieces]
    (attn_out,) = kernel_call(
        functools.partial(project_kernel, ranks),
        (*pieces, out_weight),
        [jax.ShapeDtypeStruct((rows, out_weight.shape[1]), bf16)],
        "project",
        [pltpu.VMEM((rows, ranks * feat), bf16)],
        flops=2 * rows * math.prod(out_weight.shape),
    )
    return (hyena_out, attn_out)


def solution(mesh):
    placed = (
        P("ctx", "tp"),
        P("ctx", "tp"),
        P("ctx", "tp"),
        P("tp", None),
        P("tp"),
        P("ctx", "tp"),
        P("ctx", "tp"),
        P("ctx", "tp"),
        P("ctx"),
        P(None, "tp"),
    )
    return jax.shard_map(
        local,
        mesh=mesh,
        in_specs=placed,
        out_specs=(P("ctx", "tp"), P("ctx", "tp")),
        check_vma=False,
    )
```

```python
import functools
import math

import jax
import jax.numpy as jnp
from jax import lax
from jax.experimental import pallas as pl
from jax.experimental.pallas import tpu as pltpu
from jax.sharding import PartitionSpec as P

HD = 128
SQUAD = 4
NEG = -1e30
TAG = 16
LANES = 128
VMEM_LIMIT = 32 * 1024 * 1024
VMEM = pl.BlockSpec(memory_space=pltpu.VMEM)


def corner_of():
    return lax.rem(lax.axis_index("ctx"), SQUAD)


def kernel_call(kernel, args, shapes, name, scratch=(), flops=0, exps=0):
    total = sum(math.prod(x.shape) * x.dtype.itemsize for x in (*args, *shapes))
    return list(pl.pallas_call(
        kernel,
        in_specs=[VMEM] * len(args),
        out_specs=[VMEM] * len(shapes),
        out_shape=shapes,
        scratch_shapes=scratch,
        compiler_params=pltpu.CompilerParams(vmem_limit_bytes=VMEM_LIMIT),
        cost_estimate=pl.CostEstimate(flops=flops, bytes_accessed=total, transcendentals=exps),
        name=name,
    )(*args))


def hyena_kernel(q_ref, k_ref, v_ref, near_rim, ring_rim, far_rim, taps_ref, direct_ref, out_ref, taps, rim):
    rows, chans = q_ref.shape
    groups = taps_ref.shape[0]
    group = chans // groups
    per_tile = LANES // group
    windows = rows // LANES
    shape = (LANES, LANES)
    down, along = (lax.broadcasted_iota(jnp.int32, shape, i) for i in range(2))
    turn = jnp.where((down + along) % LANES == 0, 1.0, 0.0).astype(jnp.bfloat16)
    before = jnp.where(along > down, 1.0, 0.0).astype(jnp.bfloat16)
    within = jnp.where(along > down, 0.0, 1.0).astype(jnp.bfloat16)
    taps[...] = jnp.dot(taps_ref[...], turn, preferred_element_type=jnp.float32)
    lane_group = lax.broadcasted_iota(jnp.int32, (LANES, windows * LANES), 1) % LANES // group

    half = chans // 2
    rim[:, :half] = near_rim[...]
    rim[:, half:] = ring_rim[...]

    @pl.when(corner_of() == 0)
    def _():
        rim[:, half:] = far_rim[...]

    @pl.loop(0, chans // LANES, unroll=2)
    def _(tile):
        cols = pl.ds(pl.multiple_of(tile * LANES, LANES), LANES)
        rings = taps[pl.ds(pl.multiple_of(tile * per_tile, per_tile), per_tile), :]
        mixed = (k_ref[:, cols].astype(jnp.float32) * v_ref[:, cols].astype(jnp.float32)).astype(
            jnp.bfloat16
        )
        full = jnp.concatenate([rim[:, cols], mixed], axis=0)
        stacked = jnp.concatenate(
            [full[w * LANES : (w + 2) * LANES] for w in range(windows)], axis=1
        )
        conv = jnp.zeros((LANES, windows * LANES), jnp.float32)
        for g in range(per_tile):
            ring = pltpu.roll(
                jnp.broadcast_to(rings[g : g + 1], shape), 0, 1, stride=1, stride_axis=0
            ).astype(jnp.bfloat16)
            table = jnp.concatenate([ring * before, ring * within], axis=1)
            part = jnp.dot(table, stacked, preferred_element_type=jnp.float32)
            conv = jnp.where(lane_group == g, part, conv)
        conv = jnp.concatenate(
            [conv[:, w * LANES : (w + 1) * LANES] for w in range(windows)], axis=0
        )
        out_ref[:, cols] = (
            q_ref[:, cols].astype(jnp.float32)
            * (conv + direct_ref[:, cols].astype(jnp.float32) * mixed.astype(jnp.float32))
        ).astype(jnp.bfloat16)


def hyena(hyena_q, hyena_k, hyena_v, rims, filters, direct):
    rows, chans = hyena_q.shape
    groups, kernel = filters.shape
    taps = jnp.pad(filters, ((0, 0), (0, LANES - kernel)))
    (out,) = kernel_call(
        hyena_kernel,
        (hyena_q, hyena_k, hyena_v, *rims, taps, direct[None]),
        [jax.ShapeDtypeStruct((rows, chans), jnp.bfloat16)],
        "hyena",
        [pltpu.VMEM((groups, LANES), jnp.float32), pltpu.VMEM((LANES, chans), jnp.bfloat16)],
        flops=4 * rows * chans * 2 * LANES * 8,
    )
    return out


def deal_kernel(q_ref, k_ref, v_ref, id_ref, *refs):
    outs, (held, arrive, told) = refs[:-3], refs[-3:]
    tell = pltpu.make_async_copy(id_ref, held, told)
    tell.start()
    rows, feat = q_ref.shape
    width = feat // SQUAD
    corner = corner_of()
    copies = []
    for k in (*range(1, SQUAD), 0):
        cols = pl.ds(pl.multiple_of(jnp.bitwise_xor(corner, k) * width, width), width)
        base = rows if k else 0
        places = (
            (q_ref, outs[k + 1] if k else outs[0], 0),
            (k_ref, outs[k + 1], base + TAG),
            (v_ref, outs[k + 1], base + TAG + rows),
        )
        copies += [
            pltpu.make_async_copy(
                source.at[:, cols], target.at[pl.ds(begin, rows)], arrive.at[k, i]
            )
            for i, (source, target, begin) in enumerate(places)
        ]
    for copy in copies:
        copy.start()
    tell.wait()
    ids = (held[...] + 1).astype(jnp.float32)
    spare = jnp.zeros((TAG - ids.shape[0], LANES), jnp.float32)
    ids = jnp.concatenate([ids, spare], axis=0)
    tag = jnp.concatenate([ids] * (width // LANES), axis=1).astype(jnp.bfloat16)
    for i, target in enumerate(outs):
        begin = 0 if i == 1 else rows
        target[begin : begin + TAG, :] = tag
    for copy in copies:
        copy.wait()


def deal(queries, keys, values, ids):
    rows, feat = queries.shape
    tall = [rows + TAG, 2 * rows + TAG] + [3 * rows + TAG] * (SQUAD - 1)
    shapes = [(x, feat // SQUAD) for x in tall]
    held = [pltpu.with_memory_space_constraint(x, pltpu.HBM) for x in (queries, keys, values, ids)]
    return list(
        pl.pallas_call(
            deal_kernel,
            in_specs=[pl.BlockSpec(memory_space=pl.ANY)] * 4,
            out_specs=[VMEM] * len(tall),
            out_shape=[jax.ShapeDtypeStruct(x, jnp.bfloat16) for x in shapes],
            scratch_shapes=[
                pltpu.VMEM(ids.shape, ids.dtype),
                pltpu.SemaphoreType.DMA((SQUAD, 3)),
                pltpu.SemaphoreType.DMA,
            ],
            compiler_params=pltpu.CompilerParams(vmem_limit_bytes=VMEM_LIMIT),
            cost_estimate=pl.CostEstimate(
                flops=0, bytes_accessed=12 * rows * feat, transcendentals=0
            ),
            name="deal",
        )(*held)
    )


def id_columns(tag_ref, rows):
    tag = tag_ref[:, :LANES].astype(jnp.float32)
    tiles = [jnp.broadcast_to(tag[t : t + 1], (LANES, LANES)).T for t in range(rows // LANES)]
    return jnp.concatenate(tiles, axis=0)


def place_keys(parts, corner, base, rows, keys, values):
    heads = keys.shape[0]
    marks = lax.broadcasted_iota(jnp.int32, (rows, LANES), 1).astype(jnp.float32) + 1.0
    for k, part in enumerate(parts):
        begin = pl.multiple_of((jnp.bitwise_xor(corner, k) + base) * rows, rows)
        span = pl.ds(begin, rows)
        ids = id_columns(part.at[:TAG], rows)
        mask = jnp.where(ids == marks, 0.0, -NEG).astype(jnp.bfloat16)
        for h in range(heads):
            cols = slice(h * HD, (h + 1) * HD)
            keys[h, span, :HD] = part[TAG : TAG + rows, cols]
            keys[h, span, HD:] = mask
            values[h, span, :] = part[TAG + rows : TAG + 2 * rows, cols]


def near_parts(near, rows):
    tall = 2 * rows + TAG
    return [near[0], near[1].at[:tall], near[1].at[tall:], near[2]]


def place_queries(parts, corner, rows, queries):
    heads = queries.shape[0]
    marks = lax.broadcasted_iota(jnp.int32, (rows, LANES), 1).astype(jnp.float32) + 1.0
    for k, part in enumerate(parts):
        begin = pl.multiple_of(jnp.bitwise_xor(corner, k) * rows, rows)
        span = pl.ds(begin, rows)
        ids = id_columns(part.at[rows : rows + TAG], rows)
        mask = jnp.where(ids == marks, -1.0, 0.0).astype(jnp.bfloat16)
        for h in range(heads):
            queries[h, span, :HD] = part[:rows, h * HD : (h + 1) * HD]
            queries[h, span, HD:] = mask


def attend(query, keys, values, diagonal):
    factor = math.log2(math.e) / math.sqrt(HD)
    rows = query.shape[0]
    score = lax.dot_general(
        keys, query, (((1,), (1,)), ((), ())), preferred_element_type=jnp.float32
    )
    if diagonal:
        older = lax.broadcasted_iota(jnp.int32, (rows, rows), 0) <= lax.broadcasted_iota(
            jnp.int32, (rows, rows), 1
        )
        score = jnp.concatenate(
            [score[:-rows], jnp.where(older, score[-rows:], NEG)], axis=0
        )
    high = jnp.max(score, axis=0, keepdims=True)
    expo = jnp.exp2((score - high) * factor)
    total = jnp.sum(expo, axis=0, keepdims=True)
    summed = lax.dot_general(
        values,
        expo.astype(jnp.bfloat16),
        (((0,), (0,)), ((), ())),
        preferred_element_type=jnp.float32,
    )
    return summed / total, high * factor + jnp.log2(total)


def main_kernel(*refs):
    own, near, out, (queries, keys, values) = refs[:5], refs[5:8], refs[8], refs[9:]
    heads, span, _ = queries.shape
    rows = span // SQUAD
    width = heads * HD
    corner = corner_of()
    asked = [own[0]] + [p.at[: rows + TAG] for p in own[2:]]
    held = [own[1]] + [p.at[rows:] for p in own[2:]]
    place_queries(asked, corner, rows, queries)
    place_keys(held, corner, SQUAD, rows, keys, values)
    place_keys(near_parts(near, rows), corner, 0, rows, keys, values)
    for j in range(SQUAD):
        cols = slice(j * rows, (j + 1) * rows)
        reach = (SQUAD + 1 + j) * rows
        for h in range(heads):
            mixed, lse = attend(queries[h, cols], keys[h, :reach], values[h, :reach], True)
            out[h * HD : (h + 1) * HD, cols] = mixed
            out[width + h : width + h + 1, cols] = lse
        out[width + heads :, cols] = jnp.zeros((TAG - heads, rows), jnp.float32)


def far_kernel(*refs):
    asked, near, out, (queries, keys, values) = refs[:2], refs[2:5], refs[5], refs[6:]
    heads, span, _ = queries.shape
    rows = span // SQUAD
    width = heads * HD
    corner = corner_of()
    tall = rows + TAG
    asked = [asked[0].at[k * tall : (k + 1) * tall] for k in range(SQUAD - 1)] + [asked[1]]
    place_queries(asked, corner, rows, queries)
    place_keys(near_parts(near, rows), corner, 0, rows, keys, values)
    for j in range(SQUAD - 1):
        cols = slice(j * rows, (j + 1) * rows)
        stats = []
        for h in range(heads):
            mixed, lse = attend(
                queries[h, cols], keys[h, cols.stop :], values[h, cols.stop :], False
            )
            out[h * HD : (h + 1) * HD, cols] = mixed.astype(out.dtype)
            top = lse.astype(jnp.bfloat16).astype(jnp.float32)
            mid = (lse - top).astype(jnp.bfloat16).astype(jnp.float32)
            stats += [top, mid, lse - top - mid]
        stats.append(jnp.zeros((TAG - len(stats), rows), jnp.float32))
        out[width:, cols] = jnp.concatenate(stats, axis=0).astype(out.dtype)


def merge_kernel(main_ref, far_ref, *refs):
    outs, ready = refs[:-1], refs[-1]
    _, rows, width = ready.shape
    corner = corner_of()
    served = lax.axis_index("ctx") >= 2 * SQUAD
    for j in range(SQUAD):
        cols = slice(j * rows, (j + 1) * rows)
        for h in range(width // HD):
            feats = slice(h * HD, (h + 1) * HD)
            mixed = main_ref[feats, cols]
            if j < SQUAD - 1:
                here = main_ref[width + h : width + h + 1, cols]
                stats = far_ref[width:, cols].astype(jnp.float32)
                there = stats[3 * h : 3 * h + 1] + stats[3 * h + 1 : 3 * h + 2]
                there = jnp.where(served, there + stats[3 * h + 2 : 3 * h + 3], NEG)
                high = jnp.maximum(here, there)
                here, there = jnp.exp2(here - high), jnp.exp2(there - high)
                total = here + there
                mixed = mixed * (here / total) + far_ref[feats, cols].astype(jnp.float32) * (
                    there / total
                )
            ready[j, :, feats] = mixed.T.astype(ready.dtype)
    for k, out in enumerate(outs):
        out[...] = ready[jnp.bitwise_xor(corner, k)]


def project_kernel(ranks, *refs):
    parts, weight_ref, out_ref, whole = refs[:-3], refs[-3], refs[-2], refs[-1]
    mine, corner = lax.axis_index("tp"), corner_of()
    width = parts[0].shape[1]
    for r in range(ranks):
        source = lax.rem(mine + ranks - r, ranks)
        for k in range(SQUAD):
            begin = (source * SQUAD + jnp.bitwise_xor(corner, k)) * width
            whole[:, pl.ds(pl.multiple_of(begin, width), width)] = parts[r * SQUAD + k][...]
    block = 2 * LANES
    for c in range(out_ref.shape[1] // block):
        cols = slice(c * block, (c + 1) * block)
        out_ref[:, cols] = jnp.dot(
            whole[...], weight_ref[:, cols], preferred_element_type=jnp.float32
        ).astype(out_ref.dtype)


def local(
    hyena_q, hyena_k, hyena_v, filters, direct, queries, keys, values, segment_ids, out_weight
):
    rows, feat = queries.shape
    count, ranks = lax.axis_size("ctx"), lax.axis_size("tp")
    width = feat // SQUAD
    heads = width // HD
    bf16, f32 = jnp.bfloat16, jnp.float32

    def swap(value, mask):
        return lax.ppermute(value, "ctx", [(i, i ^ mask) for i in range(count)])

    def climb(value, first=0):
        return lax.ppermute(value, "ctx", [(i, i + SQUAD) for i in range(first, count - SQUAD)])

    def descend(value):
        return lax.ppermute(
            value, "ctx", [(i, i - SQUAD) for i in range(2 * SQUAD, count)]
        )

    asked, kept, *sent = deal(
        queries, keys, values, segment_ids.reshape(rows // LANES, LANES)
    )
    tall = rows + TAG
    near = [climb(kept)]
    beside = [swap(sent[0], 1), swap(sent[1], 2)]
    sent[2], beside[0] = lax.optimization_barrier((sent[2], beside[0]))
    across = swap(sent[2], 3)
    beside[1], near[0] = lax.optimization_barrier((beside[1], near[0]))
    near.append(climb(jnp.concatenate([x[rows:] for x in beside], axis=0)))
    back = [descend(jnp.concatenate([asked] + [x[:tall] for x in beside], axis=0))]
    near.append(climb(across[rows:]))
    tail_k = hyena_k[rows - LANES :].astype(f32)
    tail_v = hyena_v[rows - LANES :].astype(f32)
    tail = (tail_k * tail_v).astype(bf16)
    half = tail.shape[1] // 2
    ring = lax.ppermute(
        tail[:, half:], "ctx", [(i, i - i % SQUAD + (i + 1) % SQUAD) for i in range(count)]
    )
    across, ring = lax.optimization_barrier((across, ring))
    back.append(descend(across[:tall]))
    rims = [
        lax.ppermute(tail[:, :half], "ctx", [(i, i + 1) for i in range(count - 1)]),
        ring,
        lax.ppermute(ring, "ctx", [(i, i + SQUAD) for i in range(0, count - SQUAD, SQUAD)]),
    ]
    own = [asked, kept, *beside, across]
    def store(blocks):
        return [
            pltpu.VMEM((heads, SQUAD * rows, 2 * HD), bf16),
            pltpu.VMEM((heads, blocks * rows, 2 * HD), bf16),
            pltpu.VMEM((heads, blocks * rows, HD), bf16),
        ]

    (far,) = kernel_call(
        far_kernel,
        (*back, *near),
        [jax.ShapeDtypeStruct((width + TAG, (SQUAD - 1) * rows), bf16)],
        "far",
        store(SQUAD),
        flops=6 * 4 * rows * rows * width,
        exps=6 * rows * rows * heads,
    )
    far = climb(far, SQUAD)
    own[1], *rims = lax.optimization_barrier((own[1], *rims))
    (main,) = kernel_call(
        main_kernel,
        (*own, *near),
        [jax.ShapeDtypeStruct((width + TAG, SQUAD * rows), f32)],
        "main",
        store(2 * SQUAD),
        flops=26 * 4 * rows * rows * width,
        exps=26 * rows * rows * heads,
    )
    done = kernel_call(
        merge_kernel,
        (main, far),
        [jax.ShapeDtypeStruct((rows, width), bf16)] * SQUAD,
        "merge",
        [pltpu.VMEM((SQUAD, rows, width), bf16)],
    )
    *rims, done[0] = lax.optimization_barrier((*rims, done[0]))
    hyena_out = hyena(hyena_q, hyena_k, hyena_v, rims, filters, direct)

    def turn(value, r):
        return lax.ppermute(value, "tp", [(t, (t + r) % ranks) for t in range(ranks)])

    pieces = [swap(done[k], k) for k in range(1, SQUAD)]
    hyena_out, *pieces = lax.optimization_barrier((hyena_out, done[0], *pieces))
    pieces += [turn(piece, r) for r in range(1, ranks) for piece in pieces]
    (attn_out,) = kernel_call(
        functools.partial(project_kernel, ranks),
        (*pieces, out_weight),
        [jax.ShapeDtypeStruct((rows, out_weight.shape[1]), bf16)],
        "project",
        [pltpu.VMEM((rows, ranks * feat), bf16)],
        flops=2 * rows * math.prod(out_weight.shape),
    )
    return (hyena_out, attn_out)


def solution(mesh):
    placed = (
        P("ctx", "tp"),
        P("ctx", "tp"),
        P("ctx", "tp"),
        P("tp", None),
        P("tp"),
        P("ctx", "tp"),
        P("ctx", "tp"),
        P("ctx", "tp"),
        P("ctx"),
        P(None, "tp"),
    )
    return jax.shard_map(
        local,
        mesh=mesh,
        in_specs=placed,
        out_specs=(P("ctx", "tp"), P("ctx", "tp")),
        check_vma=False,
    )
```

```python
import functools
import math

import jax
import jax.numpy as jnp
from jax import lax
from jax.experimental import pallas as pl
from jax.experimental.pallas import tpu as pltpu
from jax.sharding import PartitionSpec as P

HD = 128
SQUAD = 4
NEG = -1e30
TAG = 16
LANES = 128
VMEM_LIMIT = 32 * 1024 * 1024
VMEM = pl.BlockSpec(memory_space=pltpu.VMEM)


def corner_of():
    return lax.rem(lax.axis_index("ctx"), SQUAD)


def kernel_call(kernel, args, shapes, name, scratch=(), flops=0, exps=0):
    total = sum(math.prod(x.shape) * x.dtype.itemsize for x in (*args, *shapes))
    return list(pl.pallas_call(
        kernel,
        in_specs=[VMEM] * len(args),
        out_specs=[VMEM] * len(shapes),
        out_shape=shapes,
        scratch_shapes=scratch,
        compiler_params=pltpu.CompilerParams(vmem_limit_bytes=VMEM_LIMIT),
        cost_estimate=pl.CostEstimate(flops=flops, bytes_accessed=total, transcendentals=exps),
        name=name,
    )(*args))


def hyena_kernel(q_ref, k_ref, v_ref, rim_ref, taps_ref, direct_ref, out_ref, taps):
    rows, chans = q_ref.shape
    groups = taps_ref.shape[0]
    group = chans // groups
    per_tile = LANES // group
    windows = rows // LANES
    shape = (LANES, LANES)
    down, along = (lax.broadcasted_iota(jnp.int32, shape, i) for i in range(2))
    turn = jnp.where((down + along) % LANES == 0, 1.0, 0.0).astype(jnp.bfloat16)
    before = jnp.where(along > down, 1.0, 0.0).astype(jnp.bfloat16)
    within = jnp.where(along > down, 0.0, 1.0).astype(jnp.bfloat16)
    taps[...] = jnp.dot(taps_ref[...], turn, preferred_element_type=jnp.float32)
    lane_group = lax.broadcasted_iota(jnp.int32, (LANES, windows * LANES), 1) % LANES // group

    @pl.loop(0, chans // LANES, unroll=2)
    def _(tile):
        cols = pl.ds(pl.multiple_of(tile * LANES, LANES), LANES)
        rings = taps[pl.ds(pl.multiple_of(tile * per_tile, per_tile), per_tile), :]
        mixed = (k_ref[:, cols].astype(jnp.float32) * v_ref[:, cols].astype(jnp.float32)).astype(
            jnp.bfloat16
        )
        full = jnp.concatenate([rim_ref[:, cols], mixed], axis=0)
        stacked = jnp.concatenate(
            [full[w * LANES : (w + 2) * LANES] for w in range(windows)], axis=1
        )
        conv = jnp.zeros((LANES, windows * LANES), jnp.float32)
        for g in range(per_tile):
            ring = pltpu.roll(
                jnp.broadcast_to(rings[g : g + 1], shape), 0, 1, stride=1, stride_axis=0
            ).astype(jnp.bfloat16)
            table = jnp.concatenate([ring * before, ring * within], axis=1)
            part = jnp.dot(table, stacked, preferred_element_type=jnp.float32)
            conv = jnp.where(lane_group == g, part, conv)
        conv = jnp.concatenate(
            [conv[:, w * LANES : (w + 1) * LANES] for w in range(windows)], axis=0
        )
        out_ref[:, cols] = (
            q_ref[:, cols].astype(jnp.float32)
            * (conv + direct_ref[:, cols].astype(jnp.float32) * mixed.astype(jnp.float32))
        ).astype(jnp.bfloat16)


def hyena(hyena_q, hyena_k, hyena_v, rim, filters, direct):
    rows, chans = hyena_q.shape
    groups, kernel = filters.shape
    taps = jnp.pad(filters, ((0, 0), (0, LANES - kernel)))
    (out,) = kernel_call(
        hyena_kernel,
        (hyena_q, hyena_k, hyena_v, rim, taps, direct[None]),
        [jax.ShapeDtypeStruct((rows, chans), jnp.bfloat16)],
        "hyena",
        [pltpu.VMEM((groups, LANES), jnp.float32)],
        flops=4 * rows * chans * 2 * LANES * 8,
    )
    return out


def deal_kernel(q_ref, k_ref, v_ref, id_ref, *refs):
    outs, (held, arrive, told) = refs[:-3], refs[-3:]
    tell = pltpu.make_async_copy(id_ref, held, told)
    tell.start()
    rows, feat = q_ref.shape
    width = feat // SQUAD
    corner = corner_of()
    copies = []
    for k in (*range(1, SQUAD), 0):
        cols = pl.ds(pl.multiple_of(jnp.bitwise_xor(corner, k) * width, width), width)
        base = rows if k else 0
        places = (
            (q_ref, outs[k + 1] if k else outs[0], 0),
            (k_ref, outs[k + 1], base + TAG),
            (v_ref, outs[k + 1], base + TAG + rows),
        )
        copies += [
            pltpu.make_async_copy(
                source.at[:, cols], target.at[pl.ds(begin, rows)], arrive.at[k, i]
            )
            for i, (source, target, begin) in enumerate(places)
        ]
    for copy in copies:
        copy.start()
    tell.wait()
    ids = (held[...] + 1).astype(jnp.float32)
    spare = jnp.zeros((TAG - ids.shape[0], LANES), jnp.float32)
    ids = jnp.concatenate([ids, spare], axis=0)
    tag = jnp.concatenate([ids] * (width // LANES), axis=1).astype(jnp.bfloat16)
    for i, target in enumerate(outs):
        begin = 0 if i == 1 else rows
        target[begin : begin + TAG, :] = tag
    for copy in copies:
        copy.wait()


def deal(queries, keys, values, ids):
    rows, feat = queries.shape
    tall = [rows + TAG, 2 * rows + TAG] + [3 * rows + TAG] * (SQUAD - 1)
    shapes = [(x, feat // SQUAD) for x in tall]
    held = [pltpu.with_memory_space_constraint(x, pltpu.HBM) for x in (queries, keys, values, ids)]
    return list(
        pl.pallas_call(
            deal_kernel,
            in_specs=[pl.BlockSpec(memory_space=pl.ANY)] * 4,
            out_specs=[VMEM] * len(tall),
            out_shape=[jax.ShapeDtypeStruct(x, jnp.bfloat16) for x in shapes],
            scratch_shapes=[
                pltpu.VMEM(ids.shape, ids.dtype),
                pltpu.SemaphoreType.DMA((SQUAD, 3)),
                pltpu.SemaphoreType.DMA,
            ],
            compiler_params=pltpu.CompilerParams(vmem_limit_bytes=VMEM_LIMIT),
            cost_estimate=pl.CostEstimate(
                flops=0, bytes_accessed=12 * rows * feat, transcendentals=0
            ),
            name="deal",
        )(*held)
    )


def id_columns(tag_ref, rows):
    tag = tag_ref[:, :LANES].astype(jnp.float32)
    tiles = [jnp.broadcast_to(tag[t : t + 1], (LANES, LANES)).T for t in range(rows // LANES)]
    return jnp.concatenate(tiles, axis=0)


def place_keys(parts, corner, base, rows, keys, values):
    heads = keys.shape[0]
    marks = lax.broadcasted_iota(jnp.int32, (rows, LANES), 1).astype(jnp.float32) + 1.0
    for k, part in enumerate(parts):
        begin = pl.multiple_of((jnp.bitwise_xor(corner, k) + base) * rows, rows)
        span = pl.ds(begin, rows)
        ids = id_columns(part.at[:TAG], rows)
        mask = jnp.where(ids == marks, 0.0, -NEG).astype(jnp.bfloat16)
        for h in range(heads):
            cols = slice(h * HD, (h + 1) * HD)
            keys[h, span, :HD] = part[TAG : TAG + rows, cols]
            keys[h, span, HD:] = mask
            values[h, span, :] = part[TAG + rows : TAG + 2 * rows, cols]


def near_parts(near, rows):
    tall = 2 * rows + TAG
    return [near[0], near[1].at[:tall], near[1].at[tall:], near[2]]


def place_queries(parts, corner, rows, queries):
    heads = queries.shape[0]
    marks = lax.broadcasted_iota(jnp.int32, (rows, LANES), 1).astype(jnp.float32) + 1.0
    for k, part in enumerate(parts):
        begin = pl.multiple_of(jnp.bitwise_xor(corner, k) * rows, rows)
        span = pl.ds(begin, rows)
        ids = id_columns(part.at[rows : rows + TAG], rows)
        mask = jnp.where(ids == marks, -1.0, 0.0).astype(jnp.bfloat16)
        for h in range(heads):
            queries[h, span, :HD] = part[:rows, h * HD : (h + 1) * HD]
            queries[h, span, HD:] = mask


def attend(query, keys, values, diagonal):
    factor = math.log2(math.e) / math.sqrt(HD)
    rows = query.shape[0]
    score = lax.dot_general(
        keys, query, (((1,), (1,)), ((), ())), preferred_element_type=jnp.float32
    )
    if diagonal:
        older = lax.broadcasted_iota(jnp.int32, (rows, rows), 0) <= lax.broadcasted_iota(
            jnp.int32, (rows, rows), 1
        )
        score = jnp.concatenate(
            [score[:-rows], jnp.where(older, score[-rows:], NEG)], axis=0
        )
    high = jnp.max(score, axis=0, keepdims=True)
    expo = jnp.exp2((score - high) * factor)
    total = jnp.sum(expo, axis=0, keepdims=True)
    summed = lax.dot_general(
        values,
        expo.astype(jnp.bfloat16),
        (((0,), (0,)), ((), ())),
        preferred_element_type=jnp.float32,
    )
    return summed / total, high * factor + jnp.log2(total)


def main_kernel(*refs):
    own, near, out, (queries, keys, values) = refs[:5], refs[5:8], refs[8], refs[9:]
    heads, span, _ = queries.shape
    rows = span // SQUAD
    width = heads * HD
    corner = corner_of()
    asked = [own[0]] + [p.at[: rows + TAG] for p in own[2:]]
    held = [own[1]] + [p.at[rows:] for p in own[2:]]
    place_queries(asked, corner, rows, queries)
    place_keys(held, corner, SQUAD, rows, keys, values)
    place_keys(near_parts(near, rows), corner, 0, rows, keys, values)
    for j in range(SQUAD):
        cols = slice(j * rows, (j + 1) * rows)
        reach = (SQUAD + 1 + j) * rows
        for h in range(heads):
            mixed, lse = attend(queries[h, cols], keys[h, :reach], values[h, :reach], True)
            out[h * HD : (h + 1) * HD, cols] = mixed
            out[width + h : width + h + 1, cols] = lse
        out[width + heads :, cols] = jnp.zeros((TAG - heads, rows), jnp.float32)


def ask_kernel(*refs):
    parts, out = refs[:-1], refs[-1]
    tall = parts[0].shape[0]
    corner = corner_of()
    for k, part in enumerate(parts):
        block = jnp.bitwise_xor(corner, k)

        @pl.when(block < SQUAD - 1)
        def _():
            out[pl.ds(pl.multiple_of(block * tall, TAG), tall), :] = part[:tall]


def far_kernel(*refs):
    asked, near, out, (queries, keys, values) = refs[0], refs[1:4], refs[4], refs[5:]
    heads, span, _ = queries.shape
    rows = span // SQUAD
    width = heads * HD
    corner = corner_of()
    tall = rows + TAG
    blocks = [asked.at[j * tall : (j + 1) * tall] for j in range(SQUAD - 1)]
    place_queries(blocks, 0, rows, queries)
    place_keys(near_parts(near, rows), corner, 0, rows, keys, values)
    for j in range(SQUAD - 1):
        cols = slice(j * rows, (j + 1) * rows)
        stats = []
        for h in range(heads):
            mixed, lse = attend(
                queries[h, cols], keys[h, cols.stop :], values[h, cols.stop :], False
            )
            out[h * HD : (h + 1) * HD, cols] = mixed.astype(out.dtype)
            top = lse.astype(jnp.bfloat16).astype(jnp.float32)
            mid = (lse - top).astype(jnp.bfloat16).astype(jnp.float32)
            stats += [top, mid, lse - top - mid]
        stats.append(jnp.zeros((TAG - len(stats), rows), jnp.float32))
        out[width:, cols] = jnp.concatenate(stats, axis=0).astype(out.dtype)


def merge_kernel(main_ref, far_ref, *refs):
    outs, ready = refs[:-1], refs[-1]
    _, rows, width = ready.shape
    corner = corner_of()
    served = lax.axis_index("ctx") >= 2 * SQUAD
    for j in range(SQUAD):
        cols = slice(j * rows, (j + 1) * rows)
        for h in range(width // HD):
            feats = slice(h * HD, (h + 1) * HD)
            mixed = main_ref[feats, cols]
            if j < SQUAD - 1:
                here = main_ref[width + h : width + h + 1, cols]
                stats = far_ref[width:, cols].astype(jnp.float32)
                there = stats[3 * h : 3 * h + 1] + stats[3 * h + 1 : 3 * h + 2]
                there = jnp.where(served, there + stats[3 * h + 2 : 3 * h + 3], NEG)
                high = jnp.maximum(here, there)
                here, there = jnp.exp2(here - high), jnp.exp2(there - high)
                total = here + there
                mixed = mixed * (here / total) + far_ref[feats, cols].astype(jnp.float32) * (
                    there / total
                )
            ready[j, :, feats] = mixed.T.astype(ready.dtype)
    for k, out in enumerate(outs):
        out[...] = ready[jnp.bitwise_xor(corner, k)]


def project_kernel(ranks, *refs):
    parts, weight_ref, out_ref, whole = refs[:-3], refs[-3], refs[-2], refs[-1]
    mine, corner = lax.axis_index("tp"), corner_of()
    width = parts[0].shape[1]
    for r in range(ranks):
        source = lax.rem(mine + ranks - r, ranks)
        for k in range(SQUAD):
            begin = (source * SQUAD + jnp.bitwise_xor(corner, k)) * width
            whole[:, pl.ds(pl.multiple_of(begin, width), width)] = parts[r * SQUAD + k][...]
    block = 2 * LANES
    for c in range(out_ref.shape[1] // block):
        cols = slice(c * block, (c + 1) * block)
        out_ref[:, cols] = jnp.dot(
            whole[...], weight_ref[:, cols], preferred_element_type=jnp.float32
        ).astype(out_ref.dtype)


def local(
    hyena_q, hyena_k, hyena_v, filters, direct, queries, keys, values, segment_ids, out_weight
):
    rows, feat = queries.shape
    count, ranks = lax.axis_size("ctx"), lax.axis_size("tp")
    width = feat // SQUAD
    heads = width // HD
    bf16, f32 = jnp.bfloat16, jnp.float32

    def swap(value, mask):
        return lax.ppermute(value, "ctx", [(i, i ^ mask) for i in range(count)])

    def climb(value, first=0):
        return lax.ppermute(value, "ctx", [(i, i + SQUAD) for i in range(first, count - SQUAD)])

    def descend(value):
        return lax.ppermute(
            value, "ctx", [(i, i - SQUAD) for i in range(2 * SQUAD, count)]
        )

    asked, kept, *sent = deal(
        queries, keys, values, segment_ids.reshape(rows // LANES, LANES)
    )
    tall = rows + TAG
    near = [climb(kept)]
    beside = [swap(sent[0], 1), swap(sent[1], 2)]
    sent[2], beside[0] = lax.optimization_barrier((sent[2], beside[0]))
    across = swap(sent[2], 3)
    beside[1], near[0] = lax.optimization_barrier((beside[1], near[0]))
    near.append(climb(jnp.concatenate([x[rows:] for x in beside], axis=0)))
    (back,) = kernel_call(
        ask_kernel,
        (asked, *beside, across),
        [jax.ShapeDtypeStruct(((SQUAD - 1) * tall, width), bf16)],
        "ask",
    )
    back = descend(back)
    near.append(climb(across[rows:]))
    tail_k = hyena_k[rows - LANES :].astype(f32)
    tail_v = hyena_v[rows - LANES :].astype(f32)
    rim = lax.ppermute(
        (tail_k * tail_v).astype(bf16), "ctx", [(i, i + 1) for i in range(count - 1)]
    )
    own = [asked, kept, *beside, across]
    def store(blocks):
        return [
            pltpu.VMEM((heads, SQUAD * rows, 2 * HD), bf16),
            pltpu.VMEM((heads, blocks * rows, 2 * HD), bf16),
            pltpu.VMEM((heads, blocks * rows, HD), bf16),
        ]

    (far,) = kernel_call(
        far_kernel,
        (back, *near),
        [jax.ShapeDtypeStruct((width + TAG, (SQUAD - 1) * rows), bf16)],
        "far",
        store(SQUAD),
        flops=6 * 4 * rows * rows * width,
        exps=6 * rows * rows * heads,
    )
    far = climb(far, SQUAD)
    (main,) = kernel_call(
        main_kernel,
        (*own, *near),
        [jax.ShapeDtypeStruct((width + TAG, SQUAD * rows), f32)],
        "main",
        store(2 * SQUAD),
        flops=26 * 4 * rows * rows * width,
        exps=26 * rows * rows * heads,
    )
    done = kernel_call(
        merge_kernel,
        (main, far),
        [jax.ShapeDtypeStruct((rows, width), bf16)] * SQUAD,
        "merge",
        [pltpu.VMEM((SQUAD, rows, width), bf16)],
    )
    rim, done[0] = lax.optimization_barrier((rim, done[0]))
    hyena_out = hyena(hyena_q, hyena_k, hyena_v, rim, filters, direct)

    def turn(value, r):
        return lax.ppermute(value, "tp", [(t, (t + r) % ranks) for t in range(ranks)])

    pieces = [swap(done[k], k) for k in range(1, SQUAD)]
    hyena_out, *pieces = lax.optimization_barrier((hyena_out, done[0], *pieces))
    pieces += [turn(piece, r) for r in range(1, ranks) for piece in pieces]
    (attn_out,) = kernel_call(
        functools.partial(project_kernel, ranks),
        (*pieces, out_weight),
        [jax.ShapeDtypeStruct((rows, out_weight.shape[1]), bf16)],
        "project",
        [pltpu.VMEM((rows, ranks * feat), bf16)],
        flops=2 * rows * math.prod(out_weight.shape),
    )
    return (hyena_out, attn_out)


def solution(mesh):
    placed = (
        P("ctx", "tp"),
        P("ctx", "tp"),
        P("ctx", "tp"),
        P("tp", None),
        P("tp"),
        P("ctx", "tp"),
        P("ctx", "tp"),
        P("ctx", "tp"),
        P("ctx"),
        P(None, "tp"),
    )
    return jax.shard_map(
        local,
        mesh=mesh,
        in_specs=placed,
        out_specs=(P("ctx", "tp"), P("ctx", "tp")),
        check_vma=False,
    )
```

```python
import functools
import math

import jax
import jax.numpy as jnp
from jax import lax
from jax.experimental import pallas as pl
from jax.experimental.pallas import tpu as pltpu
from jax.sharding import PartitionSpec as P

HD = 128
SQUAD = 4
NEG = -1e30
TAG = 16
LANES = 128
VMEM_LIMIT = 32 * 1024 * 1024
VMEM = pl.BlockSpec(memory_space=pltpu.VMEM)


def corner_of():
    return lax.rem(lax.axis_index("ctx"), SQUAD)


def kernel_call(kernel, args, shapes, name, scratch=(), flops=0, exps=0):
    total = sum(math.prod(x.shape) * x.dtype.itemsize for x in (*args, *shapes))
    return list(pl.pallas_call(
        kernel,
        in_specs=[VMEM] * len(args),
        out_specs=[VMEM] * len(shapes),
        out_shape=shapes,
        scratch_shapes=scratch,
        compiler_params=pltpu.CompilerParams(vmem_limit_bytes=VMEM_LIMIT),
        cost_estimate=pl.CostEstimate(flops=flops, bytes_accessed=total, transcendentals=exps),
        name=name,
    )(*args))


def hyena_kernel(q_ref, k_ref, v_ref, next_rim, far_rim, taps_ref, direct_ref, out_ref, taps, rim):
    rows, chans = q_ref.shape
    groups = taps_ref.shape[0]
    group = chans // groups
    per_tile = LANES // group
    windows = rows // LANES
    shape = (LANES, LANES)
    down, along = (lax.broadcasted_iota(jnp.int32, shape, i) for i in range(2))
    turn = jnp.where((down + along) % LANES == 0, 1.0, 0.0).astype(jnp.bfloat16)
    before = jnp.where(along > down, 1.0, 0.0).astype(jnp.bfloat16)
    within = jnp.where(along > down, 0.0, 1.0).astype(jnp.bfloat16)
    taps[...] = jnp.dot(taps_ref[...], turn, preferred_element_type=jnp.float32)
    lane_group = lax.broadcasted_iota(jnp.int32, (LANES, windows * LANES), 1) % LANES // group

    relayed = (corner_of() == 0) & (lax.axis_index("tp") % 2 == 1)

    @pl.when(relayed)
    def _():
        rim[...] = far_rim[...]

    @pl.when(jnp.logical_not(relayed))
    def _():
        rim[...] = next_rim[...]

    @pl.loop(0, chans // LANES, unroll=2)
    def _(tile):
        cols = pl.ds(pl.multiple_of(tile * LANES, LANES), LANES)
        rings = taps[pl.ds(pl.multiple_of(tile * per_tile, per_tile), per_tile), :]
        mixed = (k_ref[:, cols].astype(jnp.float32) * v_ref[:, cols].astype(jnp.float32)).astype(
            jnp.bfloat16
        )
        full = jnp.concatenate([rim[:, cols], mixed], axis=0)
        stacked = jnp.concatenate(
            [full[w * LANES : (w + 2) * LANES] for w in range(windows)], axis=1
        )
        conv = jnp.zeros((LANES, windows * LANES), jnp.float32)
        for g in range(per_tile):
            ring = pltpu.roll(
                jnp.broadcast_to(rings[g : g + 1], shape), 0, 1, stride=1, stride_axis=0
            ).astype(jnp.bfloat16)
            table = jnp.concatenate([ring * before, ring * within], axis=1)
            part = jnp.dot(table, stacked, preferred_element_type=jnp.float32)
            conv = jnp.where(lane_group == g, part, conv)
        conv = jnp.concatenate(
            [conv[:, w * LANES : (w + 1) * LANES] for w in range(windows)], axis=0
        )
        out_ref[:, cols] = (
            q_ref[:, cols].astype(jnp.float32)
            * (conv + direct_ref[:, cols].astype(jnp.float32) * mixed.astype(jnp.float32))
        ).astype(jnp.bfloat16)


def hyena(hyena_q, hyena_k, hyena_v, rims, filters, direct):
    rows, chans = hyena_q.shape
    groups, kernel = filters.shape
    taps = jnp.pad(filters, ((0, 0), (0, LANES - kernel)))
    (out,) = kernel_call(
        hyena_kernel,
        (hyena_q, hyena_k, hyena_v, *rims, taps, direct[None]),
        [jax.ShapeDtypeStruct((rows, chans), jnp.bfloat16)],
        "hyena",
        [pltpu.VMEM((groups, LANES), jnp.float32), pltpu.VMEM((LANES, chans), jnp.bfloat16)],
        flops=4 * rows * chans * 2 * LANES * 8,
    )
    return out


def deal_kernel(q_ref, k_ref, v_ref, id_ref, *refs):
    outs, (held, arrive, told) = refs[:-3], refs[-3:]
    tell = pltpu.make_async_copy(id_ref, held, told)
    tell.start()
    rows, feat = q_ref.shape
    width = feat // SQUAD
    corner = corner_of()
    copies = []
    for k in (*range(1, SQUAD), 0):
        cols = pl.ds(pl.multiple_of(jnp.bitwise_xor(corner, k) * width, width), width)
        base = rows if k else 0
        places = (
            (q_ref, outs[k + 1] if k else outs[0], 0),
            (k_ref, outs[k + 1], base + TAG),
            (v_ref, outs[k + 1], base + TAG + rows),
        )
        copies += [
            pltpu.make_async_copy(
                source.at[:, cols], target.at[pl.ds(begin, rows)], arrive.at[k, i]
            )
            for i, (source, target, begin) in enumerate(places)
        ]
    for copy in copies:
        copy.start()
    tell.wait()
    ids = (held[...] + 1).astype(jnp.float32)
    spare = jnp.zeros((TAG - ids.shape[0], LANES), jnp.float32)
    ids = jnp.concatenate([ids, spare], axis=0)
    tag = jnp.concatenate([ids] * (width // LANES), axis=1).astype(jnp.bfloat16)
    for i, target in enumerate(outs):
        begin = 0 if i == 1 else rows
        target[begin : begin + TAG, :] = tag
    for copy in copies:
        copy.wait()


def deal(queries, keys, values, ids):
    rows, feat = queries.shape
    tall = [rows + TAG, 2 * rows + TAG] + [3 * rows + TAG] * (SQUAD - 1)
    shapes = [(x, feat // SQUAD) for x in tall]
    held = [pltpu.with_memory_space_constraint(x, pltpu.HBM) for x in (queries, keys, values, ids)]
    return list(
        pl.pallas_call(
            deal_kernel,
            in_specs=[pl.BlockSpec(memory_space=pl.ANY)] * 4,
            out_specs=[VMEM] * len(tall),
            out_shape=[jax.ShapeDtypeStruct(x, jnp.bfloat16) for x in shapes],
            scratch_shapes=[
                pltpu.VMEM(ids.shape, ids.dtype),
                pltpu.SemaphoreType.DMA((SQUAD, 3)),
                pltpu.SemaphoreType.DMA,
            ],
            compiler_params=pltpu.CompilerParams(vmem_limit_bytes=VMEM_LIMIT),
            cost_estimate=pl.CostEstimate(
                flops=0, bytes_accessed=12 * rows * feat, transcendentals=0
            ),
            name="deal",
        )(*held)
    )


def id_columns(tag_ref, rows):
    tag = tag_ref[:, :LANES].astype(jnp.float32)
    tiles = [jnp.broadcast_to(tag[t : t + 1], (LANES, LANES)).T for t in range(rows // LANES)]
    return jnp.concatenate(tiles, axis=0)


def place_keys(parts, corner, base, rows, keys, values):
    heads = keys.shape[0]
    marks = lax.broadcasted_iota(jnp.int32, (rows, LANES), 1).astype(jnp.float32) + 1.0
    for k, part in enumerate(parts):
        begin = pl.multiple_of((jnp.bitwise_xor(corner, k) + base) * rows, rows)
        span = pl.ds(begin, rows)
        ids = id_columns(part.at[:TAG], rows)
        mask = jnp.where(ids == marks, 0.0, -NEG).astype(jnp.bfloat16)
        for h in range(heads):
            cols = slice(h * HD, (h + 1) * HD)
            keys[h, span, :HD] = part[TAG : TAG + rows, cols]
            keys[h, span, HD:] = mask
            values[h, span, :] = part[TAG + rows : TAG + 2 * rows, cols]


def near_parts(near, rows):
    tall = 2 * rows + TAG
    return [near[0], near[1].at[:tall], near[1].at[tall:], near[2]]


def place_queries(parts, corner, rows, queries):
    heads = queries.shape[0]
    marks = lax.broadcasted_iota(jnp.int32, (rows, LANES), 1).astype(jnp.float32) + 1.0
    for k, part in enumerate(parts):
        begin = pl.multiple_of(jnp.bitwise_xor(corner, k) * rows, rows)
        span = pl.ds(begin, rows)
        ids = id_columns(part.at[rows : rows + TAG], rows)
        mask = jnp.where(ids == marks, -1.0, 0.0).astype(jnp.bfloat16)
        for h in range(heads):
            queries[h, span, :HD] = part[:rows, h * HD : (h + 1) * HD]
            queries[h, span, HD:] = mask


def attend(query, keys, values, diagonal):
    factor = math.log2(math.e) / math.sqrt(HD)
    rows = query.shape[0]
    score = lax.dot_general(
        keys, query, (((1,), (1,)), ((), ())), preferred_element_type=jnp.float32
    )
    if diagonal:
        older = lax.broadcasted_iota(jnp.int32, (rows, rows), 0) <= lax.broadcasted_iota(
            jnp.int32, (rows, rows), 1
        )
        score = jnp.concatenate(
            [score[:-rows], jnp.where(older, score[-rows:], NEG)], axis=0
        )
    high = jnp.max(score, axis=0, keepdims=True)
    expo = jnp.exp2((score - high) * factor)
    total = jnp.sum(expo, axis=0, keepdims=True)
    summed = lax.dot_general(
        values,
        expo.astype(jnp.bfloat16),
        (((0,), (0,)), ((), ())),
        preferred_element_type=jnp.float32,
    )
    return summed / total, high * factor + jnp.log2(total)


def main_kernel(*refs):
    own, near, out, (queries, keys, values) = refs[:5], refs[5:8], refs[8], refs[9:]
    heads, span, _ = queries.shape
    rows = span // SQUAD
    width = heads * HD
    corner = corner_of()
    asked = [own[0]] + [p.at[: rows + TAG] for p in own[2:]]
    held = [own[1]] + [p.at[rows:] for p in own[2:]]
    place_queries(asked, corner, rows, queries)
    place_keys(held, corner, SQUAD, rows, keys, values)
    place_keys(near_parts(near, rows), corner, 0, rows, keys, values)
    for j in range(SQUAD):
        cols = slice(j * rows, (j + 1) * rows)
        reach = (SQUAD + 1 + j) * rows
        for h in range(heads):
            mixed, lse = attend(queries[h, cols], keys[h, :reach], values[h, :reach], True)
            out[h * HD : (h + 1) * HD, cols] = mixed
            out[width + h : width + h + 1, cols] = lse
        out[width + heads :, cols] = jnp.zeros((TAG - heads, rows), jnp.float32)


def ask_kernel(*refs):
    parts, out = refs[:-1], refs[-1]
    tall = parts[0].shape[0]
    corner = corner_of()
    for k, part in enumerate(parts):
        block = jnp.bitwise_xor(corner, k)

        @pl.when(block < SQUAD - 1)
        def _():
            out[pl.ds(pl.multiple_of(block * tall, TAG), tall), :] = part[:tall]


def far_kernel(*refs):
    asked, near, out, (queries, keys, values) = refs[0], refs[1:4], refs[4], refs[5:]
    heads, span, _ = queries.shape
    rows = span // SQUAD
    width = heads * HD
    corner = corner_of()
    tall = rows + TAG
    blocks = [asked.at[j * tall : (j + 1) * tall] for j in range(SQUAD - 1)]
    place_queries(blocks, 0, rows, queries)
    place_keys(near_parts(near, rows), corner, 0, rows, keys, values)
    for j in range(SQUAD - 1):
        cols = slice(j * rows, (j + 1) * rows)
        stats = []
        for h in range(heads):
            mixed, lse = attend(
                queries[h, cols], keys[h, cols.stop :], values[h, cols.stop :], False
            )
            out[h * HD : (h + 1) * HD, cols] = mixed.astype(out.dtype)
            top = lse.astype(jnp.bfloat16).astype(jnp.float32)
            mid = (lse - top).astype(jnp.bfloat16).astype(jnp.float32)
            stats += [top, mid, lse - top - mid]
        stats.append(jnp.zeros((TAG - len(stats), rows), jnp.float32))
        out[width:, cols] = jnp.concatenate(stats, axis=0).astype(out.dtype)


def merge_kernel(main_ref, far_ref, *refs):
    outs, ready = refs[:-1], refs[-1]
    _, rows, width = ready.shape
    corner = corner_of()
    served = lax.axis_index("ctx") >= 2 * SQUAD
    for j in range(SQUAD):
        cols = slice(j * rows, (j + 1) * rows)
        for h in range(width // HD):
            feats = slice(h * HD, (h + 1) * HD)
            mixed = main_ref[feats, cols]
            if j < SQUAD - 1:
                here = main_ref[width + h : width + h + 1, cols]
                stats = far_ref[width:, cols].astype(jnp.float32)
                there = stats[3 * h : 3 * h + 1] + stats[3 * h + 1 : 3 * h + 2]
                there = jnp.where(served, there + stats[3 * h + 2 : 3 * h + 3], NEG)
                high = jnp.maximum(here, there)
                here, there = jnp.exp2(here - high), jnp.exp2(there - high)
                total = here + there
                mixed = mixed * (here / total) + far_ref[feats, cols].astype(jnp.float32) * (
                    there / total
                )
            ready[j, :, feats] = mixed.T.astype(ready.dtype)
    for k, out in enumerate(outs):
        out[...] = ready[jnp.bitwise_xor(corner, k)]


def project_kernel(ranks, *refs):
    parts, weight_ref, out_ref, whole = refs[:-3], refs[-3], refs[-2], refs[-1]
    mine, corner = lax.axis_index("tp"), corner_of()
    width = parts[0].shape[1]
    for r in range(ranks):
        source = lax.rem(mine + ranks - r, ranks)
        for k in range(SQUAD):
            begin = (source * SQUAD + jnp.bitwise_xor(corner, k)) * width
            whole[:, pl.ds(pl.multiple_of(begin, width), width)] = parts[r * SQUAD + k][...]
    block = 2 * LANES
    for c in range(out_ref.shape[1] // block):
        cols = slice(c * block, (c + 1) * block)
        out_ref[:, cols] = jnp.dot(
            whole[...], weight_ref[:, cols], preferred_element_type=jnp.float32
        ).astype(out_ref.dtype)


def local(
    hyena_q, hyena_k, hyena_v, filters, direct, queries, keys, values, segment_ids, out_weight
):
    rows, feat = queries.shape
    count, ranks = lax.axis_size("ctx"), lax.axis_size("tp")
    width = feat // SQUAD
    heads = width // HD
    bf16, f32 = jnp.bfloat16, jnp.float32

    def swap(value, mask):
        return lax.ppermute(value, "ctx", [(i, i ^ mask) for i in range(count)])

    def climb(value, first=0):
        return lax.ppermute(value, "ctx", [(i, i + SQUAD) for i in range(first, count - SQUAD)])

    def descend(value):
        return lax.ppermute(
            value, "ctx", [(i, i - SQUAD) for i in range(2 * SQUAD, count)]
        )

    asked, kept, *sent = deal(
        queries, keys, values, segment_ids.reshape(rows // LANES, LANES)
    )
    tall = rows + TAG
    near = [climb(kept)]
    beside = [swap(sent[0], 1), swap(sent[1], 2)]
    sent[2], beside[0] = lax.optimization_barrier((sent[2], beside[0]))
    across = swap(sent[2], 3)
    beside[1], near[0] = lax.optimization_barrier((beside[1], near[0]))
    near.append(climb(jnp.concatenate([x[rows:] for x in beside], axis=0)))
    (back,) = kernel_call(
        ask_kernel,
        (asked, *beside, across),
        [jax.ShapeDtypeStruct(((SQUAD - 1) * tall, width), bf16)],
        "ask",
    )
    back = descend(back)
    near.append(climb(across[rows:]))
    tail_k = hyena_k[rows - LANES :].astype(f32)
    tail_v = hyena_v[rows - LANES :].astype(f32)
    tail = (tail_k * tail_v).astype(bf16)

    def hand(value, pairs):
        ends = [(i * ranks + t, j * ranks + t) for i, j, t in pairs]
        return lax.ppermute(value, ("ctx", "tp"), ends)

    tail, beside[1] = lax.optimization_barrier((tail, beside[1]))
    odd = range(1, ranks, 2)
    ring = hand(
        tail, [(i, i + 1 - SQUAD, t) for i in range(SQUAD - 1, count, SQUAD) for t in odd]
    )
    straight = [
        (i, i + 1, t)
        for i in range(count - 1)
        for t in range(ranks)
        if (i + 1) % SQUAD or t not in odd
    ]
    lifted = [(i, i + SQUAD, t) for i in range(0, count - SQUAD, SQUAD) for t in odd]
    rims = [hand(tail, straight), hand(ring, lifted)]
    own = [asked, kept, *beside, across]
    def store(blocks):
        return [
            pltpu.VMEM((heads, SQUAD * rows, 2 * HD), bf16),
            pltpu.VMEM((heads, blocks * rows, 2 * HD), bf16),
            pltpu.VMEM((heads, blocks * rows, HD), bf16),
        ]

    (far,) = kernel_call(
        far_kernel,
        (back, *near),
        [jax.ShapeDtypeStruct((width + TAG, (SQUAD - 1) * rows), bf16)],
        "far",
        store(SQUAD),
        flops=6 * 4 * rows * rows * width,
        exps=6 * rows * rows * heads,
    )
    far = climb(far, SQUAD)
    own[1], *rims = lax.optimization_barrier((own[1], *rims))
    (main,) = kernel_call(
        main_kernel,
        (*own, *near),
        [jax.ShapeDtypeStruct((width + TAG, SQUAD * rows), f32)],
        "main",
        store(2 * SQUAD),
        flops=26 * 4 * rows * rows * width,
        exps=26 * rows * rows * heads,
    )
    done = kernel_call(
        merge_kernel,
        (main, far),
        [jax.ShapeDtypeStruct((rows, width), bf16)] * SQUAD,
        "merge",
        [pltpu.VMEM((SQUAD, rows, width), bf16)],
    )
    *rims, done[0] = lax.optimization_barrier((*rims, done[0]))
    hyena_out = hyena(hyena_q, hyena_k, hyena_v, rims, filters, direct)

    def turn(value, r):
        return lax.ppermute(value, "tp", [(t, (t + r) % ranks) for t in range(ranks)])

    pieces = [swap(done[k], k) for k in range(1, SQUAD)]
    hyena_out, *pieces = lax.optimization_barrier((hyena_out, done[0], *pieces))
    pieces += [turn(piece, r) for r in range(1, ranks) for piece in pieces]
    (attn_out,) = kernel_call(
        functools.partial(project_kernel, ranks),
        (*pieces, out_weight),
        [jax.ShapeDtypeStruct((rows, out_weight.shape[1]), bf16)],
        "project",
        [pltpu.VMEM((rows, ranks * feat), bf16)],
        flops=2 * rows * math.prod(out_weight.shape),
    )
    return (hyena_out, attn_out)


def solution(mesh):
    placed = (
        P("ctx", "tp"),
        P("ctx", "tp"),
        P("ctx", "tp"),
        P("tp", None),
        P("tp"),
        P("ctx", "tp"),
        P("ctx", "tp"),
        P("ctx", "tp"),
        P("ctx"),
        P(None, "tp"),
    )
    return jax.shard_map(
        local,
        mesh=mesh,
        in_specs=placed,
        out_specs=(P("ctx", "tp"), P("ctx", "tp")),
        check_vma=False,
    )
```

```python
import functools
import math

import jax
import jax.numpy as jnp
from jax import lax
from jax.experimental import pallas as pl
from jax.experimental.pallas import tpu as pltpu
from jax.sharding import PartitionSpec as P

HD = 128
SQUAD = 4
NEG = -1e30
TAG = 16
LANES = 128
VMEM_LIMIT = 32 * 1024 * 1024
VMEM = pl.BlockSpec(memory_space=pltpu.VMEM)


def corner_of():
    return lax.rem(lax.axis_index("ctx"), SQUAD)


def kernel_call(kernel, args, shapes, name, scratch=(), flops=0, exps=0):
    total = sum(math.prod(x.shape) * x.dtype.itemsize for x in (*args, *shapes))
    return list(pl.pallas_call(
        kernel,
        in_specs=[VMEM] * len(args),
        out_specs=[VMEM] * len(shapes),
        out_shape=shapes,
        scratch_shapes=scratch,
        compiler_params=pltpu.CompilerParams(vmem_limit_bytes=VMEM_LIMIT),
        cost_estimate=pl.CostEstimate(flops=flops, bytes_accessed=total, transcendentals=exps),
        name=name,
    )(*args))


def filtered(tables, stacked, per_tile):
    lanes = stacked.shape[1]
    lane_group = lax.broadcasted_iota(jnp.int32, (LANES, lanes), 1) % LANES // (LANES // per_tile)
    conv = jnp.zeros((LANES, lanes), jnp.float32)
    for g, table in enumerate(tables):
        part = jnp.dot(table, stacked, preferred_element_type=jnp.float32)
        conv = jnp.where(lane_group == g, part, conv)
    return conv


def halves():
    down, along = (lax.broadcasted_iota(jnp.int32, (LANES, LANES), i) for i in range(2))
    before = jnp.where(along > down, 1.0, 0.0).astype(jnp.bfloat16)
    within = jnp.where(along > down, 0.0, 1.0).astype(jnp.bfloat16)
    return before, within


def gate(q, conv, direct, mixed):
    return (
        q.astype(jnp.float32) * (conv + direct.astype(jnp.float32) * mixed.astype(jnp.float32))
    ).astype(jnp.bfloat16)


def later_kernel(q_ref, k_ref, v_ref, taps_ref, direct_ref, out_ref, rings, taps):
    rows, chans = q_ref.shape
    per_tile = taps_ref.shape[0] * LANES // chans
    windows = rows // LANES
    down, along = (lax.broadcasted_iota(jnp.int32, (LANES, LANES), i) for i in range(2))
    turn = jnp.where((down + along) % LANES == 0, 1.0, 0.0).astype(jnp.bfloat16)
    taps[...] = jnp.dot(taps_ref[...], turn, preferred_element_type=jnp.float32)
    before, within = halves()

    @pl.loop(0, chans // LANES, unroll=2)
    def _(tile):
        cols = pl.ds(pl.multiple_of(tile * LANES, LANES), LANES)
        first = pl.multiple_of(tile * per_tile, per_tile)
        lines = taps[pl.ds(first, per_tile), :]
        mixed = (k_ref[:, cols].astype(jnp.float32) * v_ref[:, cols].astype(jnp.float32)).astype(
            jnp.bfloat16
        )
        stacked = jnp.concatenate(
            [mixed[w * LANES : (w + 2) * LANES] for w in range(windows - 1)], axis=1
        )
        tables = []
        for g in range(per_tile):
            ring = pltpu.roll(
                jnp.broadcast_to(lines[g : g + 1], (LANES, LANES)), 0, 1, stride=1, stride_axis=0
            ).astype(jnp.bfloat16)
            rings[first + g] = ring
            tables.append(jnp.concatenate([ring * before, ring * within], axis=1))
        conv = filtered(tables, stacked, per_tile)
        conv = jnp.concatenate(
            [conv[:, w * LANES : (w + 1) * LANES] for w in range(windows - 1)], axis=0
        )
        out_ref[LANES:, cols] = gate(q_ref[LANES:, cols], conv, direct_ref[:, cols], mixed[LANES:])


def first_kernel(
    q_ref, k_ref, v_ref, near_rim, ring_rim, far_rim, direct_ref, rings, _, out_ref, rim
):
    chans = q_ref.shape[1]
    per_tile = rings.shape[0] * LANES // chans
    before, within = halves()
    half = chans // 2
    rim[:, :half] = near_rim[...]
    rim[:, half:] = ring_rim[...]

    @pl.when(corner_of() == 0)
    def _():
        rim[:, half:] = far_rim[...]

    @pl.loop(0, chans // LANES, unroll=2)
    def _(tile):
        cols = pl.ds(pl.multiple_of(tile * LANES, LANES), LANES)
        first = pl.multiple_of(tile * per_tile, per_tile)
        mixed = (k_ref[:, cols].astype(jnp.float32) * v_ref[:, cols].astype(jnp.float32)).astype(
            jnp.bfloat16
        )
        stacked = jnp.concatenate([rim[:, cols], mixed], axis=0)
        tables = []
        for g in range(per_tile):
            ring = rings[first + g]
            tables.append(jnp.concatenate([ring * before, ring * within], axis=1))
        conv = filtered(tables, stacked, per_tile)
        out_ref[:, cols] = gate(q_ref[:, cols], conv, direct_ref[:, cols], mixed)


def hyena_later(hyena_q, hyena_k, hyena_v, filters, direct):
    rows, chans = hyena_q.shape
    groups, kernel = filters.shape
    taps = jnp.pad(filters, ((0, 0), (0, LANES - kernel)))
    return kernel_call(
        later_kernel,
        (hyena_q, hyena_k, hyena_v, taps, direct[None]),
        [
            jax.ShapeDtypeStruct((rows, chans), jnp.bfloat16),
            jax.ShapeDtypeStruct((groups, LANES, LANES), jnp.bfloat16),
        ],
        "hyena_later",
        [pltpu.VMEM((groups, LANES), jnp.float32)],
        flops=4 * rows * chans * LANES * 8,
    )


def hyena_first(hyena_q, hyena_k, hyena_v, rims, direct, rings, later):
    rows, chans = hyena_q.shape
    top = pl.BlockSpec((LANES, chans), lambda i: (0, 0))
    return pl.pallas_call(
        first_kernel,
        grid=(1,),
        in_specs=[top] * 3 + [VMEM] * 5 + [pl.BlockSpec(memory_space=pl.ANY)],
        out_specs=top,
        out_shape=jax.ShapeDtypeStruct((rows, chans), jnp.bfloat16),
        scratch_shapes=[pltpu.VMEM((LANES, chans), jnp.bfloat16)],
        input_output_aliases={8: 0},
        compiler_params=pltpu.CompilerParams(vmem_limit_bytes=VMEM_LIMIT),
        cost_estimate=pl.CostEstimate(
            flops=4 * LANES * chans * LANES * 8, bytes_accessed=16 * LANES * chans, transcendentals=0
        ),
        name="hyena_first",
    )(hyena_q, hyena_k, hyena_v, *rims, direct[None], rings, later)


def deal_kernel(q_ref, k_ref, v_ref, id_ref, *refs):
    outs, (held, arrive, told) = refs[:-3], refs[-3:]
    tell = pltpu.make_async_copy(id_ref, held, told)
    tell.start()
    rows, feat = q_ref.shape
    width = feat // SQUAD
    corner = corner_of()
    copies = []
    for k in (*range(1, SQUAD), 0):
        cols = pl.ds(pl.multiple_of(jnp.bitwise_xor(corner, k) * width, width), width)
        base = rows if k else 0
        places = (
            (q_ref, outs[k + 1] if k else outs[0], 0),
            (k_ref, outs[k + 1], base + TAG),
            (v_ref, outs[k + 1], base + TAG + rows),
        )
        copies += [
            pltpu.make_async_copy(
                source.at[:, cols], target.at[pl.ds(begin, rows)], arrive.at[k, i]
            )
            for i, (source, target, begin) in enumerate(places)
        ]
    for copy in copies:
        copy.start()
    tell.wait()
    ids = (held[...] + 1).astype(jnp.float32)
    spare = jnp.zeros((TAG - ids.shape[0], LANES), jnp.float32)
    ids = jnp.concatenate([ids, spare], axis=0)
    tag = jnp.concatenate([ids] * (width // LANES), axis=1).astype(jnp.bfloat16)
    for i, target in enumerate(outs):
        begin = 0 if i == 1 else rows
        target[begin : begin + TAG, :] = tag
    for copy in copies:
        copy.wait()


def deal(queries, keys, values, ids):
    rows, feat = queries.shape
    tall = [rows + TAG, 2 * rows + TAG] + [3 * rows + TAG] * (SQUAD - 1)
    shapes = [(x, feat // SQUAD) for x in tall]
    held = [pltpu.with_memory_space_constraint(x, pltpu.HBM) for x in (queries, keys, values, ids)]
    return list(
        pl.pallas_call(
            deal_kernel,
            in_specs=[pl.BlockSpec(memory_space=pl.ANY)] * 4,
            out_specs=[VMEM] * len(tall),
            out_shape=[jax.ShapeDtypeStruct(x, jnp.bfloat16) for x in shapes],
            scratch_shapes=[
                pltpu.VMEM(ids.shape, ids.dtype),
                pltpu.SemaphoreType.DMA((SQUAD, 3)),
                pltpu.SemaphoreType.DMA,
            ],
            compiler_params=pltpu.CompilerParams(vmem_limit_bytes=VMEM_LIMIT),
            cost_estimate=pl.CostEstimate(
                flops=0, bytes_accessed=12 * rows * feat, transcendentals=0
            ),
            name="deal",
        )(*held)
    )


def id_columns(tag_ref, rows):
    tag = tag_ref[:, :LANES].astype(jnp.float32)
    tiles = [jnp.broadcast_to(tag[t : t + 1], (LANES, LANES)).T for t in range(rows // LANES)]
    return jnp.concatenate(tiles, axis=0)


def place_keys(parts, corner, base, rows, keys, values):
    heads = keys.shape[0]
    marks = lax.broadcasted_iota(jnp.int32, (rows, LANES), 1).astype(jnp.float32) + 1.0
    for k, part in enumerate(parts):
        begin = pl.multiple_of((jnp.bitwise_xor(corner, k) + base) * rows, rows)
        span = pl.ds(begin, rows)
        ids = id_columns(part.at[:TAG], rows)
        mask = jnp.where(ids == marks, 0.0, -NEG).astype(jnp.bfloat16)
        for h in range(heads):
            cols = slice(h * HD, (h + 1) * HD)
            keys[h, span, :HD] = part[TAG : TAG + rows, cols]
            keys[h, span, HD:] = mask
            values[h, span, :] = part[TAG + rows : TAG + 2 * rows, cols]


def near_parts(near, rows):
    tall = 2 * rows + TAG
    return [near[0], near[1].at[:tall], near[1].at[tall:], near[2]]


def place_queries(parts, corner, rows, queries):
    heads = queries.shape[0]
    marks = lax.broadcasted_iota(jnp.int32, (rows, LANES), 1).astype(jnp.float32) + 1.0
    for k, part in enumerate(parts):
        begin = pl.multiple_of(jnp.bitwise_xor(corner, k) * rows, rows)
        span = pl.ds(begin, rows)
        ids = id_columns(part.at[rows : rows + TAG], rows)
        mask = jnp.where(ids == marks, -1.0, 0.0).astype(jnp.bfloat16)
        for h in range(heads):
            queries[h, span, :HD] = part[:rows, h * HD : (h + 1) * HD]
            queries[h, span, HD:] = mask


def score_of(query, keys):
    return lax.dot_general(
        keys, query, (((1,), (1,)), ((), ())), preferred_element_type=jnp.float32
    )


def attend(score, values, diagonal):
    factor = math.log2(math.e) / math.sqrt(HD)
    rows = score.shape[1]
    if diagonal:
        older = lax.broadcasted_iota(jnp.int32, (rows, rows), 0) <= lax.broadcasted_iota(
            jnp.int32, (rows, rows), 1
        )
        score = jnp.concatenate([score[:-rows], jnp.where(older, score[-rows:], NEG)], axis=0)
    high = jnp.max(score, axis=0, keepdims=True)
    expo = jnp.exp2((score - high) * factor)
    total = jnp.sum(expo, axis=0, keepdims=True)
    summed = lax.dot_general(
        values,
        expo.astype(jnp.bfloat16),
        (((0,), (0,)), ((), ())),
        preferred_element_type=jnp.float32,
    )
    return summed / total, high * factor + jnp.log2(total)


def ahead(steps, product):
    late = product(*steps[0])
    for step, following in zip(steps, steps[1:] + [None]):
        now, late = late, product(*following) if following else None
        yield step, now


def main_kernel(*refs):
    own, near, out, (queries, keys, values) = refs[:5], refs[5:8], refs[8], refs[9:]
    heads, span, _ = queries.shape
    rows = span // SQUAD
    width = heads * HD
    corner = corner_of()
    asked = [own[0]] + [p.at[: rows + TAG] for p in own[2:]]
    held = [own[1]] + [p.at[rows:] for p in own[2:]]
    place_queries(asked, corner, rows, queries)
    place_keys(held, corner, SQUAD, rows, keys, values)
    place_keys(near_parts(near, rows), corner, 0, rows, keys, values)
    span = [slice(j * rows, (j + 1) * rows) for j in range(SQUAD)]
    reach = [(SQUAD + 1 + j) * rows for j in range(SQUAD)]
    steps = [(j, h) for j in range(SQUAD) for h in range(heads)]
    for (j, h), score in ahead(
        steps, lambda j, h: score_of(queries[h, span[j]], keys[h, : reach[j]])
    ):
        mixed, lse = attend(score, values[h, : reach[j]], True)
        out[h * HD : (h + 1) * HD, span[j]] = mixed
        out[width + h : width + h + 1, span[j]] = lse
    out[width + heads :, :] = jnp.zeros((TAG - heads, SQUAD * rows), jnp.float32)


def far_kernel(*refs):
    asked, near, out, (queries, keys, values) = refs[:2], refs[2:5], refs[5], refs[6:]
    heads, span, _ = queries.shape
    rows = span // SQUAD
    width = heads * HD
    corner = corner_of()
    tall = rows + TAG
    asked = [asked[0].at[k * tall : (k + 1) * tall] for k in range(SQUAD - 1)] + [asked[1]]
    place_queries(asked, corner, rows, queries)
    place_keys(near_parts(near, rows), corner, 0, rows, keys, values)
    span = [slice(j * rows, (j + 1) * rows) for j in range(SQUAD)]
    stats = [[] for _ in range(SQUAD - 1)]
    steps = [(j, h) for j in range(SQUAD - 1) for h in range(heads)]
    for (j, h), score in ahead(
        steps, lambda j, h: score_of(queries[h, span[j]], keys[h, span[j].stop :])
    ):
        mixed, lse = attend(score, values[h, span[j].stop :], False)
        out[h * HD : (h + 1) * HD, span[j]] = mixed.astype(out.dtype)
        top = lse.astype(jnp.bfloat16).astype(jnp.float32)
        mid = (lse - top).astype(jnp.bfloat16).astype(jnp.float32)
        stats[j] += [top, mid, lse - top - mid]
    for j, stat in enumerate(stats):
        stat.append(jnp.zeros((TAG - len(stat), rows), jnp.float32))
        out[width:, span[j]] = jnp.concatenate(stat, axis=0).astype(out.dtype)


def merge_kernel(main_ref, far_ref, *refs):
    outs, ready = refs[:-1], refs[-1]
    _, rows, width = ready.shape
    corner = corner_of()
    served = lax.axis_index("ctx") >= 2 * SQUAD
    for j in range(SQUAD):
        cols = slice(j * rows, (j + 1) * rows)
        for h in range(width // HD):
            feats = slice(h * HD, (h + 1) * HD)
            mixed = main_ref[feats, cols]
            if j < SQUAD - 1:
                here = main_ref[width + h : width + h + 1, cols]
                stats = far_ref[width:, cols].astype(jnp.float32)
                there = stats[3 * h : 3 * h + 1] + stats[3 * h + 1 : 3 * h + 2]
                there = jnp.where(served, there + stats[3 * h + 2 : 3 * h + 3], NEG)
                high = jnp.maximum(here, there)
                here, there = jnp.exp2(here - high), jnp.exp2(there - high)
                total = here + there
                mixed = mixed * (here / total) + far_ref[feats, cols].astype(jnp.float32) * (
                    there / total
                )
            ready[j, :, feats] = mixed.T.astype(ready.dtype)
    for k, out in enumerate(outs):
        out[...] = ready[jnp.bitwise_xor(corner, k)]


def project_kernel(ranks, *refs):
    parts, weight_ref, out_ref, whole = refs[:-3], refs[-3], refs[-2], refs[-1]
    mine, corner = lax.axis_index("tp"), corner_of()
    width = parts[0].shape[1]
    for r in range(ranks):
        source = lax.rem(mine + ranks - r, ranks)
        for k in range(SQUAD):
            begin = (source * SQUAD + jnp.bitwise_xor(corner, k)) * width
            whole[:, pl.ds(pl.multiple_of(begin, width), width)] = parts[r * SQUAD + k][...]
    block = 2 * LANES
    for c in range(out_ref.shape[1] // block):
        cols = slice(c * block, (c + 1) * block)
        out_ref[:, cols] = jnp.dot(
            whole[...], weight_ref[:, cols], preferred_element_type=jnp.float32
        ).astype(out_ref.dtype)


def local(
    hyena_q, hyena_k, hyena_v, filters, direct, queries, keys, values, segment_ids, out_weight
):
    rows, feat = queries.shape
    count, ranks = lax.axis_size("ctx"), lax.axis_size("tp")
    width = feat // SQUAD
    heads = width // HD
    bf16, f32 = jnp.bfloat16, jnp.float32

    def swap(value, mask):
        return lax.ppermute(value, "ctx", [(i, i ^ mask) for i in range(count)])

    def climb(value, first=0):
        return lax.ppermute(value, "ctx", [(i, i + SQUAD) for i in range(first, count - SQUAD)])

    def descend(value):
        return lax.ppermute(
            value, "ctx", [(i, i - SQUAD) for i in range(2 * SQUAD, count)]
        )

    asked, kept, *sent = deal(
        queries, keys, values, segment_ids.reshape(rows // LANES, LANES)
    )
    tall = rows + TAG
    near = [climb(kept)]
    beside = [swap(sent[0], 1), swap(sent[1], 2)]
    later, rings = hyena_later(hyena_q, hyena_k, hyena_v, filters, direct)
    beside[0], rings = lax.optimization_barrier((beside[0], rings))
    sent[2], beside[0] = lax.optimization_barrier((sent[2], beside[0]))
    across = swap(sent[2], 3)
    beside[1], near[0] = lax.optimization_barrier((beside[1], near[0]))
    near.append(climb(jnp.concatenate([x[rows:] for x in beside], axis=0)))
    back = [descend(jnp.concatenate([asked] + [x[:tall] for x in beside], axis=0))]
    near.append(climb(across[rows:]))
    tail_k = hyena_k[rows - LANES :].astype(f32)
    tail_v = hyena_v[rows - LANES :].astype(f32)
    tail = (tail_k * tail_v).astype(bf16)
    half = tail.shape[1] // 2
    ring = lax.ppermute(
        tail[:, half:], "ctx", [(i, i - i % SQUAD + (i + 1) % SQUAD) for i in range(count)]
    )
    across, ring = lax.optimization_barrier((across, ring))
    back.append(descend(across[:tall]))
    rims = [
        lax.ppermute(tail[:, :half], "ctx", [(i, i + 1) for i in range(count - 1)]),
        ring,
        lax.ppermute(ring, "ctx", [(i, i + SQUAD) for i in range(0, count - SQUAD, SQUAD)]),
    ]
    own = [asked, kept, *beside, across]
    def store(blocks):
        return [
            pltpu.VMEM((heads, SQUAD * rows, 2 * HD), bf16),
            pltpu.VMEM((heads, blocks * rows, 2 * HD), bf16),
            pltpu.VMEM((heads, blocks * rows, HD), bf16),
        ]

    (far,) = kernel_call(
        far_kernel,
        (*back, *near),
        [jax.ShapeDtypeStruct((width + TAG, (SQUAD - 1) * rows), bf16)],
        "far",
        store(SQUAD),
        flops=6 * 4 * rows * rows * width,
        exps=6 * rows * rows * heads,
    )
    far = climb(far, SQUAD)
    own[1], *rims = lax.optimization_barrier((own[1], *rims))
    (main,) = kernel_call(
        main_kernel,
        (*own, *near),
        [jax.ShapeDtypeStruct((width + TAG, SQUAD * rows), f32)],
        "main",
        store(2 * SQUAD),
        flops=26 * 4 * rows * rows * width,
        exps=26 * rows * rows * heads,
    )
    done = kernel_call(
        merge_kernel,
        (main, far),
        [jax.ShapeDtypeStruct((rows, width), bf16)] * SQUAD,
        "merge",
        [pltpu.VMEM((SQUAD, rows, width), bf16)],
    )
    *rims, done[0] = lax.optimization_barrier((*rims, done[0]))
    hyena_out = hyena_first(hyena_q, hyena_k, hyena_v, rims, direct, rings, later)

    def turn(value, r):
        return lax.ppermute(value, "tp", [(t, (t + r) % ranks) for t in range(ranks)])

    pieces = [swap(done[k], k) for k in range(1, SQUAD)]
    hyena_out, *pieces = lax.optimization_barrier((hyena_out, done[0], *pieces))
    pieces += [turn(piece, r) for r in range(1, ranks) for piece in pieces]
    (attn_out,) = kernel_call(
        functools.partial(project_kernel, ranks),
        (*pieces, out_weight),
        [jax.ShapeDtypeStruct((rows, out_weight.shape[1]), bf16)],
        "project",
        [pltpu.VMEM((rows, ranks * feat), bf16)],
        flops=2 * rows * math.prod(out_weight.shape),
    )
    return (hyena_out, attn_out)


def solution(mesh):
    placed = (
        P("ctx", "tp"),
        P("ctx", "tp"),
        P("ctx", "tp"),
        P("tp", None),
        P("tp"),
        P("ctx", "tp"),
        P("ctx", "tp"),
        P("ctx", "tp"),
        P("ctx"),
        P(None, "tp"),
    )
    return jax.shard_map(
        local,
        mesh=mesh,
        in_specs=placed,
        out_specs=(P("ctx", "tp"), P("ctx", "tp")),
        check_vma=False,
    )
```

```python
import functools
import math

import jax
import jax.numpy as jnp
from jax import lax
from jax.experimental import pallas as pl
from jax.experimental.pallas import tpu as pltpu
from jax.sharding import PartitionSpec as P

HD = 128
SQUAD = 4
NEG = -1e30
TAG = 16
LANES = 128
VMEM_LIMIT = 32 * 1024 * 1024
VMEM = pl.BlockSpec(memory_space=pltpu.VMEM)


def corner_of():
    return lax.rem(lax.axis_index("ctx"), SQUAD)


def kernel_call(kernel, args, shapes, name, scratch=(), flops=0, exps=0):
    total = sum(math.prod(x.shape) * x.dtype.itemsize for x in (*args, *shapes))
    return list(pl.pallas_call(
        kernel,
        in_specs=[VMEM] * len(args),
        out_specs=[VMEM] * len(shapes),
        out_shape=shapes,
        scratch_shapes=scratch,
        compiler_params=pltpu.CompilerParams(vmem_limit_bytes=VMEM_LIMIT),
        cost_estimate=pl.CostEstimate(flops=flops, bytes_accessed=total, transcendentals=exps),
        name=name,
    )(*args))


def hyena_kernel(q_ref, k_ref, v_ref, near_rim, ring_rim, far_rim, taps_ref, direct_ref, out_ref, taps, rim):
    rows, chans = q_ref.shape
    groups = taps_ref.shape[0]
    group = chans // groups
    per_tile = LANES // group
    windows = rows // LANES
    shape = (LANES, LANES)
    down, along = (lax.broadcasted_iota(jnp.int32, shape, i) for i in range(2))
    turn = jnp.where((down + along) % LANES == 0, 1.0, 0.0).astype(jnp.bfloat16)
    before = jnp.where(along > down, 1.0, 0.0).astype(jnp.bfloat16)
    within = jnp.where(along > down, 0.0, 1.0).astype(jnp.bfloat16)
    taps[...] = jnp.dot(taps_ref[...], turn, preferred_element_type=jnp.float32)
    lane_group = lax.broadcasted_iota(jnp.int32, (LANES, windows * LANES), 1) % LANES // group

    half = near_rim.shape[1]
    rim[:, :half] = near_rim[...]
    rim[:, half:] = ring_rim[...]

    @pl.when(corner_of() == 0)
    def _():
        rim[:, half:] = far_rim[...]

    def table(at):
        ring = pltpu.roll(
            jnp.broadcast_to(taps[pl.ds(at, 1), :], shape), 0, 1, stride=1, stride_axis=0
        ).astype(jnp.bfloat16)
        return jnp.concatenate([ring * before, ring * within], axis=1)

    pair = 2

    @pl.loop(0, chans // LANES, step=pair)
    def _(begin):
        tiles = [
            pl.ds(pl.multiple_of((begin + t) * LANES, LANES), LANES) for t in range(pair)
        ]
        mixed, stacked = [], []
        for cols in tiles:
            product = k_ref[:, cols].astype(jnp.float32) * v_ref[:, cols].astype(jnp.float32)
            mixed.append(product.astype(jnp.bfloat16))
            full = jnp.concatenate([rim[:, cols], mixed[-1]], axis=0)
            stacked.append(
                jnp.concatenate(
                    [full[w * LANES : (w + 2) * LANES] for w in range(windows)], axis=1
                )
            )
        steps = [(t, g) for t in range(pair) for g in range(per_tile)]
        tables = [table((begin + t) * per_tile + g) for t, g in steps[:2]]
        parts = [jnp.dot(tables[0], stacked[0], preferred_element_type=jnp.float32)]
        conv = None
        for i, (t, g) in enumerate(steps):
            if i + 2 < len(steps):
                t2, g2 = steps[i + 2]
                tables.append(table((begin + t2) * per_tile + g2))
            if i + 1 < len(steps):
                parts.append(
                    jnp.dot(
                        tables[i + 1], stacked[steps[i + 1][0]], preferred_element_type=jnp.float32
                    )
                )
            conv = parts[i] if g == 0 else jnp.where(lane_group == g, parts[i], conv)
            if g == per_tile - 1:
                cols = tiles[t]
                joined = jnp.concatenate(
                    [conv[:, w * LANES : (w + 1) * LANES] for w in range(windows)], axis=0
                )
                passed = direct_ref[:, cols].astype(jnp.float32) * mixed[t].astype(jnp.float32)
                out_ref[:, cols] = (
                    q_ref[:, cols].astype(jnp.float32) * (joined + passed)
                ).astype(jnp.bfloat16)


def hyena(hyena_q, hyena_k, hyena_v, rims, filters, direct):
    rows, chans = hyena_q.shape
    groups, kernel = filters.shape
    taps = jnp.pad(filters, ((0, 0), (0, LANES - kernel)))
    (out,) = kernel_call(
        hyena_kernel,
        (hyena_q, hyena_k, hyena_v, *rims, taps, direct[None]),
        [jax.ShapeDtypeStruct((rows, chans), jnp.bfloat16)],
        "hyena",
        [pltpu.VMEM((groups, LANES), jnp.float32), pltpu.VMEM((LANES, chans), jnp.bfloat16)],
        flops=4 * rows * chans * 2 * LANES * 8,
    )
    return out


def deal_kernel(q_ref, k_ref, v_ref, id_ref, *refs):
    outs, (held, arrive, told) = refs[:-3], refs[-3:]
    tell = pltpu.make_async_copy(id_ref, held, told)
    tell.start()
    rows, feat = q_ref.shape
    width = feat // SQUAD
    corner = corner_of()
    copies = []
    for k in (*range(1, SQUAD), 0):
        cols = pl.ds(pl.multiple_of(jnp.bitwise_xor(corner, k) * width, width), width)
        base = rows if k else 0
        places = (
            (q_ref, outs[k + 1] if k else outs[0], 0),
            (k_ref, outs[k + 1], base + TAG),
            (v_ref, outs[k + 1], base + TAG + rows),
        )
        copies += [
            pltpu.make_async_copy(
                source.at[:, cols], target.at[pl.ds(begin, rows)], arrive.at[k, i]
            )
            for i, (source, target, begin) in enumerate(places)
        ]
    for copy in copies:
        copy.start()
    tell.wait()
    ids = (held[...] + 1).astype(jnp.float32)
    spare = jnp.zeros((TAG - ids.shape[0], LANES), jnp.float32)
    ids = jnp.concatenate([ids, spare], axis=0)
    tag = jnp.concatenate([ids] * (width // LANES), axis=1).astype(jnp.bfloat16)
    for i, target in enumerate(outs):
        begin = 0 if i == 1 else rows
        target[begin : begin + TAG, :] = tag
    for copy in copies:
        copy.wait()


def deal(queries, keys, values, ids):
    rows, feat = queries.shape
    tall = [rows + TAG, 2 * rows + TAG] + [3 * rows + TAG] * (SQUAD - 1)
    shapes = [(x, feat // SQUAD) for x in tall]
    held = [pltpu.with_memory_space_constraint(x, pltpu.HBM) for x in (queries, keys, values, ids)]
    return list(
        pl.pallas_call(
            deal_kernel,
            in_specs=[pl.BlockSpec(memory_space=pl.ANY)] * 4,
            out_specs=[VMEM] * len(tall),
            out_shape=[jax.ShapeDtypeStruct(x, jnp.bfloat16) for x in shapes],
            scratch_shapes=[
                pltpu.VMEM(ids.shape, ids.dtype),
                pltpu.SemaphoreType.DMA((SQUAD, 3)),
                pltpu.SemaphoreType.DMA,
            ],
            compiler_params=pltpu.CompilerParams(vmem_limit_bytes=VMEM_LIMIT),
            cost_estimate=pl.CostEstimate(
                flops=0, bytes_accessed=12 * rows * feat, transcendentals=0
            ),
            name="deal",
        )(*held)
    )


def id_columns(tag_ref, rows):
    tag = tag_ref[:, :LANES].astype(jnp.float32)
    tiles = [jnp.broadcast_to(tag[t : t + 1], (LANES, LANES)).T for t in range(rows // LANES)]
    return jnp.concatenate(tiles, axis=0)


def place_keys(parts, corner, base, rows, keys, values):
    heads = keys.shape[0]
    marks = lax.broadcasted_iota(jnp.int32, (rows, LANES), 1).astype(jnp.float32) + 1.0
    for k, part in enumerate(parts):
        begin = pl.multiple_of((jnp.bitwise_xor(corner, k) + base) * rows, rows)
        span = pl.ds(begin, rows)
        ids = id_columns(part.at[:TAG], rows)
        mask = jnp.where(ids == marks, 0.0, -NEG).astype(jnp.bfloat16)
        for h in range(heads):
            cols = slice(h * HD, (h + 1) * HD)
            keys[h, span, :HD] = part[TAG : TAG + rows, cols]
            keys[h, span, HD:] = mask
            values[h, span, :] = part[TAG + rows : TAG + 2 * rows, cols]


def near_parts(near, rows):
    tall = 2 * rows + TAG
    return [near[0], near[1].at[:tall], near[1].at[tall:], near[2]]


def place_queries(parts, corner, rows, queries):
    heads = queries.shape[0]
    marks = lax.broadcasted_iota(jnp.int32, (rows, LANES), 1).astype(jnp.float32) + 1.0
    for k, part in enumerate(parts):
        begin = pl.multiple_of(jnp.bitwise_xor(corner, k) * rows, rows)
        span = pl.ds(begin, rows)
        ids = id_columns(part.at[rows : rows + TAG], rows)
        mask = jnp.where(ids == marks, -1.0, 0.0).astype(jnp.bfloat16)
        for h in range(heads):
            queries[h, span, :HD] = part[:rows, h * HD : (h + 1) * HD]
            queries[h, span, HD:] = mask


def score_of(query, keys):
    return lax.dot_general(
        keys, query, (((1,), (1,)), ((), ())), preferred_element_type=jnp.float32
    )


def attend(score, values, diagonal):
    factor = math.log2(math.e) / math.sqrt(HD)
    rows = score.shape[1]
    if diagonal:
        older = lax.broadcasted_iota(jnp.int32, (rows, rows), 0) <= lax.broadcasted_iota(
            jnp.int32, (rows, rows), 1
        )
        score = jnp.concatenate([score[:-rows], jnp.where(older, score[-rows:], NEG)], axis=0)
    high = jnp.max(score, axis=0, keepdims=True)
    expo = jnp.exp2((score - high) * factor)
    total = jnp.sum(expo, axis=0, keepdims=True)
    summed = lax.dot_general(
        values,
        expo.astype(jnp.bfloat16),
        (((0,), (0,)), ((), ())),
        preferred_element_type=jnp.float32,
    )
    return summed / total, high * factor + jnp.log2(total)


def ahead(steps, product):
    late = product(*steps[0])
    for step, following in zip(steps, steps[1:] + [None]):
        now, late = late, product(*following) if following else None
        yield step, now


def main_kernel(*refs):
    own, near, out, (queries, keys, values) = refs[:5], refs[5:8], refs[8], refs[9:]
    heads, span, _ = queries.shape
    rows = span // SQUAD
    width = heads * HD
    corner = corner_of()
    asked = [own[0]] + [p.at[: rows + TAG] for p in own[2:]]
    held = [own[1]] + [p.at[rows:] for p in own[2:]]
    place_queries(asked, corner, rows, queries)
    place_keys(held, corner, SQUAD, rows, keys, values)
    place_keys(near_parts(near, rows), corner, 0, rows, keys, values)
    span = [slice(j * rows, (j + 1) * rows) for j in range(SQUAD)]
    reach = [(SQUAD + 1 + j) * rows for j in range(SQUAD)]
    steps = [(j, h) for j in range(SQUAD) for h in range(heads)]
    for (j, h), score in ahead(
        steps, lambda j, h: score_of(queries[h, span[j]], keys[h, : reach[j]])
    ):
        mixed, lse = attend(score, values[h, : reach[j]], True)
        out[h * HD : (h + 1) * HD, span[j]] = mixed
        out[width + h : width + h + 1, span[j]] = lse
    out[width + heads :, :] = jnp.zeros((TAG - heads, SQUAD * rows), jnp.float32)


def far_kernel(*refs):
    asked, near, out, (queries, keys, values) = refs[:2], refs[2:5], refs[5], refs[6:]
    heads, span, _ = queries.shape
    rows = span // SQUAD
    width = heads * HD
    corner = corner_of()
    tall = rows + TAG
    asked = [asked[0].at[k * tall : (k + 1) * tall] for k in range(SQUAD - 1)] + [asked[1]]
    place_queries(asked, corner, rows, queries)
    place_keys(near_parts(near, rows), corner, 0, rows, keys, values)
    span = [slice(j * rows, (j + 1) * rows) for j in range(SQUAD)]
    stats = [[] for _ in range(SQUAD - 1)]
    steps = [(j, h) for j in range(SQUAD - 1) for h in range(heads)]
    for (j, h), score in ahead(
        steps, lambda j, h: score_of(queries[h, span[j]], keys[h, span[j].stop :])
    ):
        mixed, lse = attend(score, values[h, span[j].stop :], False)
        out[h * HD : (h + 1) * HD, span[j]] = mixed.astype(out.dtype)
        top = lse.astype(jnp.bfloat16).astype(jnp.float32)
        mid = (lse - top).astype(jnp.bfloat16).astype(jnp.float32)
        stats[j] += [top, mid, lse - top - mid]
    for j, stat in enumerate(stats):
        stat.append(jnp.zeros((TAG - len(stat), rows), jnp.float32))
        out[width:, span[j]] = jnp.concatenate(stat, axis=0).astype(out.dtype)


def merge_kernel(main_ref, far_ref, *refs):
    outs, ready = refs[:-1], refs[-1]
    _, rows, width = ready.shape
    corner = corner_of()
    served = lax.axis_index("ctx") >= 2 * SQUAD
    for j in range(SQUAD):
        cols = slice(j * rows, (j + 1) * rows)
        for h in range(width // HD):
            feats = slice(h * HD, (h + 1) * HD)
            mixed = main_ref[feats, cols]
            if j < SQUAD - 1:
                here = main_ref[width + h : width + h + 1, cols]
                stats = far_ref[width:, cols].astype(jnp.float32)
                there = stats[3 * h : 3 * h + 1] + stats[3 * h + 1 : 3 * h + 2]
                there = jnp.where(served, there + stats[3 * h + 2 : 3 * h + 3], NEG)
                high = jnp.maximum(here, there)
                here, there = jnp.exp2(here - high), jnp.exp2(there - high)
                total = here + there
                mixed = mixed * (here / total) + far_ref[feats, cols].astype(jnp.float32) * (
                    there / total
                )
            ready[j, :, feats] = mixed.T.astype(ready.dtype)
    for k, out in enumerate(outs):
        out[...] = ready[jnp.bitwise_xor(corner, k)]


def project_kernel(ranks, *refs):
    parts, weight_ref, out_ref, whole = refs[:-3], refs[-3], refs[-2], refs[-1]
    mine, corner = lax.axis_index("tp"), corner_of()
    width = parts[0].shape[1]
    for r in range(ranks):
        source = lax.rem(mine + ranks - r, ranks)
        for k in range(SQUAD):
            begin = (source * SQUAD + jnp.bitwise_xor(corner, k)) * width
            whole[:, pl.ds(pl.multiple_of(begin, width), width)] = parts[r * SQUAD + k][...]
    block = 2 * LANES
    for c in range(out_ref.shape[1] // block):
        cols = slice(c * block, (c + 1) * block)
        out_ref[:, cols] = jnp.dot(
            whole[...], weight_ref[:, cols], preferred_element_type=jnp.float32
        ).astype(out_ref.dtype)


def local(
    hyena_q, hyena_k, hyena_v, filters, direct, queries, keys, values, segment_ids, out_weight
):
    rows, feat = queries.shape
    count, ranks = lax.axis_size("ctx"), lax.axis_size("tp")
    width = feat // SQUAD
    heads = width // HD
    bf16, f32 = jnp.bfloat16, jnp.float32

    def swap(value, mask):
        return lax.ppermute(value, "ctx", [(i, i ^ mask) for i in range(count)])

    def climb(value, first=0):
        return lax.ppermute(value, "ctx", [(i, i + SQUAD) for i in range(first, count - SQUAD)])

    def descend(value):
        return lax.ppermute(
            value, "ctx", [(i, i - SQUAD) for i in range(2 * SQUAD, count)]
        )

    asked, kept, *sent = deal(
        queries, keys, values, segment_ids.reshape(rows // LANES, LANES)
    )
    tall = rows + TAG
    near = [climb(kept)]
    beside = [swap(sent[0], 1), swap(sent[1], 2)]
    sent[2], beside[0] = lax.optimization_barrier((sent[2], beside[0]))
    across = swap(sent[2], 3)
    beside[1], near[0] = lax.optimization_barrier((beside[1], near[0]))
    near.append(climb(jnp.concatenate([x[rows:] for x in beside], axis=0)))
    back = [descend(jnp.concatenate([asked] + [x[:tall] for x in beside], axis=0))]
    near.append(climb(across[rows:]))
    tail_k = hyena_k[rows - LANES :].astype(f32)
    tail_v = hyena_v[rows - LANES :].astype(f32)
    tail = (tail_k * tail_v).astype(bf16)
    half = tail.shape[1] * 12 // 16
    ring = lax.ppermute(
        tail[:, half:], "ctx", [(i, i - i % SQUAD + (i + 1) % SQUAD) for i in range(count)]
    )
    across, ring = lax.optimization_barrier((across, ring))
    back.append(descend(across[:tall]))
    rims = [lax.ppermute(tail[:, :half], "ctx", [(i, i + 1) for i in range(count - 1)]), ring]
    own = [asked, kept, *beside, across]
    def store(blocks):
        return [
            pltpu.VMEM((heads, SQUAD * rows, 2 * HD), bf16),
            pltpu.VMEM((heads, blocks * rows, 2 * HD), bf16),
            pltpu.VMEM((heads, blocks * rows, HD), bf16),
        ]

    (far,) = kernel_call(
        far_kernel,
        (*back, *near),
        [jax.ShapeDtypeStruct((width + TAG, (SQUAD - 1) * rows), bf16)],
        "far",
        store(SQUAD),
        flops=6 * 4 * rows * rows * width,
        exps=6 * rows * rows * heads,
    )
    far = climb(far, SQUAD)
    own[1], rims[0] = lax.optimization_barrier((own[1], rims[0]))
    (main,) = kernel_call(
        main_kernel,
        (*own, *near),
        [jax.ShapeDtypeStruct((width + TAG, SQUAD * rows), f32)],
        "main",
        store(2 * SQUAD),
        flops=26 * 4 * rows * rows * width,
        exps=26 * rows * rows * heads,
    )
    main, rims[1] = lax.optimization_barrier((main, rims[1]))
    rims.append(
        lax.ppermute(rims[1], "ctx", [(i, i + SQUAD) for i in range(0, count - SQUAD, SQUAD)])
    )
    done = kernel_call(
        merge_kernel,
        (main, far),
        [jax.ShapeDtypeStruct((rows, width), bf16)] * SQUAD,
        "merge",
        [pltpu.VMEM((SQUAD, rows, width), bf16)],
    )
    *rims, done[0] = lax.optimization_barrier((*rims, done[0]))
    hyena_out = hyena(hyena_q, hyena_k, hyena_v, rims, filters, direct)

    def turn(value, r):
        return lax.ppermute(value, "tp", [(t, (t + r) % ranks) for t in range(ranks)])

    pieces = [swap(done[k], k) for k in range(1, SQUAD)]
    hyena_out, *pieces = lax.optimization_barrier((hyena_out, done[0], *pieces))
    pieces += [turn(piece, r) for r in range(1, ranks) for piece in pieces]
    (attn_out,) = kernel_call(
        functools.partial(project_kernel, ranks),
        (*pieces, out_weight),
        [jax.ShapeDtypeStruct((rows, out_weight.shape[1]), bf16)],
        "project",
        [pltpu.VMEM((rows, ranks * feat), bf16)],
        flops=2 * rows * math.prod(out_weight.shape),
    )
    return (hyena_out, attn_out)


def solution(mesh):
    placed = (
        P("ctx", "tp"),
        P("ctx", "tp"),
        P("ctx", "tp"),
        P("tp", None),
        P("tp"),
        P("ctx", "tp"),
        P("ctx", "tp"),
        P("ctx", "tp"),
        P("ctx"),
        P(None, "tp"),
    )
    return jax.shard_map(
        local,
        mesh=mesh,
        in_specs=placed,
        out_specs=(P("ctx", "tp"), P("ctx", "tp")),
        check_vma=False,
    )
```

```python
import functools
import math

import jax
import jax.numpy as jnp
from jax import lax
from jax.experimental import pallas as pl
from jax.experimental.pallas import tpu as pltpu
from jax.sharding import PartitionSpec as P

HD = 128
SQUAD = 4
NEG = -1e30
TAG = 16
LANES = 128
VMEM_LIMIT = 32 * 1024 * 1024
VMEM = pl.BlockSpec(memory_space=pltpu.VMEM)


def corner_of():
    return lax.rem(lax.axis_index("ctx"), SQUAD)


def kernel_call(kernel, args, shapes, name, scratch=(), flops=0, exps=0):
    total = sum(math.prod(x.shape) * x.dtype.itemsize for x in (*args, *shapes))
    return list(pl.pallas_call(
        kernel,
        in_specs=[VMEM] * len(args),
        out_specs=[VMEM] * len(shapes),
        out_shape=shapes,
        scratch_shapes=scratch,
        compiler_params=pltpu.CompilerParams(vmem_limit_bytes=VMEM_LIMIT),
        cost_estimate=pl.CostEstimate(flops=flops, bytes_accessed=total, transcendentals=exps),
        name=name,
    )(*args))


def hyena_kernel(q_ref, k_ref, v_ref, near_rim, ring_rim, far_rim, taps_ref, direct_ref, out_ref, taps, rim):
    rows, chans = q_ref.shape
    groups = taps_ref.shape[0]
    group = chans // groups
    per_tile = LANES // group
    windows = rows // LANES
    shape = (LANES, LANES)
    down, along = (lax.broadcasted_iota(jnp.int32, shape, i) for i in range(2))
    turn = jnp.where((down + along) % LANES == 0, 1.0, 0.0).astype(jnp.bfloat16)
    before = jnp.where(along > down, 1.0, 0.0).astype(jnp.bfloat16)
    within = jnp.where(along > down, 0.0, 1.0).astype(jnp.bfloat16)
    taps[...] = jnp.dot(taps_ref[...], turn, preferred_element_type=jnp.float32)
    lane_group = lax.broadcasted_iota(jnp.int32, (LANES, windows * LANES), 1) % LANES // group

    half = chans // 2
    rim[:, :half] = near_rim[...]
    rim[:, half:] = ring_rim[...]

    @pl.when(corner_of() == 0)
    def _():
        rim[:, half:] = far_rim[...]

    @pl.loop(0, chans // LANES, unroll=2)
    def _(tile):
        cols = pl.ds(pl.multiple_of(tile * LANES, LANES), LANES)
        rings = taps[pl.ds(pl.multiple_of(tile * per_tile, per_tile), per_tile), :]
        mixed = (k_ref[:, cols].astype(jnp.float32) * v_ref[:, cols].astype(jnp.float32)).astype(
            jnp.bfloat16
        )
        full = jnp.concatenate([rim[:, cols], mixed], axis=0)
        stacked = jnp.concatenate(
            [full[w * LANES : (w + 2) * LANES] for w in range(windows)], axis=1
        )
        conv = jnp.zeros((LANES, windows * LANES), jnp.float32)
        for g in range(per_tile):
            ring = pltpu.roll(
                jnp.broadcast_to(rings[g : g + 1], shape), 0, 1, stride=1, stride_axis=0
            ).astype(jnp.bfloat16)
            table = jnp.concatenate([ring * before, ring * within], axis=1)
            part = jnp.dot(table, stacked, preferred_element_type=jnp.float32)
            conv = jnp.where(lane_group == g, part, conv)
        conv = jnp.concatenate(
            [conv[:, w * LANES : (w + 1) * LANES] for w in range(windows)], axis=0
        )
        out_ref[:, cols] = (
            q_ref[:, cols].astype(jnp.float32)
            * (conv + direct_ref[:, cols].astype(jnp.float32) * mixed.astype(jnp.float32))
        ).astype(jnp.bfloat16)


def hyena(hyena_q, hyena_k, hyena_v, rims, filters, direct):
    rows, chans = hyena_q.shape
    groups, kernel = filters.shape
    taps = jnp.pad(filters, ((0, 0), (0, LANES - kernel)))
    (out,) = kernel_call(
        hyena_kernel,
        (hyena_q, hyena_k, hyena_v, *rims, taps, direct[None]),
        [jax.ShapeDtypeStruct((rows, chans), jnp.bfloat16)],
        "hyena",
        [pltpu.VMEM((groups, LANES), jnp.float32), pltpu.VMEM((LANES, chans), jnp.bfloat16)],
        flops=4 * rows * chans * 2 * LANES * 8,
    )
    return out


def deal_kernel(q_ref, k_ref, v_ref, id_ref, *refs):
    outs, (held, arrive, told) = refs[:-3], refs[-3:]
    tell = pltpu.make_async_copy(id_ref, held, told)
    tell.start()
    rows, feat = q_ref.shape
    width = feat // SQUAD
    corner = corner_of()
    copies = []
    for k in (*range(1, SQUAD), 0):
        cols = pl.ds(pl.multiple_of(jnp.bitwise_xor(corner, k) * width, width), width)
        base = rows if k else 0
        places = (
            (q_ref, outs[k + 1] if k else outs[0], 0),
            (k_ref, outs[k + 1], base + TAG),
            (v_ref, outs[k + 1], base + TAG + rows),
        )
        copies += [
            pltpu.make_async_copy(
                source.at[:, cols], target.at[pl.ds(begin, rows)], arrive.at[k, i]
            )
            for i, (source, target, begin) in enumerate(places)
        ]
    for copy in copies:
        copy.start()
    tell.wait()
    ids = (held[...] + 1).astype(jnp.float32)
    spare = jnp.zeros((TAG - ids.shape[0], LANES), jnp.float32)
    ids = jnp.concatenate([ids, spare], axis=0)
    tag = jnp.concatenate([ids] * (width // LANES), axis=1).astype(jnp.bfloat16)
    for i, target in enumerate(outs):
        begin = 0 if i == 1 else rows
        target[begin : begin + TAG, :] = tag
    for copy in copies:
        copy.wait()


def deal(queries, keys, values, ids):
    rows, feat = queries.shape
    tall = [rows + TAG, 2 * rows + TAG] + [3 * rows + TAG] * (SQUAD - 1)
    shapes = [(x, feat // SQUAD) for x in tall]
    held = [pltpu.with_memory_space_constraint(x, pltpu.HBM) for x in (queries, keys, values, ids)]
    return list(
        pl.pallas_call(
            deal_kernel,
            in_specs=[pl.BlockSpec(memory_space=pl.ANY)] * 4,
            out_specs=[VMEM] * len(tall),
            out_shape=[jax.ShapeDtypeStruct(x, jnp.bfloat16) for x in shapes],
            scratch_shapes=[
                pltpu.VMEM(ids.shape, ids.dtype),
                pltpu.SemaphoreType.DMA((SQUAD, 3)),
                pltpu.SemaphoreType.DMA,
            ],
            compiler_params=pltpu.CompilerParams(vmem_limit_bytes=VMEM_LIMIT),
            cost_estimate=pl.CostEstimate(
                flops=0, bytes_accessed=12 * rows * feat, transcendentals=0
            ),
            name="deal",
        )(*held)
    )


def id_columns(tag_ref, rows):
    tag = tag_ref[:, :LANES].astype(jnp.float32)
    tiles = [jnp.broadcast_to(tag[t : t + 1], (LANES, LANES)).T for t in range(rows // LANES)]
    return jnp.concatenate(tiles, axis=0)


def place_keys(parts, corner, base, rows, keys, values):
    heads = keys.shape[0]
    marks = lax.broadcasted_iota(jnp.int32, (rows, LANES), 1).astype(jnp.float32) + 1.0
    for k, part in enumerate(parts):
        begin = pl.multiple_of((jnp.bitwise_xor(corner, k) + base) * rows, rows)
        span = pl.ds(begin, rows)
        ids = id_columns(part.at[:TAG], rows)
        mask = jnp.where(ids == marks, 0.0, -NEG).astype(jnp.bfloat16)
        for h in range(heads):
            cols = slice(h * HD, (h + 1) * HD)
            keys[h, span, :HD] = part[TAG : TAG + rows, cols]
            keys[h, span, HD:] = mask
            values[h, span, :] = part[TAG + rows : TAG + 2 * rows, cols]


def near_parts(near, rows):
    tall = 2 * rows + TAG
    return [near[0], near[1].at[:tall], near[1].at[tall:], near[2]]


def place_queries(parts, corner, rows, queries):
    heads = queries.shape[0]
    marks = lax.broadcasted_iota(jnp.int32, (rows, LANES), 1).astype(jnp.float32) + 1.0
    for k, part in enumerate(parts):
        begin = pl.multiple_of(jnp.bitwise_xor(corner, k) * rows, rows)
        span = pl.ds(begin, rows)
        ids = id_columns(part.at[rows : rows + TAG], rows)
        mask = jnp.where(ids == marks, -1.0, 0.0).astype(jnp.bfloat16)
        for h in range(heads):
            queries[h, span, :HD] = part[:rows, h * HD : (h + 1) * HD]
            queries[h, span, HD:] = mask


def score_of(query, keys):
    return lax.dot_general(
        keys, query, (((1,), (1,)), ((), ())), preferred_element_type=jnp.float32
    )


def attend(score, values, diagonal):
    factor = math.log2(math.e) / math.sqrt(HD)
    rows = score.shape[1]
    if diagonal:
        older = lax.broadcasted_iota(jnp.int32, (rows, rows), 0) <= lax.broadcasted_iota(
            jnp.int32, (rows, rows), 1
        )
        score = jnp.concatenate([score[:-rows], jnp.where(older, score[-rows:], NEG)], axis=0)
    high = jnp.max(score, axis=0, keepdims=True)
    expo = jnp.exp2((score - high) * factor)
    total = jnp.sum(expo, axis=0, keepdims=True)
    summed = lax.dot_general(
        values,
        expo.astype(jnp.bfloat16),
        (((0,), (0,)), ((), ())),
        preferred_element_type=jnp.float32,
    )
    return summed / total, high * factor + jnp.log2(total)


def ahead(steps, product):
    late = product(*steps[0])
    for step, following in zip(steps, steps[1:] + [None]):
        now, late = late, product(*following) if following else None
        yield step, now


def main_kernel(*refs):
    own, near, out, (queries, keys, values) = refs[:5], refs[5:8], refs[8], refs[9:]
    heads, span, _ = queries.shape
    rows = span // SQUAD
    width = heads * HD
    corner = corner_of()
    asked = [own[0]] + [p.at[: rows + TAG] for p in own[2:]]
    held = [own[1]] + [p.at[rows:] for p in own[2:]]
    place_queries(asked, corner, rows, queries)
    place_keys(held, corner, SQUAD, rows, keys, values)
    place_keys(near_parts(near, rows), corner, 0, rows, keys, values)
    span = [slice(j * rows, (j + 1) * rows) for j in range(SQUAD)]
    reach = [(SQUAD + 1 + j) * rows for j in range(SQUAD)]
    steps = [(j, h) for j in range(SQUAD) for h in range(heads)]
    for (j, h), score in ahead(
        steps, lambda j, h: score_of(queries[h, span[j]], keys[h, : reach[j]])
    ):
        mixed, lse = attend(score, values[h, : reach[j]], True)
        out[h * HD : (h + 1) * HD, span[j]] = mixed
        out[width + h : width + h + 1, span[j]] = lse
    out[width + heads :, :] = jnp.zeros((TAG - heads, SQUAD * rows), jnp.float32)


def far_kernel(*refs):
    asked, near, out, (queries, keys, values) = refs[:2], refs[2:5], refs[5], refs[6:]
    heads, span, _ = queries.shape
    rows = span // SQUAD
    width = heads * HD
    corner = corner_of()
    tall = rows + TAG
    asked = [asked[0].at[k * tall : (k + 1) * tall] for k in range(SQUAD - 1)] + [asked[1]]
    place_queries(asked, corner, rows, queries)
    place_keys(near_parts(near, rows), corner, 0, rows, keys, values)
    span = [slice(j * rows, (j + 1) * rows) for j in range(SQUAD)]
    stats = [[] for _ in range(SQUAD - 1)]
    steps = [(j, h) for j in range(SQUAD - 1) for h in range(heads)]
    for (j, h), score in ahead(
        steps, lambda j, h: score_of(queries[h, span[j]], keys[h, span[j].stop :])
    ):
        mixed, lse = attend(score, values[h, span[j].stop :], False)
        out[h * HD : (h + 1) * HD, span[j]] = mixed.astype(out.dtype)
        top = lse.astype(jnp.bfloat16).astype(jnp.float32)
        mid = (lse - top).astype(jnp.bfloat16).astype(jnp.float32)
        stats[j] += [top, mid, lse - top - mid]
    for j, stat in enumerate(stats):
        stat.append(jnp.zeros((TAG - len(stat), rows), jnp.float32))
        out[width:, span[j]] = jnp.concatenate(stat, axis=0).astype(out.dtype)


def merge_kernel(main_ref, far_ref, *refs):
    outs, ready = refs[:-1], refs[-1]
    _, rows, width = ready.shape
    corner = corner_of()
    served = lax.axis_index("ctx") >= 2 * SQUAD
    for j in range(SQUAD):
        cols = slice(j * rows, (j + 1) * rows)
        for h in range(width // HD):
            feats = slice(h * HD, (h + 1) * HD)
            mixed = main_ref[feats, cols]
            if j < SQUAD - 1:
                here = main_ref[width + h : width + h + 1, cols]
                stats = far_ref[width:, cols].astype(jnp.float32)
                there = stats[3 * h : 3 * h + 1] + stats[3 * h + 1 : 3 * h + 2]
                there = jnp.where(served, there + stats[3 * h + 2 : 3 * h + 3], NEG)
                high = jnp.maximum(here, there)
                here, there = jnp.exp2(here - high), jnp.exp2(there - high)
                total = here + there
                mixed = mixed * (here / total) + far_ref[feats, cols].astype(jnp.float32) * (
                    there / total
                )
            ready[j, :, feats] = mixed.T.astype(ready.dtype)
    for k, out in enumerate(outs):
        out[...] = ready[jnp.bitwise_xor(corner, k)]


def project_kernel(ranks, *refs):
    parts, weight_ref, out_ref, whole = refs[:-3], refs[-3], refs[-2], refs[-1]
    mine, corner = lax.axis_index("tp"), corner_of()
    width = parts[0].shape[1]
    for r in range(ranks):
        source = lax.rem(mine + ranks - r, ranks)
        for k in range(SQUAD):
            begin = (source * SQUAD + jnp.bitwise_xor(corner, k)) * width
            whole[:, pl.ds(pl.multiple_of(begin, width), width)] = parts[r * SQUAD + k][...]
    block = 2 * LANES
    for c in range(out_ref.shape[1] // block):
        cols = slice(c * block, (c + 1) * block)
        out_ref[:, cols] = jnp.dot(
            whole[...], weight_ref[:, cols], preferred_element_type=jnp.float32
        ).astype(out_ref.dtype)


def local(
    hyena_q, hyena_k, hyena_v, filters, direct, queries, keys, values, segment_ids, out_weight
):
    rows, feat = queries.shape
    count, ranks = lax.axis_size("ctx"), lax.axis_size("tp")
    width = feat // SQUAD
    heads = width // HD
    bf16, f32 = jnp.bfloat16, jnp.float32

    def swap(value, mask):
        return lax.ppermute(value, "ctx", [(i, i ^ mask) for i in range(count)])

    def climb(value, first=0):
        return lax.ppermute(value, "ctx", [(i, i + SQUAD) for i in range(first, count - SQUAD)])

    def descend(value):
        return lax.ppermute(
            value, "ctx", [(i, i - SQUAD) for i in range(2 * SQUAD, count)]
        )

    asked, kept, *sent = deal(
        queries, keys, values, segment_ids.reshape(rows // LANES, LANES)
    )
    tall = rows + TAG
    near = [climb(kept)]
    beside = [swap(sent[0], 1), swap(sent[1], 2)]
    sent[2], beside[0] = lax.optimization_barrier((sent[2], beside[0]))
    across = swap(sent[2], 3)
    beside[1], near[0] = lax.optimization_barrier((beside[1], near[0]))
    near.append(climb(jnp.concatenate([x[rows:] for x in beside], axis=0)))
    back = [descend(jnp.concatenate([asked] + [x[:tall] for x in beside], axis=0))]
    near.append(climb(across[rows:]))
    tail_k = hyena_k[rows - LANES :].astype(f32)
    tail_v = hyena_v[rows - LANES :].astype(f32)
    tail = (tail_k * tail_v).astype(bf16)
    half = tail.shape[1] // 2
    ring = lax.ppermute(
        tail[:, half:], "ctx", [(i, i - i % SQUAD + (i + 1) % SQUAD) for i in range(count)]
    )
    across, ring = lax.optimization_barrier((across, ring))
    back.append(descend(across[:tall]))
    rims = [
        lax.ppermute(tail[:, :half], "ctx", [(i, i + 1) for i in range(count - 1)]),
        ring,
        lax.ppermute(ring, "ctx", [(i, i + SQUAD) for i in range(0, count - SQUAD, SQUAD)]),
    ]
    own = [asked, kept, *beside, across]
    def store(blocks):
        return [
            pltpu.VMEM((heads, SQUAD * rows, 2 * HD), bf16),
            pltpu.VMEM((heads, blocks * rows, 2 * HD), bf16),
            pltpu.VMEM((heads, blocks * rows, HD), bf16),
        ]

    (far,) = kernel_call(
        far_kernel,
        (*back, *near),
        [jax.ShapeDtypeStruct((width + TAG, (SQUAD - 1) * rows), bf16)],
        "far",
        store(SQUAD),
        flops=6 * 4 * rows * rows * width,
        exps=6 * rows * rows * heads,
    )
    far = climb(far, SQUAD)
    own[1], *rims = lax.optimization_barrier((own[1], *rims))
    (main,) = kernel_call(
        main_kernel,
        (*own, *near),
        [jax.ShapeDtypeStruct((width + TAG, SQUAD * rows), f32)],
        "main",
        store(2 * SQUAD),
        flops=26 * 4 * rows * rows * width,
        exps=26 * rows * rows * heads,
    )
    done = kernel_call(
        merge_kernel,
        (main, far),
        [jax.ShapeDtypeStruct((rows, width), bf16)] * SQUAD,
        "merge",
        [pltpu.VMEM((SQUAD, rows, width), bf16)],
    )
    *rims, done[0] = lax.optimization_barrier((*rims, done[0]))
    hyena_out = hyena(hyena_q, hyena_k, hyena_v, rims, filters, direct)

    def turn(value, r):
        return lax.ppermute(value, "tp", [(t, (t + r) % ranks) for t in range(ranks)])

    pieces = [swap(done[k], k) for k in range(1, SQUAD)]
    hyena_out, *pieces = lax.optimization_barrier((hyena_out, done[0], *pieces))
    pieces += [turn(piece, r) for r in range(1, ranks) for piece in pieces]
    (attn_out,) = kernel_call(
        functools.partial(project_kernel, ranks),
        (*pieces, out_weight),
        [jax.ShapeDtypeStruct((rows, out_weight.shape[1]), bf16)],
        "project",
        [pltpu.VMEM((rows, ranks * feat), bf16)],
        flops=2 * rows * math.prod(out_weight.shape),
    )
    return (hyena_out, attn_out)


def solution(mesh):
    placed = (
        P("ctx", "tp"),
        P("ctx", "tp"),
        P("ctx", "tp"),
        P("tp", None),
        P("tp"),
        P("ctx", "tp"),
        P("ctx", "tp"),
        P("ctx", "tp"),
        P("ctx"),
        P(None, "tp"),
    )
    return jax.shard_map(
        local,
        mesh=mesh,
        in_specs=placed,
        out_specs=(P("ctx", "tp"), P("ctx", "tp")),
        check_vma=False,
    )
```

```python
import functools
import math

import jax
import jax.numpy as jnp
from jax import lax
from jax.experimental import pallas as pl
from jax.experimental.pallas import tpu as pltpu
from jax.sharding import PartitionSpec as P

HD = 128
SQUAD = 4
NEG = -1e30
TAG = 16
LANES = 128
VMEM_LIMIT = 32 * 1024 * 1024
VMEM = pl.BlockSpec(memory_space=pltpu.VMEM)


def corner_of():
    return lax.rem(lax.axis_index("ctx"), SQUAD)


def kernel_call(kernel, args, shapes, name, scratch=(), flops=0, exps=0):
    total = sum(math.prod(x.shape) * x.dtype.itemsize for x in (*args, *shapes))
    return list(pl.pallas_call(
        kernel,
        in_specs=[VMEM] * len(args),
        out_specs=[VMEM] * len(shapes),
        out_shape=shapes,
        scratch_shapes=scratch,
        compiler_params=pltpu.CompilerParams(vmem_limit_bytes=VMEM_LIMIT),
        cost_estimate=pl.CostEstimate(flops=flops, bytes_accessed=total, transcendentals=exps),
        name=name,
    )(*args))


def hyena_kernel(q_ref, k_ref, v_ref, near_rim, ring_rim, far_rim, taps_ref, direct_ref, out_ref, taps, rim):
    rows, chans = q_ref.shape
    groups = taps_ref.shape[0]
    group = chans // groups
    per_tile = LANES // group
    windows = rows // LANES
    shape = (LANES, LANES)
    down, along = (lax.broadcasted_iota(jnp.int32, shape, i) for i in range(2))
    turn = jnp.where((down + along) % LANES == 0, 1.0, 0.0).astype(jnp.bfloat16)
    before = jnp.where(along > down, 1.0, 0.0).astype(jnp.bfloat16)
    within = jnp.where(along > down, 0.0, 1.0).astype(jnp.bfloat16)
    taps[...] = jnp.dot(taps_ref[...], turn, preferred_element_type=jnp.float32)
    lane_group = lax.broadcasted_iota(jnp.int32, (LANES, windows * LANES), 1) % LANES // group

    half = chans // 2
    rim[:, :half] = near_rim[...]
    rim[:, half:] = ring_rim[...]

    @pl.when(corner_of() == 0)
    def _():
        rim[:, half:] = far_rim[...]

    @pl.loop(0, chans // LANES, unroll=2)
    def _(tile):
        cols = pl.ds(pl.multiple_of(tile * LANES, LANES), LANES)
        rings = taps[pl.ds(pl.multiple_of(tile * per_tile, per_tile), per_tile), :]
        mixed = (k_ref[:, cols].astype(jnp.float32) * v_ref[:, cols].astype(jnp.float32)).astype(
            jnp.bfloat16
        )
        full = jnp.concatenate([rim[:, cols], mixed], axis=0)
        stacked = jnp.concatenate(
            [full[w * LANES : (w + 2) * LANES] for w in range(windows)], axis=1
        )
        conv = jnp.zeros((LANES, windows * LANES), jnp.float32)
        for g in range(per_tile):
            ring = pltpu.roll(
                jnp.broadcast_to(rings[g : g + 1], shape), 0, 1, stride=1, stride_axis=0
            ).astype(jnp.bfloat16)
            table = jnp.concatenate([ring * before, ring * within], axis=1)
            part = jnp.dot(table, stacked, preferred_element_type=jnp.float32)
            conv = jnp.where(lane_group == g, part, conv)
        conv = jnp.concatenate(
            [conv[:, w * LANES : (w + 1) * LANES] for w in range(windows)], axis=0
        )
        out_ref[:, cols] = (
            q_ref[:, cols].astype(jnp.float32)
            * (conv + direct_ref[:, cols].astype(jnp.float32) * mixed.astype(jnp.float32))
        ).astype(jnp.bfloat16)


def hyena(hyena_q, hyena_k, hyena_v, rims, filters, direct):
    rows, chans = hyena_q.shape
    groups, kernel = filters.shape
    taps = jnp.pad(filters, ((0, 0), (0, LANES - kernel)))
    (out,) = kernel_call(
        hyena_kernel,
        (hyena_q, hyena_k, hyena_v, *rims, taps, direct[None]),
        [jax.ShapeDtypeStruct((rows, chans), jnp.bfloat16)],
        "hyena",
        [pltpu.VMEM((groups, LANES), jnp.float32), pltpu.VMEM((LANES, chans), jnp.bfloat16)],
        flops=4 * rows * chans * 2 * LANES * 8,
    )
    return out


def deal_kernel(q_ref, k_ref, v_ref, id_ref, *refs):
    outs, (held, arrive, told) = refs[:-3], refs[-3:]
    tell = pltpu.make_async_copy(id_ref, held, told)
    tell.start()
    rows, feat = q_ref.shape
    width = feat // SQUAD
    corner = corner_of()
    homes = {0: (outs[0], outs[1]), 1: (outs[2], outs[2]), 2: (outs[3], outs[3]), 3: outs[4:]}
    copies = []
    for k in (1, 2, 0, 3):
        cols = pl.ds(pl.multiple_of(jnp.bitwise_xor(corner, k) * width, width), width)
        asking, keeping = homes[k]
        base = TAG if asking is not keeping else rows + TAG
        places = (
            (q_ref, asking, 0),
            (k_ref, keeping, base),
            (v_ref, keeping, base + rows),
        )
        copies += [
            pltpu.make_async_copy(
                source.at[:, cols], target.at[pl.ds(begin, rows)], arrive.at[k, i]
            )
            for i, (source, target, begin) in enumerate(places)
        ]
    for copy in copies:
        copy.start()
    tell.wait()
    ids = (held[...] + 1).astype(jnp.float32)
    spare = jnp.zeros((TAG - ids.shape[0], LANES), jnp.float32)
    ids = jnp.concatenate([ids, spare], axis=0)
    tag = jnp.concatenate([ids] * (width // LANES), axis=1).astype(jnp.bfloat16)
    for i, target in enumerate(outs):
        begin = 0 if i in (1, 5) else rows
        target[begin : begin + TAG, :] = tag
    for copy in copies:
        copy.wait()


def deal(queries, keys, values, ids):
    rows, feat = queries.shape
    asking, keeping = rows + TAG, 2 * rows + TAG
    tall = [asking, keeping, asking + 2 * rows, asking + 2 * rows, asking, keeping]
    shapes = [(x, feat // SQUAD) for x in tall]
    held = [pltpu.with_memory_space_constraint(x, pltpu.HBM) for x in (queries, keys, values, ids)]
    return list(
        pl.pallas_call(
            deal_kernel,
            in_specs=[pl.BlockSpec(memory_space=pl.ANY)] * 4,
            out_specs=[VMEM] * len(tall),
            out_shape=[jax.ShapeDtypeStruct(x, jnp.bfloat16) for x in shapes],
            scratch_shapes=[
                pltpu.VMEM(ids.shape, ids.dtype),
                pltpu.SemaphoreType.DMA((SQUAD, 3)),
                pltpu.SemaphoreType.DMA,
            ],
            compiler_params=pltpu.CompilerParams(vmem_limit_bytes=VMEM_LIMIT),
            cost_estimate=pl.CostEstimate(
                flops=0, bytes_accessed=12 * rows * feat, transcendentals=0
            ),
            name="deal",
        )(*held)
    )


def id_columns(tag_ref, rows):
    tag = tag_ref[:, :LANES].astype(jnp.float32)
    tiles = [jnp.broadcast_to(tag[t : t + 1], (LANES, LANES)).T for t in range(rows // LANES)]
    return jnp.concatenate(tiles, axis=0)


def place_keys(parts, corner, base, rows, keys, values):
    heads = keys.shape[0]
    marks = lax.broadcasted_iota(jnp.int32, (rows, LANES), 1).astype(jnp.float32) + 1.0
    for k, part in enumerate(parts):
        begin = pl.multiple_of((jnp.bitwise_xor(corner, k) + base) * rows, rows)
        span = pl.ds(begin, rows)
        ids = id_columns(part.at[:TAG], rows)
        mask = jnp.where(ids == marks, 0.0, -NEG).astype(jnp.bfloat16)
        for h in range(heads):
            cols = slice(h * HD, (h + 1) * HD)
            keys[h, span, :HD] = part[TAG : TAG + rows, cols]
            keys[h, span, HD:] = mask
            values[h, span, :] = part[TAG + rows : TAG + 2 * rows, cols]


def near_parts(near, rows):
    tall = 2 * rows + TAG
    return [near[0], near[1].at[:tall], near[1].at[tall:], near[2]]


def place_queries(parts, corner, rows, queries):
    heads = queries.shape[0]
    marks = lax.broadcasted_iota(jnp.int32, (rows, LANES), 1).astype(jnp.float32) + 1.0
    for k, part in enumerate(parts):
        begin = pl.multiple_of(jnp.bitwise_xor(corner, k) * rows, rows)
        span = pl.ds(begin, rows)
        ids = id_columns(part.at[rows : rows + TAG], rows)
        mask = jnp.where(ids == marks, -1.0, 0.0).astype(jnp.bfloat16)
        for h in range(heads):
            queries[h, span, :HD] = part[:rows, h * HD : (h + 1) * HD]
            queries[h, span, HD:] = mask


def score_of(query, keys):
    return lax.dot_general(
        keys, query, (((1,), (1,)), ((), ())), preferred_element_type=jnp.float32
    )


def attend(score, values, diagonal):
    factor = math.log2(math.e) / math.sqrt(HD)
    rows = score.shape[1]
    if diagonal:
        older = lax.broadcasted_iota(jnp.int32, (rows, rows), 0) <= lax.broadcasted_iota(
            jnp.int32, (rows, rows), 1
        )
        score = jnp.concatenate([score[:-rows], jnp.where(older, score[-rows:], NEG)], axis=0)
    high = jnp.max(score, axis=0, keepdims=True)
    expo = jnp.exp2((score - high) * factor)
    total = jnp.sum(expo, axis=0, keepdims=True)
    summed = lax.dot_general(
        values,
        expo.astype(jnp.bfloat16),
        (((0,), (0,)), ((), ())),
        preferred_element_type=jnp.float32,
    )
    return summed / total, high * factor + jnp.log2(total)


def ahead(steps, product):
    late = product(*steps[0])
    for step, following in zip(steps, steps[1:] + [None]):
        now, late = late, product(*following) if following else None
        yield step, now


def main_kernel(*refs):
    own, near, out, (queries, keys, values) = refs[:6], refs[6:9], refs[9], refs[10:]
    heads, span, _ = queries.shape
    rows = span // SQUAD
    width = heads * HD
    corner = corner_of()
    asked = [own[0]] + [p.at[: rows + TAG] for p in own[2:4]] + [own[4]]
    held = [own[1]] + [p.at[rows:] for p in own[2:4]] + [own[5]]
    place_queries(asked, corner, rows, queries)
    place_keys(held, corner, SQUAD, rows, keys, values)
    place_keys(near_parts(near, rows), corner, 0, rows, keys, values)
    span = [slice(j * rows, (j + 1) * rows) for j in range(SQUAD)]
    reach = [(SQUAD + 1 + j) * rows for j in range(SQUAD)]
    steps = [(j, h) for j in range(SQUAD) for h in range(heads)]
    for (j, h), score in ahead(
        steps, lambda j, h: score_of(queries[h, span[j]], keys[h, : reach[j]])
    ):
        mixed, lse = attend(score, values[h, : reach[j]], True)
        out[h * HD : (h + 1) * HD, span[j]] = mixed
        out[width + h : width + h + 1, span[j]] = lse
    out[width + heads :, :] = jnp.zeros((TAG - heads, SQUAD * rows), jnp.float32)


def far_kernel(*refs):
    asked, near, out, (queries, keys, values) = refs[:2], refs[2:5], refs[5], refs[6:]
    heads, span, _ = queries.shape
    rows = span // SQUAD
    width = heads * HD
    corner = corner_of()
    tall = rows + TAG
    asked = [asked[0].at[k * tall : (k + 1) * tall] for k in range(SQUAD - 1)] + [asked[1]]
    place_queries(asked, corner, rows, queries)
    place_keys(near_parts(near, rows), corner, 0, rows, keys, values)
    span = [slice(j * rows, (j + 1) * rows) for j in range(SQUAD)]
    stats = [[] for _ in range(SQUAD - 1)]
    steps = [(j, h) for j in range(SQUAD - 1) for h in range(heads)]
    for (j, h), score in ahead(
        steps, lambda j, h: score_of(queries[h, span[j]], keys[h, span[j].stop :])
    ):
        mixed, lse = attend(score, values[h, span[j].stop :], False)
        out[h * HD : (h + 1) * HD, span[j]] = mixed.astype(out.dtype)
        top = lse.astype(jnp.bfloat16).astype(jnp.float32)
        mid = (lse - top).astype(jnp.bfloat16).astype(jnp.float32)
        stats[j] += [top, mid, lse - top - mid]
    for j, stat in enumerate(stats):
        stat.append(jnp.zeros((TAG - len(stat), rows), jnp.float32))
        out[width:, span[j]] = jnp.concatenate(stat, axis=0).astype(out.dtype)


def merge_kernel(main_ref, far_ref, *refs):
    outs, ready = refs[:-1], refs[-1]
    _, rows, width = ready.shape
    corner = corner_of()
    served = lax.axis_index("ctx") >= 2 * SQUAD
    for j in range(SQUAD):
        cols = slice(j * rows, (j + 1) * rows)
        for h in range(width // HD):
            feats = slice(h * HD, (h + 1) * HD)
            mixed = main_ref[feats, cols]
            if j < SQUAD - 1:
                here = main_ref[width + h : width + h + 1, cols]
                stats = far_ref[width:, cols].astype(jnp.float32)
                there = stats[3 * h : 3 * h + 1] + stats[3 * h + 1 : 3 * h + 2]
                there = jnp.where(served, there + stats[3 * h + 2 : 3 * h + 3], NEG)
                high = jnp.maximum(here, there)
                here, there = jnp.exp2(here - high), jnp.exp2(there - high)
                total = here + there
                mixed = mixed * (here / total) + far_ref[feats, cols].astype(jnp.float32) * (
                    there / total
                )
            ready[j, :, feats] = mixed.T.astype(ready.dtype)
    for k, out in enumerate(outs):
        out[...] = ready[jnp.bitwise_xor(corner, k)]


def project_kernel(ranks, *refs):
    parts, weight_ref, out_ref, whole = refs[:-3], refs[-3], refs[-2], refs[-1]
    mine, corner = lax.axis_index("tp"), corner_of()
    width = parts[0].shape[1]
    for r in range(ranks):
        source = lax.rem(mine + ranks - r, ranks)
        for k in range(SQUAD):
            begin = (source * SQUAD + jnp.bitwise_xor(corner, k)) * width
            whole[:, pl.ds(pl.multiple_of(begin, width), width)] = parts[r * SQUAD + k][...]
    block = 2 * LANES
    for c in range(out_ref.shape[1] // block):
        cols = slice(c * block, (c + 1) * block)
        out_ref[:, cols] = jnp.dot(
            whole[...], weight_ref[:, cols], preferred_element_type=jnp.float32
        ).astype(out_ref.dtype)


def local(
    hyena_q, hyena_k, hyena_v, filters, direct, queries, keys, values, segment_ids, out_weight
):
    rows, feat = queries.shape
    count, ranks = lax.axis_size("ctx"), lax.axis_size("tp")
    width = feat // SQUAD
    heads = width // HD
    bf16, f32 = jnp.bfloat16, jnp.float32

    def swap(value, mask):
        return lax.ppermute(value, "ctx", [(i, i ^ mask) for i in range(count)])

    def climb(value, first=0):
        return lax.ppermute(value, "ctx", [(i, i + SQUAD) for i in range(first, count - SQUAD)])

    def descend(value):
        return lax.ppermute(
            value, "ctx", [(i, i - SQUAD) for i in range(2 * SQUAD, count)]
        )

    asked, kept, *sent = deal(
        queries, keys, values, segment_ids.reshape(rows // LANES, LANES)
    )
    tall = rows + TAG
    near = [climb(kept)]
    beside = [swap(sent[0], 1), swap(sent[1], 2)]
    sent[3], beside[0] = lax.optimization_barrier((sent[3], beside[0]))
    across = swap(sent[3], 3)
    sent[2], beside[1] = lax.optimization_barrier((sent[2], beside[1]))
    across_asked = swap(sent[2], 3)
    beside[1], near[0] = lax.optimization_barrier((beside[1], near[0]))
    near.append(climb(jnp.concatenate([x[rows:] for x in beside], axis=0)))
    back = [descend(jnp.concatenate([asked] + [x[:tall] for x in beside], axis=0))]
    near.append(climb(across))
    tail_k = hyena_k[rows - LANES :].astype(f32)
    tail_v = hyena_v[rows - LANES :].astype(f32)
    tail = (tail_k * tail_v).astype(bf16)
    half = tail.shape[1] // 2
    ring = lax.ppermute(
        tail[:, half:], "ctx", [(i, i - i % SQUAD + (i + 1) % SQUAD) for i in range(count)]
    )
    across_asked, ring = lax.optimization_barrier((across_asked, ring))
    back.append(descend(across_asked))
    rims = [
        lax.ppermute(tail[:, :half], "ctx", [(i, i + 1) for i in range(count - 1)]),
        ring,
        lax.ppermute(ring, "ctx", [(i, i + SQUAD) for i in range(0, count - SQUAD, SQUAD)]),
    ]
    own = [asked, kept, *beside, across_asked, across]
    def store(blocks):
        return [
            pltpu.VMEM((heads, SQUAD * rows, 2 * HD), bf16),
            pltpu.VMEM((heads, blocks * rows, 2 * HD), bf16),
            pltpu.VMEM((heads, blocks * rows, HD), bf16),
        ]

    (far,) = kernel_call(
        far_kernel,
        (*back, *near),
        [jax.ShapeDtypeStruct((width + TAG, (SQUAD - 1) * rows), bf16)],
        "far",
        store(SQUAD),
        flops=6 * 4 * rows * rows * width,
        exps=6 * rows * rows * heads,
    )
    far = climb(far, SQUAD)
    own[1], *rims = lax.optimization_barrier((own[1], *rims))
    (main,) = kernel_call(
        main_kernel,
        (*own, *near),
        [jax.ShapeDtypeStruct((width + TAG, SQUAD * rows), f32)],
        "main",
        store(2 * SQUAD),
        flops=26 * 4 * rows * rows * width,
        exps=26 * rows * rows * heads,
    )
    done = kernel_call(
        merge_kernel,
        (main, far),
        [jax.ShapeDtypeStruct((rows, width), bf16)] * SQUAD,
        "merge",
        [pltpu.VMEM((SQUAD, rows, width), bf16)],
    )
    *rims, done[0] = lax.optimization_barrier((*rims, done[0]))
    hyena_out = hyena(hyena_q, hyena_k, hyena_v, rims, filters, direct)

    def turn(value, r):
        return lax.ppermute(value, "tp", [(t, (t + r) % ranks) for t in range(ranks)])

    pieces = [swap(done[k], k) for k in range(1, SQUAD)]
    hyena_out, *pieces = lax.optimization_barrier((hyena_out, done[0], *pieces))
    pieces += [turn(piece, r) for r in range(1, ranks) for piece in pieces]
    (attn_out,) = kernel_call(
        functools.partial(project_kernel, ranks),
        (*pieces, out_weight),
        [jax.ShapeDtypeStruct((rows, out_weight.shape[1]), bf16)],
        "project",
        [pltpu.VMEM((rows, ranks * feat), bf16)],
        flops=2 * rows * math.prod(out_weight.shape),
    )
    return (hyena_out, attn_out)


def solution(mesh):
    placed = (
        P("ctx", "tp"),
        P("ctx", "tp"),
        P("ctx", "tp"),
        P("tp", None),
        P("tp"),
        P("ctx", "tp"),
        P("ctx", "tp"),
        P("ctx", "tp"),
        P("ctx"),
        P(None, "tp"),
    )
    return jax.shard_map(
        local,
        mesh=mesh,
        in_specs=placed,
        out_specs=(P("ctx", "tp"), P("ctx", "tp")),
        check_vma=False,
    )
```

```python
import functools
import math

import jax
import jax.numpy as jnp
from jax import lax
from jax.experimental import pallas as pl
from jax.experimental.pallas import tpu as pltpu
from jax.sharding import PartitionSpec as P

HD = 128
SQUAD = 4
NEG = -1e30
TAG = 16
LANES = 128
VMEM_LIMIT = 32 * 1024 * 1024
VMEM = pl.BlockSpec(memory_space=pltpu.VMEM)


def corner_of():
    return lax.rem(lax.axis_index("ctx"), SQUAD)


def kernel_call(kernel, args, shapes, name, scratch=(), flops=0, exps=0, out=VMEM):
    total = sum(math.prod(x.shape) * x.dtype.itemsize for x in (*args, *shapes))
    return list(pl.pallas_call(
        kernel,
        in_specs=[VMEM] * len(args),
        out_specs=[out] * len(shapes),
        out_shape=shapes,
        scratch_shapes=scratch,
        compiler_params=pltpu.CompilerParams(vmem_limit_bytes=VMEM_LIMIT),
        cost_estimate=pl.CostEstimate(flops=flops, bytes_accessed=total, transcendentals=exps),
        name=name,
    )(*args))


def hyena_kernel(q_ref, k_ref, v_ref, near_rim, ring_rim, far_rim, taps_ref, direct_ref, out_ref, taps, rim, made, sent):
    rows, chans = q_ref.shape
    groups = taps_ref.shape[0]
    group = chans // groups
    per_tile = LANES // group
    windows = rows // LANES
    shape = (LANES, LANES)
    down, along = (lax.broadcasted_iota(jnp.int32, shape, i) for i in range(2))
    turn = jnp.where((down + along) % LANES == 0, 1.0, 0.0).astype(jnp.bfloat16)
    before = jnp.where(along > down, 1.0, 0.0).astype(jnp.bfloat16)
    within = jnp.where(along > down, 0.0, 1.0).astype(jnp.bfloat16)
    taps[...] = jnp.dot(taps_ref[...], turn, preferred_element_type=jnp.float32)
    lane_group = lax.broadcasted_iota(jnp.int32, (LANES, windows * LANES), 1) % LANES // group

    half = chans // 2
    rim[:, :half] = near_rim[...]
    rim[:, half:] = ring_rim[...]

    @pl.when(corner_of() == 0)
    def _():
        rim[:, half:] = far_rim[...]

    def leave(tile):
        begin = tile * LANES if isinstance(tile, int) else pl.multiple_of(tile * LANES, LANES)
        cols = pl.ds(begin, LANES)
        return pltpu.make_async_copy(made.at[:, cols], out_ref.at[:, cols], sent.at[tile])

    @pl.loop(0, chans // LANES, unroll=2)
    def _(tile):
        cols = pl.ds(pl.multiple_of(tile * LANES, LANES), LANES)
        rings = taps[pl.ds(pl.multiple_of(tile * per_tile, per_tile), per_tile), :]
        mixed = (k_ref[:, cols].astype(jnp.float32) * v_ref[:, cols].astype(jnp.float32)).astype(
            jnp.bfloat16
        )
        full = jnp.concatenate([rim[:, cols], mixed], axis=0)
        stacked = jnp.concatenate(
            [full[w * LANES : (w + 2) * LANES] for w in range(windows)], axis=1
        )
        conv = jnp.zeros((LANES, windows * LANES), jnp.float32)
        for g in range(per_tile):
            ring = pltpu.roll(
                jnp.broadcast_to(rings[g : g + 1], shape), 0, 1, stride=1, stride_axis=0
            ).astype(jnp.bfloat16)
            table = jnp.concatenate([ring * before, ring * within], axis=1)
            part = jnp.dot(table, stacked, preferred_element_type=jnp.float32)
            conv = jnp.where(lane_group == g, part, conv)
        conv = jnp.concatenate(
            [conv[:, w * LANES : (w + 1) * LANES] for w in range(windows)], axis=0
        )
        made[:, cols] = (
            q_ref[:, cols].astype(jnp.float32)
            * (conv + direct_ref[:, cols].astype(jnp.float32) * mixed.astype(jnp.float32))
        ).astype(jnp.bfloat16)
        leave(tile).start()

    for tile in range(chans // LANES):
        leave(tile).wait()


def hyena(hyena_q, hyena_k, hyena_v, rims, filters, direct):
    rows, chans = hyena_q.shape
    groups, kernel = filters.shape
    taps = jnp.pad(filters, ((0, 0), (0, LANES - kernel)))
    (out,) = kernel_call(
        hyena_kernel,
        (hyena_q, hyena_k, hyena_v, *rims, taps, direct[None]),
        [jax.ShapeDtypeStruct((rows, chans), jnp.bfloat16)],
        "hyena",
        [
            pltpu.VMEM((groups, LANES), jnp.float32),
            pltpu.VMEM((LANES, chans), jnp.bfloat16),
            pltpu.VMEM((rows, chans), jnp.bfloat16),
            pltpu.SemaphoreType.DMA((chans // LANES,)),
        ],
        flops=4 * rows * chans * 2 * LANES * 8,
        out=pl.BlockSpec(memory_space=pl.ANY),
    )
    return out


def deal_kernel(q_ref, k_ref, v_ref, id_ref, *refs):
    outs, (held, arrive, told) = refs[:-3], refs[-3:]
    tell = pltpu.make_async_copy(id_ref, held, told)
    tell.start()
    rows, feat = q_ref.shape
    width = feat // SQUAD
    corner = corner_of()
    copies = []
    for k in (*range(1, SQUAD), 0):
        cols = pl.ds(pl.multiple_of(jnp.bitwise_xor(corner, k) * width, width), width)
        base = rows if k else 0
        places = (
            (q_ref, outs[k + 1] if k else outs[0], 0),
            (k_ref, outs[k + 1], base + TAG),
            (v_ref, outs[k + 1], base + TAG + rows),
        )
        copies += [
            pltpu.make_async_copy(
                source.at[:, cols], target.at[pl.ds(begin, rows)], arrive.at[k, i]
            )
            for i, (source, target, begin) in enumerate(places)
        ]
    for copy in copies:
        copy.start()
    tell.wait()
    ids = (held[...] + 1).astype(jnp.float32)
    spare = jnp.zeros((TAG - ids.shape[0], LANES), jnp.float32)
    ids = jnp.concatenate([ids, spare], axis=0)
    tag = jnp.concatenate([ids] * (width // LANES), axis=1).astype(jnp.bfloat16)
    for i, target in enumerate(outs):
        begin = 0 if i == 1 else rows
        target[begin : begin + TAG, :] = tag
    for copy in copies:
        copy.wait()


def deal(queries, keys, values, ids):
    rows, feat = queries.shape
    tall = [rows + TAG, 2 * rows + TAG] + [3 * rows + TAG] * (SQUAD - 1)
    shapes = [(x, feat // SQUAD) for x in tall]
    held = [pltpu.with_memory_space_constraint(x, pltpu.HBM) for x in (queries, keys, values, ids)]
    return list(
        pl.pallas_call(
            deal_kernel,
            in_specs=[pl.BlockSpec(memory_space=pl.ANY)] * 4,
            out_specs=[VMEM] * len(tall),
            out_shape=[jax.ShapeDtypeStruct(x, jnp.bfloat16) for x in shapes],
            scratch_shapes=[
                pltpu.VMEM(ids.shape, ids.dtype),
                pltpu.SemaphoreType.DMA((SQUAD, 3)),
                pltpu.SemaphoreType.DMA,
            ],
            compiler_params=pltpu.CompilerParams(vmem_limit_bytes=VMEM_LIMIT),
            cost_estimate=pl.CostEstimate(
                flops=0, bytes_accessed=12 * rows * feat, transcendentals=0
            ),
            name="deal",
        )(*held)
    )


def id_columns(tag_ref, rows):
    tag = tag_ref[:, :LANES].astype(jnp.float32)
    tiles = [jnp.broadcast_to(tag[t : t + 1], (LANES, LANES)).T for t in range(rows // LANES)]
    return jnp.concatenate(tiles, axis=0)


def place_keys(parts, corner, base, rows, keys, values):
    heads = keys.shape[0]
    marks = lax.broadcasted_iota(jnp.int32, (rows, LANES), 1).astype(jnp.float32) + 1.0
    for k, part in enumerate(parts):
        begin = pl.multiple_of((jnp.bitwise_xor(corner, k) + base) * rows, rows)
        span = pl.ds(begin, rows)
        ids = id_columns(part.at[:TAG], rows)
        mask = jnp.where(ids == marks, 0.0, -NEG).astype(jnp.bfloat16)
        for h in range(heads):
            cols = slice(h * HD, (h + 1) * HD)
            keys[h, span, :HD] = part[TAG : TAG + rows, cols]
            keys[h, span, HD:] = mask
            values[h, span, :] = part[TAG + rows : TAG + 2 * rows, cols]


def near_parts(near, rows):
    tall = 2 * rows + TAG
    return [near[0], near[1].at[:tall], near[1].at[tall:], near[2]]


def place_queries(parts, corner, rows, queries):
    heads = queries.shape[0]
    marks = lax.broadcasted_iota(jnp.int32, (rows, LANES), 1).astype(jnp.float32) + 1.0
    for k, part in enumerate(parts):
        begin = pl.multiple_of(jnp.bitwise_xor(corner, k) * rows, rows)
        span = pl.ds(begin, rows)
        ids = id_columns(part.at[rows : rows + TAG], rows)
        mask = jnp.where(ids == marks, -1.0, 0.0).astype(jnp.bfloat16)
        for h in range(heads):
            queries[h, span, :HD] = part[:rows, h * HD : (h + 1) * HD]
            queries[h, span, HD:] = mask


def score_of(query, keys):
    return lax.dot_general(
        keys, query, (((1,), (1,)), ((), ())), preferred_element_type=jnp.float32
    )


def attend(score, values, diagonal):
    factor = math.log2(math.e) / math.sqrt(HD)
    rows = score.shape[1]
    if diagonal:
        older = lax.broadcasted_iota(jnp.int32, (rows, rows), 0) <= lax.broadcasted_iota(
            jnp.int32, (rows, rows), 1
        )
        score = jnp.concatenate([score[:-rows], jnp.where(older, score[-rows:], NEG)], axis=0)
    high = jnp.max(score, axis=0, keepdims=True)
    expo = jnp.exp2((score - high) * factor)
    total = jnp.sum(expo, axis=0, keepdims=True)
    summed = lax.dot_general(
        values,
        expo.astype(jnp.bfloat16),
        (((0,), (0,)), ((), ())),
        preferred_element_type=jnp.float32,
    )
    return summed / total, high * factor + jnp.log2(total)


def ahead(steps, product):
    late = product(*steps[0])
    for step, following in zip(steps, steps[1:] + [None]):
        now, late = late, product(*following) if following else None
        yield step, now


def main_kernel(*refs):
    own, near, out, (queries, keys, values) = refs[:5], refs[5:8], refs[8], refs[9:]
    heads, span, _ = queries.shape
    rows = span // SQUAD
    width = heads * HD
    corner = corner_of()
    asked = [own[0]] + [p.at[: rows + TAG] for p in own[2:]]
    held = [own[1]] + [p.at[rows:] for p in own[2:]]
    place_queries(asked, corner, rows, queries)
    place_keys(held, corner, SQUAD, rows, keys, values)
    place_keys(near_parts(near, rows), corner, 0, rows, keys, values)
    span = [slice(j * rows, (j + 1) * rows) for j in range(SQUAD)]
    reach = [(SQUAD + 1 + j) * rows for j in range(SQUAD)]
    steps = [(j, h) for j in range(SQUAD) for h in range(heads)]
    for (j, h), score in ahead(
        steps, lambda j, h: score_of(queries[h, span[j]], keys[h, : reach[j]])
    ):
        mixed, lse = attend(score, values[h, : reach[j]], True)
        out[h * HD : (h + 1) * HD, span[j]] = mixed
        out[width + h : width + h + 1, span[j]] = lse
    out[width + heads :, :] = jnp.zeros((TAG - heads, SQUAD * rows), jnp.float32)


def far_kernel(*refs):
    asked, near, out, (queries, keys, values) = refs[:2], refs[2:5], refs[5], refs[6:]
    heads, span, _ = queries.shape
    rows = span // SQUAD
    width = heads * HD
    corner = corner_of()
    tall = rows + TAG
    asked = [asked[0].at[k * tall : (k + 1) * tall] for k in range(SQUAD - 1)] + [asked[1]]
    place_queries(asked, corner, rows, queries)
    place_keys(near_parts(near, rows), corner, 0, rows, keys, values)
    span = [slice(j * rows, (j + 1) * rows) for j in range(SQUAD)]
    stats = [[] for _ in range(SQUAD - 1)]
    steps = [(j, h) for j in range(SQUAD - 1) for h in range(heads)]
    for (j, h), score in ahead(
        steps, lambda j, h: score_of(queries[h, span[j]], keys[h, span[j].stop :])
    ):
        mixed, lse = attend(score, values[h, span[j].stop :], False)
        out[h * HD : (h + 1) * HD, span[j]] = mixed.astype(out.dtype)
        top = lse.astype(jnp.bfloat16).astype(jnp.float32)
        mid = (lse - top).astype(jnp.bfloat16).astype(jnp.float32)
        stats[j] += [top, mid, lse - top - mid]
    for j, stat in enumerate(stats):
        stat.append(jnp.zeros((TAG - len(stat), rows), jnp.float32))
        out[width:, span[j]] = jnp.concatenate(stat, axis=0).astype(out.dtype)


def merge_kernel(main_ref, far_ref, *refs):
    outs, ready = refs[:-1], refs[-1]
    _, rows, width = ready.shape
    corner = corner_of()
    served = lax.axis_index("ctx") >= 2 * SQUAD
    for j in range(SQUAD):
        cols = slice(j * rows, (j + 1) * rows)
        for h in range(width // HD):
            feats = slice(h * HD, (h + 1) * HD)
            mixed = main_ref[feats, cols]
            if j < SQUAD - 1:
                here = main_ref[width + h : width + h + 1, cols]
                stats = far_ref[width:, cols].astype(jnp.float32)
                there = stats[3 * h : 3 * h + 1] + stats[3 * h + 1 : 3 * h + 2]
                there = jnp.where(served, there + stats[3 * h + 2 : 3 * h + 3], NEG)
                high = jnp.maximum(here, there)
                here, there = jnp.exp2(here - high), jnp.exp2(there - high)
                total = here + there
                mixed = mixed * (here / total) + far_ref[feats, cols].astype(jnp.float32) * (
                    there / total
                )
            ready[j, :, feats] = mixed.T.astype(ready.dtype)
    for k, out in enumerate(outs):
        out[...] = ready[jnp.bitwise_xor(corner, k)]


def project_kernel(ranks, *refs):
    parts, (weight_ref, out_ref, whole, made, sent) = refs[:-5], refs[-5:]
    mine, corner = lax.axis_index("tp"), corner_of()
    width = parts[0].shape[1]
    for r in range(ranks):
        source = lax.rem(mine + ranks - r, ranks)
        for k in range(SQUAD):
            begin = (source * SQUAD + jnp.bitwise_xor(corner, k)) * width
            whole[:, pl.ds(pl.multiple_of(begin, width), width)] = parts[r * SQUAD + k][...]
    block = 2 * LANES
    copies = []
    for c in range(out_ref.shape[1] // block):
        cols = slice(c * block, (c + 1) * block)
        made[:, cols] = jnp.dot(
            whole[...], weight_ref[:, cols], preferred_element_type=jnp.float32
        ).astype(made.dtype)
        span = pl.ds(c * block, block)
        copies.append(
            pltpu.make_async_copy(made.at[:, span], out_ref.at[:, span], sent.at[c])
        )
        copies[-1].start()
    for copy in copies:
        copy.wait()


def local(
    hyena_q, hyena_k, hyena_v, filters, direct, queries, keys, values, segment_ids, out_weight
):
    rows, feat = queries.shape
    count, ranks = lax.axis_size("ctx"), lax.axis_size("tp")
    width = feat // SQUAD
    heads = width // HD
    bf16, f32 = jnp.bfloat16, jnp.float32

    def swap(value, mask):
        return lax.ppermute(value, "ctx", [(i, i ^ mask) for i in range(count)])

    def climb(value, first=0):
        return lax.ppermute(value, "ctx", [(i, i + SQUAD) for i in range(first, count - SQUAD)])

    def descend(value):
        return lax.ppermute(
            value, "ctx", [(i, i - SQUAD) for i in range(2 * SQUAD, count)]
        )

    asked, kept, *sent = deal(
        queries, keys, values, segment_ids.reshape(rows // LANES, LANES)
    )
    tall = rows + TAG
    near = [climb(kept)]
    beside = [swap(sent[0], 1), swap(sent[1], 2)]
    sent[2], beside[0] = lax.optimization_barrier((sent[2], beside[0]))
    across = swap(sent[2], 3)
    beside[1], near[0] = lax.optimization_barrier((beside[1], near[0]))
    near.append(climb(jnp.concatenate([x[rows:] for x in beside], axis=0)))
    back = [descend(jnp.concatenate([asked] + [x[:tall] for x in beside], axis=0))]
    near.append(climb(across[rows:]))
    tail_k = hyena_k[rows - LANES :].astype(f32)
    tail_v = hyena_v[rows - LANES :].astype(f32)
    tail = (tail_k * tail_v).astype(bf16)
    half = tail.shape[1] // 2
    ring = lax.ppermute(
        tail[:, half:], "ctx", [(i, i - i % SQUAD + (i + 1) % SQUAD) for i in range(count)]
    )
    across, ring = lax.optimization_barrier((across, ring))
    back.append(descend(across[:tall]))
    rims = [
        lax.ppermute(tail[:, :half], "ctx", [(i, i + 1) for i in range(count - 1)]),
        ring,
        lax.ppermute(ring, "ctx", [(i, i + SQUAD) for i in range(0, count - SQUAD, SQUAD)]),
    ]
    own = [asked, kept, *beside, across]
    def store(blocks):
        return [
            pltpu.VMEM((heads, SQUAD * rows, 2 * HD), bf16),
            pltpu.VMEM((heads, blocks * rows, 2 * HD), bf16),
            pltpu.VMEM((heads, blocks * rows, HD), bf16),
        ]

    (far,) = kernel_call(
        far_kernel,
        (*back, *near),
        [jax.ShapeDtypeStruct((width + TAG, (SQUAD - 1) * rows), bf16)],
        "far",
        store(SQUAD),
        flops=6 * 4 * rows * rows * width,
        exps=6 * rows * rows * heads,
    )
    far = climb(far, SQUAD)
    own[1], *rims = lax.optimization_barrier((own[1], *rims))
    (main,) = kernel_call(
        main_kernel,
        (*own, *near),
        [jax.ShapeDtypeStruct((width + TAG, SQUAD * rows), f32)],
        "main",
        store(2 * SQUAD),
        flops=26 * 4 * rows * rows * width,
        exps=26 * rows * rows * heads,
    )
    done = kernel_call(
        merge_kernel,
        (main, far),
        [jax.ShapeDtypeStruct((rows, width), bf16)] * SQUAD,
        "merge",
        [pltpu.VMEM((SQUAD, rows, width), bf16)],
    )
    *rims, done[0] = lax.optimization_barrier((*rims, done[0]))
    hyena_out = hyena(hyena_q, hyena_k, hyena_v, rims, filters, direct)

    def turn(value, r):
        return lax.ppermute(value, "tp", [(t, (t + r) % ranks) for t in range(ranks)])

    pieces = [swap(done[k], k) for k in range(1, SQUAD)]
    hyena_out, *pieces = lax.optimization_barrier((hyena_out, done[0], *pieces))
    pieces += [turn(piece, r) for r in range(1, ranks) for piece in pieces]
    (attn_out,) = kernel_call(
        functools.partial(project_kernel, ranks),
        (*pieces, out_weight),
        [jax.ShapeDtypeStruct((rows, out_weight.shape[1]), bf16)],
        "project",
        [
            pltpu.VMEM((rows, ranks * feat), bf16),
            pltpu.VMEM((rows, out_weight.shape[1]), bf16),
            pltpu.SemaphoreType.DMA((out_weight.shape[1] // (2 * LANES),)),
        ],
        flops=2 * rows * math.prod(out_weight.shape),
        out=pl.BlockSpec(memory_space=pl.ANY),
    )
    return (hyena_out, attn_out)


def solution(mesh):
    placed = (
        P("ctx", "tp"),
        P("ctx", "tp"),
        P("ctx", "tp"),
        P("tp", None),
        P("tp"),
        P("ctx", "tp"),
        P("ctx", "tp"),
        P("ctx", "tp"),
        P("ctx"),
        P(None, "tp"),
    )
    return jax.shard_map(
        local,
        mesh=mesh,
        in_specs=placed,
        out_specs=(P("ctx", "tp"), P("ctx", "tp")),
        check_vma=False,
    )
```

```python
import functools
import math

import jax
import jax.numpy as jnp
from jax import lax
from jax.experimental import pallas as pl
from jax.experimental.pallas import tpu as pltpu
from jax.sharding import PartitionSpec as P

HD = 128
SQUAD = 4
NEG = -1e30
TAG = 16
LANES = 128
VMEM_LIMIT = 32 * 1024 * 1024
VMEM = pl.BlockSpec(memory_space=pltpu.VMEM)


def corner_of():
    return lax.rem(lax.axis_index("ctx"), SQUAD)


def kernel_call(kernel, args, shapes, name, scratch=(), flops=0, exps=0, out=VMEM):
    total = sum(math.prod(x.shape) * x.dtype.itemsize for x in (*args, *shapes))
    return list(pl.pallas_call(
        kernel,
        in_specs=[VMEM] * len(args),
        out_specs=[out] * len(shapes),
        out_shape=shapes,
        scratch_shapes=scratch,
        compiler_params=pltpu.CompilerParams(vmem_limit_bytes=VMEM_LIMIT),
        cost_estimate=pl.CostEstimate(flops=flops, bytes_accessed=total, transcendentals=exps),
        name=name,
    )(*args))


def hyena_kernel(q_ref, k_ref, v_ref, near_rim, ring_rim, far_rim, taps_ref, direct_ref, out_ref, taps, rim, made, sent):
    rows, chans = q_ref.shape
    groups = taps_ref.shape[0]
    group = chans // groups
    per_tile = LANES // group
    windows = rows // LANES
    shape = (LANES, LANES)
    down, along = (lax.broadcasted_iota(jnp.int32, shape, i) for i in range(2))
    turn = jnp.where((down + along) % LANES == 0, 1.0, 0.0).astype(jnp.bfloat16)
    before = jnp.where(along > down, 1.0, 0.0).astype(jnp.bfloat16)
    within = jnp.where(along > down, 0.0, 1.0).astype(jnp.bfloat16)
    taps[...] = jnp.dot(taps_ref[...], turn, preferred_element_type=jnp.float32)
    lane_group = lax.broadcasted_iota(jnp.int32, (LANES, windows * LANES), 1) % LANES // group

    half = chans // 2
    rim[:, :half] = near_rim[...]
    rim[:, half:] = ring_rim[...]

    @pl.when(corner_of() == 0)
    def _():
        rim[:, half:] = far_rim[...]

    def leave(tile):
        begin = tile * LANES if isinstance(tile, int) else pl.multiple_of(tile * LANES, LANES)
        cols = pl.ds(begin, LANES)
        return pltpu.make_async_copy(made.at[:, cols], out_ref.at[:, cols], sent.at[tile])

    @pl.loop(0, chans // LANES, unroll=2)
    def _(tile):
        cols = pl.ds(pl.multiple_of(tile * LANES, LANES), LANES)
        rings = taps[pl.ds(pl.multiple_of(tile * per_tile, per_tile), per_tile), :]
        mixed = (k_ref[:, cols].astype(jnp.float32) * v_ref[:, cols].astype(jnp.float32)).astype(
            jnp.bfloat16
        )
        full = jnp.concatenate([rim[:, cols], mixed], axis=0)
        stacked = jnp.concatenate(
            [full[w * LANES : (w + 2) * LANES] for w in range(windows)], axis=1
        )
        conv = jnp.zeros((LANES, windows * LANES), jnp.float32)
        for g in range(per_tile):
            ring = pltpu.roll(
                jnp.broadcast_to(rings[g : g + 1], shape), 0, 1, stride=1, stride_axis=0
            ).astype(jnp.bfloat16)
            table = jnp.concatenate([ring * before, ring * within], axis=1)
            part = jnp.dot(table, stacked, preferred_element_type=jnp.float32)
            conv = jnp.where(lane_group == g, part, conv)
        conv = jnp.concatenate(
            [conv[:, w * LANES : (w + 1) * LANES] for w in range(windows)], axis=0
        )
        made[:, cols] = (
            q_ref[:, cols].astype(jnp.float32)
            * (conv + direct_ref[:, cols].astype(jnp.float32) * mixed.astype(jnp.float32))
        ).astype(jnp.bfloat16)
        leave(tile).start()

    for tile in range(chans // LANES):
        leave(tile).wait()


def hyena(hyena_q, hyena_k, hyena_v, rims, filters, direct):
    rows, chans = hyena_q.shape
    groups, kernel = filters.shape
    taps = jnp.pad(filters, ((0, 0), (0, LANES - kernel)))
    (out,) = kernel_call(
        hyena_kernel,
        (hyena_q, hyena_k, hyena_v, *rims, taps, direct[None]),
        [jax.ShapeDtypeStruct((rows, chans), jnp.bfloat16)],
        "hyena",
        [
            pltpu.VMEM((groups, LANES), jnp.float32),
            pltpu.VMEM((LANES, chans), jnp.bfloat16),
            pltpu.VMEM((rows, chans), jnp.bfloat16),
            pltpu.SemaphoreType.DMA((chans // LANES,)),
        ],
        flops=4 * rows * chans * 2 * LANES * 8,
        out=pl.BlockSpec(memory_space=pl.ANY),
    )
    return out


def deal_kernel(q_ref, k_ref, v_ref, id_ref, *refs):
    outs, (held, arrive, told) = refs[:-3], refs[-3:]
    tell = pltpu.make_async_copy(id_ref, held, told)
    tell.start()
    rows, feat = q_ref.shape
    width = feat // SQUAD
    corner = corner_of()
    copies = []
    for k in (*range(1, SQUAD), 0):
        cols = pl.ds(pl.multiple_of(jnp.bitwise_xor(corner, k) * width, width), width)
        base = rows if k else 0
        places = (
            (q_ref, outs[k + 1] if k else outs[0], 0),
            (k_ref, outs[k + 1], base + TAG),
            (v_ref, outs[k + 1], base + TAG + rows),
        )
        copies += [
            pltpu.make_async_copy(
                source.at[:, cols], target.at[pl.ds(begin, rows)], arrive.at[k, i]
            )
            for i, (source, target, begin) in enumerate(places)
        ]
    for copy in copies:
        copy.start()
    tell.wait()
    ids = (held[...] + 1).astype(jnp.float32)
    spare = jnp.zeros((TAG - ids.shape[0], LANES), jnp.float32)
    ids = jnp.concatenate([ids, spare], axis=0)
    tag = jnp.concatenate([ids] * (width // LANES), axis=1).astype(jnp.bfloat16)
    for i, target in enumerate(outs):
        begin = 0 if i == 1 else rows
        target[begin : begin + TAG, :] = tag
    for copy in copies:
        copy.wait()


def deal(queries, keys, values, ids):
    rows, feat = queries.shape
    tall = [rows + TAG, 2 * rows + TAG] + [3 * rows + TAG] * (SQUAD - 1)
    shapes = [(x, feat // SQUAD) for x in tall]
    held = [pltpu.with_memory_space_constraint(x, pltpu.HBM) for x in (queries, keys, values, ids)]
    return list(
        pl.pallas_call(
            deal_kernel,
            in_specs=[pl.BlockSpec(memory_space=pl.ANY)] * 4,
            out_specs=[VMEM] * len(tall),
            out_shape=[jax.ShapeDtypeStruct(x, jnp.bfloat16) for x in shapes],
            scratch_shapes=[
                pltpu.VMEM(ids.shape, ids.dtype),
                pltpu.SemaphoreType.DMA((SQUAD, 3)),
                pltpu.SemaphoreType.DMA,
            ],
            compiler_params=pltpu.CompilerParams(vmem_limit_bytes=VMEM_LIMIT),
            cost_estimate=pl.CostEstimate(
                flops=0, bytes_accessed=12 * rows * feat, transcendentals=0
            ),
            name="deal",
        )(*held)
    )


def id_columns(tag_ref, rows):
    tag = tag_ref[:, :LANES].astype(jnp.float32)
    tiles = [jnp.broadcast_to(tag[t : t + 1], (LANES, LANES)).T for t in range(rows // LANES)]
    return jnp.concatenate(tiles, axis=0)


def place_keys(parts, corner, base, rows, keys, values):
    heads = keys.shape[0]
    marks = lax.broadcasted_iota(jnp.int32, (rows, LANES), 1).astype(jnp.float32) + 1.0
    for k, part in enumerate(parts):
        begin = pl.multiple_of((jnp.bitwise_xor(corner, k) + base) * rows, rows)
        span = pl.ds(begin, rows)
        ids = id_columns(part.at[:TAG], rows)
        mask = jnp.where(ids == marks, 0.0, -NEG).astype(jnp.bfloat16)
        for h in range(heads):
            cols = slice(h * HD, (h + 1) * HD)
            keys[h, span, :HD] = part[TAG : TAG + rows, cols]
            keys[h, span, HD:] = mask
            values[h, span, :] = part[TAG + rows : TAG + 2 * rows, cols]


def near_parts(near, rows):
    tall = 2 * rows + TAG
    return [near[0], near[1].at[:tall], near[1].at[tall:], near[2]]


def place_queries(parts, corner, rows, queries):
    heads = queries.shape[0]
    marks = lax.broadcasted_iota(jnp.int32, (rows, LANES), 1).astype(jnp.float32) + 1.0
    for k, part in enumerate(parts):
        begin = pl.multiple_of(jnp.bitwise_xor(corner, k) * rows, rows)
        span = pl.ds(begin, rows)
        ids = id_columns(part.at[rows : rows + TAG], rows)
        mask = jnp.where(ids == marks, -1.0, 0.0).astype(jnp.bfloat16)
        for h in range(heads):
            queries[h, span, :HD] = part[:rows, h * HD : (h + 1) * HD]
            queries[h, span, HD:] = mask


def score_of(query, keys):
    return lax.dot_general(
        keys, query, (((1,), (1,)), ((), ())), preferred_element_type=jnp.float32
    )


def attend(score, values, diagonal):
    factor = math.log2(math.e) / math.sqrt(HD)
    rows = score.shape[1]
    if diagonal:
        older = lax.broadcasted_iota(jnp.int32, (rows, rows), 0) <= lax.broadcasted_iota(
            jnp.int32, (rows, rows), 1
        )
        score = jnp.concatenate([score[:-rows], jnp.where(older, score[-rows:], NEG)], axis=0)
    high = jnp.max(score, axis=0, keepdims=True)
    expo = jnp.exp2((score - high) * factor)
    total = jnp.sum(expo, axis=0, keepdims=True)
    summed = lax.dot_general(
        values,
        expo.astype(jnp.bfloat16),
        (((0,), (0,)), ((), ())),
        preferred_element_type=jnp.float32,
    )
    return summed / total, high * factor + jnp.log2(total)


def ahead(steps, product):
    late = product(*steps[0])
    for step, following in zip(steps, steps[1:] + [None]):
        now, late = late, product(*following) if following else None
        yield step, now


def main_kernel(*refs):
    own, near, out, (queries, keys, values) = refs[:5], refs[5:8], refs[8], refs[9:]
    heads, span, _ = queries.shape
    rows = span // SQUAD
    width = heads * HD
    corner = corner_of()
    asked = [own[0]] + [p.at[: rows + TAG] for p in own[2:]]
    held = [own[1]] + [p.at[rows:] for p in own[2:]]
    place_queries(asked, corner, rows, queries)
    place_keys(held, corner, SQUAD, rows, keys, values)
    place_keys(near_parts(near, rows), corner, 0, rows, keys, values)
    span = [slice(j * rows, (j + 1) * rows) for j in range(SQUAD)]
    reach = [(SQUAD + 1 + j) * rows for j in range(SQUAD)]
    steps = [(j, h) for j in range(SQUAD) for h in range(heads)]
    for (j, h), score in ahead(
        steps, lambda j, h: score_of(queries[h, span[j]], keys[h, : reach[j]])
    ):
        mixed, lse = attend(score, values[h, : reach[j]], True)
        out[h * HD : (h + 1) * HD, span[j]] = mixed
        out[width + h : width + h + 1, span[j]] = lse
    out[width + heads :, :] = jnp.zeros((TAG - heads, SQUAD * rows), jnp.float32)


def far_kernel(*refs):
    asked, near, out, (queries, keys, values) = refs[:2], refs[2:5], refs[5], refs[6:]
    heads, span, _ = queries.shape
    rows = span // SQUAD
    width = heads * HD
    corner = corner_of()
    tall = rows + TAG
    asked = [asked[0].at[k * tall : (k + 1) * tall] for k in range(SQUAD - 1)] + [asked[1]]
    place_queries(asked, corner, rows, queries)
    place_keys(near_parts(near, rows), corner, 0, rows, keys, values)
    span = [slice(j * rows, (j + 1) * rows) for j in range(SQUAD)]
    stats = [[] for _ in range(SQUAD - 1)]
    steps = [(j, h) for j in range(SQUAD - 1) for h in range(heads)]
    for (j, h), score in ahead(
        steps, lambda j, h: score_of(queries[h, span[j]], keys[h, span[j].stop :])
    ):
        mixed, lse = attend(score, values[h, span[j].stop :], False)
        out[h * HD : (h + 1) * HD, span[j]] = mixed.astype(out.dtype)
        top = lse.astype(jnp.bfloat16).astype(jnp.float32)
        mid = (lse - top).astype(jnp.bfloat16).astype(jnp.float32)
        stats[j] += [top, mid, lse - top - mid]
    for j, stat in enumerate(stats):
        stat.append(jnp.zeros((TAG - len(stat), rows), jnp.float32))
        out[width:, span[j]] = jnp.concatenate(stat, axis=0).astype(out.dtype)


def merge_kernel(main_ref, far_ref, *refs):
    outs, ready = refs[:-1], refs[-1]
    _, rows, width = ready.shape
    corner = corner_of()
    served = lax.axis_index("ctx") >= 2 * SQUAD
    for j in range(SQUAD):
        cols = slice(j * rows, (j + 1) * rows)
        for h in range(width // HD):
            feats = slice(h * HD, (h + 1) * HD)
            mixed = main_ref[feats, cols]
            if j < SQUAD - 1:
                here = main_ref[width + h : width + h + 1, cols]
                stats = far_ref[width:, cols].astype(jnp.float32)
                there = stats[3 * h : 3 * h + 1] + stats[3 * h + 1 : 3 * h + 2]
                there = jnp.where(served, there + stats[3 * h + 2 : 3 * h + 3], NEG)
                high = jnp.maximum(here, there)
                here, there = jnp.exp2(here - high), jnp.exp2(there - high)
                total = here + there
                mixed = mixed * (here / total) + far_ref[feats, cols].astype(jnp.float32) * (
                    there / total
                )
            ready[j, :, feats] = mixed.T.astype(ready.dtype)
    for k, out in enumerate(outs):
        out[...] = ready[jnp.bitwise_xor(corner, k)]


def join_kernel(*refs):
    parts, out = refs[:-1], refs[-1]
    width = parts[0].shape[1]
    for i, part in enumerate(parts):
        out[:, i * width : (i + 1) * width] = part[...]


def project_kernel(ranks, *refs):
    parts, (weight_ref, out_ref, whole, made, sent) = refs[:-5], refs[-5:]
    mine, corner = lax.axis_index("tp"), corner_of()
    width = parts[0].shape[1] // SQUAD
    for r, part in enumerate(parts):
        source = lax.rem(mine + ranks - r, ranks)
        for k in range(SQUAD):
            begin = (source * SQUAD + jnp.bitwise_xor(corner, k)) * width
            cols = pl.ds(pl.multiple_of(begin, width), width)
            whole[:, cols] = part[:, k * width : (k + 1) * width]
    block = 2 * LANES
    copies = []
    for c in range(out_ref.shape[1] // block):
        cols = slice(c * block, (c + 1) * block)
        made[:, cols] = jnp.dot(
            whole[...], weight_ref[:, cols], preferred_element_type=jnp.float32
        ).astype(made.dtype)
        span = pl.ds(c * block, block)
        copies.append(
            pltpu.make_async_copy(made.at[:, span], out_ref.at[:, span], sent.at[c])
        )
        copies[-1].start()
    for copy in copies:
        copy.wait()


def local(
    hyena_q, hyena_k, hyena_v, filters, direct, queries, keys, values, segment_ids, out_weight
):
    rows, feat = queries.shape
    count, ranks = lax.axis_size("ctx"), lax.axis_size("tp")
    width = feat // SQUAD
    heads = width // HD
    bf16, f32 = jnp.bfloat16, jnp.float32

    def swap(value, mask):
        return lax.ppermute(value, "ctx", [(i, i ^ mask) for i in range(count)])

    def climb(value, first=0):
        return lax.ppermute(value, "ctx", [(i, i + SQUAD) for i in range(first, count - SQUAD)])

    def descend(value):
        return lax.ppermute(
            value, "ctx", [(i, i - SQUAD) for i in range(2 * SQUAD, count)]
        )

    asked, kept, *sent = deal(
        queries, keys, values, segment_ids.reshape(rows // LANES, LANES)
    )
    tall = rows + TAG
    near = [climb(kept)]
    beside = [swap(sent[0], 1), swap(sent[1], 2)]
    sent[2], beside[0] = lax.optimization_barrier((sent[2], beside[0]))
    across = swap(sent[2], 3)
    beside[1], near[0] = lax.optimization_barrier((beside[1], near[0]))
    near.append(climb(jnp.concatenate([x[rows:] for x in beside], axis=0)))
    back = [descend(jnp.concatenate([asked] + [x[:tall] for x in beside], axis=0))]
    near.append(climb(across[rows:]))
    tail_k = hyena_k[rows - LANES :].astype(f32)
    tail_v = hyena_v[rows - LANES :].astype(f32)
    tail = (tail_k * tail_v).astype(bf16)
    half = tail.shape[1] // 2
    ring = lax.ppermute(
        tail[:, half:], "ctx", [(i, i - i % SQUAD + (i + 1) % SQUAD) for i in range(count)]
    )
    across, ring = lax.optimization_barrier((across, ring))
    back.append(descend(across[:tall]))
    rims = [
        lax.ppermute(tail[:, :half], "ctx", [(i, i + 1) for i in range(count - 1)]),
        ring,
        lax.ppermute(ring, "ctx", [(i, i + SQUAD) for i in range(0, count - SQUAD, SQUAD)]),
    ]
    own = [asked, kept, *beside, across]
    def store(blocks):
        return [
            pltpu.VMEM((heads, SQUAD * rows, 2 * HD), bf16),
            pltpu.VMEM((heads, blocks * rows, 2 * HD), bf16),
            pltpu.VMEM((heads, blocks * rows, HD), bf16),
        ]

    (far,) = kernel_call(
        far_kernel,
        (*back, *near),
        [jax.ShapeDtypeStruct((width + TAG, (SQUAD - 1) * rows), bf16)],
        "far",
        store(SQUAD),
        flops=6 * 4 * rows * rows * width,
        exps=6 * rows * rows * heads,
    )
    far = climb(far, SQUAD)
    own[1], *rims = lax.optimization_barrier((own[1], *rims))
    (main,) = kernel_call(
        main_kernel,
        (*own, *near),
        [jax.ShapeDtypeStruct((width + TAG, SQUAD * rows), f32)],
        "main",
        store(2 * SQUAD),
        flops=26 * 4 * rows * rows * width,
        exps=26 * rows * rows * heads,
    )
    done = kernel_call(
        merge_kernel,
        (main, far),
        [jax.ShapeDtypeStruct((rows, width), bf16)] * SQUAD,
        "merge",
        [pltpu.VMEM((SQUAD, rows, width), bf16)],
    )
    *rims, done[0] = lax.optimization_barrier((*rims, done[0]))
    hyena_out = hyena(hyena_q, hyena_k, hyena_v, rims, filters, direct)

    def turn(value, r):
        return lax.ppermute(value, "tp", [(t, (t + r) % ranks) for t in range(ranks)])

    pieces = [swap(done[k], k) for k in range(1, SQUAD)]
    hyena_out, *pieces = lax.optimization_barrier((hyena_out, done[0], *pieces))
    (joined,) = kernel_call(
        join_kernel,
        pieces,
        [jax.ShapeDtypeStruct((rows, feat), bf16)],
        "join",
    )
    pieces = [joined] + [turn(joined, r) for r in range(1, ranks)]
    (attn_out,) = kernel_call(
        functools.partial(project_kernel, ranks),
        (*pieces, out_weight),
        [jax.ShapeDtypeStruct((rows, out_weight.shape[1]), bf16)],
        "project",
        [
            pltpu.VMEM((rows, ranks * feat), bf16),
            pltpu.VMEM((rows, out_weight.shape[1]), bf16),
            pltpu.SemaphoreType.DMA((out_weight.shape[1] // (2 * LANES),)),
        ],
        flops=2 * rows * math.prod(out_weight.shape),
        out=pl.BlockSpec(memory_space=pl.ANY),
    )
    return (hyena_out, attn_out)


def solution(mesh):
    placed = (
        P("ctx", "tp"),
        P("ctx", "tp"),
        P("ctx", "tp"),
        P("tp", None),
        P("tp"),
        P("ctx", "tp"),
        P("ctx", "tp"),
        P("ctx", "tp"),
        P("ctx"),
        P(None, "tp"),
    )
    return jax.shard_map(
        local,
        mesh=mesh,
        in_specs=placed,
        out_specs=(P("ctx", "tp"), P("ctx", "tp")),
        check_vma=False,
    )
```

```python
import functools
import math

import jax
import jax.numpy as jnp
from jax import lax
from jax.experimental import pallas as pl
from jax.experimental.pallas import tpu as pltpu
from jax.sharding import PartitionSpec as P

HD = 128
SQUAD = 4
NEG = -1e30
TAG = 16
LANES = 128
VMEM_LIMIT = 32 * 1024 * 1024
VMEM = pl.BlockSpec(memory_space=pltpu.VMEM)


def corner_of():
    return lax.rem(lax.axis_index("ctx"), SQUAD)


def kernel_call(kernel, args, shapes, name, scratch=(), flops=0, exps=0, out=VMEM):
    total = sum(math.prod(x.shape) * x.dtype.itemsize for x in (*args, *shapes))
    return list(pl.pallas_call(
        kernel,
        in_specs=[VMEM] * len(args),
        out_specs=[out] * len(shapes),
        out_shape=shapes,
        scratch_shapes=scratch,
        compiler_params=pltpu.CompilerParams(vmem_limit_bytes=VMEM_LIMIT),
        cost_estimate=pl.CostEstimate(flops=flops, bytes_accessed=total, transcendentals=exps),
        name=name,
    )(*args))


def hyena_kernel(q_ref, k_ref, v_ref, near_rim, ring_rim, far_rim, taps_ref, direct_ref, out_ref, taps, rim, made, sent):
    rows, chans = q_ref.shape
    groups = taps_ref.shape[0]
    group = chans // groups
    per_tile = LANES // group
    windows = rows // LANES
    shape = (LANES, LANES)
    down, along = (lax.broadcasted_iota(jnp.int32, shape, i) for i in range(2))
    turn = jnp.where((down + along) % LANES == 0, 1.0, 0.0).astype(jnp.bfloat16)
    before = jnp.where(along > down, 1.0, 0.0).astype(jnp.bfloat16)
    within = jnp.where(along > down, 0.0, 1.0).astype(jnp.bfloat16)
    taps[...] = jnp.dot(taps_ref[...], turn, preferred_element_type=jnp.float32)
    lane_group = lax.broadcasted_iota(jnp.int32, (LANES, windows * LANES), 1) % LANES // group

    half = chans // 2
    rim[:, :half] = near_rim[...]
    rim[:, half:] = ring_rim[...]

    @pl.when(corner_of() == 0)
    def _():
        rim[:, half:] = far_rim[...]

    def leave(tile):
        begin = tile * LANES if isinstance(tile, int) else pl.multiple_of(tile * LANES, LANES)
        cols = pl.ds(begin, LANES)
        return pltpu.make_async_copy(made.at[:, cols], out_ref.at[:, cols], sent.at[tile])

    @pl.loop(0, chans // LANES, unroll=4)
    def _(tile):
        cols = pl.ds(pl.multiple_of(tile * LANES, LANES), LANES)
        rings = taps[pl.ds(pl.multiple_of(tile * per_tile, per_tile), per_tile), :]
        mixed = (k_ref[:, cols].astype(jnp.float32) * v_ref[:, cols].astype(jnp.float32)).astype(
            jnp.bfloat16
        )
        full = jnp.concatenate([rim[:, cols], mixed], axis=0)
        stacked = jnp.concatenate(
            [full[w * LANES : (w + 2) * LANES] for w in range(windows)], axis=1
        )
        conv = jnp.zeros((LANES, windows * LANES), jnp.float32)
        for g in range(per_tile):
            ring = pltpu.roll(
                jnp.broadcast_to(rings[g : g + 1], shape), 0, 1, stride=1, stride_axis=0
            ).astype(jnp.bfloat16)
            table = jnp.concatenate([ring * before, ring * within], axis=1)
            part = jnp.dot(table, stacked, preferred_element_type=jnp.float32)
            conv = jnp.where(lane_group == g, part, conv)
        conv = jnp.concatenate(
            [conv[:, w * LANES : (w + 1) * LANES] for w in range(windows)], axis=0
        )
        made[:, cols] = (
            q_ref[:, cols].astype(jnp.float32)
            * (conv + direct_ref[:, cols].astype(jnp.float32) * mixed.astype(jnp.float32))
        ).astype(jnp.bfloat16)
        leave(tile).start()

    for tile in range(chans // LANES):
        leave(tile).wait()


def hyena(hyena_q, hyena_k, hyena_v, rims, filters, direct):
    rows, chans = hyena_q.shape
    groups, kernel = filters.shape
    taps = jnp.pad(filters, ((0, 0), (0, LANES - kernel)))
    (out,) = kernel_call(
        hyena_kernel,
        (hyena_q, hyena_k, hyena_v, *rims, taps, direct[None]),
        [jax.ShapeDtypeStruct((rows, chans), jnp.bfloat16)],
        "hyena",
        [
            pltpu.VMEM((groups, LANES), jnp.float32),
            pltpu.VMEM((LANES, chans), jnp.bfloat16),
            pltpu.VMEM((rows, chans), jnp.bfloat16),
            pltpu.SemaphoreType.DMA((chans // LANES,)),
        ],
        flops=4 * rows * chans * 2 * LANES * 8,
        out=pl.BlockSpec(memory_space=pl.ANY),
    )
    return out


def deal_kernel(q_ref, k_ref, v_ref, id_ref, *refs):
    outs, (held, arrive, told) = refs[:-3], refs[-3:]
    tell = pltpu.make_async_copy(id_ref, held, told)
    tell.start()
    rows, feat = q_ref.shape
    width = feat // SQUAD
    corner = corner_of()
    copies = []
    for k in (*range(1, SQUAD), 0):
        cols = pl.ds(pl.multiple_of(jnp.bitwise_xor(corner, k) * width, width), width)
        base = rows if k else 0
        places = (
            (q_ref, outs[k + 1] if k else outs[0], 0),
            (k_ref, outs[k + 1], base + TAG),
            (v_ref, outs[k + 1], base + TAG + rows),
        )
        copies += [
            pltpu.make_async_copy(
                source.at[:, cols], target.at[pl.ds(begin, rows)], arrive.at[k, i]
            )
            for i, (source, target, begin) in enumerate(places)
        ]
    for copy in copies:
        copy.start()
    tell.wait()
    ids = (held[...] + 1).astype(jnp.float32)
    spare = jnp.zeros((TAG - ids.shape[0], LANES), jnp.float32)
    ids = jnp.concatenate([ids, spare], axis=0)
    tag = jnp.concatenate([ids] * (width // LANES), axis=1).astype(jnp.bfloat16)
    for i, target in enumerate(outs):
        begin = 0 if i == 1 else rows
        target[begin : begin + TAG, :] = tag
    for copy in copies:
        copy.wait()


def deal(queries, keys, values, ids):
    rows, feat = queries.shape
    tall = [rows + TAG, 2 * rows + TAG] + [3 * rows + TAG] * (SQUAD - 1)
    shapes = [(x, feat // SQUAD) for x in tall]
    held = [pltpu.with_memory_space_constraint(x, pltpu.HBM) for x in (queries, keys, values, ids)]
    return list(
        pl.pallas_call(
            deal_kernel,
            in_specs=[pl.BlockSpec(memory_space=pl.ANY)] * 4,
            out_specs=[VMEM] * len(tall),
            out_shape=[jax.ShapeDtypeStruct(x, jnp.bfloat16) for x in shapes],
            scratch_shapes=[
                pltpu.VMEM(ids.shape, ids.dtype),
                pltpu.SemaphoreType.DMA((SQUAD, 3)),
                pltpu.SemaphoreType.DMA,
            ],
            compiler_params=pltpu.CompilerParams(vmem_limit_bytes=VMEM_LIMIT),
            cost_estimate=pl.CostEstimate(
                flops=0, bytes_accessed=12 * rows * feat, transcendentals=0
            ),
            name="deal",
        )(*held)
    )


def id_columns(tag_ref, rows):
    tag = tag_ref[:, :LANES].astype(jnp.float32)
    tiles = [jnp.broadcast_to(tag[t : t + 1], (LANES, LANES)).T for t in range(rows // LANES)]
    return jnp.concatenate(tiles, axis=0)


def place_keys(parts, corner, base, rows, keys, values):
    heads = keys.shape[0]
    marks = lax.broadcasted_iota(jnp.int32, (rows, LANES), 1).astype(jnp.float32) + 1.0
    for k, part in enumerate(parts):
        begin = pl.multiple_of((jnp.bitwise_xor(corner, k) + base) * rows, rows)
        span = pl.ds(begin, rows)
        ids = id_columns(part.at[:TAG], rows)
        mask = jnp.where(ids == marks, 0.0, -NEG).astype(jnp.bfloat16)
        for h in range(heads):
            cols = slice(h * HD, (h + 1) * HD)
            keys[h, span, :HD] = part[TAG : TAG + rows, cols]
            keys[h, span, HD:] = mask
            values[h, span, :] = part[TAG + rows : TAG + 2 * rows, cols]


def near_parts(near, rows):
    tall = 2 * rows + TAG
    return [near[0], near[1].at[:tall], near[1].at[tall:], near[2]]


def place_queries(parts, corner, rows, queries):
    heads = queries.shape[0]
    marks = lax.broadcasted_iota(jnp.int32, (rows, LANES), 1).astype(jnp.float32) + 1.0
    for k, part in enumerate(parts):
        begin = pl.multiple_of(jnp.bitwise_xor(corner, k) * rows, rows)
        span = pl.ds(begin, rows)
        ids = id_columns(part.at[rows : rows + TAG], rows)
        mask = jnp.where(ids == marks, -1.0, 0.0).astype(jnp.bfloat16)
        for h in range(heads):
            queries[h, span, :HD] = part[:rows, h * HD : (h + 1) * HD]
            queries[h, span, HD:] = mask


def score_of(query, keys):
    return lax.dot_general(
        keys, query, (((1,), (1,)), ((), ())), preferred_element_type=jnp.float32
    )


def attend(score, values, diagonal):
    factor = math.log2(math.e) / math.sqrt(HD)
    rows = score.shape[1]
    if diagonal:
        older = lax.broadcasted_iota(jnp.int32, (rows, rows), 0) <= lax.broadcasted_iota(
            jnp.int32, (rows, rows), 1
        )
        score = jnp.concatenate([score[:-rows], jnp.where(older, score[-rows:], NEG)], axis=0)
    high = jnp.max(score, axis=0, keepdims=True)
    expo = jnp.exp2((score - high) * factor)
    total = jnp.sum(expo, axis=0, keepdims=True)
    summed = lax.dot_general(
        values,
        expo.astype(jnp.bfloat16),
        (((0,), (0,)), ((), ())),
        preferred_element_type=jnp.float32,
    )
    return summed / total, high * factor + jnp.log2(total)


def ahead(steps, product):
    late = product(*steps[0])
    for step, following in zip(steps, steps[1:] + [None]):
        now, late = late, product(*following) if following else None
        yield step, now


def main_kernel(*refs):
    own, near, out, (queries, keys, values) = refs[:5], refs[5:8], refs[8], refs[9:]
    heads, span, _ = queries.shape
    rows = span // SQUAD
    width = heads * HD
    corner = corner_of()
    asked = [own[0]] + [p.at[: rows + TAG] for p in own[2:]]
    held = [own[1]] + [p.at[rows:] for p in own[2:]]
    place_queries(asked, corner, rows, queries)
    place_keys(held, corner, SQUAD, rows, keys, values)
    place_keys(near_parts(near, rows), corner, 0, rows, keys, values)
    span = [slice(j * rows, (j + 1) * rows) for j in range(SQUAD)]
    reach = [(SQUAD + 1 + j) * rows for j in range(SQUAD)]
    steps = [(j, h) for j in range(SQUAD) for h in range(heads)]
    for (j, h), score in ahead(
        steps, lambda j, h: score_of(queries[h, span[j]], keys[h, : reach[j]])
    ):
        mixed, lse = attend(score, values[h, : reach[j]], True)
        out[h * HD : (h + 1) * HD, span[j]] = mixed
        out[width + h : width + h + 1, span[j]] = lse
    out[width + heads :, :] = jnp.zeros((TAG - heads, SQUAD * rows), jnp.float32)


def far_kernel(*refs):
    asked, near, out, (queries, keys, values) = refs[:2], refs[2:5], refs[5], refs[6:]
    heads, span, _ = queries.shape
    rows = span // SQUAD
    width = heads * HD
    corner = corner_of()
    tall = rows + TAG
    asked = [asked[0].at[k * tall : (k + 1) * tall] for k in range(SQUAD - 1)] + [asked[1]]
    place_queries(asked, corner, rows, queries)
    place_keys(near_parts(near, rows), corner, 0, rows, keys, values)
    span = [slice(j * rows, (j + 1) * rows) for j in range(SQUAD)]
    stats = [[] for _ in range(SQUAD - 1)]
    steps = [(j, h) for j in range(SQUAD - 1) for h in range(heads)]
    for (j, h), score in ahead(
        steps, lambda j, h: score_of(queries[h, span[j]], keys[h, span[j].stop :])
    ):
        mixed, lse = attend(score, values[h, span[j].stop :], False)
        out[h * HD : (h + 1) * HD, span[j]] = mixed.astype(out.dtype)
        top = lse.astype(jnp.bfloat16).astype(jnp.float32)
        mid = (lse - top).astype(jnp.bfloat16).astype(jnp.float32)
        stats[j] += [top, mid, lse - top - mid]
    for j, stat in enumerate(stats):
        stat.append(jnp.zeros((TAG - len(stat), rows), jnp.float32))
        out[width:, span[j]] = jnp.concatenate(stat, axis=0).astype(out.dtype)


def merge_kernel(main_ref, far_ref, *refs):
    outs, ready = refs[:-1], refs[-1]
    _, rows, width = ready.shape
    corner = corner_of()
    served = lax.axis_index("ctx") >= 2 * SQUAD
    for j in range(SQUAD):
        cols = slice(j * rows, (j + 1) * rows)
        for h in range(width // HD):
            feats = slice(h * HD, (h + 1) * HD)
            mixed = main_ref[feats, cols]
            if j < SQUAD - 1:
                here = main_ref[width + h : width + h + 1, cols]
                stats = far_ref[width:, cols].astype(jnp.float32)
                there = stats[3 * h : 3 * h + 1] + stats[3 * h + 1 : 3 * h + 2]
                there = jnp.where(served, there + stats[3 * h + 2 : 3 * h + 3], NEG)
                high = jnp.maximum(here, there)
                here, there = jnp.exp2(here - high), jnp.exp2(there - high)
                total = here + there
                mixed = mixed * (here / total) + far_ref[feats, cols].astype(jnp.float32) * (
                    there / total
                )
            ready[j, :, feats] = mixed.T.astype(ready.dtype)
    for k, out in enumerate(outs):
        out[...] = ready[jnp.bitwise_xor(corner, k)]


def join_kernel(*refs):
    parts, out = refs[:-1], refs[-1]
    width = parts[0].shape[1]
    for i, part in enumerate(parts):
        out[:, i * width : (i + 1) * width] = part[...]


def project_kernel(ranks, *refs):
    parts, (weight_ref, out_ref, whole, made, sent) = refs[:-5], refs[-5:]
    mine, corner = lax.axis_index("tp"), corner_of()
    width = parts[0].shape[1] // SQUAD
    for r, part in enumerate(parts):
        source = lax.rem(mine + ranks - r, ranks)
        for k in range(SQUAD):
            begin = (source * SQUAD + jnp.bitwise_xor(corner, k)) * width
            cols = pl.ds(pl.multiple_of(begin, width), width)
            whole[:, cols] = part[:, k * width : (k + 1) * width]
    block = 2 * LANES
    spans = [slice(c, c + block) for c in range(0, out_ref.shape[1], block)]

    def product(cols):
        return jnp.dot(whole[...], weight_ref[:, cols], preferred_element_type=jnp.float32)

    copies = []
    for (cols,), total in ahead([(x,) for x in spans], product):
        made[:, cols] = total.astype(made.dtype)
        span = pl.ds(cols.start, block)
        copies.append(
            pltpu.make_async_copy(
                made.at[:, span], out_ref.at[:, span], sent.at[cols.start // block]
            )
        )
        copies[-1].start()
    for copy in copies:
        copy.wait()


def local(
    hyena_q, hyena_k, hyena_v, filters, direct, queries, keys, values, segment_ids, out_weight
):
    rows, feat = queries.shape
    count, ranks = lax.axis_size("ctx"), lax.axis_size("tp")
    width = feat // SQUAD
    heads = width // HD
    bf16, f32 = jnp.bfloat16, jnp.float32

    def swap(value, mask):
        return lax.ppermute(value, "ctx", [(i, i ^ mask) for i in range(count)])

    def climb(value, first=0):
        return lax.ppermute(value, "ctx", [(i, i + SQUAD) for i in range(first, count - SQUAD)])

    def descend(value):
        return lax.ppermute(
            value, "ctx", [(i, i - SQUAD) for i in range(2 * SQUAD, count)]
        )

    asked, kept, *sent = deal(
        queries, keys, values, segment_ids.reshape(rows // LANES, LANES)
    )
    tall = rows + TAG
    near = [climb(kept)]
    beside = [swap(sent[0], 1), swap(sent[1], 2)]
    sent[2], beside[0] = lax.optimization_barrier((sent[2], beside[0]))
    across = swap(sent[2], 3)
    beside[1], near[0] = lax.optimization_barrier((beside[1], near[0]))
    near.append(climb(jnp.concatenate([x[rows:] for x in beside], axis=0)))
    back = [descend(jnp.concatenate([asked] + [x[:tall] for x in beside], axis=0))]
    near.append(climb(across[rows:]))
    tail_k = hyena_k[rows - LANES :].astype(f32)
    tail_v = hyena_v[rows - LANES :].astype(f32)
    tail = (tail_k * tail_v).astype(bf16)
    half = tail.shape[1] // 2
    ring = lax.ppermute(
        tail[:, half:], "ctx", [(i, i - i % SQUAD + (i + 1) % SQUAD) for i in range(count)]
    )
    across, ring = lax.optimization_barrier((across, ring))
    back.append(descend(across[:tall]))
    rims = [
        lax.ppermute(tail[:, :half], "ctx", [(i, i + 1) for i in range(count - 1)]),
        ring,
        lax.ppermute(ring, "ctx", [(i, i + SQUAD) for i in range(0, count - SQUAD, SQUAD)]),
    ]
    own = [asked, kept, *beside, across]
    def store(blocks):
        return [
            pltpu.VMEM((heads, SQUAD * rows, 2 * HD), bf16),
            pltpu.VMEM((heads, blocks * rows, 2 * HD), bf16),
            pltpu.VMEM((heads, blocks * rows, HD), bf16),
        ]

    (far,) = kernel_call(
        far_kernel,
        (*back, *near),
        [jax.ShapeDtypeStruct((width + TAG, (SQUAD - 1) * rows), bf16)],
        "far",
        store(SQUAD),
        flops=6 * 4 * rows * rows * width,
        exps=6 * rows * rows * heads,
    )
    far = climb(far, SQUAD)
    own[1], *rims = lax.optimization_barrier((own[1], *rims))
    (main,) = kernel_call(
        main_kernel,
        (*own, *near),
        [jax.ShapeDtypeStruct((width + TAG, SQUAD * rows), f32)],
        "main",
        store(2 * SQUAD),
        flops=26 * 4 * rows * rows * width,
        exps=26 * rows * rows * heads,
    )
    done = kernel_call(
        merge_kernel,
        (main, far),
        [jax.ShapeDtypeStruct((rows, width), bf16)] * SQUAD,
        "merge",
        [pltpu.VMEM((SQUAD, rows, width), bf16)],
    )
    *rims, done[0] = lax.optimization_barrier((*rims, done[0]))
    hyena_out = hyena(hyena_q, hyena_k, hyena_v, rims, filters, direct)

    def turn(value, r):
        return lax.ppermute(value, "tp", [(t, (t + r) % ranks) for t in range(ranks)])

    pieces = [swap(done[k], k) for k in range(1, SQUAD)]
    hyena_out, *pieces = lax.optimization_barrier((hyena_out, done[0], *pieces))
    (joined,) = kernel_call(
        join_kernel,
        pieces,
        [jax.ShapeDtypeStruct((rows, feat), bf16)],
        "join",
    )
    pieces = [joined] + [turn(joined, r) for r in range(1, ranks)]
    (attn_out,) = kernel_call(
        functools.partial(project_kernel, ranks),
        (*pieces, out_weight),
        [jax.ShapeDtypeStruct((rows, out_weight.shape[1]), bf16)],
        "project",
        [
            pltpu.VMEM((rows, ranks * feat), bf16),
            pltpu.VMEM((rows, out_weight.shape[1]), bf16),
            pltpu.SemaphoreType.DMA((out_weight.shape[1] // (2 * LANES),)),
        ],
        flops=2 * rows * math.prod(out_weight.shape),
        out=pl.BlockSpec(memory_space=pl.ANY),
    )
    return (hyena_out, attn_out)


def solution(mesh):
    placed = (
        P("ctx", "tp"),
        P("ctx", "tp"),
        P("ctx", "tp"),
        P("tp", None),
        P("tp"),
        P("ctx", "tp"),
        P("ctx", "tp"),
        P("ctx", "tp"),
        P("ctx"),
        P(None, "tp"),
    )
    return jax.shard_map(
        local,
        mesh=mesh,
        in_specs=placed,
        out_specs=(P("ctx", "tp"), P("ctx", "tp")),
        check_vma=False,
    )
```

```python
import functools
import math

import jax
import jax.numpy as jnp
from jax import lax
from jax.experimental import pallas as pl
from jax.experimental.pallas import tpu as pltpu
from jax.sharding import PartitionSpec as P

HD = 128
SQUAD = 4
NEG = -1e30
TAG = 16
LANES = 128
VMEM_LIMIT = 32 * 1024 * 1024
VMEM = pl.BlockSpec(memory_space=pltpu.VMEM)


def corner_of():
    return lax.rem(lax.axis_index("ctx"), SQUAD)


def kernel_call(kernel, args, shapes, name, scratch=(), flops=0, exps=0, out=VMEM):
    total = sum(math.prod(x.shape) * x.dtype.itemsize for x in (*args, *shapes))
    return list(pl.pallas_call(
        kernel,
        in_specs=[VMEM] * len(args),
        out_specs=[out] * len(shapes),
        out_shape=shapes,
        scratch_shapes=scratch,
        compiler_params=pltpu.CompilerParams(vmem_limit_bytes=VMEM_LIMIT),
        cost_estimate=pl.CostEstimate(flops=flops, bytes_accessed=total, transcendentals=exps),
        name=name,
    )(*args))


def hyena_kernel(q_ref, k_ref, v_ref, near_rim, ring_rim, far_rim, taps_ref, direct_ref, out_ref, taps, rim, made, sent):
    rows, chans = q_ref.shape
    groups = taps_ref.shape[0]
    group = chans // groups
    per_tile = LANES // group
    windows = rows // LANES
    shape = (LANES, LANES)
    down, along = (lax.broadcasted_iota(jnp.int32, shape, i) for i in range(2))
    turn = jnp.where((down + along) % LANES == 0, 1.0, 0.0).astype(jnp.bfloat16)
    before = jnp.where(along > down, 1.0, 0.0).astype(jnp.bfloat16)
    within = jnp.where(along > down, 0.0, 1.0).astype(jnp.bfloat16)
    taps[...] = jnp.dot(taps_ref[...], turn, preferred_element_type=jnp.float32)
    lane_group = lax.broadcasted_iota(jnp.int32, (LANES, windows * LANES), 1) % LANES // group

    half = chans // 2
    rim[:, :half] = near_rim[...]
    rim[:, half:] = ring_rim[...]

    @pl.when(corner_of() == 0)
    def _():
        rim[:, half:] = far_rim[...]

    def leave(tile):
        begin = tile * LANES if isinstance(tile, int) else pl.multiple_of(tile * LANES, LANES)
        cols = pl.ds(begin, LANES)
        return pltpu.make_async_copy(made.at[:, cols], out_ref.at[:, cols], sent.at[tile])

    @pl.loop(0, chans // LANES, unroll=8)
    def _(tile):
        cols = pl.ds(pl.multiple_of(tile * LANES, LANES), LANES)
        rings = taps[pl.ds(pl.multiple_of(tile * per_tile, per_tile), per_tile), :]
        mixed = (k_ref[:, cols].astype(jnp.float32) * v_ref[:, cols].astype(jnp.float32)).astype(
            jnp.bfloat16
        )
        full = jnp.concatenate([rim[:, cols], mixed], axis=0)
        stacked = jnp.concatenate(
            [full[w * LANES : (w + 2) * LANES] for w in range(windows)], axis=1
        )
        conv = jnp.zeros((LANES, windows * LANES), jnp.float32)
        for g in range(per_tile):
            ring = pltpu.roll(
                jnp.broadcast_to(rings[g : g + 1], shape), 0, 1, stride=1, stride_axis=0
            ).astype(jnp.bfloat16)
            table = jnp.concatenate([ring * before, ring * within], axis=1)
            part = jnp.dot(table, stacked, preferred_element_type=jnp.float32)
            conv = jnp.where(lane_group == g, part, conv)
        conv = jnp.concatenate(
            [conv[:, w * LANES : (w + 1) * LANES] for w in range(windows)], axis=0
        )
        made[:, cols] = (
            q_ref[:, cols].astype(jnp.float32)
            * (conv + direct_ref[:, cols].astype(jnp.float32) * mixed.astype(jnp.float32))
        ).astype(jnp.bfloat16)
        leave(tile).start()

    for tile in range(chans // LANES):
        leave(tile).wait()


def hyena(hyena_q, hyena_k, hyena_v, rims, filters, direct):
    rows, chans = hyena_q.shape
    groups, kernel = filters.shape
    taps = jnp.pad(filters, ((0, 0), (0, LANES - kernel)))
    (out,) = kernel_call(
        hyena_kernel,
        (hyena_q, hyena_k, hyena_v, *rims, taps, direct[None]),
        [jax.ShapeDtypeStruct((rows, chans), jnp.bfloat16)],
        "hyena",
        [
            pltpu.VMEM((groups, LANES), jnp.float32),
            pltpu.VMEM((LANES, chans), jnp.bfloat16),
            pltpu.VMEM((rows, chans), jnp.bfloat16),
            pltpu.SemaphoreType.DMA((chans // LANES,)),
        ],
        flops=4 * rows * chans * 2 * LANES * 8,
        out=pl.BlockSpec(memory_space=pl.ANY),
    )
    return out


def deal_kernel(q_ref, k_ref, v_ref, id_ref, *refs):
    outs, (held, arrive, told) = refs[:-3], refs[-3:]
    tell = pltpu.make_async_copy(id_ref, held, told)
    tell.start()
    rows, feat = q_ref.shape
    width = feat // SQUAD
    corner = corner_of()
    copies = []
    for k in (*range(1, SQUAD), 0):
        cols = pl.ds(pl.multiple_of(jnp.bitwise_xor(corner, k) * width, width), width)
        base = rows if k else 0
        places = (
            (q_ref, outs[k + 1] if k else outs[0], 0),
            (k_ref, outs[k + 1], base + TAG),
            (v_ref, outs[k + 1], base + TAG + rows),
        )
        copies += [
            pltpu.make_async_copy(
                source.at[:, cols], target.at[pl.ds(begin, rows)], arrive.at[k, i]
            )
            for i, (source, target, begin) in enumerate(places)
        ]
    for copy in copies:
        copy.start()
    tell.wait()
    ids = (held[...] + 1).astype(jnp.float32)
    spare = jnp.zeros((TAG - ids.shape[0], LANES), jnp.float32)
    ids = jnp.concatenate([ids, spare], axis=0)
    tag = jnp.concatenate([ids] * (width // LANES), axis=1).astype(jnp.bfloat16)
    for i, target in enumerate(outs):
        begin = 0 if i == 1 else rows
        target[begin : begin + TAG, :] = tag
    for copy in copies:
        copy.wait()


def deal(queries, keys, values, ids):
    rows, feat = queries.shape
    tall = [rows + TAG, 2 * rows + TAG] + [3 * rows + TAG] * (SQUAD - 1)
    shapes = [(x, feat // SQUAD) for x in tall]
    held = [pltpu.with_memory_space_constraint(x, pltpu.HBM) for x in (queries, keys, values, ids)]
    return list(
        pl.pallas_call(
            deal_kernel,
            in_specs=[pl.BlockSpec(memory_space=pl.ANY)] * 4,
            out_specs=[VMEM] * len(tall),
            out_shape=[jax.ShapeDtypeStruct(x, jnp.bfloat16) for x in shapes],
            scratch_shapes=[
                pltpu.VMEM(ids.shape, ids.dtype),
                pltpu.SemaphoreType.DMA((SQUAD, 3)),
                pltpu.SemaphoreType.DMA,
            ],
            compiler_params=pltpu.CompilerParams(vmem_limit_bytes=VMEM_LIMIT),
            cost_estimate=pl.CostEstimate(
                flops=0, bytes_accessed=12 * rows * feat, transcendentals=0
            ),
            name="deal",
        )(*held)
    )


def id_columns(tag_ref, rows):
    tag = tag_ref[:, :LANES].astype(jnp.float32)
    tiles = [jnp.broadcast_to(tag[t : t + 1], (LANES, LANES)).T for t in range(rows // LANES)]
    return jnp.concatenate(tiles, axis=0)


def place_keys(parts, corner, base, rows, keys, values):
    heads = keys.shape[0]
    marks = lax.broadcasted_iota(jnp.int32, (rows, LANES), 1).astype(jnp.float32) + 1.0
    for k, part in enumerate(parts):
        begin = pl.multiple_of((jnp.bitwise_xor(corner, k) + base) * rows, rows)
        span = pl.ds(begin, rows)
        ids = id_columns(part.at[:TAG], rows)
        mask = jnp.where(ids == marks, 0.0, -NEG).astype(jnp.bfloat16)
        for h in range(heads):
            cols = slice(h * HD, (h + 1) * HD)
            keys[h, span, :HD] = part[TAG : TAG + rows, cols]
            keys[h, span, HD:] = mask
            values[h, span, :] = part[TAG + rows : TAG + 2 * rows, cols]


def near_parts(near, rows):
    tall = 2 * rows + TAG
    return [near[0], near[1].at[:tall], near[1].at[tall:], near[2]]


def place_queries(parts, corner, rows, queries):
    heads = queries.shape[0]
    marks = lax.broadcasted_iota(jnp.int32, (rows, LANES), 1).astype(jnp.float32) + 1.0
    for k, part in enumerate(parts):
        begin = pl.multiple_of(jnp.bitwise_xor(corner, k) * rows, rows)
        span = pl.ds(begin, rows)
        ids = id_columns(part.at[rows : rows + TAG], rows)
        mask = jnp.where(ids == marks, -1.0, 0.0).astype(jnp.bfloat16)
        for h in range(heads):
            queries[h, span, :HD] = part[:rows, h * HD : (h + 1) * HD]
            queries[h, span, HD:] = mask


def score_of(query, keys):
    return lax.dot_general(
        keys, query, (((1,), (1,)), ((), ())), preferred_element_type=jnp.float32
    )


def attend(score, values, diagonal):
    factor = math.log2(math.e) / math.sqrt(HD)
    rows = score.shape[1]
    if diagonal:
        older = lax.broadcasted_iota(jnp.int32, (rows, rows), 0) <= lax.broadcasted_iota(
            jnp.int32, (rows, rows), 1
        )
        score = jnp.concatenate([score[:-rows], jnp.where(older, score[-rows:], NEG)], axis=0)
    high = jnp.max(score, axis=0, keepdims=True)
    expo = jnp.exp2((score - high) * factor)
    total = jnp.sum(expo, axis=0, keepdims=True)
    summed = lax.dot_general(
        values,
        expo.astype(jnp.bfloat16),
        (((0,), (0,)), ((), ())),
        preferred_element_type=jnp.float32,
    )
    return summed / total, high * factor + jnp.log2(total)


def ahead(steps, product):
    late = product(*steps[0])
    for step, following in zip(steps, steps[1:] + [None]):
        now, late = late, product(*following) if following else None
        yield step, now


def main_kernel(*refs):
    own, near, out, (queries, keys, values) = refs[:5], refs[5:8], refs[8], refs[9:]
    heads, span, _ = queries.shape
    rows = span // SQUAD
    width = heads * HD
    corner = corner_of()
    asked = [own[0]] + [p.at[: rows + TAG] for p in own[2:]]
    held = [own[1]] + [p.at[rows:] for p in own[2:]]
    place_queries(asked, corner, rows, queries)
    place_keys(held, corner, SQUAD, rows, keys, values)
    place_keys(near_parts(near, rows), corner, 0, rows, keys, values)
    span = [slice(j * rows, (j + 1) * rows) for j in range(SQUAD)]
    reach = [(SQUAD + 1 + j) * rows for j in range(SQUAD)]
    steps = [(j, h) for j in range(SQUAD) for h in range(heads)]
    for (j, h), score in ahead(
        steps, lambda j, h: score_of(queries[h, span[j]], keys[h, : reach[j]])
    ):
        mixed, lse = attend(score, values[h, : reach[j]], True)
        out[h * HD : (h + 1) * HD, span[j]] = mixed
        out[width + h : width + h + 1, span[j]] = lse
    out[width + heads :, :] = jnp.zeros((TAG - heads, SQUAD * rows), jnp.float32)


def far_kernel(*refs):
    asked, near, out, (queries, keys, values) = refs[:2], refs[2:5], refs[5], refs[6:]
    heads, span, _ = queries.shape
    rows = span // SQUAD
    width = heads * HD
    corner = corner_of()
    tall = rows + TAG
    asked = [asked[0].at[k * tall : (k + 1) * tall] for k in range(SQUAD - 1)] + [asked[1]]
    place_queries(asked, corner, rows, queries)
    place_keys(near_parts(near, rows), corner, 0, rows, keys, values)
    span = [slice(j * rows, (j + 1) * rows) for j in range(SQUAD)]
    stats = [[] for _ in range(SQUAD - 1)]
    steps = [(j, h) for j in range(SQUAD - 1) for h in range(heads)]
    for (j, h), score in ahead(
        steps, lambda j, h: score_of(queries[h, span[j]], keys[h, span[j].stop :])
    ):
        mixed, lse = attend(score, values[h, span[j].stop :], False)
        out[h * HD : (h + 1) * HD, span[j]] = mixed.astype(out.dtype)
        top = lse.astype(jnp.bfloat16).astype(jnp.float32)
        mid = (lse - top).astype(jnp.bfloat16).astype(jnp.float32)
        stats[j] += [top, mid, lse - top - mid]
    for j, stat in enumerate(stats):
        stat.append(jnp.zeros((TAG - len(stat), rows), jnp.float32))
        out[width:, span[j]] = jnp.concatenate(stat, axis=0).astype(out.dtype)


def merge_kernel(main_ref, far_ref, *refs):
    outs, ready = refs[:-1], refs[-1]
    _, rows, width = ready.shape
    corner = corner_of()
    served = lax.axis_index("ctx") >= 2 * SQUAD
    for j in range(SQUAD):
        cols = slice(j * rows, (j + 1) * rows)
        for h in range(width // HD):
            feats = slice(h * HD, (h + 1) * HD)
            mixed = main_ref[feats, cols]
            if j < SQUAD - 1:
                here = main_ref[width + h : width + h + 1, cols]
                stats = far_ref[width:, cols].astype(jnp.float32)
                there = stats[3 * h : 3 * h + 1] + stats[3 * h + 1 : 3 * h + 2]
                there = jnp.where(served, there + stats[3 * h + 2 : 3 * h + 3], NEG)
                high = jnp.maximum(here, there)
                here, there = jnp.exp2(here - high), jnp.exp2(there - high)
                total = here + there
                mixed = mixed * (here / total) + far_ref[feats, cols].astype(jnp.float32) * (
                    there / total
                )
            ready[j, :, feats] = mixed.T.astype(ready.dtype)
    for k, out in enumerate(outs):
        out[...] = ready[jnp.bitwise_xor(corner, k)]


def join_kernel(*refs):
    parts, out = refs[:-1], refs[-1]
    width = parts[0].shape[1]
    for i, part in enumerate(parts):
        out[:, i * width : (i + 1) * width] = part[...]


def project_kernel(ranks, *refs):
    parts, (weight_ref, out_ref, whole, made, sent) = refs[:-5], refs[-5:]
    mine, corner = lax.axis_index("tp"), corner_of()
    width = parts[0].shape[1] // SQUAD
    for r, part in enumerate(parts):
        source = lax.rem(mine + ranks - r, ranks)
        for k in range(SQUAD):
            begin = (source * SQUAD + jnp.bitwise_xor(corner, k)) * width
            cols = pl.ds(pl.multiple_of(begin, width), width)
            whole[:, cols] = part[:, k * width : (k + 1) * width]
    block = 2 * LANES
    spans = [slice(c, c + block) for c in range(0, out_ref.shape[1], block)]

    def product(cols):
        return jnp.dot(whole[...], weight_ref[:, cols], preferred_element_type=jnp.float32)

    copies = []
    for (cols,), total in ahead([(x,) for x in spans], product):
        made[:, cols] = total.astype(made.dtype)
        span = pl.ds(cols.start, block)
        copies.append(
            pltpu.make_async_copy(
                made.at[:, span], out_ref.at[:, span], sent.at[cols.start // block]
            )
        )
        copies[-1].start()
    for copy in copies:
        copy.wait()


def local(
    hyena_q, hyena_k, hyena_v, filters, direct, queries, keys, values, segment_ids, out_weight
):
    rows, feat = queries.shape
    count, ranks = lax.axis_size("ctx"), lax.axis_size("tp")
    width = feat // SQUAD
    heads = width // HD
    bf16, f32 = jnp.bfloat16, jnp.float32

    def swap(value, mask):
        return lax.ppermute(value, "ctx", [(i, i ^ mask) for i in range(count)])

    def climb(value, first=0):
        return lax.ppermute(value, "ctx", [(i, i + SQUAD) for i in range(first, count - SQUAD)])

    def descend(value):
        return lax.ppermute(
            value, "ctx", [(i, i - SQUAD) for i in range(2 * SQUAD, count)]
        )

    asked, kept, *sent = deal(
        queries, keys, values, segment_ids.reshape(rows // LANES, LANES)
    )
    tall = rows + TAG
    near = [climb(kept)]
    beside = [swap(sent[0], 1), swap(sent[1], 2)]
    sent[2], beside[0] = lax.optimization_barrier((sent[2], beside[0]))
    across = swap(sent[2], 3)
    beside[1], near[0] = lax.optimization_barrier((beside[1], near[0]))
    near.append(climb(jnp.concatenate([x[rows:] for x in beside], axis=0)))
    back = [descend(jnp.concatenate([asked] + [x[:tall] for x in beside], axis=0))]
    near.append(climb(across[rows:]))
    tail_k = hyena_k[rows - LANES :].astype(f32)
    tail_v = hyena_v[rows - LANES :].astype(f32)
    tail = (tail_k * tail_v).astype(bf16)
    half = tail.shape[1] // 2
    ring = lax.ppermute(
        tail[:, half:], "ctx", [(i, i - i % SQUAD + (i + 1) % SQUAD) for i in range(count)]
    )
    across, ring = lax.optimization_barrier((across, ring))
    back.append(descend(across[:tall]))
    rims = [
        lax.ppermute(tail[:, :half], "ctx", [(i, i + 1) for i in range(count - 1)]),
        ring,
        lax.ppermute(ring, "ctx", [(i, i + SQUAD) for i in range(0, count - SQUAD, SQUAD)]),
    ]
    own = [asked, kept, *beside, across]
    def store(blocks):
        return [
            pltpu.VMEM((heads, SQUAD * rows, 2 * HD), bf16),
            pltpu.VMEM((heads, blocks * rows, 2 * HD), bf16),
            pltpu.VMEM((heads, blocks * rows, HD), bf16),
        ]

    (far,) = kernel_call(
        far_kernel,
        (*back, *near),
        [jax.ShapeDtypeStruct((width + TAG, (SQUAD - 1) * rows), bf16)],
        "far",
        store(SQUAD),
        flops=6 * 4 * rows * rows * width,
        exps=6 * rows * rows * heads,
    )
    far = climb(far, SQUAD)
    own[1], *rims = lax.optimization_barrier((own[1], *rims))
    (main,) = kernel_call(
        main_kernel,
        (*own, *near),
        [jax.ShapeDtypeStruct((width + TAG, SQUAD * rows), f32)],
        "main",
        store(2 * SQUAD),
        flops=26 * 4 * rows * rows * width,
        exps=26 * rows * rows * heads,
    )
    done = kernel_call(
        merge_kernel,
        (main, far),
        [jax.ShapeDtypeStruct((rows, width), bf16)] * SQUAD,
        "merge",
        [pltpu.VMEM((SQUAD, rows, width), bf16)],
    )
    *rims, done[0] = lax.optimization_barrier((*rims, done[0]))
    hyena_out = hyena(hyena_q, hyena_k, hyena_v, rims, filters, direct)

    def turn(value, r):
        return lax.ppermute(value, "tp", [(t, (t + r) % ranks) for t in range(ranks)])

    pieces = [swap(done[k], k) for k in range(1, SQUAD)]
    hyena_out, *pieces = lax.optimization_barrier((hyena_out, done[0], *pieces))
    (joined,) = kernel_call(
        join_kernel,
        pieces,
        [jax.ShapeDtypeStruct((rows, feat), bf16)],
        "join",
    )
    pieces = [joined] + [turn(joined, r) for r in range(1, ranks)]
    (attn_out,) = kernel_call(
        functools.partial(project_kernel, ranks),
        (*pieces, out_weight),
        [jax.ShapeDtypeStruct((rows, out_weight.shape[1]), bf16)],
        "project",
        [
            pltpu.VMEM((rows, ranks * feat), bf16),
            pltpu.VMEM((rows, out_weight.shape[1]), bf16),
            pltpu.SemaphoreType.DMA((out_weight.shape[1] // (2 * LANES),)),
        ],
        flops=2 * rows * math.prod(out_weight.shape),
        out=pl.BlockSpec(memory_space=pl.ANY),
    )
    return (hyena_out, attn_out)


def solution(mesh):
    placed = (
        P("ctx", "tp"),
        P("ctx", "tp"),
        P("ctx", "tp"),
        P("tp", None),
        P("tp"),
        P("ctx", "tp"),
        P("ctx", "tp"),
        P("ctx", "tp"),
        P("ctx"),
        P(None, "tp"),
    )
    return jax.shard_map(
        local,
        mesh=mesh,
        in_specs=placed,
        out_specs=(P("ctx", "tp"), P("ctx", "tp")),
        check_vma=False,
    )
```
